32 devices in a mesh: heads: 4 (over y, x), rows: 8 (over z, core).
Axes of the slice: x: 2, y: 2, z: 4, core: 2. Of those that a mesh axis runs over, the one named last changes fastest.
Arguments:
- layer_input: bfloat16 [17408, 768], P(('rows', 'heads')), may hold values from -6 to 6
- encoder_out: bfloat16 [16384, 768], P(('rows', 'heads')), may hold values from -6 to 6
- doc_lengths: int32 [16, 8], P('rows'), may hold values from 1 to 817, as said below
- self_query: bfloat16 [768, 768], P(None, 'heads'), may hold values from -0.21875 to 0.21875
- self_qbias: float32 [768], P('heads'), may hold values from -3 to 3
- self_key_weight: bfloat16 [768, 768], P(None, 'heads'), may hold values from -0.21875 to 0.21875
- self_value: bfloat16 [768, 768], P(None, 'heads'), may hold values from -0.21875 to 0.21875
- self_vbias: float32 [768], P('heads'), may hold values from -3 to 3
- self_out: bfloat16 [768, 768], P('heads'), may hold values from -1.5 to 1.5
- self_obias: float32 [768], replicated, may hold values from -2 to 2
- first_gain: float32 [768], replicated, may hold values from 0.5 to 1.5
- first_shift: float32 [768], replicated, may hold values from -2 to 2
- cross_query: bfloat16 [768, 768], P(None, 'heads'), may hold values from -0.21875 to 0.21875
- cross_qbias: float32 [768], P('heads'), may hold values from -3 to 3
- cross_key: bfloat16 [768, 768], P(None, 'heads'), may hold values from -0.21875 to 0.21875
- cross_value: bfloat16 [768, 768], P(None, 'heads'), may hold values from -0.21875 to 0.21875
- cross_vbias: float32 [768], P('heads'), may hold values from -3 to 3
- cross_out: bfloat16 [768, 768], P('heads'), may hold values from -3 to 3
- cross_obias: float32 [768], replicated, may hold values from -2 to 2
- second_gain: float32 [768], replicated, may hold values from 0.5 to 1.5
- second_shift: float32 [768], replicated, may hold values from -2 to 2
- up_weight: bfloat16 [768, 3072], replicated, may hold values from -0.21875 to 0.21875
- up_bias: float32 [3072], replicated, may hold values from -3 to 3
- down_weight: bfloat16 [3072, 768], replicated, may hold values from -0.109375 to 0.109375
- down_bias: float32 [768], replicated, may hold values from -2 to 2
- third_gain: float32 [768], replicated, may hold values from 0.5 to 1.5
- third_shift: float32 [768], replicated, may hold values from -2 to 2
- out_grad: bfloat16 [17408, 768], P(('rows', 'heads')), may hold values from -6 to 6
Outputs:
- output: bfloat16 [17408, 768], P(('rows', 'heads'))
- input_grad: bfloat16 [17408, 768], P(('rows', 'heads'))
- encoder_grad: bfloat16 [16384, 768], P(('rows', 'heads'))
- selfquery_grad: float32 [768, 768], P(None, 'heads')
- selfqbias_grad: float32 [768], P('heads')
- selfkey_grad: float32 [768, 768], P(None, 'heads')
- selfvalue_grad: float32 [768, 768], P(None, 'heads')
- selfvbias_grad: float32 [768], P('heads')
- selfout_grad: float32 [768, 768], P('heads')
- selfobias_grad: float32 [768], replicated
- firstgain_grad: float32 [768], replicated
- firstshift_grad: float32 [768], replicated
- crossquery_grad: float32 [768, 768], P(None, 'heads')
- crossqbias_grad: float32 [768], P('heads')
- crosskey_grad: float32 [768, 768], P(None, 'heads')
- crossvalue_grad: float32 [768, 768], P(None, 'heads')
- crossvbias_grad: float32 [768], P('heads')
- crossout_grad: float32 [768, 768], P('heads')
- crossobias_grad: float32 [768], replicated
- secondgain_grad: float32 [768], replicated
- secondshift_grad: float32 [768], replicated
- upweight_grad: float32 [768, 3072], P(None, ('heads', 'rows'))
- upbias_grad: float32 [3072], P(('heads', 'rows'))
- downweight_grad: float32 [3072, 768], P(('heads', 'rows'))
- downbias_grad: float32 [768], replicated
- thirdgain_grad: float32 [768], replicated
- thirdshift_grad: float32 [768], replicated
The draws below stay inside these ranges and needn't reach their ends.
Inputs may be any that keep to these rules, and one draw needn't show every extreme that they name: `doc_lengths`: each row's 8 lengths sum to 1088; exactly one of them is 817 and the others sum to 271.
All inputs are finite; a program needn't handle non-finite values.
Results may differ from the reference program's by a relative error of at most 0.025.
The reference program's roundings to bfloat16 on the way count: a program that leaves them out, or rounds other values in their place, can miss the bound.
Values may be sent and summed in bfloat16 or wider, within the bound.
No kernel may reach another device: no remote copies, remote signals or barrier semaphores. Data moves between devices by JAX's collectives and lax.ppermute only.
A program may use at most 192 MiB of HBM per device.

```python
import jax
import jax.numpy as jnp
from jax import lax

D = 768
HEADS = 12
HEAD = 64
FF = 3072
ROW_TOKEN_COUNT = 1088
ENC = 1024
DOCS = 8
NROWS = 16
TOKENS = 17408
ENC_TOK = 16384


def draw_doc_lengths(key, part):
    key = jax.random.fold_in(key, 7)
    rest = ROW_TOKEN_COUNT // 4 - 1
    longest = ROW_TOKEN_COUNT - rest

    def one_row(row_key):
        cut_key, place_key = jax.random.split(row_key)
        cuts = jnp.sort(jax.random.permutation(cut_key, rest - 1)[:DOCS - 2] + 1).astype(jnp.int32)
        bounds = jnp.concatenate([jnp.zeros((1,), jnp.int32), cuts, jnp.full((1,), rest, jnp.int32)])
        smaller = bounds[1:] - bounds[:-1]
        place = jax.random.randint(place_key, (), 0, DOCS)
        index = jnp.arange(DOCS, dtype=jnp.int32)
        before = smaller[jnp.minimum(index, DOCS - 2)]
        after = smaller[jnp.maximum(index - 1, 0)]
        return jnp.where(index < place, before, jnp.where(index == place, longest, after)).astype(jnp.int32)
    return jax.vmap(one_row)(jax.random.split(key, NROWS))


def block_levels(rng, shape, shards, least, high):
    def one(axis_at, shards_of):
        heights = jax.random.uniform(jax.random.fold_in(jax.random.fold_in(rng, 6), axis_at), (shards_of,), jnp.float32, least / len(shards), high / len(shards))
        return jnp.repeat(jnp.exp(heights), shape[axis_at] // shards_of).reshape((-1,) + (1,) * (len(shape) - axis_at - 1))

    loudness = one(*shards[0])
    for cut in shards[1:]:
        loudness = loudness * one(*cut)
    return loudness


def noise(key, shape, scale, reach, shards=(), held_as=jnp.bfloat16):
    level = block_levels(key, shape, shards, -0.22, 0.18) if shards else 1.0
    values = jax.random.normal(key, shape, jnp.float32) * scale * level
    return jnp.minimum(jnp.maximum(values, -reach), reach).astype(held_as)


def setup_inputs(seed: int = 0) -> dict:
    arg_keys = jax.random.split(jax.random.key(seed), 29)
    layer_input = noise(arg_keys[0], (TOKENS, D), 1.0, 6.0, ((0, 32),))
    encoder_out = noise(arg_keys[1], (ENC_TOK, D), 1.0, 6.0, ((0, 32),))
    doc_lengths = draw_doc_lengths(jax.random.fold_in(arg_keys[28], 71), 0)
    self_query = noise(arg_keys[3], (D, D), D ** -0.5, 0.21875, ((1, 4),))
    self_qbias = noise(arg_keys[4], (D,), 0.5, 3.0, ((0, 4),), jnp.float32)
    self_key_weight = noise(arg_keys[5], (D, D), D ** -0.5, 0.21875, ((1, 4),))
    self_value = noise(arg_keys[6], (D, D), D ** -0.5, 0.21875, ((1, 4),))
    self_vbias = noise(arg_keys[7], (D,), 0.5, 3.0, ((0, 4),), jnp.float32)
    self_out = noise(arg_keys[8], (D, D), (max(D // 48, 1)) ** -0.5, 1.5, ((0, 4),))
    self_obias = noise(arg_keys[9], (D,), 0.3, 2.0, (), jnp.float32)
    first_gain = jnp.clip(1.0 + 0.1 * jax.random.normal(arg_keys[10], (D,), jnp.float32), 0.5, 1.5)
    first_shift = noise(arg_keys[11], (D,), 0.3, 2.0, (), jnp.float32)
    cross_query = noise(arg_keys[12], (D, D), D ** -0.5, 0.21875, ((1, 4),))
    cross_qbias = noise(arg_keys[13], (D,), 0.5, 3.0, ((0, 4),), jnp.float32)
    cross_key = noise(arg_keys[14], (D, D), D ** -0.5, 0.21875, ((1, 4),))
    cross_value = noise(arg_keys[15], (D, D), D ** -0.5, 0.21875, ((1, 4),))
    cross_vbias = noise(arg_keys[16], (D,), 0.5, 3.0, ((0, 4),), jnp.float32)
    cross_out = noise(arg_keys[17], (D, D), (max(D // 192, 1)) ** -0.5, 3.0, ((0, 4),))
    cross_obias = noise(arg_keys[18], (D,), 0.3, 2.0, (), jnp.float32)
    second_gain = jnp.clip(1.0 + 0.1 * jax.random.normal(arg_keys[19], (D,), jnp.float32), 0.5, 1.5)
    second_shift = noise(arg_keys[20], (D,), 0.3, 2.0, (), jnp.float32)
    up_weight = noise(arg_keys[21], (D, FF), D ** -0.5, 0.21875)
    up_bias = noise(arg_keys[22], (FF,), 0.5, 3.0, (), jnp.float32)
    down_weight = noise(arg_keys[23], (FF, D), FF ** -0.5, 0.109375)
    down_bias = noise(arg_keys[24], (D,), 0.3, 2.0, (), jnp.float32)
    third_gain = jnp.clip(1.0 + 0.1 * jax.random.normal(arg_keys[25], (D,), jnp.float32), 0.5, 1.5)
    third_shift = noise(arg_keys[26], (D,), 0.3, 2.0, (), jnp.float32)
    out_grad = noise(arg_keys[27], (TOKENS, D), 1.0, 6.0, ((0, 32),))
    return dict(layer_input=layer_input, encoder_out=encoder_out, doc_lengths=doc_lengths, self_query=self_query, self_qbias=self_qbias, self_key_weight=self_key_weight, self_value=self_value, self_vbias=self_vbias, self_out=self_out, self_obias=self_obias, first_gain=first_gain, first_shift=first_shift, cross_query=cross_query, cross_qbias=cross_qbias, cross_key=cross_key, cross_value=cross_value, cross_vbias=cross_vbias, cross_out=cross_out, cross_obias=cross_obias, second_gain=second_gain, second_shift=second_shift, up_weight=up_weight, up_bias=up_bias, down_weight=down_weight, down_bias=down_bias, third_gain=third_gain, third_shift=third_shift, out_grad=out_grad)


EPS = 1e-05
HIGHEST = lax.Precision.HIGHEST

@jax.custom_vjp
def low(v):
    return lax.optimization_barrier(v.astype(jnp.bfloat16)).astype(jnp.float32)

@jax.custom_vjp
def low_back(v):
    return v

def low_keep(v):
    return (low(v), None)

def low_pass(kept, grad):
    return (grad,)

def back_keep(v):
    return (v, None)

def back_low(kept, grad):
    return (low(grad),)
low.defvjp(low_keep, low_pass)
low_back.defvjp(back_keep, back_low)

def matrix_product(left, right):
    return jnp.dot(left, right, precision=HIGHEST, preferred_element_type=jnp.float32)

def layer_norm(values, gain, shift):
    center = values - lax.optimization_barrier(jnp.mean(values, axis=-1, keepdims=True))
    spread = lax.optimization_barrier(jnp.mean(center * center, axis=-1, keepdims=True))
    return center * lax.rsqrt(spread + EPS) * gain + shift

def segments(doc_lengths):
    ends = jnp.cumsum(doc_lengths, axis=1)
    position = jnp.arange(ROW_TOKEN_COUNT, dtype=jnp.int32)
    return lax.optimization_barrier(jnp.sum((position[None, :, None] >= ends[:, None, :]).astype(jnp.int32), axis=2))

def attend(query, keys, values, allowed):
    scores = low_back(jnp.einsum('qhe,khe->hqk', query, keys, precision=HIGHEST))
    scores = jnp.where(allowed[None], scores, -1000000000.0)
    highest = lax.optimization_barrier(jnp.max(scores, axis=2, keepdims=True))
    raised = jnp.exp(scores - highest)
    shares = low(raised / lax.optimization_barrier(jnp.sum(raised, axis=2, keepdims=True)))
    return jnp.einsum('hqk,khe->qhe', shares, values, precision=HIGHEST)

def self_block(pack):
    query, keys, values, segment_row = pack
    position = jnp.arange(ROW_TOKEN_COUNT, dtype=jnp.int32)
    allowed = (segment_row[:, None] == segment_row[None, :]) & (position[None, :] <= position[:, None])
    return attend(query, keys, values, allowed)

def cross_block(pack):
    query, keys, values = pack
    return attend(query, keys, values, jnp.ones((ROW_TOKEN_COUNT, ENC), dtype=jnp.bool_))

def forward(segment_ids, layer_input, encoder_out, self_query, self_qbias, self_key_weight, self_value, self_vbias, self_out, self_obias, first_gain, first_shift, cross_query, cross_qbias, cross_key, cross_value, cross_vbias, cross_out, cross_obias, second_gain, second_shift, up_weight, up_bias, down_weight, down_bias, third_gain, third_shift):
    query = low_back(low((matrix_product(layer_input, self_query) + self_qbias) * 0.125)).reshape(NROWS, ROW_TOKEN_COUNT, HEADS, HEAD)
    keys = low_back(low(matrix_product(layer_input, self_key_weight))).reshape(NROWS, ROW_TOKEN_COUNT, HEADS, HEAD)
    values = low_back(low(matrix_product(layer_input, self_value) + self_vbias)).reshape(NROWS, ROW_TOKEN_COUNT, HEADS, HEAD)
    attended = lax.map(jax.checkpoint(self_block), (query, keys, values, segment_ids))
    attended = low_back(low(attended.reshape(TOKENS, D)))
    branch = low_back(matrix_product(attended, self_out) + self_obias)
    first_hidden = layer_norm(layer_input + branch, first_gain, first_shift)
    first_low = low(first_hidden)
    cquery = low_back(low((matrix_product(first_low, cross_query) + cross_qbias) * 0.125)).reshape(NROWS, ROW_TOKEN_COUNT, HEADS, HEAD)
    ckeys = low_back(low(matrix_product(encoder_out, cross_key))).reshape(NROWS, ENC, HEADS, HEAD)
    cvalues = low_back(low(matrix_product(encoder_out, cross_value) + cross_vbias)).reshape(NROWS, ENC, HEADS, HEAD)
    crossed = lax.map(jax.checkpoint(cross_block), (cquery, ckeys, cvalues))
    crossed = low_back(low(crossed.reshape(TOKENS, D)))
    branch = low_back(matrix_product(crossed, cross_out) + cross_obias)
    second_hidden = layer_norm(first_hidden + branch, second_gain, second_shift)
    second_low = low(second_hidden)
    upper = low_back(matrix_product(second_low, up_weight) + up_bias)
    active = low(jax.nn.gelu(upper, approximate=False))
    branch = low_back(matrix_product(active, down_weight) + down_bias)
    return layer_norm(second_hidden + branch, third_gain, third_shift)

def reference(layer_input, encoder_out, doc_lengths, self_query, self_qbias, self_key_weight, self_value, self_vbias, self_out, self_obias, first_gain, first_shift, cross_query, cross_qbias, cross_key, cross_value, cross_vbias, cross_out, cross_obias, second_gain, second_shift, up_weight, up_bias, down_weight, down_bias, third_gain, third_shift, out_grad):
    segment_ids = segments(doc_lengths)
    inputs = [array.astype(jnp.float32) for array in (layer_input, encoder_out, self_query, self_qbias, self_key_weight, self_value, self_vbias, self_out, self_obias, first_gain, first_shift, cross_query, cross_qbias, cross_key, cross_value, cross_vbias, cross_out, cross_obias, second_gain, second_shift, up_weight, up_bias, down_weight, down_bias, third_gain, third_shift)]
    result, backward = jax.vjp(lambda *items: forward(segment_ids, *items), *inputs)
    grads = backward(out_grad.astype(jnp.float32))
    return (result.astype(jnp.bfloat16), grads[0].astype(jnp.bfloat16), grads[1].astype(jnp.bfloat16), grads[2], grads[3], grads[4], grads[5], grads[6], grads[7], grads[8], grads[9], grads[10], grads[11], grads[12], grads[13], grads[14], grads[15], grads[16], grads[17], grads[18], grads[19], grads[20], grads[21], grads[22], grads[23], grads[24], grads[25])
```

```python
import jax
import jax.numpy as jnp
from jax import lax
from jax.experimental import pallas as pl
from jax.experimental.pallas import tpu as pltpu
from jax.sharding import PartitionSpec as P

BF = jnp.bfloat16
F32 = jnp.float32
HEAD = 64
PAIR = 128
EPS = 1e-05
ROW = 1088
CHUNK = 272
OWN = 544
ENC = 1024
HALF_ENC = 512
D = 768
GROUP = 192
PIECE = 96
FF = 3072
MIB = 1 << 20


def nn(a, b):
    return jnp.dot(a, b, preferred_element_type=F32)


def nt(a, b):
    return lax.dot_general(a, b, (((1,), (1,)), ((), ())), preferred_element_type=F32)


def tn(a, b):
    return lax.dot_general(a, b, (((0,), (0,)), ((), ())), preferred_element_type=F32)


def lane_ids(shape):
    return lax.broadcasted_iota(jnp.int32, shape, len(shape) - 1)


def pair_lanes(p):
    return pl.ds(pl.multiple_of(p * PAIR, PAIR), PAIR)


def normalize(total):
    center = total - jnp.mean(total, axis=-1, keepdims=True)
    scale = lax.rsqrt(jnp.mean(center * center, axis=-1, keepdims=True) + EPS)
    return center * scale, scale


def norm_back(grad, hat, scale, gain):
    scaled = grad * gain
    inner = scaled - jnp.mean(scaled, axis=-1, keepdims=True)
    return scale * (inner - hat * jnp.mean(scaled * hat, axis=-1, keepdims=True))


def column(values):
    return jnp.sum(values.astype(F32), axis=0, keepdims=True)


def pick_lane(ref, rows, lane):
    block = ref[rows, :]
    return jnp.sum(jnp.where(lane_ids(block.shape) == lane, block, 0.0), axis=-1, keepdims=True)


def weight_copies(w, slot, core, own, near, far, dst, sems, groups=(0, 1, 2, 3)):
    copies = []
    for n, i in enumerate(groups):
        base = GROUP * n
        if i == 0:
            copies.append(
                pltpu.make_async_copy(own[w], dst.at[pl.ds(base, GROUP)], sems.at[slot, 0])
            )
            continue
        rows = pl.ds(w * PIECE, PIECE)
        for which, refs in ((core, near), (1 - core, far)):
            to = pl.multiple_of(base + PIECE * which, PIECE)
            at = i if refs is near else 3 + i
            copies.append(
                pltpu.make_async_copy(
                    refs[i - 1].at[rows], dst.at[pl.ds(to, PIECE)], sems.at[slot, at]
                )
            )
    return copies


def gathered_bias(own_line, near, which):
    lines = [own_line]
    for ref in near:
        at = 3 * which
        split = ref[at : at + 3, :GROUP].astype(F32)
        lines.append(split[0:1] + split[1:2] + split[2:3])
    return jnp.concatenate(lines, axis=1)


def start(copies):
    for one in copies:
        one.start()


def finish(copies):
    for one in copies:
        one.wait()


def by_core(core, body):
    for value in (0, 1):

        @pl.when(core == value)
        def _():
            body(value)


def store_pieces(core, block, first_group, at, own, snd):
    def put(value):
        for g in range(block.shape[0] // GROUP):
            for half in (0, 1):
                row = g * GROUP + half * PIECE
                target = own if half == value else snd
                target[first_group + g, at : at + PIECE, :] = block[row : row + PIECE]

    by_core(core, put)


def store_bias_rows(lines, own, snd, at):
    for i in range(2):
        block = jnp.concatenate([one[:, i * GROUP : (i + 1) * GROUP] for one in lines], axis=0)
        block = jnp.concatenate([block, jnp.zeros((len(lines), D - GROUP), F32)], axis=1)
        block = jnp.concatenate([block, jnp.zeros((32 - len(lines), D), F32)], axis=0).astype(BF)
        own[i, at : at + 32, :] = block
        snd[i, at : at + 32, :] = block


def forward_heads(q2, keys, values, bias, row_stats, p):
    lane = lane_ids(q2.shape)
    outs = []
    for t in (0, 1):
        query = jnp.where((lane // HEAD) == t, q2, jnp.zeros_like(q2))
        scores = nt(query, keys)
        if bias is not None:
            scores = scores + bias
        highest = jnp.max(scores, axis=-1, keepdims=True)
        raised = jnp.exp(scores - highest)
        total = jnp.sum(raised, axis=-1, keepdims=True)
        outs.append(nn(raised.astype(BF), values) / total)
        row_stats = jnp.where(
            lane_ids(row_stats.shape) == 2 * p + t, highest + jnp.log(total), row_stats
        )
    return jnp.where((lane // HEAD) == 0, outs[0], outs[1]).astype(BF), row_stats


def backward_heads(q2, g2, o2, keys, values, bias, stats, p):
    lane = lane_ids(q2.shape)
    key_lane = lane_ids(keys.shape)
    product = g2.astype(F32) * o2.astype(F32)
    zero = jnp.zeros_like(q2)
    grad_q = grad_k = grad_v = 0.0
    for t in (0, 1):
        mine = (lane // HEAD) == t
        query = jnp.where(mine, q2, zero)
        grad = jnp.where(mine, g2, zero)
        inner = jnp.sum(jnp.where(mine, product, 0.0), axis=-1, keepdims=True)
        lse = jnp.sum(
            jnp.where(lane_ids(stats.shape) == 2 * p + t, stats, 0.0), axis=-1, keepdims=True
        )
        scores = nt(query, keys)
        if bias is not None:
            scores = scores + bias
        shares = jnp.exp(scores - lse)
        grad_shares = nt(grad, values)
        grad_scores = (shares * (grad_shares - inner)).astype(BF)
        grad_v = grad_v + tn(shares.astype(BF), grad)
        grad_k = grad_k + tn(grad_scores, query)
        grad_q = grad_q + nn(
            grad_scores, jnp.where((key_lane // HEAD) == t, keys, jnp.zeros_like(keys))
        )
    return grad_q, grad_k, grad_v


def document_ends(xa, place):
    pair_at = place[1] // 2
    lengths = jnp.where(
        pair_at == 0,
        xa[CHUNK : CHUNK + 1, :8].astype(F32) * 16.0 + xa[CHUNK + 2 : CHUNK + 3, :8].astype(F32),
        xa[CHUNK + 1 : CHUNK + 2, :8].astype(F32) * 16.0
        + xa[CHUNK + 3 : CHUNK + 4, :8].astype(F32),
    )
    ends, total = [], 0.0
    for d in range(8):
        total = total + lengths[:, d : d + 1]
        ends.append(total)
    return ends


def mask_bias(ends, chunk, width):
    qpos = chunk * CHUNK + lax.broadcasted_iota(jnp.int32, (CHUNK, 1), 0)
    kpos = lax.broadcasted_iota(jnp.int32, (1, width), 1)
    qat, kat = qpos.astype(F32), kpos.astype(F32)
    qseg = jnp.zeros((CHUNK, 1), F32)
    kseg = jnp.zeros((1, width), F32)
    for end in ends:
        qseg = qseg + jnp.where(qat >= end, 1.0, 0.0)
        kseg = kseg + jnp.where(kat >= end, 1.0, 0.0)
    return jnp.where((qseg == kseg) & (kpos <= qpos), 0.0, -1000000000.0)


def chunk_of(core, which):
    return (2 * core, 3 - 2 * core, 2 - 2 * core, 1 + 2 * core)[which]


def chunk_rows(core, which):
    return pl.ds(pl.multiple_of(chunk_of(core, which) * CHUNK, 16), CHUNK)


def key_counts(core):
    return ((0, 1), (1, 4)) if core == 0 else ((0, 3), (1, 2))


def self_forward(
    place, xa, xb, ya, yb, w0, w1, w2, n1, n2, n3, f1, f2, f3, qbias, vbias,
    q_out, k_out, v_out, att, stats,
    wq, wk, wv, bias, lines, sems, line_sems,
):
    core = place[0]
    near, far = (n1, n2, n3), (f1, f2, f3)
    bias_copies = [
        pltpu.make_async_copy(ref.at[pl.ds(4 * PIECE, 16)], lines.at[i], line_sems.at[i])
        for i, ref in enumerate(near)
    ]
    sets = [
        weight_copies(w, w, core, (w0, w1, w2), near, far, dst, sems)
        for w, dst in enumerate((wq, wk, wv))
    ]
    start(bias_copies)
    for one in sets:
        start(one)
    ends = document_ends(xa, place)
    for slot in (0, 1):
        bias[slot] = mask_bias(ends, chunk_of(core, slot), ROW)
    xs = (xa[0:CHUNK, :], xb[...], ya[0:CHUNK, :], yb[...])
    finish(bias_copies)
    held = [lines.at[i] for i in range(3)]
    finish(sets[0])
    line = gathered_bias(qbias[...], held, 0)
    for which in (0, 1):
        q_out[which * CHUNK : (which + 1) * CHUNK, :] = (
            (nt(xs[which], wq[...]) + line) * 0.125
        ).astype(BF)
    finish(sets[1])
    for which, x in enumerate(xs):
        k_out[chunk_rows(core, which), :] = nt(x, wk[...]).astype(BF)
    finish(sets[2])
    line = gathered_bias(vbias[...], held, 1)
    for which, x in enumerate(xs):
        v_out[chunk_rows(core, which), :] = (nt(x, wv[...]) + line).astype(BF)
    stats[...] = jnp.zeros_like(stats)

    def attend(value):
        def pair(p, carry):
            lanes = pair_lanes(p)
            for slot, count in key_counts(value):
                rows = pl.ds(slot * CHUNK, CHUNK)
                width = count * CHUNK
                out, now = forward_heads(
                    q_out[rows, lanes], k_out[0:width, lanes], v_out[0:width, lanes],
                    bias[slot, :, 0:width], stats[rows, :], p,
                )
                att[rows, lanes] = out
                stats[rows, :] = now
            return carry

        lax.fori_loop(0, 6, pair, 0)

    by_core(core, attend)


def self_finish(
    place, xa, xb, att, w3, n1, n2, n3, f1, f2, f3, obias,
    hat_out, scale_out, wo, sems,
):
    copies = weight_copies(
        3, 0, place[0], (None, None, None, w3), (n1, n2, n3), (f1, f2, f3), wo, sems
    )
    start(copies)
    finish(copies)
    for which, x in enumerate((xa[0:CHUNK, :], xb[...])):
        rows = pl.ds(which * CHUNK, CHUNK)
        total = x.astype(F32) + (nn(att[rows, :], wo[...]) + obias[...])
        hat, scale = normalize(total)
        hat_out[rows, :] = hat
        scale_out[rows, :] = jnp.broadcast_to(scale, (CHUNK, 128))


def cross_forward(
    place, hat1, gain1, shift1, ea, eb, w0, w1, w2, w3, n1, n2, n3, f1, f2, f3,
    qbias, vbias, obias,
    q_out, k_out, v_out, att, stats, hat_out,
    wq, wk, wv, wo, lines, sems, line_sems,
):
    core = place[0]
    near, far = (n1, n2, n3), (f1, f2, f3)
    bias_copies = [
        pltpu.make_async_copy(ref.at[pl.ds(4 * PIECE, 16)], lines.at[i], line_sems.at[i])
        for i, ref in enumerate(near)
    ]
    sets = [
        weight_copies(w, w, core, (w0, w1, w2, w3), near, far, dst, sems)
        for w, dst in enumerate((wq, wk, wv, wo))
    ]
    start(bias_copies)
    for one in (1, 2, 0, 3):
        start(sets[one])
    finish(bias_copies)
    held = [lines.at[i] for i in range(3)]
    finish(sets[1])
    for which, e in enumerate((ea, eb)):
        rows = pl.ds(which * HALF_ENC, HALF_ENC)
        k_out[rows, :] = nt(e[...], wk[...]).astype(BF)
    finish(sets[2])
    line = gathered_bias(vbias[...], held, 1)
    for which, e in enumerate((ea, eb)):
        rows = pl.ds(which * HALF_ENC, HALF_ENC)
        v_out[rows, :] = (nt(e[...], wv[...]) + line).astype(BF)
    finish(sets[0])
    line = gathered_bias(qbias[...], held, 0)
    for slot in (0, 1):
        rows = pl.ds(slot * CHUNK, CHUNK)
        hidden = (hat1[rows, :] * gain1[...] + shift1[...]).astype(BF)
        q_out[rows, :] = ((nt(hidden, wq[...]) + line) * 0.125).astype(BF)
    stats[...] = jnp.zeros_like(stats)

    def pair(p, carry):
        lanes = pair_lanes(p)
        for slot in (0, 1):
            rows = pl.ds(slot * CHUNK, CHUNK)
            out, now = forward_heads(
                q_out[rows, lanes], k_out[:, lanes], v_out[:, lanes], None, stats[rows, :], p
            )
            att[rows, lanes] = out
            stats[rows, :] = now
        return carry

    lax.fori_loop(0, 6, pair, 0)
    finish(sets[3])
    for slot in (0, 1):
        rows = pl.ds(slot * CHUNK, CHUNK)
        hidden = hat1[rows, :] * gain1[...] + shift1[...]
        total = hidden + (nn(att[rows, :], wo[...]) + obias[...])
        hat, scale = normalize(total)
        hat_out[rows, :] = hat
        block = stats[rows, :]
        stats[rows, :] = jnp.where(lane_ids(block.shape) == 12, scale, block)


FF_STEP = 512
FF_BLOCK = 384


def gelu_parts(u):
    size = jnp.abs(u)
    t = 1.0 / (1.0 + (0.3275911 * 0.7071067811865476) * size)
    poly = t * (
        0.254829592
        + t * (-0.284496736 + t * (1.421413741 + t * (-1.453152027 + t * 1.061405429)))
    )
    bell = jnp.exp(-0.5 * u * u)
    tail = 0.5 * poly * bell
    phi = jnp.where(u >= 0.0, 1.0 - tail, tail)
    return u * phi, phi + u * bell * 0.3989422804014327


def feed_forward(piece):
    def kernel(
        place, hat2, stats, gain2, shift2, up_hbm, up_bias, down_hbm, down_bias, gain3, shift3,
        ga, gb,
        out, dsecond, own, snd, vec, upb,
        up, down, active, slope, hid, total, third, sems,
    ):
        core, group = place[0], place[1]
        steps = FF // FF_STEP
        ups = [
            pltpu.make_async_copy(
                up_hbm.at[:, pl.ds(i * FF_STEP, FF_STEP)],
                up.at[:, pl.ds(i * FF_STEP, FF_STEP)],
                sems.at[0, i],
            )
            for i in range(steps)
        ]
        downs = [
            pltpu.make_async_copy(
                down_hbm.at[pl.ds(i * FF_STEP, FF_STEP)],
                down.at[pl.ds(i * FF_STEP, FF_STEP)],
                sems.at[1, i],
            )
            for i in range(steps)
        ]
        for i in range(steps):
            ups[i].start()
            downs[i].start()
        second = hat2[...] * gain2[...] + shift2[...]
        hid[...] = second.astype(BF)
        total[...] = second + down_bias[...]
        for i in range(steps):
            cols = pl.ds(i * FF_STEP, FF_STEP)
            ups[i].wait()
            u = nn(hid[...], up[:, cols]) + up_bias[:, cols]
            act, slo = gelu_parts(u)
            active[:, cols] = act.astype(BF)
            slope[:, cols] = slo
            downs[i].wait()
            total[...] += nn(active[:, cols], down[cols, :])
        hat3, scale3 = normalize(total[...])
        out[...] = (hat3 * gain3[...] + shift3[...]).astype(BF)
        grad = jnp.concatenate([ga[...], gb[...]], axis=0).astype(F32)
        vec[0:1, :] = column(grad * hat3)
        vec[1:2, :] = column(grad)
        dthird = norm_back(grad, hat3, scale3, gain3[...])
        total[...] = dthird
        third[...] = dthird.astype(BF)
        vec[2:3, :] = column(third[...])

        def block(i, carry):
            for s in (0, 1):
                at = pl.multiple_of((group ^ i) * D + s * FF_BLOCK, FF_BLOCK)
                cols = pl.ds(at, FF_BLOCK)
                du = (nt(third[...], down[cols, :]) * slope[:, cols]).astype(BF)
                upb[:, cols] = column(du)
                total[...] += nt(du, up[:, cols])
                grads = (tn(du, hid[...]).astype(BF), tn(active[:, cols], third[...]).astype(BF))

                def put(value):
                    for which in (0, 1):
                        for m in range(FF_BLOCK // piece):
                            target = own if m % 2 == value else snd
                            to = s * (FF_BLOCK // 2) + (m // 2) * piece
                            target[i, which, to : to + piece, :] = grads[which][
                                m * piece : (m + 1) * piece
                            ]

                by_core(core, put)
            return carry

        lax.fori_loop(0, 4, block, 0)
        grad = total[...]
        hat = hat2[...]
        scale = pick_lane(stats, slice(None), 12)
        vec[3:4, :] = column(grad * hat)
        vec[4:5, :] = column(grad)
        dsec = norm_back(grad, hat, scale, gain2[...])
        dsecond[...] = dsec
        vec[5:6, :] = column(dsec.astype(BF))
        vec[6:8, :] = jnp.zeros((2, D), F32)

    return kernel


def cross_pairs(first, grad, att, q, k, v, stats, dq, dk, dv):
    def pair(p, carry):
        lanes = pair_lanes(first + p)
        out = pair_lanes(p)
        grad_k = grad_v = 0.0
        for slot in (0, 1):
            rows = pl.ds(slot * CHUNK, CHUNK)
            gq, gk, gv = backward_heads(
                q[rows, lanes], grad[rows, lanes], att[rows, lanes], k[:, lanes], v[:, lanes],
                None, stats[rows, :], first + p,
            )
            dq[rows, out] = (gq * 0.125).astype(BF)
            grad_k = grad_k + gk
            grad_v = grad_v + gv
        dk[:, out] = grad_k.astype(BF)
        dv[:, out] = grad_v.astype(BF)
        return carry

    lax.fori_loop(0, 3, pair, 0)


def weight_grads(core, dq, dk, dv, queries, keys, own, snd):
    store_pieces(core, tn(dq[...], queries).astype(BF), 0, 0, own, snd)
    for which, full in ((1, dk), (2, dv)):
        block = 0.0
        for rows, x in keys:
            block = block + tn(full[rows, :], x)
        store_pieces(core, block.astype(BF), 0, which * PIECE, own, snd)
    store_bias_rows([column(dq[...]), column(dv[...])], own, snd, 3 * PIECE)


def out_grads(core, att, low, wo, grad, own, snd):
    for g in (0, 2):
        block = tn(att[:, g * GROUP : (g + 2) * GROUP], low[...]).astype(BF)
        store_pieces(core, block, g, 0, own, snd)
    grad[...] = nt(low[...], wo[...]).astype(BF)


def cross_backward_a(
    place, dsecond, att, q, k, v, stats, hat1, gain1, shift1, ea, eb,
    w0, w1, w2, w3, n1, n2, n3, f1, f2, f3,
    grad, dfirst, enc_own, enc_other, own, snd, own_o, snd_o,
    wq, wk, wv, wo, dq, dk, dv, low, sems,
):
    core = place[0]
    near, far, ws = (n1, n2, n3), (f1, f2, f3), (w0, w1, w2, w3)
    sets = [weight_copies(3, 3, core, ws, near, far, wo, sems)] + [
        weight_copies(w, w, core, ws, near, far, dst, sems, (2, 3))
        for w, dst in enumerate((wq, wk, wv))
    ]
    for one in sets:
        start(one)
    low[...] = dsecond[...].astype(BF)
    finish(sets[0])
    out_grads(core, att, low, wo, grad, own_o, snd_o)
    cross_pairs(3, grad, att, q, k, v, stats, dq, dk, dv)
    low[...] = (hat1[...] * gain1[...] + shift1[...]).astype(BF)
    halves = (pl.ds(0, HALF_ENC), pl.ds(HALF_ENC, HALF_ENC))
    weight_grads(
        core, dq, dk, dv, low[...], ((halves[0], ea[...]), (halves[1], eb[...])), own, snd
    )
    for one in sets[1:]:
        finish(one)
    for half, target in zip(halves, (enc_own, enc_other)):
        target[...] = nn(dk[half, :], wk[...]) + nn(dv[half, :], wv[...])
    dfirst[...] = dsecond[...] + nn(dq[...], wq[...])


def cross_backward_b(
    place, dfirst_a, enc_own_a, enc_other_a, grad, att, q, k, v, stats, hat1, scale1, gain1,
    shift1, ea, eb, w0, w1, w2, n1, n2, n3, f1, f2, f3,
    dfirst, enc_own, enc_other, own, snd, vec,
    wq, wk, wv, dq, dk, dv, low, sems,
):
    core = place[0]
    near, far, ws = (n1, n2, n3), (f1, f2, f3), (w0, w1, w2)
    sets = [
        weight_copies(w, w, core, ws, near, far, dst, sems, (0, 1))
        for w, dst in enumerate((wq, wk, wv))
    ]
    for one in sets:
        start(one)
    cross_pairs(0, grad, att, q, k, v, stats, dq, dk, dv)
    hat = hat1[...]
    low[...] = (hat * gain1[...] + shift1[...]).astype(BF)
    halves = (pl.ds(0, HALF_ENC), pl.ds(HALF_ENC, HALF_ENC))
    weight_grads(
        core, dq, dk, dv, low[...], ((halves[0], ea[...]), (halves[1], eb[...])), own, snd
    )
    for one in sets:
        finish(one)
    enc_own[...] = enc_own_a[...] + nn(dk[halves[0], :], wk[...]) + nn(dv[halves[0], :], wv[...])
    enc_other[...] = (
        enc_other_a[...] + nn(dk[halves[1], :], wk[...]) + nn(dv[halves[1], :], wv[...])
    ).astype(BF)
    total = dfirst_a[...] + nn(dq[...], wq[...])
    vec[0:1, :] = column(total * hat)
    vec[1:2, :] = column(total)
    dfi = norm_back(total, hat, scale1[:, 0:1], gain1[...])
    dfirst[...] = dfi
    vec[2:3, :] = column(dfi.astype(BF))
    vec[3:8, :] = jnp.zeros((5, D), F32)


def self_pairs(core, first, ends, grad, att, q, k, v, stats, dq, dk, dv, bias, sum_k, sum_v):
    for slot in (0, 1):
        bias[slot] = mask_bias(ends, chunk_of(core, slot), ROW)

    def attend(value):
        def pair(p, carry):
            lanes = pair_lanes(first + p)
            out = pair_lanes(p)
            sum_k[...] = jnp.zeros_like(sum_k)
            sum_v[...] = jnp.zeros_like(sum_v)
            for slot, count in key_counts(value):
                rows = pl.ds(slot * CHUNK, CHUNK)
                width = count * CHUNK
                gq, gk, gv = backward_heads(
                    q[rows, lanes], grad[rows, lanes], att[rows, lanes],
                    k[0:width, lanes], v[0:width, lanes],
                    bias[slot, :, 0:width], stats[rows, :], first + p,
                )
                dq[rows, out] = (gq * 0.125).astype(BF)
                sum_k[0:width, :] += gk
                sum_v[0:width, :] += gv
            dk[:, out] = sum_k[...].astype(BF)
            dv[:, out] = sum_v[...].astype(BF)
            return carry

        lax.fori_loop(0, 3, pair, 0)

    by_core(core, attend)


def self_part(core, first, ends, grad, att, q, k, v, stats, xs, sets, own, snd, scratch):
    wq, wk, wv, dq, dk, dv, bias, sum_k, sum_v = scratch
    self_pairs(core, first, ends, grad, att, q, k, v, stats, dq, dk, dv, bias, sum_k, sum_v)
    keys = [(chunk_rows(core, c4), x) for c4, x in enumerate(xs)]
    queries = jnp.concatenate([xs[0], xs[1]], axis=0)
    weight_grads(core, dq, dk, dv, queries, keys, own, snd)
    for one in sets:
        finish(one)
    parts = []
    for c4 in range(4):
        rows = chunk_rows(core, c4)
        part = nn(dk[rows, :], wk[...]) + nn(dv[rows, :], wv[...])
        if c4 < 2:
            part = part + nn(dq[c4 * CHUNK : (c4 + 1) * CHUNK, :], wq[...])
        parts.append(part)
    return parts


def self_backward_a(
    place, dfirst, att, q, k, v, stats, xa, xb, ya, yb, w0, w1, w2, w3, n1, n2, n3, f1, f2, f3,
    in_own, in_other, grad, own, snd, own_o, snd_o,
    wq, wk, wv, wo, dq, dk, dv, low, bias, sum_k, sum_v, sems,
):
    core = place[0]
    near, far, ws = (n1, n2, n3), (f1, f2, f3), (w0, w1, w2, w3)
    sets = [weight_copies(3, 3, core, ws, near, far, wo, sems)] + [
        weight_copies(w, w, core, ws, near, far, dst, sems, (2, 3))
        for w, dst in enumerate((wq, wk, wv))
    ]
    for one in sets:
        start(one)
    low[...] = dfirst[...].astype(BF)
    finish(sets[0])
    out_grads(core, att, low, wo, grad, own_o, snd_o)
    xs = (xa[0:CHUNK, :], xb[...], ya[0:CHUNK, :], yb[...])
    parts = self_part(
        core, 3, document_ends(xa, place), grad, att, q, k, v, stats, xs, sets[1:], own, snd,
        (wq, wk, wv, dq, dk, dv, bias, sum_k, sum_v),
    )
    for n in (0, 1):
        in_own[n] = parts[n] + dfirst[n * CHUNK : (n + 1) * CHUNK, :]
        in_other[n] = parts[2 + n]


def self_backward_b(
    place, grad, in_own_a, in_other_a, att, q, k, v, stats, xa, xb, ya, yb,
    w0, w1, w2, n1, n2, n3, f1, f2, f3,
    in_own, in_other, own, snd,
    wq, wk, wv, dq, dk, dv, bias, sum_k, sum_v, sems,
):
    core = place[0]
    near, far, ws = (n1, n2, n3), (f1, f2, f3), (w0, w1, w2)
    sets = [
        weight_copies(w, w, core, ws, near, far, dst, sems, (0, 1))
        for w, dst in enumerate((wq, wk, wv))
    ]
    for one in sets:
        start(one)
    xs = (xa[0:CHUNK, :], xb[...], ya[0:CHUNK, :], yb[...])
    parts = self_part(
        core, 0, document_ends(xa, place), grad, att, q, k, v, stats, xs, sets, own, snd,
        (wq, wk, wv, dq, dk, dv, bias, sum_k, sum_v),
    )
    for n in (0, 1):
        in_own[n] = parts[n] + in_own_a[n]
        in_other[n] = (parts[2 + n] + in_other_a[n]).astype(BF)


def mark(place):
    pass


def in_vmem(n):
    return [pl.BlockSpec(memory_space=pltpu.VMEM)] * n


def in_any(n):
    return [pl.BlockSpec(memory_space=pl.ANY)] * n


def call(kernel, specs, outs, scratch, args, name, pins=()):
    first = 1 + len(specs)
    last = first + len(pins)
    end = last + len(outs)

    def body(*refs):
        kernel(*refs[:first], *refs[last:end], *refs[end + 1 :])
        refs[end][...] = jnp.zeros((8, 128), F32)

    return pl.pallas_call(
        body,
        in_specs=[pl.BlockSpec(memory_space=pltpu.SMEM)] + specs + in_any(len(pins)),
        out_specs=in_vmem(len(outs) + 1),
        out_shape=[jax.ShapeDtypeStruct(shape, dtype) for shape, dtype in outs + [((8, 128), F32)]],
        scratch_shapes=scratch,
        compiler_params=pltpu.CompilerParams(vmem_limit_bytes=56 * MIB),
        cost_estimate=pl.CostEstimate(flops=1000, bytes_accessed=1000, transcendentals=0),
        name=name,
    )(*args, *pins)


def after(value, zero):
    return value + zero[0, 0].astype(value.dtype)


def solution(mesh):
    names = tuple(mesh.axis_names)
    heads, rows = mesh.shape["heads"], mesh.shape["rows"]
    depth = rows // 2
    piece = FF // (heads * rows)

    def send(value, where, label="moved"):
        pairs = []
        for r in range(rows):
            for h in range(heads):
                to_r, to_h = where(r, h)
                index = {"rows": (r, to_r), "heads": (h, to_h)}
                a = b = 0
                for name in names:
                    a = a * mesh.shape[name] + index[name][0]
                    b = b * mesh.shape[name] + index[name][1]
                pairs.append((a, b))
        with jax.named_scope(label):
            return lax.ppermute(value, names, pairs)

    def swap(r, h):
        return (r & ~1) | (h & 1), (h & ~1) | (r & 1)

    def swap_b(r, h):
        return (r & ~1) | (1 - (h & 1)), (h & ~1) | (r & 1)

    def swap_b_back(r, h):
        return (r & ~1) | (h & 1), (h & ~1) | (1 - (r & 1))

    def core_to(r, h):
        return r ^ 1, h

    def head_to(d):
        return lambda r, h: (r, h ^ d)

    def depth_to(d):
        return lambda r, h: (r ^ (2 * d), h)

    def unrelate(parts, k):
        parts = list(parts)
        bit = 1
        while bit < len(parts):
            odd = (k & bit) != 0
            parts = [jnp.where(odd, parts[n ^ bit], parts[n]) for n in range(len(parts))]
            bit *= 2
        return parts

    def shards(
        layer_input, encoder_out, doc_lengths,
        self_query, self_qbias, self_key_weight, self_value, self_vbias, self_out, self_obias,
        first_gain, first_shift,
        cross_query, cross_qbias, cross_key, cross_value, cross_vbias, cross_out, cross_obias,
        second_gain, second_shift, up_weight, up_bias, down_weight, down_bias,
        third_gain, third_shift, out_grad,
    ):
        h = lax.axis_index("heads")
        r = lax.axis_index("rows")
        core, k = r % 2, r // 2
        place = jnp.stack([core, h]).astype(jnp.int32)

        def line(vector):
            return vector.reshape(1, -1)

        def split_rows(biases):
            rows = []
            for one in biases:
                for _ in range(3):
                    top = one.astype(BF)
                    rows.append(top)
                    one = one - top.astype(F32)
            rows = jnp.stack(rows)
            return jnp.pad(rows, ((0, 16 - rows.shape[0]), (0, D - GROUP)))

        def half_of(parts, biases):
            rows = [lax.dynamic_slice_in_dim(one, core * PIECE, PIECE, axis=0) for one in parts]
            return jnp.concatenate(rows + [split_rows(biases)], axis=0)

        lengths = jnp.concatenate([doc_lengths // 16, doc_lengths % 16], axis=0).astype(BF)
        lengths = jnp.pad(lengths, ((0, 12), (0, D - 8)))
        xa = send(jnp.concatenate([layer_input[:CHUNK], lengths], axis=0), swap, "x_a")
        xb = send(layer_input[CHUNK:], swap_b, "x_b")
        self_own = [self_query.T, self_key_weight.T, self_value.T, self_out]
        mine = half_of(self_own, [self_qbias, self_vbias])
        self_near = [send(mine, head_to(d), "w_self_near") for d in (1, 2, 3)]
        ya = send(xa, core_to, "y_a")
        yb = send(xb, core_to, "y_b")
        self_far = [send(one, core_to, "w_self_far") for one in self_near]
        self_w = self_near + self_far
        (zero,) = call(mark, [], [], [], [place], "arrived", pins=self_near)
        cross_own = [cross_query.T, cross_key.T, cross_value.T, cross_out]
        mine = after(half_of(cross_own, [cross_qbias, cross_vbias]), zero)
        enc = after(encoder_out, zero)
        cross_near = [send(mine, head_to(d), "w_cross_near") for d in (1, 2, 3)]
        ea = send(enc, swap, "e_a")

        weight = pltpu.VMEM((D, D), BF)
        half_weight = pltpu.VMEM((D // 2, D), BF)
        half_tokens = pltpu.VMEM((OWN, D // 2), BF)
        bias_lines = [pltpu.VMEM((3, 16, D), BF)]
        masks = pltpu.VMEM((2, CHUNK, ROW), F32)
        token_bf = ((OWN, D), BF)
        token_f32 = ((OWN, D), F32)
        lines = ((OWN, 128), F32)
        dma = pltpu.SemaphoreType.DMA
        q, kk, v, att, stats1, zero = call(
            self_forward,
            in_vmem(4) + in_any(9) + in_vmem(2),
            [token_bf, ((ROW, D), BF), ((ROW, D), BF), token_bf, lines],
            [weight] * 3 + [masks] + bias_lines + [dma((3, 7)), dma((3,))],
            [place, xa, xb, ya, yb] + self_own[:3] + self_w + [line(self_qbias), line(self_vbias)],
            "self_forward", pins=[mine, enc],
        )
        cross_far = [send(after(one, zero), core_to, "w_cross_far") for one in cross_near]
        eb = send(after(ea, zero), core_to, "e_b")
        hat1, scale1, zero = call(
            self_finish,
            in_vmem(3) + in_any(7) + in_vmem(1),
            [token_f32, lines],
            [weight, dma((1, 7))],
            [place, xa, xb, att, self_own[3]] + self_w + [line(self_obias)],
            "self_finish", pins=cross_near + [ea],
        )
        ga = send(after(out_grad[:CHUNK], zero), swap, "g_a")
        gb = send(after(out_grad[CHUNK:], zero), swap_b, "g_b")
        cross_w = cross_near + cross_far
        cq, ck, cv, catt, stats2, hat2, zero = call(
            cross_forward,
            in_vmem(5) + in_any(10) + in_vmem(3),
            [token_bf, ((ENC, D), BF), ((ENC, D), BF), token_bf, lines, token_f32],
            [weight] * 4 + bias_lines + [dma((4, 7)), dma((3,))],
            [place, hat1, line(first_gain), line(first_shift), ea, eb] + cross_own + cross_w
            + [line(cross_qbias), line(cross_vbias), line(cross_obias)],
            "cross_forward",
        )
        ff_shape = ((4, 2, FF // 8, D), BF)
        out, dsecond, ff_own, ff_snd, vec_a, upb, zero = call(
            feed_forward(piece),
            in_vmem(4) + in_any(1) + in_vmem(1) + in_any(1) + in_vmem(5),
            [token_bf, token_f32, ff_shape, ff_shape, ((8, D), F32), ((1, FF), F32)],
            [
                pltpu.VMEM((D, FF), BF), pltpu.VMEM((FF, D), BF), pltpu.VMEM((OWN, FF), BF),
                pltpu.VMEM((OWN, FF), F32), pltpu.VMEM((OWN, D), BF), pltpu.VMEM((OWN, D), F32),
                pltpu.VMEM((OWN, D), BF), dma((2, FF // FF_STEP)),
            ],
            [
                place, hat2, stats2, line(second_gain), line(second_shift), up_weight,
                line(up_bias), down_weight, line(down_bias), line(third_gain), line(third_shift),
                ga, gb,
            ],
            "feed_forward",
        )

        ff_got = send(ff_snd, core_to, "ff_core")
        out_a = send(out[:CHUNK], swap, "out_a")
        out_b = send(out[CHUNK:], swap_b_back, "out_b")

        piece_rows = ((2, 3 * PIECE + 32, D), BF)
        out_rows = ((4, PIECE, D), BF)
        enc_f32 = ((HALF_ENC, D), F32)
        key_grads = [pltpu.VMEM((ENC, D // 2), BF)] * 2
        grad, dfirst_a, enc_own, enc_snd, ca_own, ca_snd, co_own, co_snd, zero = call(
            cross_backward_a,
            in_vmem(11) + in_any(10),
            [token_bf, token_f32, enc_f32, enc_f32, piece_rows, piece_rows, out_rows, out_rows],
            [half_weight] * 3 + [weight, half_tokens] + key_grads
            + [pltpu.VMEM((OWN, D), BF), dma((4, 7))],
            [place, dsecond, catt, cq, ck, cv, stats2, hat1, line(first_gain), line(first_shift),
             ea, eb] + cross_own + cross_w,
            "cross_backward_a",
        )

        def both(own, got, d, w):
            return own[d, w].astype(F32) + got[d, w].astype(F32)

        ff_x = after(jnp.stack([both(ff_own, ff_got, d, 0) for d in (1, 3)]).astype(BF), zero)
        ff_y = after(jnp.stack([both(ff_own, ff_got, d, 1) for d in (2, 3)]).astype(BF), zero)
        ff_gx = send(ff_x, head_to(1), "ff_heads")
        ff_gy = send(ff_y, head_to(2), "ff_heads")
        ca_got = send(after(ca_snd, zero), core_to, "ca_core")
        co_got = send(after(co_snd, zero), core_to, "co_core")
        dfirst, enc_own, enc_snd, cb_own, cb_snd, vec_b, zero = call(
            cross_backward_b,
            in_vmem(15) + in_any(9),
            [token_f32, enc_f32, ((HALF_ENC, D), BF), piece_rows, piece_rows, ((8, D), F32)],
            [half_weight] * 3 + [half_tokens] + key_grads
            + [pltpu.VMEM((OWN, D), BF), dma((3, 7))],
            [place, dfirst_a, enc_own, enc_snd, grad, catt, cq, ck, cv, stats2, hat1, scale1,
             line(first_gain), line(first_shift), ea, eb] + cross_own[:3] + cross_w,
            "cross_backward_b", pins=[ff_x, ff_y, out_a, out_b],
        )
        output = jnp.concatenate([out_a, out_b], axis=0)
        vectors = jnp.concatenate([vec_a[:6], vec_b[:3], upb.reshape(4, D)], axis=0)
        vectors = lax.all_gather(vectors, names)
        ff_x2 = after((both(ff_own, ff_got, 2, 0) + ff_gx[1].astype(F32)).astype(BF), zero)
        ff_y2 = after((both(ff_own, ff_got, 1, 1) + ff_gy[1].astype(F32)).astype(BF), zero)
        ff_gx2 = send(ff_x2, head_to(2), "ff_heads_2")
        ff_gy2 = send(ff_y2, head_to(1), "ff_heads_2")
        cb_got = send(after(cb_snd, zero), core_to, "cb_core")
        enc_got = send(after(enc_snd, zero), core_to, "enc_core")

        slots_f32 = ((2, CHUNK, D), F32)
        row_grads = [pltpu.VMEM((ROW, D // 2), BF)] * 2
        sums = [pltpu.VMEM((ROW, PAIR), F32)] * 2
        in_own, in_snd, sgrad, sa_own, sa_snd, so_own, so_snd, zero = call(
            self_backward_a,
            in_vmem(10) + in_any(10),
            [slots_f32, slots_f32, token_bf, piece_rows, piece_rows, out_rows, out_rows],
            [half_weight] * 3 + [weight, half_tokens] + row_grads
            + [pltpu.VMEM((OWN, D), BF), masks] + sums + [dma((4, 7))],
            [place, dfirst, att, q, kk, v, stats1, xa, xb, ya, yb] + self_own + self_w,
            "self_backward_a", pins=[ff_x2, ff_y2, ca_got, co_got],
        )
        sa_got = send(after(sa_snd, zero), core_to, "sa_core")
        so_got = send(after(so_snd, zero), core_to, "so_core")

        def depth_parts(blocks):
            return lax.dynamic_index_in_dim(blocks, k, 0, keepdims=False), [
                lax.dynamic_index_in_dim(blocks, k ^ d, 0, keepdims=False).astype(BF)
                for d in range(1, depth)
            ]

        def depth_send(parts, label):
            return [send(one, depth_to(d + 1), label) for d, one in enumerate(parts)]

        def summed(first, rest):
            for one in rest:
                first = first + one.astype(F32)
            return first

        ff_up = both(ff_own, ff_got, 0, 0) + ff_gx[0].astype(F32) + ff_gx2.astype(F32)
        ff_down = both(ff_own, ff_got, 0, 1) + ff_gy[0].astype(F32) + ff_gy2.astype(F32)
        ff_sum = after(jnp.stack([ff_up, ff_down]), zero)
        ff_mine, ff_parts = depth_parts(ff_sum.reshape(2, depth, piece, D).swapaxes(0, 1))
        ff_back = depth_send(ff_parts, "ff_depth")
        enc_sum = after((enc_own + enc_got.astype(F32)).astype(BF), zero)
        encoder_g = send(enc_sum, swap, "enc_grad")

        class Heads:
            def __init__(self, a_own, a_got, b_own, b_got, o_own, o_got, zero, label):
                pairs = ((b_own, b_got), (a_own, a_got))
                cut = 2 * PIECE

                def first(d):
                    own, got = pairs[d // 2]
                    return own[d % 2, :cut].astype(F32) + got[d % 2, :cut].astype(F32)

                def last(d):
                    own, got = pairs[d // 2]
                    rest = own[d % 2, cut:].astype(F32) + got[d % 2, cut:].astype(F32)
                    return jnp.concatenate(
                        [rest, o_own[d].astype(F32) + o_got[d].astype(F32)], axis=0
                    )

                self.first, self.last, self.label = first, last, label
                self.x = after(jnp.stack([first(1), first(3)]).astype(BF), zero)
                self.y = after(jnp.stack([last(2), last(3)]).astype(BF), zero)
                self.gx = send(self.x, head_to(1), label)
                self.gy = send(self.y, head_to(2), label)

            def second(self):
                x = (self.first(2) + self.gx[1].astype(F32)).astype(BF)
                y = (self.last(1) + self.gy[1].astype(F32)).astype(BF)
                gx = send(x, head_to(2), self.label + "_2")
                gy = send(y, head_to(1), self.label + "_2")
                return jnp.concatenate(
                    [
                        self.first(0) + self.gx[0].astype(F32) + gx.astype(F32),
                        self.last(0) + self.gy[0].astype(F32) + gy.astype(F32),
                    ],
                    axis=0,
                )

        cross_heads = Heads(ca_own, ca_got, cb_own, cb_got, co_own, co_got, zero, "c_heads")
        in_own, in_snd, sb_own, sb_snd, zero = call(
            self_backward_b,
            in_vmem(12) + in_any(9),
            [slots_f32, ((2, CHUNK, D), BF), piece_rows, piece_rows],
            [half_weight] * 3 + [half_tokens] + row_grads + [masks] + sums + [dma((3, 7))],
            [place, sgrad, in_own, in_snd, att, q, kk, v, stats1, xa, xb, ya, yb]
            + self_own[:3] + self_w,
            "self_backward_b", pins=ff_parts + [cross_heads.x, cross_heads.y, enc_sum],
        )
        sb_got = send(sb_snd, core_to, "sb_core")
        in_got = send(in_snd, core_to, "in_core")
        self_heads = Heads(sa_own, sa_got, sb_own, sb_got, so_own, so_got, zero, "s_heads")
        totals = [after(cross_heads.second(), zero), self_heads.second()]
        ff = after(summed(ff_mine, ff_back), zero)
        upweight_g = ff[0].T
        downweight_g = ff[1]
        in_sum = (in_own + in_got.astype(F32)).astype(BF)
        input_g = jnp.concatenate(
            [send(in_sum[0], swap, "in_a"), send(in_sum[1], swap_b_back, "in_b")], axis=0
        )

        grads, bias_rows = [], []
        for total, label in zip(totals, ("c", "s")):
            size = total.shape[0]
            mine, parts = depth_parts(total.reshape(depth, size // depth, D))
            part = summed(mine, depth_send(parts, label + "_depth")).astype(BF)
            parts = unrelate(
                [part] + [send(part, depth_to(d), label + "_back") for d in range(1, depth)], k
            )
            mine = jnp.concatenate(parts, axis=0)
            other = send(mine, core_to, label + "_far")
            for at in (0, PIECE, 2 * PIECE, 3 * PIECE + 32):
                a, b = mine[at : at + PIECE], other[at : at + PIECE]
                grads.append(
                    jnp.concatenate(
                        [jnp.where(core == 0, a, b), jnp.where(core == 0, b, a)], axis=0
                    ).astype(F32)
                )
            bias_rows += [mine[3 * PIECE + n, :GROUP].astype(F32) for n in (0, 1)]
        cq_g, ck_g, cv_g, co_g, sq_g, sk_g, sv_g, so_g = grads
        cqb, cvb, sqb, svb = bias_rows
        vectors = jnp.sum(vectors, axis=0)
        ff_at = (h * rows + r) * piece
        upbias_g = lax.dynamic_slice_in_dim(vectors[9:].reshape(FF), ff_at, piece)
        return (
            output, input_g, encoder_g,
            sq_g.T, sqb, sk_g.T, sv_g.T, svb, so_g, vectors[8], vectors[6], vectors[7],
            cq_g.T, cqb, ck_g.T, cv_g.T, cvb, co_g, vectors[5],
            vectors[3], vectors[4], upweight_g, upbias_g, downweight_g, vectors[2],
            vectors[0], vectors[1],
        )

    rowed, headed = P(("rows", "heads"), None), P(None, "heads")
    by_head, by_head_rows, whole = P("heads"), P("heads", None), P()
    ffed = ("heads", "rows")
    return jax.shard_map(
        shards,
        mesh=mesh,
        in_specs=(
            rowed, rowed, P("rows", None),
            headed, by_head, headed, headed, by_head, by_head_rows, whole, whole, whole,
            headed, by_head, headed, headed, by_head, by_head_rows, whole, whole, whole,
            whole, whole, whole, whole, whole, whole, rowed,
        ),
        out_specs=(
            rowed, rowed, rowed,
            headed, by_head, headed, headed, by_head, by_head_rows, whole, whole, whole,
            headed, by_head, headed, headed, by_head, by_head_rows, whole, whole, whole,
            P(None, ffed), P(ffed), P(ffed, None), whole, whole, whole,
        ),
        check_vma=False,
    )
```

```python
import jax
import jax.numpy as jnp
from jax import lax
from jax.experimental import pallas as pl
from jax.experimental.pallas import tpu as pltpu
from jax.sharding import PartitionSpec as P

BF = jnp.bfloat16
F32 = jnp.float32
HEAD = 64
PAIR = 128
EPS = 1e-05
ROW = 1088
CHUNK = 272
OWN = 544
ENC = 1024
HALF_ENC = 512
D = 768
GROUP = 192
PIECE = 96
BIAS_ROWS = 16
FF = 3072
MIB = 1 << 20


def nn(a, b):
    return jnp.dot(a, b, preferred_element_type=F32)


def nt(a, b):
    return lax.dot_general(a, b, (((1,), (1,)), ((), ())), preferred_element_type=F32)


def tn(a, b):
    return lax.dot_general(a, b, (((0,), (0,)), ((), ())), preferred_element_type=F32)


def lane_ids(shape):
    return lax.broadcasted_iota(jnp.int32, shape, len(shape) - 1)


def pair_lanes(p):
    return pl.ds(pl.multiple_of(p * PAIR, PAIR), PAIR)


def normalize(total):
    center = total - jnp.mean(total, axis=-1, keepdims=True)
    scale = lax.rsqrt(jnp.mean(center * center, axis=-1, keepdims=True) + EPS)
    return center * scale, scale


def norm_back(grad, hat, scale, gain):
    scaled = grad * gain
    inner = scaled - jnp.mean(scaled, axis=-1, keepdims=True)
    return scale * (inner - hat * jnp.mean(scaled * hat, axis=-1, keepdims=True))


def column(values):
    return jnp.sum(values.astype(F32), axis=0, keepdims=True)


def pick_lane(ref, rows, lane):
    block = ref[rows, :]
    return jnp.sum(jnp.where(lane_ids(block.shape) == lane, block, 0.0), axis=-1, keepdims=True)


def start(copies):
    for one in copies:
        one.start()


def finish(copies):
    for one in copies:
        one.wait()


def by_core(core, body):
    for value in (0, 1):

        @pl.when(core == value)
        def _():
            body(value)


class Late:
    def __init__(self, source, held, sem):
        self.copy = pltpu.make_async_copy(source, held, sem)
        self.copy.start()
        self.held = held
        self.waited = False

    def get(self):
        if not self.waited:
            self.copy.wait()
            self.waited = True
        return self.held


class Early:
    def __init__(self, held, target, sem):
        self.copy = pltpu.make_async_copy(held, target, sem)
        self.held = held
        self.sent = False

    def send(self):
        self.copy.start()
        self.sent = True


def call(kernel, ins, outs, scratch, name, pins=()):
    vmem, anywhere = pl.BlockSpec(memory_space=pltpu.VMEM), pl.BlockSpec(memory_space=pltpu.HBM)
    smem = pl.BlockSpec(memory_space=pltpu.SMEM)
    specs = {"v": vmem, "a": anywhere, "l": anywhere, "e": anywhere, "s": smem}
    late = [(n, x) for n, (x, kind) in enumerate(ins) if kind == "l"]
    early = [(n, out) for n, out in enumerate(outs) if out[2] == "e"]
    first = len(ins)
    last = first + len(pins)
    end = last + len(outs)

    def body(*refs):
        took, gave, rest = list(refs[:first]), list(refs[last:end]), list(refs[end + 1 :])
        own, rest = rest[: len(scratch)], rest[len(scratch) :]
        for n, (at, _) in enumerate(late):
            took[at] = Late(took[at], rest[n], rest[-1].at[n])
        rest = rest[len(late) :]
        for n, (at, _) in enumerate(early):
            gave[at] = Early(rest[n], gave[at], rest[-1].at[len(late) + n])
        kernel(*took, *gave, *own)
        refs[end][...] = jnp.zeros((8, 128), F32)
        for at, _ in late:
            took[at].get()
        for at, _ in early:
            if not gave[at].sent:
                gave[at].send()
        for at, _ in early:
            gave[at].copy.wait()

    extra = [pltpu.VMEM(x.shape, x.dtype) for _, x in late]
    extra += [pltpu.VMEM(out[0], out[1]) for _, out in early]
    extra += [pltpu.SemaphoreType.DMA((max(len(late) + len(early), 1),))]
    return pl.pallas_call(
        body,
        in_specs=[specs[kind] for _, kind in ins] + [anywhere] * len(pins),
        out_specs=[specs[out[2]] for out in outs] + [vmem],
        out_shape=[jax.ShapeDtypeStruct(out[0], out[1]) for out in outs]
        + [jax.ShapeDtypeStruct((8, 128), F32)],
        scratch_shapes=list(scratch) + extra,
        compiler_params=pltpu.CompilerParams(vmem_limit_bytes=58 * MIB),
        cost_estimate=pl.CostEstimate(flops=1000, bytes_accessed=1000, transcendentals=0),
        name=name,
    )(*[x for x, _ in ins], *pins)


def after(value, zero):
    return value + zero[0, 0].astype(value.dtype)


def weight_copies(w, slot, core, own, near, far, dst, sems):
    copies = [pltpu.make_async_copy(own[w], dst.at[pl.ds(0, GROUP)], sems.at[slot, 0])]
    rows = pl.ds(w * PIECE, PIECE)
    for i in (1, 2, 3):
        for at, which, refs in ((i, core, near), (3 + i, 1 - core, far)):
            to = pl.multiple_of(GROUP * i + PIECE * which, PIECE)
            copies.append(
                pltpu.make_async_copy(
                    refs[i - 1].at[rows], dst.at[pl.ds(to, PIECE)], sems.at[slot, at]
                )
            )
    return copies


def bias_copies(near, lines, sems):
    return [
        pltpu.make_async_copy(ref.at[pl.ds(ref.shape[0] - 16, 16)], lines.at[i], sems.at[i])
        for i, ref in enumerate(near)
    ]


def gathered_bias(own_line, lines, which):
    parts = [own_line]
    for i in range(3):
        split = lines[i, 3 * which : 3 * which + 3, :GROUP].astype(F32)
        parts.append(split[0:1] + split[1:2] + split[2:3])
    return jnp.concatenate(parts, axis=1)


def put_rows(target, at, block):
    target[at : at + block.shape[0], :] = block


def store_pieces(core, block, places, own, snd):
    def put(value):
        for g, at in enumerate(places):
            for half in (0, 1):
                row = g * GROUP + half * PIECE
                put_rows(own if half == value else snd, at, block[row : row + PIECE])

    by_core(core, put)


def store_bias(row, places, own, snd):
    for i, at in enumerate(places):
        one = jnp.concatenate(
            [row[:, i * GROUP : (i + 1) * GROUP], jnp.zeros((1, D - GROUP), F32)], axis=1
        )
        block = jnp.concatenate([one, jnp.zeros((BIAS_ROWS - 1, D), F32)], axis=0).astype(BF)
        put_rows(own, at + PIECE, block)
        put_rows(snd, at + PIECE, block)


def forward_heads(q2, keys, values, bias, row_stats, p):
    lane = lane_ids(q2.shape)
    outs = []
    for t in (0, 1):
        query = jnp.where((lane // HEAD) == t, q2, jnp.zeros_like(q2))
        scores = nt(query, keys)
        if bias is not None:
            scores = scores + bias
        highest = jnp.max(scores, axis=-1, keepdims=True)
        raised = jnp.exp(scores - highest)
        total = jnp.sum(raised, axis=-1, keepdims=True)
        outs.append(nn(raised.astype(BF), values) / total)
        row_stats = jnp.where(
            lane_ids(row_stats.shape) == 2 * p + t, highest + jnp.log(total), row_stats
        )
    return jnp.where((lane // HEAD) == 0, outs[0], outs[1]).astype(BF), row_stats


def backward_heads(q2, g2, o2, keys, values, bias, stats, p):
    lane = lane_ids(q2.shape)
    key_lane = lane_ids(keys.shape)
    product = g2.astype(F32) * o2.astype(F32)
    zero = jnp.zeros_like(q2)
    grad_q = grad_k = grad_v = 0.0
    for t in (0, 1):
        mine = (lane // HEAD) == t
        query = jnp.where(mine, q2, zero)
        grad = jnp.where(mine, g2, zero)
        inner = jnp.sum(jnp.where(mine, product, 0.0), axis=-1, keepdims=True)
        lse = jnp.sum(
            jnp.where(lane_ids(stats.shape) == 2 * p + t, stats, 0.0), axis=-1, keepdims=True
        )
        scores = nt(query, keys)
        if bias is not None:
            scores = scores + bias
        shares = jnp.exp(scores - lse)
        grad_shares = nt(grad, values)
        grad_scores = (shares * (grad_shares - inner)).astype(BF)
        grad_v = grad_v + tn(shares.astype(BF), grad)
        grad_k = grad_k + tn(grad_scores, query)
        grad_q = grad_q + nn(
            grad_scores, jnp.where((key_lane // HEAD) == t, keys, jnp.zeros_like(keys))
        )
    return grad_q, grad_k, grad_v


def document_ends(xa, place):
    pair_at = place[1] // 2
    lengths = jnp.where(
        pair_at == 0,
        xa[0:1, :8] * 16.0 + xa[2:3, :8],
        xa[1:2, :8] * 16.0
        + xa[3:4, :8],
    )
    ends, total = [], 0.0
    for d in range(8):
        total = total + lengths[:, d : d + 1]
        ends.append(total)
    return ends


def mask_bias(ends, chunk, width):
    qpos = chunk * CHUNK + lax.broadcasted_iota(jnp.int32, (CHUNK, 1), 0)
    kpos = lax.broadcasted_iota(jnp.int32, (1, width), 1)
    qat, kat = qpos.astype(F32), kpos.astype(F32)
    qseg = jnp.zeros((CHUNK, 1), F32)
    kseg = jnp.zeros((1, width), F32)
    for end in ends:
        qseg = qseg + jnp.where(qat >= end, 1.0, 0.0)
        kseg = kseg + jnp.where(kat >= end, 1.0, 0.0)
    return jnp.where((qseg == kseg) & (kpos <= qpos), 0.0, -1000000000.0)


def chunk_of(core, which):
    return (2 * core, 3 - 2 * core, 2 - 2 * core, 1 + 2 * core)[which]


def chunk_rows(core, which):
    return pl.ds(pl.multiple_of(chunk_of(core, which) * CHUNK, 16), CHUNK)


def key_counts(core):
    return ((0, 1), (1, 4)) if core == 0 else ((0, 3), (1, 2))


def prepare(
    place, x, lengths, wq, wk, wv, qbias, vbias, so, cwq, cwk, cwv, cwo, cqbias, cvbias, out_grad,
    xa, xb, mine, mine_cross, ga, gb,
):
    core = place[0]
    ga[...] = out_grad[0:CHUNK, :]
    gb[...] = out_grad[CHUNK:OWN, :]
    xa[0:CHUNK, :] = x[0:CHUNK, :]
    xa[CHUNK : CHUNK + 16, :] = jnp.zeros((16, D), BF)
    xa[CHUNK : CHUNK + 16, 0:128] = lengths[...]
    xb[...] = x[CHUNK:OWN, :]
    prepare_weights(core, (wq, wk, wv), qbias, vbias, mine)
    prepare_weights(core, (cwq, cwk, cwv, cwo, so), cqbias, cvbias, mine_cross)


def prepare_weights(core, weights, qbias, vbias, mine):
    half = pl.ds(pl.multiple_of(core * PIECE, PIECE), PIECE)
    for w, one in enumerate(weights):
        mine[w * PIECE : (w + 1) * PIECE, :] = one[half, :]
    rows = []
    for one in (qbias[...], vbias[...]):
        for _ in range(3):
            top = one.astype(BF).astype(F32)
            rows.append(top)
            one = one - top
    rows = jnp.concatenate(rows + [jnp.zeros((10, GROUP), F32)], axis=0)
    at = len(weights) * PIECE
    mine[at : at + 16, :] = jnp.concatenate(
        [rows, jnp.zeros((16, D - GROUP), F32)], axis=1
    ).astype(BF)


def gate(*refs):
    pass


def row_copies(core, xs, full, sems):
    return [
        pltpu.make_async_copy(
            x.at[pl.ds(0, CHUNK)], full.at[chunk_rows(core, which)], sems.at[which]
        )
        for which, x in enumerate(xs)
    ]


def self_forward(
    place, xa, xb, ya, yb, w0, w1, w2, n1, n2, n3, f1, f2, f3, qbias, vbias,
    q_out, k_out, v_out, att, stats,
    wq, wk, wv, full, bias, lines, sems, line_sems, row_sems,
):
    core = place[0]
    near, far = (n1, n2, n3), (f1, f2, f3)
    sets = [
        weight_copies(w, w, core, (w0, w1, w2), near, far, dst, sems)
        for w, dst in enumerate((wq, wk, wv))
    ]
    held = bias_copies(near, lines, line_sems)
    rows = row_copies(core, (xa, xb, ya, yb), full, row_sems)
    start(rows)
    start(held)
    for one in sets:
        start(one)
    finish(rows[:1])
    tail = pltpu.make_async_copy(xa.at[pl.ds(CHUNK, 16)], lines.at[3], line_sems.at[3])
    tail.start()
    tail.wait()
    ends = document_ends(lines[3].astype(F32), place)
    for slot in (0, 1):
        bias[slot] = mask_bias(ends, chunk_of(core, slot), ROW)
    finish(rows[1:])
    finish(held)
    for one in sets:
        finish(one)
    line = gathered_bias(qbias[...], lines, 0)
    k_out.held[...] = nt(full[...], wk[...]).astype(BF)
    k_out.send()
    for which in (0, 1):
        q_out.held[which * CHUNK : (which + 1) * CHUNK, :] = (
            (nt(full[chunk_rows(core, which), :], wq[...]) + line) * 0.125
        ).astype(BF)
    q_out.send()
    line = gathered_bias(vbias[...], lines, 1)
    v_out.held[...] = (nt(full[...], wv[...]) + line).astype(BF)
    v_out.send()
    q, k, v = q_out.held, k_out.held, v_out.held
    stats[...] = jnp.zeros_like(stats)

    def attend(value):
        def pair(p, carry):
            lanes = pair_lanes(p)
            for slot, count in key_counts(value):
                rows = pl.ds(slot * CHUNK, CHUNK)
                width = count * CHUNK
                out, now = forward_heads(
                    q[rows, lanes], k[0:width, lanes], v[0:width, lanes],
                    bias[slot, :, 0:width], stats[rows, :], p,
                )
                att[rows, lanes] = out
                stats[rows, :] = now
            return carry

        lax.fori_loop(0, 6, pair, 0)

    by_core(core, attend)


def cross_forward(
    place, xa, xb, self_att, self_bias, gain1, shift1, ea, eb, w0, w1, w2, w3, w4, n1, n2, n3,
    f1, f2, f3, qbias, vbias, obias,
    hat1, scale1, q_out, k_out, v_out, att, stats, hat_out,
    wq, wk, wv, wo, full, lines, sems, line_sems, row_sems, self_wo, self_sems,
):
    core = place[0]
    near, far = (n1, n2, n3), (f1, f2, f3)
    rows = [
        pltpu.make_async_copy(e, full.at[pl.ds(i * HALF_ENC, HALF_ENC)], row_sems.at[i])
        for i, e in enumerate((ea, eb))
    ]
    held = bias_copies(near, lines, line_sems)
    sets = [
        weight_copies(w, w, core, (w0, w1, w2, w3), near, far, dst, sems)
        for w, dst in enumerate((wq, wk, wv, wo))
    ]
    self_set = weight_copies(
        4, 0, core, (None, None, None, None, w4), near, far, self_wo, self_sems
    )
    start(self_set)
    start(held)
    start(sets[0])
    start(rows)
    for one in sets[1:]:
        start(one)
    finish(self_set)
    product = nn(self_att[...], self_wo[...]) + self_bias[...]
    for which, x in enumerate((xa, xb)):
        part = slice(which * CHUNK, (which + 1) * CHUNK)
        hat, scale = normalize(x[0:CHUNK, :].astype(F32) + product[part])
        hat1.held[part, :] = hat
        scale1[part, :] = jnp.broadcast_to(scale, (CHUNK, 128))
    hat1.send()
    hidden = (hat1.held[...] * gain1[...] + shift1[...]).astype(BF)
    finish(held)
    finish(sets[0])
    line = gathered_bias(qbias[...], lines, 0)
    q_out.held[...] = ((nt(hidden, wq[...]) + line) * 0.125).astype(BF)
    q_out.send()
    finish(rows)
    finish(sets[1])
    k_out.held[...] = nt(full[...], wk[...]).astype(BF)
    k_out.send()
    finish(sets[2])
    line = gathered_bias(vbias[...], lines, 1)
    v_out.held[...] = (nt(full[...], wv[...]) + line).astype(BF)
    v_out.send()
    finish(sets[3])
    q, k, v = q_out.held, k_out.held, v_out.held
    stats[...] = jnp.zeros_like(stats)

    def pair(p, carry):
        lanes = pair_lanes(p)
        out, now = forward_heads(q[:, lanes], k[:, lanes], v[:, lanes], None, stats[...], p)
        att[:, lanes] = out
        stats[...] = now
        return carry

    lax.fori_loop(0, 6, pair, 0)
    hidden = hat1.held[...] * gain1[...] + shift1[...]
    hat, scale = normalize(hidden + (nn(att[...], wo[...]) + obias[...]))
    hat_out[...] = hat
    stats[...] = jnp.where(lane_ids(stats.shape) == 12, scale, stats[...])


FF_STEP = 512
FF_BLOCK = 768


def gelu_parts(u):
    size = jnp.abs(u)
    t = 1.0 / (1.0 + (0.3275911 * 0.7071067811865476) * size)
    poly = t * (
        0.254829592
        + t * (-0.284496736 + t * (1.421413741 + t * (-1.453152027 + t * 1.061405429)))
    )
    bell = jnp.exp(-0.5 * u * u)
    tail = 0.5 * poly * bell
    phi = jnp.where(u >= 0.0, 1.0 - tail, tail)
    return u * phi, phi + u * bell * 0.3989422804014327


def feed_forward(
    place, hat2, stats, gain2, shift2, up_hbm, up_bias, down_hbm, down_bias, gain3, shift3,
    ga, gb,
    out_a, out_b, dsecond, left, right, vec, upb,
    up, down, active, slope, hid, total, third, grads, sems, left_sems, right_sems,
):
    steps = FF // FF_STEP
    ups = [
        pltpu.make_async_copy(
            up_hbm.at[:, pl.ds(i * FF_STEP, FF_STEP)],
            up.at[:, pl.ds(i * FF_STEP, FF_STEP)],
            sems.at[0, i],
        )
        for i in range(steps)
    ]
    downs = [
        pltpu.make_async_copy(
            down_hbm.at[pl.ds(i * FF_STEP, FF_STEP)],
            down.at[pl.ds(i * FF_STEP, FF_STEP)],
            sems.at[1, i],
        )
        for i in range(steps)
    ]
    for i in range(steps):
        ups[i].start()
        downs[i].start()
    second = hat2[...] * gain2[...] + shift2[...]
    hid[...] = second.astype(BF)
    to_right = [
        pltpu.make_async_copy(ref, right.at[i], right_sems.at[i]) for i, ref in enumerate((hid, third))
    ]
    to_right[0].start()
    total[...] = second + down_bias[...]
    for i in range(steps):
        cols = pl.ds(i * FF_STEP, FF_STEP)
        ups[i].wait()
        u = nn(hid[...], up[:, cols]) + up_bias[:, cols]
        act, slo = gelu_parts(u)
        active[:, cols] = act.astype(BF)
        slope[:, cols] = slo
        downs[i].wait()
        total[...] += nn(active[:, cols], down[cols, :])
    to_left = [
        pltpu.make_async_copy(ref, left.at[i], left_sems.at[i])
        for i, ref in enumerate((grads, active))
    ]
    to_left[1].start()
    hat3, scale3 = normalize(total[...])
    out = (hat3 * gain3[...] + shift3[...]).astype(BF)
    out_a[...] = out[0:CHUNK]
    out_b[...] = out[CHUNK:OWN]
    grad = jnp.concatenate([ga.get()[...], gb.get()[...]], axis=0).astype(F32)
    vec[0:1, :] = column(grad * hat3)
    vec[1:2, :] = column(grad)
    dthird = norm_back(grad, hat3, scale3, gain3[...])
    total[...] = dthird
    third[...] = dthird.astype(BF)
    to_right[1].start()
    vec[2:3, :] = column(third[...])
    for i in range(FF // FF_BLOCK):
        cols = pl.ds(i * FF_BLOCK, FF_BLOCK)
        du = (nt(third[...], down[cols, :]) * slope[:, cols]).astype(BF)
        grads[:, cols] = du
        upb[:, cols] = column(du)
        total[...] += nt(du, up[:, cols])
    to_left[0].start()
    grad = total[...]
    hat = hat2[...]
    scale = pick_lane(stats, slice(None), 12)
    vec[3:4, :] = column(grad * hat)
    vec[4:5, :] = column(grad)
    dsec = norm_back(grad, hat, scale, gain2[...])
    dsecond[...] = dsec
    vec[5:6, :] = column(dsec.astype(BF))
    vec[6:8, :] = jnp.zeros((2, D), F32)
    finish(to_left)
    finish(to_right)


def ff_weight_grads(place, left, right, pins, out, held, left_held, right_held, sems):
    which = place[3]
    copies = [pltpu.make_async_copy(right.at[which], right_held, sems.at[0])]
    for i in range(4):
        cols = pl.ds(pl.multiple_of((place[1] ^ i) * D, D), D)
        copies.append(
            pltpu.make_async_copy(left.at[which, :, cols], left_held.at[i], sems.at[1 + i])
        )
    start(copies)
    copies[0].wait()
    outs = []
    for i in range(4):
        copies[1 + i].wait()
        rows = pl.ds(i * D, D)
        held[rows, :] = tn(left_held[i], right_held[...]).astype(BF)
        outs.append(pltpu.make_async_copy(held.at[rows], out.at[rows], sems.at[5 + i]))
        outs[i].start()
    finish(outs)


def out_grads(core, att, low, wo, grad, places, own, snd):
    store_pieces(core, tn(att[...], low[...]).astype(BF), places, own, snd)
    store_bias(jnp.zeros((1, D), F32), places, own, snd)
    grad[...] = nt(low[...], wo[...]).astype(BF)


def weight_grads(core, dq, dk, dv, queries, keys, places, own, snd):
    store_pieces(core, tn(dq[...], queries).astype(BF), places[0], own, snd)
    store_pieces(core, tn(dk[...], keys).astype(BF), places[1], own, snd)
    store_pieces(core, tn(dv[...], keys).astype(BF), places[2], own, snd)
    store_bias(column(dq[...]), places[0], own, snd)
    store_bias(jnp.zeros((1, dk.shape[1]), F32), places[1], own, snd)
    store_bias(column(dv[...]), places[2], own, snd)


def cross_part(core, first, grad, att, q, k, v, stats, queries, full, sets, places, own, snd, scratch):
    wq, wk, wv, dq, dk, dv = scratch
    q, k, v = q.get(), k.get(), v.get()

    def pair(p, carry):
        lanes = pair_lanes(first + p)
        out = pair_lanes(p)
        gq, gk, gv = backward_heads(
            q[:, lanes], grad[:, lanes], att[:, lanes], k[:, lanes], v[:, lanes],
            None, stats[...], first + p,
        )
        dq[:, out] = (gq * 0.125).astype(BF)
        dk[:, out] = gk.astype(BF)
        dv[:, out] = gv.astype(BF)
        return carry

    lax.fori_loop(0, 3, pair, 0)
    weight_grads(core, dq, dk, dv, queries(), full[...], places, own.held, snd.held)
    own.send()
    for one in sets:
        finish(one)
    return nn(dk[...], wk[...]) + nn(dv[...], wv[...]), nn(dq[...], wq[...])


def cross_backward_a(
    place, dsecond, att, q, k, v, stats, hat1, gain1, shift1, ea, eb,
    w0, w1, w2, w3, n1, n2, n3, f1, f2, f3,
    enc_out, dfirst, grad, own, snd,
    wq, wk, wv, wo, dq, dk, dv, low, full, sems, row_sems,
):
    core = place[0]
    near, far, ws = (n1, n2, n3), (f1, f2, f3), (w0, w1, w2, w3)
    sets = [weight_copies(3, 3, core, ws, near, far, wo, sems)] + [
        half_weight_copies(w, w, core, ws, near, far, 1, dst, sems)
        for w, dst in enumerate((wq, wk, wv))
    ]
    rows = [
        pltpu.make_async_copy(e, full.at[pl.ds(i * HALF_ENC, HALF_ENC)], row_sems.at[i])
        for i, e in enumerate((ea, eb))
    ]
    start(sets[0])
    start(rows)
    for one in sets[1:]:
        start(one)
    low[...] = dsecond[...].astype(BF)
    finish(sets[0])
    size = own.held.shape[0] // 10
    places = [[(4 * g + w) * size for g in (0, 1)] for w in range(3)]
    places_o = [8 * size, 9 * size, 3 * size, 7 * size]
    out_grads(core, att, low, wo, grad, places_o, own.held, snd.held)
    finish(rows)

    def queries():
        return (hat1.get()[...] * gain1[...] + shift1[...]).astype(BF)

    enc, mine = cross_part(
        core, 3, grad, att, q, k, v, stats, queries, full, sets[1:], places, own, snd,
        (wq, wk, wv, dq, dk, dv),
    )
    snd.send()
    enc_out[...] = enc
    dfirst[...] = dsecond[...] + mine


def cross_backward_b(
    place, enc_a, dfirst_a, grad, att, q, k, v, stats, hat1, scale1, gain1, shift1, ea, eb,
    vec_a, upb, w0, w1, w2, n1, n2, n3, f1, f2, f3,
    dfirst, enc_own, own, snd, vec,
    wq, wk, wv, dq, dk, dv, full, sems, row_sems,
):
    core = place[0]
    near, far, ws = (n1, n2, n3), (f1, f2, f3), (w0, w1, w2)
    sets = [
        half_weight_copies(w, w, core, ws, near, far, 0, dst, sems)
        for w, dst in enumerate((wq, wk, wv))
    ]
    rows = [
        pltpu.make_async_copy(e, full.at[pl.ds(i * HALF_ENC, HALF_ENC)], row_sems.at[i])
        for i, e in enumerate((ea, eb))
    ]
    start(rows)
    for one in sets:
        start(one)
    finish(rows)
    size = own.held.shape[0] // 6
    places = [[(3 * g + w) * size for g in (0, 1)] for w in range(3)]

    def queries():
        return (hat1.get()[...] * gain1[...] + shift1[...]).astype(BF)

    enc, mine = cross_part(
        core, 0, grad, att, q, k, v, stats, queries, full, sets, places, own, snd,
        (wq, wk, wv, dq, dk, dv),
    )
    enc = enc + enc_a.get()[...]
    enc_own.held[...] = enc[0:HALF_ENC]
    put_rows(snd.held, 6 * size, enc[HALF_ENC:ENC].astype(BF))
    snd.send()
    enc_own.send()
    total = dfirst_a.get()[...] + mine
    hat = hat1.get()[...]
    vec[0:6, :] = vec_a[0:6, :]
    vec[6:7, :] = column(total * hat)
    vec[7:8, :] = column(total)
    dfi = norm_back(total, hat, scale1[:, 0:1], gain1[...])
    dfirst[...] = dfi
    vec[8:9, :] = column(dfi.astype(BF))
    for n in range(4):
        vec[9 + n : 10 + n, :] = upb[:, n * D : (n + 1) * D]
    vec[13:16, :] = jnp.zeros((3, D), F32)


def self_part(core, first, ends, grad, att, q, k, v, stats, full, sets, places, own, snd, scratch):
    wq, wk, wv, dq, dk, dv, bias, sum_k, sum_v = scratch
    for slot in (0, 1):
        bias[slot] = mask_bias(ends, chunk_of(core, slot), ROW)
    q, k, v = q.get(), k.get(), v.get()

    def attend(value):
        def pair(p, carry):
            lanes = pair_lanes(first + p)
            out = pair_lanes(p)
            sum_k[...] = jnp.zeros_like(sum_k)
            sum_v[...] = jnp.zeros_like(sum_v)
            for slot, count in key_counts(value):
                rows = pl.ds(slot * CHUNK, CHUNK)
                width = count * CHUNK
                gq, gk, gv = backward_heads(
                    q[rows, lanes], grad[rows, lanes], att[rows, lanes],
                    k[0:width, lanes], v[0:width, lanes],
                    bias[slot, :, 0:width], stats[rows, :], first + p,
                )
                dq[rows, out] = (gq * 0.125).astype(BF)
                sum_k[0:width, :] += gk
                sum_v[0:width, :] += gv
            dk[:, out] = sum_k[...].astype(BF)
            dv[:, out] = sum_v[...].astype(BF)
            return carry

        lax.fori_loop(0, 3, pair, 0)

    by_core(core, attend)
    queries = jnp.concatenate([full[chunk_rows(core, n), :] for n in (0, 1)], axis=0)
    weight_grads(core, dq, dk, dv, queries, full[...], places, own.held, snd.held)
    own.send()
    for one in sets:
        finish(one)
    sum_all = nn(dk[...], wk[...]) + nn(dv[...], wv[...])
    return sum_all, nn(dq[...], wq[...])


def half_weight_copies(w, slot, core, own, near, far, half, dst, sems):
    copies = []
    rows = pl.ds(w * PIECE, PIECE)
    for n in (0, 1):
        i = 2 * half + n
        if i == 0:
            copies.append(
                pltpu.make_async_copy(own[w], dst.at[pl.ds(0, GROUP)], sems.at[slot, 0])
            )
            continue
        for at, which, refs in ((i, core, near), (3 + i, 1 - core, far)):
            to = pl.multiple_of(GROUP * n + PIECE * which, PIECE)
            copies.append(
                pltpu.make_async_copy(
                    refs[i - 1].at[rows], dst.at[pl.ds(to, PIECE)], sems.at[slot, at]
                )
            )
    return copies


def self_backward_a(
    place, dfirst, att, q, k, v, stats, xa, xb, ya, yb, w0, w1, w2, w3, n1, n2, n3, f1, f2, f3,
    m1, m2, m3, g1, g2, g3,
    sum_out, in_own, grad, own, snd,
    wq, wk, wv, wo, dq, dk, dv, low, bias, sum_k, sum_v, full, lines, sems, row_sems,
):
    core = place[0]
    near, far, ws = (n1, n2, n3), (f1, f2, f3), (w0, w1, w2)
    self_set = (None, None, None, None, w3)
    sets = [weight_copies(4, 3, core, self_set, (m1, m2, m3), (g1, g2, g3), wo, sems)] + [
        half_weight_copies(w, w, core, ws, near, far, 1, dst, sems)
        for w, dst in enumerate((wq, wk, wv))
    ]
    tail = pltpu.make_async_copy(xa.at[pl.ds(CHUNK, 16)], lines, row_sems.at[4])
    rows = row_copies(core, (xa, xb, ya, yb), full, row_sems)
    start(sets[0])
    tail.start()
    start(rows)
    for one in sets[1:]:
        start(one)
    low[...] = dfirst[...].astype(BF)
    finish(sets[0])
    size = own.held.shape[0] // 10
    places = [[(4 * g + w) * size for g in (0, 1)] for w in range(3)]
    places_o = [8 * size, 9 * size, 3 * size, 7 * size]
    out_grads(core, att, low, wo, grad, places_o, own.held, snd.held)
    tail.wait()
    finish(rows)
    sum_all, mine = self_part(
        core, 3, document_ends(lines[...].astype(F32), place), grad, att, q, k, v, stats, full,
        sets[1:], places, own, snd, (wq, wk, wv, dq, dk, dv, bias, sum_k, sum_v),
    )
    snd.send()
    sum_out[...] = sum_all
    in_own[...] = mine + dfirst[...]


def self_backward_b(
    place, grad, sum_a, in_own_a, att, q, k, v, stats, xa, xb, ya, yb,
    w0, w1, w2, n1, n2, n3, f1, f2, f3,
    in_own, own, snd,
    wq, wk, wv, dq, dk, dv, bias, sum_k, sum_v, full, total, lines, sems, row_sems,
):
    core = place[0]
    size = own.held.shape[0] // 6
    places = [[(3 * g + w) * size for g in (0, 1)] for w in range(3)]
    near, far, ws = (n1, n2, n3), (f1, f2, f3), (w0, w1, w2)
    sets = [
        half_weight_copies(w, w, core, ws, near, far, 0, dst, sems)
        for w, dst in enumerate((wq, wk, wv))
    ]
    tail = pltpu.make_async_copy(xa.at[pl.ds(CHUNK, 16)], lines, row_sems.at[4])
    rows = row_copies(core, (xa, xb, ya, yb), full, row_sems)
    tail.start()
    start(rows)
    for one in sets:
        start(one)
    tail.wait()
    finish(rows)
    sum_all, mine = self_part(
        core, 0, document_ends(lines[...].astype(F32), place), grad, att, q, k, v, stats, full,
        sets, places, own, snd, (wq, wk, wv, dq, dk, dv, bias, sum_k, sum_v),
    )
    total[...] = sum_all + sum_a.get()[...]
    mine = mine + in_own_a.get()[...]
    for n in (0, 1):
        in_own[n] = mine[n * CHUNK : (n + 1) * CHUNK] + total[chunk_rows(core, n), :]
        put_rows(snd.held, 6 * size + n * CHUNK, total[chunk_rows(core, 2 + n), :].astype(BF))
    snd.send()


def add_jobs(jobs, ins, store, held, sems):
    copies, at = [], 0
    for _, rows, sources in jobs:
        mine = []
        for operand, row in sources:
            mine.append(
                (
                    pltpu.make_async_copy(
                        ins[operand].at[pl.ds(row, rows)], held.at[pl.ds(at, rows)],
                        sems.at[len(copies) * 8 + len(mine)],
                    ),
                    at,
                )
            )
            at += rows
        copies.append(mine)
    for mine in copies:
        for copy, _ in mine:
            copy.start()
    for (place, rows, _), mine in zip(jobs, copies):
        total = 0.0
        for copy, row in mine:
            copy.wait()
            total = total + held[row : row + rows, :].astype(F32)
        store(place, total)


def job_rows(jobs):
    return sum(rows * len(sources) for _, rows, sources in jobs)


def add_call(name, place, arrays, outs, jobs, pins=()):
    count = len(arrays)

    def kernel(place, *refs):
        ins, targets = refs[:count], refs[count : count + len(outs)]
        held, out_held, sems, out_sems = refs[count + len(outs) :]
        copies = []

        def store(where, total):
            at = sum(outs[: where[0]]) + where[1]
            put_rows(out_held, at, total.astype(BF))
            rows = pl.ds(at, total.shape[0])
            copies.append(
                pltpu.make_async_copy(
                    out_held.at[rows],
                    targets[where[0]].at[pl.ds(where[1], total.shape[0])],
                    out_sems.at[len(copies)],
                )
            )
            copies[-1].start()

        add_jobs(jobs, ins, store, held, sems)
        finish(copies)

    dma = pltpu.SemaphoreType.DMA
    return call(
        kernel, [(place, "s")] + [(one, "a") for one in arrays],
        [((rows, D), BF, "a") for rows in outs],
        [
            pltpu.VMEM((job_rows(jobs), D), BF), pltpu.VMEM((sum(outs), D), BF),
            dma((8 * len(jobs),)), dma((len(jobs),)),
        ],
        name, pins=pins,
    )


def total_call(name, place, arrays, total_rows, jobs, groups, depth, pins=()):
    count = len(arrays)
    size = total_rows // groups // depth

    def kernel(place, *refs):
        mine, parts = refs[count], refs[count + 1 : count + depth]
        held, total, sems = refs[count + depth :]

        def store(row, value):
            put_rows(total, row, value)

        add_jobs(jobs, refs[:count], store, held, sems)
        for d in range(depth):
            for g in range(groups):
                at = pl.multiple_of(
                    g * (total_rows // groups) + (place[2] ^ d) * size, 8
                )
                block = total[pl.ds(at, size), :]
                if d == 0:
                    put_rows(mine, g * size, block)
                else:
                    put_rows(parts[d - 1], g * size, block.astype(BF))

    return call(
        kernel, [(place, "s")] + [(one, "a") for one in arrays],
        [((groups * size, D), F32, "v")] + [((groups * size, D), BF, "v")] * (depth - 1),
        [
            pltpu.VMEM((job_rows(jobs), D), BF), pltpu.VMEM((total_rows, D), F32),
            pltpu.SemaphoreType.DMA((8 * len(jobs),)),
        ],
        name, pins=pins,
    )


def spread(depth, groups):
    def kernel(place, own, other, *refs):
        outs, biases, total = refs[: 4 * groups], refs[4 * groups : -1], refs[-1]
        core, k = place[0], place[2]
        size = own.shape[0] // depth // groups
        for which, ref in enumerate((own, other)):
            for d in range(depth):
                for g in range(groups):
                    at = pl.multiple_of(g * depth * size + (k ^ d) * size, 8)
                    row = (d * groups + g) * size
                    total[which, pl.ds(at, size), :] = ref[row : row + size, :].astype(F32)
        rows = depth * size // 4
        for n, out in enumerate(outs):
            for which, half in ((0, core), (1, 1 - core)):
                to = pl.ds(pl.multiple_of(half * PIECE, PIECE), PIECE)
                out[to, :] = total[which, n * rows : n * rows + PIECE, :]
        for n, bias in enumerate(biases):
            at = (4 * (n // 2) + 2 * (n % 2)) * rows + PIECE
            bias[...] = total[0, at : at + 1, :GROUP]

    return kernel


def solution(mesh):
    names = tuple(mesh.axis_names)
    heads, rows = mesh.shape["heads"], mesh.shape["rows"]
    depth = rows // 2
    piece = FF // (heads * rows)
    weight_rows = PIECE + BIAS_ROWS
    while (4 * weight_rows) % (8 * depth):
        weight_rows += BIAS_ROWS
    def send(value, where, label="moved"):
        pairs = []
        for r in range(rows):
            for h in range(heads):
                to_r, to_h = where(r, h)
                index = {"rows": (r, to_r), "heads": (h, to_h)}
                a = b = 0
                for name in names:
                    a = a * mesh.shape[name] + index[name][0]
                    b = b * mesh.shape[name] + index[name][1]
                pairs.append((a, b))
        with jax.named_scope(label):
            return lax.ppermute(value, names, pairs)

    def swap(r, h):
        return (r & ~1) | (h & 1), (h & ~1) | (r & 1)

    def swap_b(r, h):
        return (r & ~1) | (1 - (h & 1)), (h & ~1) | (r & 1)

    def swap_b_back(r, h):
        return (r & ~1) | (h & 1), (h & ~1) | (1 - (r & 1))

    def core_to(r, h):
        return r ^ 1, h

    def head_to(d):
        return lambda r, h: (r, h ^ d)

    def depth_to(d):
        return lambda r, h: (r ^ (2 * d), h)

    def shards(
        layer_input, encoder_out, doc_lengths,
        self_query, self_qbias, self_key_weight, self_value, self_vbias, self_out, self_obias,
        first_gain, first_shift,
        cross_query, cross_qbias, cross_key, cross_value, cross_vbias, cross_out, cross_obias,
        second_gain, second_shift, up_weight, up_bias, down_weight, down_bias,
        third_gain, third_shift, out_grad,
    ):
        h = lax.axis_index("heads")
        r = lax.axis_index("rows")
        core, k = r % 2, r // 2
        place = jnp.stack([core, h, k]).astype(jnp.int32)

        def line(vector):
            return vector.reshape(1, -1)

        def v(*arrays):
            return [(one, "v") for one in arrays]

        def a(*arrays):
            return [(one, "a") for one in arrays]

        def l(*arrays):
            return [(one, "l") for one in arrays]

        here = [(place, "s")]

        lengths = jnp.concatenate([doc_lengths // 16, doc_lengths % 16], axis=0).astype(BF)
        lengths = jnp.pad(lengths, ((0, 12), (0, 120)))
        self_own = [self_query.T, self_key_weight.T, self_value.T]
        cross_own = [cross_query.T, cross_key.T, cross_value.T, cross_out, self_out]
        xa, xb, mine, mine_cross, ga, gb, _ = call(
            prepare,
            here + v(layer_input, lengths, *self_own, line(self_qbias), line(self_vbias), self_out)
            + v(*cross_own[:4], line(cross_qbias), line(cross_vbias), out_grad),
            [
                ((CHUNK + 16, D), BF, "v"), ((CHUNK, D), BF, "v"),
                ((3 * PIECE + 16, D), BF, "v"), ((5 * PIECE + 16, D), BF, "v"),
                ((CHUNK, D), BF, "v"), ((CHUNK, D), BF, "v"),
            ],
            [], "prepare",
        )

        def gather_groups(mine, label):
            x, y = send(mine, head_to(1), label), send(mine, head_to(2), label)
            return [x, y, send(x, head_to(2), label + "_2")]

        self_near = gather_groups(mine, "w_self_near")
        xa = send(xa, swap, "x_a")
        xb = send(xb, swap_b, "x_b")
        ya = send(xa, core_to, "y_a")
        yb = send(xb, core_to, "y_b")
        self_far = [send(one, core_to, "w_self_far") for one in self_near]
        self_w = self_near + self_far

        def gated(values, pins, name):
            count = len(values)
            anywhere = pl.BlockSpec(memory_space=pltpu.HBM)
            return pl.pallas_call(
                gate,
                in_specs=[anywhere] * (count + len(pins)),
                out_specs=[anywhere] * count,
                out_shape=[jax.ShapeDtypeStruct(one.shape, one.dtype) for one in values],
                input_output_aliases={n: n for n in range(count)},
                name=name,
            )(*values, *pins)

        mine_cross, enc = gated([mine_cross, encoder_out], self_near + [xa, xb], "gate_near")
        cross_near = gather_groups(mine_cross, "w_cross_near")
        ea = send(enc, swap, "e_a")

        dma = pltpu.SemaphoreType.DMA
        weight = pltpu.VMEM((D, D), BF)
        half_weight = pltpu.VMEM((D // 2, D), BF)
        masks = pltpu.VMEM((2, CHUNK, ROW), F32)
        lines_bf = pltpu.VMEM((4, 16, D), BF)
        row_full = pltpu.VMEM((ROW, D), BF)
        enc_full = pltpu.VMEM((ENC, D), BF)
        tokens = (OWN, D)
        q, kk, vv, att, stats1, zero = call(
            self_forward,
            here + a(xa, xb, ya, yb) + a(*self_own, *self_w) + v(line(self_qbias), line(self_vbias)),
            [
                (tokens, BF, "e"), ((ROW, D), BF, "e"), ((ROW, D), BF, "e"), (tokens, BF, "v"),
                ((OWN, 128), F32, "v"),
            ],
            [weight] * 3 + [row_full, masks, lines_bf, dma((3, 7)), dma((4,)), dma((4,))],
            "self_forward", pins=[mine_cross, enc],
        )
        *cross_near, ea, ga, gb = gated(cross_near + [ea, ga, gb], [zero], "gate_far")
        cross_far = [send(one, core_to, "w_cross_far") for one in cross_near]
        eb = send(ea, core_to, "e_b")
        ga = send(ga, swap, "g_a")
        gb = send(gb, swap_b, "g_b")
        cross_w = cross_near + cross_far
        hat1, scale1, cq, ck, cv, catt, stats2, hat2, zero = call(
            cross_forward,
            here + v(xa, xb, att, line(self_obias), line(first_gain), line(first_shift)) + a(ea, eb)
            + a(*cross_own, *cross_w) + v(line(cross_qbias), line(cross_vbias), line(cross_obias)),
            [
                (tokens, F32, "e"), ((OWN, 128), F32, "v"),
                (tokens, BF, "e"), ((ENC, D), BF, "e"), ((ENC, D), BF, "e"), (tokens, BF, "v"),
                ((OWN, 128), F32, "v"), (tokens, F32, "v"),
            ],
            [weight] * 4 + [
                enc_full, lines_bf, dma((4, 7)), dma((4,)), dma((2,)), weight, dma((1, 7)),
            ],
            "cross_forward",
        )
        chunk = ((CHUNK, D), BF, "v")
        out_a, out_b, dsecond, left, right, vec_a, upb, zero = call(
            feed_forward,
            here + v(hat2, stats2, line(second_gain), line(second_shift)) + a(up_weight)
            + v(line(up_bias)) + a(down_weight)
            + v(line(down_bias), line(third_gain), line(third_shift)) + l(ga, gb),
            [
                chunk, chunk, (tokens, F32, "v"), ((2, OWN, FF), BF, "a"), ((2, OWN, D), BF, "a"),
                ((8, D), F32, "v"), ((1, FF), F32, "v"),
            ],
            [
                pltpu.VMEM((D, FF), BF), pltpu.VMEM((FF, D), BF), pltpu.VMEM((OWN, FF), BF),
                pltpu.VMEM((OWN, FF), F32), pltpu.VMEM(tokens, BF), pltpu.VMEM(tokens, F32),
                pltpu.VMEM(tokens, BF), pltpu.VMEM((OWN, FF), BF), dma((2, FF // FF_STEP)),
                dma((2,)), dma((2,)),
            ],
            "feed_forward",
        )
        def ff_grads(which, pins):
            grads, zero = call(
                ff_weight_grads, [(jnp.concatenate([place, which[None]]), "s")] + a(left, right, pins),
                [((FF, D), BF, "a")],
                [
                    pltpu.VMEM((FF, D), BF), pltpu.VMEM((4, OWN, D), BF), pltpu.VMEM(tokens, BF),
                    dma((9,)),
                ],
                "ff_weight_grads",
            )
            return grads

        half = D // 2

        def ff_row(g, which):
            return g * D + which * half

        def both(row):
            return [(0, row), (1, row)]

        out_a = send(out_a, swap, "out_a")
        out_b = send(out_b, swap_b_back, "out_b")
        ff_snd = ff_grads((1 - core).astype(jnp.int32), zero)
        ff_got = send(ff_snd, core_to, "ff_core")
        ff_own = ff_grads(core.astype(jnp.int32), ff_snd)
        output = jnp.concatenate([out_a, out_b], axis=0)
        ff_x, ff_y, _ = add_call(
            "ff_add_1", place, [ff_own, ff_got], [D, D],
            [
                ((0, 0), half, both(ff_row(1, 0))), ((0, half), half, both(ff_row(3, 0))),
                ((1, 0), half, both(ff_row(2, 1))), ((1, half), half, both(ff_row(3, 1))),
            ],
            pins=[out_a, out_b],
        )
        ff_gx = send(ff_x, head_to(1), "ff_heads")
        ff_gy = send(ff_y, head_to(2), "ff_heads")

        wr = weight_rows
        rows_a = [((10 * wr, D), BF, "e")] * 2
        enc_grads = [pltpu.VMEM((ENC, D // 2), BF)] * 2
        half_tokens = pltpu.VMEM((OWN, D // 2), BF)
        enc_a, dfirst, cgrad, ca_own, ca_snd, zero = call(
            cross_backward_a,
            here + v(dsecond, catt) + l(cq, ck, cv) + v(stats2) + l(hat1)
            + v(line(first_gain), line(first_shift)) + a(ea, eb) + a(*cross_own[:4], *cross_w),
            [((ENC, D), F32, "v"), (tokens, F32, "v"), (tokens, BF, "v")] + rows_a,
            [half_weight] * 3 + [weight, half_tokens] + enc_grads
            + [pltpu.VMEM(tokens, BF), enc_full, dma((4, 7)), dma((2,))],
            "cross_backward_a", pins=[ff_x, ff_y],
        )
        (ca_snd,) = gated([ca_snd], [ff_gx, ff_gy], "gate_ca")
        ca_got = send(ca_snd, core_to, "ca_core")
        ff_x2, ff_y2, _ = add_call(
            "ff_add_2", place, [ff_own, ff_got, ff_gx, ff_gy], [half, half],
            [
                ((0, 0), half, both(ff_row(2, 0)) + [(2, half)]),
                ((1, 0), half, both(ff_row(1, 1)) + [(3, half)]),
            ],
            pins=[zero],
        )
        ff_gx2 = send(ff_x2, head_to(2), "ff_heads_2")
        ff_gy2 = send(ff_y2, head_to(1), "ff_heads_2")
        c_x3, _ = add_call(
            "c_add_1", place, [ca_own, ca_got], [4 * wr], [((0, 0), 4 * wr, both(4 * wr))],
            pins=[ff_x2],
        )
        c_gx3 = send(c_x3, head_to(1), "c_heads")
        dfirst, enc_own, cb_own, cb_snd, vectors, zero = call(
            cross_backward_b,
            here + l(enc_a, dfirst) + v(cgrad, catt) + l(cq, ck, cv) + v(stats2) + l(hat1)
            + v(scale1, line(first_gain), line(first_shift)) + a(ea, eb) + v(vec_a, upb)
            + a(*cross_own[:3], *cross_w),
            [
                (tokens, F32, "v"), ((HALF_ENC, D), F32, "e"),
                ((6 * wr, D), BF, "e"), ((6 * wr + HALF_ENC, D), BF, "e"), ((16, D), F32, "v"),
            ],
            [half_weight] * 3 + [half_tokens] + enc_grads + [enc_full, dma((4, 7)), dma((2,))],
            "cross_backward_b", pins=[ff_x2, ff_y2, c_x3],
        )
        vectors = lax.all_gather(vectors, names)
        (cb_snd,) = gated([cb_snd], [ff_gx2, ff_gy2, c_gx3], "gate_cb")
        cb_got = send(cb_snd, core_to, "cb_core")

        def depth_send(parts, label):
            return [send(one, depth_to(d + 1), label) for d, one in enumerate(parts)]

        ff_mine, *ff_parts, _ = total_call(
            "ff_add_3", place, [ff_own, ff_got, ff_gx, ff_gy, ff_gx2, ff_gy2], D,
            [
                (0, half, both(ff_row(0, 0)) + [(2, 0), (4, 0)]),
                (half, half, both(ff_row(0, 1)) + [(3, 0), (5, 0)]),
            ],
            1, depth, pins=[zero],
        )
        ff_back = depth_send(ff_parts, "ff_depth")
        c_y2, c_x1, _ = add_call(
            "c_add_2", place, [ca_own, ca_got, cb_own, cb_got, c_gx3], [4 * wr, 4 * wr],
            [
                ((0, 0), 4 * wr, both(0) + [(4, 0)]),
                ((1, 0), 3 * wr, [(2, 3 * wr), (3, 3 * wr)]), ((1, 3 * wr), wr, both(9 * wr)),
            ],
            pins=[ff_parts[0]],
        )
        c_gy2 = send(c_y2, head_to(2), "c_heads_2")
        c_gx1 = send(c_x1, head_to(1), "c_heads_2")

        row_grads = [pltpu.VMEM((ROW, D // 2), BF)] * 2
        sums = [pltpu.VMEM((ROW, PAIR), F32)] * 2
        sum_a, in_own, sgrad, sa_own, sa_snd, zero = call(
            self_backward_a,
            here + v(dfirst, att) + l(q, kk, vv) + v(stats1) + a(xa, xb, ya, yb)
            + a(*self_own, self_out, *self_w, *cross_w),
            [((ROW, D), F32, "v"), (tokens, F32, "v"), (tokens, BF, "v")] + rows_a,
            [half_weight] * 3 + [weight, half_tokens] + row_grads
            + [pltpu.VMEM(tokens, BF), masks] + sums
            + [row_full, pltpu.VMEM((16, D), BF), dma((4, 7)), dma((5,))],
            "self_backward_a", pins=[*ff_parts, c_y2, c_x1],
        )
        (sa_snd,) = gated([sa_snd], [*ff_back, c_gy2, c_gx1], "gate_sa")
        sa_got = send(sa_snd, core_to, "sa_core")
        c_mine, *c_parts, _ = total_call(
            "c_add_3", place, [ca_own, ca_got, cb_own, cb_got, c_gy2, c_gx1], 4 * wr,
            [
                (0, 3 * wr, [(2, 0), (3, 0), (4, 0), (5, 0)]),
                (3 * wr, wr, [(0, 8 * wr), (1, 8 * wr), (4, 3 * wr), (5, 3 * wr)]),
            ],
            1, depth, pins=[zero],
        )
        c_depth = depth_send(c_parts, "c_depth")
        enc_sum = after((enc_own + cb_got[6 * wr :].astype(F32)).astype(BF), zero)
        encoder_g = send(enc_sum, swap, "enc_grad")
        (s_y, _) = add_call(
            "s_add_1", place, [sa_own, sa_got], [8 * wr], [((0, 0), 8 * wr, both(0))],
            pins=[c_parts[0]],
        )
        s_gy = send(s_y, head_to(2), "s_heads")
        in_own, sb_own, sb_snd, zero = call(
            self_backward_b,
            here + v(sgrad) + l(sum_a, in_own) + v(att) + l(q, kk, vv) + v(stats1)
            + a(xa, xb, ya, yb) + a(*self_own, *self_w),
            [
                ((2, CHUNK, D), F32, "v"), ((6 * wr, D), BF, "e"),
                ((6 * wr + 2 * CHUNK, D), BF, "e"),
            ],
            [half_weight] * 3 + [half_tokens] + row_grads + [masks] + sums
            + [row_full, pltpu.VMEM((ROW, D), F32), pltpu.VMEM((16, D), BF), dma((3, 7)), dma((5,))],
            "self_backward_b", pins=[*c_parts, s_y, enc_sum],
        )
        (sb_snd,) = gated([sb_snd], [*c_depth, s_gy, encoder_g], "gate_sb")
        sb_got = send(sb_snd, core_to, "sb_core")

        def depth_sum(mine, got):
            for one in got:
                mine = mine + one.astype(F32)
            return mine

        c_part = after(depth_sum(c_mine, c_depth), zero).astype(BF)
        c_back = [send(c_part, depth_to(d), "c_back") for d in range(1, depth)]
        s_x, _ = add_call(
            "s_add_2", place, [sa_own, sa_got, sb_own, sb_got, s_gy], [4 * wr],
            [
                ((0, 0), 3 * wr, [(2, 3 * wr), (3, 3 * wr), (4, 4 * wr)]),
                ((0, 3 * wr), wr, both(9 * wr) + [(4, 7 * wr)]),
            ],
            pins=[c_part],
        )
        s_gx = send(s_x, head_to(1), "s_heads_2")
        in_sum = (in_own + sb_got[6 * wr :].reshape(2, CHUNK, D).astype(F32)).astype(BF)
        in_a = send(in_sum[0], swap, "in_a")
        in_b = send(in_sum[1], swap_b_back, "in_b")
        s_mine, *s_parts, _ = total_call(
            "s_add_3", place, [sa_own, sa_got, sb_own, sb_got, s_gy, s_gx], 4 * wr,
            [
                (0, 3 * wr, [(2, 0), (3, 0), (4, 0), (5, 0)]),
                (3 * wr, wr, [(0, 8 * wr), (1, 8 * wr), (4, 3 * wr), (5, 3 * wr)]),
            ],
            1, depth, pins=c_back,
        )
        s_depth = depth_send(s_parts, "s_depth")

        def whole_grads(part, back, label):
            own = jnp.concatenate([part] + back, axis=0)
            other = send(own, core_to, label + "_far")
            *grads, qbias, vbias, _ = call(
                spread(depth, 1), here + v(own, other),
                [((GROUP, D), F32, "v")] * 4 + [((1, GROUP), F32, "v")] * 2,
                [pltpu.VMEM((2, 4 * wr, D), F32)], label + "_spread",
            )
            return grads, qbias[0], vbias[0]

        (cq_g, ck_g, cv_g, co_g), cqb, cvb = whole_grads(c_part, c_back, "c")
        (s_part,) = gated([depth_sum(s_mine, s_depth).astype(BF)], [in_a, in_b, cq_g], "gate_back")
        s_back = [send(s_part, depth_to(d), "s_back") for d in range(1, depth)]
        (sq_g, sk_g, sv_g, so_g), sqb, svb = whole_grads(s_part, s_back, "s")
        input_g = jnp.concatenate([in_a, in_b], axis=0)

        ff = depth_sum(ff_mine, ff_back).reshape(2, piece, D)
        ff_here = lax.dynamic_index_in_dim(ff, core, 0, keepdims=False)
        ff_there = send(lax.dynamic_index_in_dim(ff, 1 - core, 0, keepdims=False), core_to, "ff_last")
        upweight_g = jnp.where(core == 0, ff_here, ff_there).T
        downweight_g = jnp.where(core == 0, ff_there, ff_here)

        vectors = jnp.sum(vectors, axis=0)
        ff_at = (h * rows + r) * piece
        upbias_g = lax.dynamic_slice_in_dim(vectors[9:13].reshape(FF), ff_at, piece)
        return (
            output, input_g, encoder_g,
            sq_g.T, sqb, sk_g.T, sv_g.T, svb, so_g, vectors[8], vectors[6], vectors[7],
            cq_g.T, cqb, ck_g.T, cv_g.T, cvb, co_g, vectors[5],
            vectors[3], vectors[4], upweight_g, upbias_g, downweight_g, vectors[2],
            vectors[0], vectors[1],
        )

    rowed, headed = P(("rows", "heads"), None), P(None, "heads")
    by_head, by_head_rows, whole = P("heads"), P("heads", None), P()
    ffed = ("heads", "rows")
    return jax.shard_map(
        shards,
        mesh=mesh,
        in_specs=(
            rowed, rowed, P("rows", None),
            headed, by_head, headed, headed, by_head, by_head_rows, whole, whole, whole,
            headed, by_head, headed, headed, by_head, by_head_rows, whole, whole, whole,
            whole, whole, whole, whole, whole, whole, rowed,
        ),
        out_specs=(
            rowed, rowed, rowed,
            headed, by_head, headed, headed, by_head, by_head_rows, whole, whole, whole,
            headed, by_head, headed, headed, by_head, by_head_rows, whole, whole, whole,
            P(None, ffed), P(ffed), P(ffed, None), whole, whole, whole,
        ),
        check_vma=False,
    )
```

```python
import jax
import jax.numpy as jnp
from jax import lax
from jax.experimental import pallas as pl
from jax.experimental.pallas import tpu as pltpu
from jax.sharding import PartitionSpec as P

BF = jnp.bfloat16
F32 = jnp.float32
HEAD = 64
PAIR = 128
EPS = 1e-05
ROW = 1088
CHUNK = 272
OWN = 544
ENC = 1024
HALF_ENC = 512
D = 768
GROUP = 192
PIECE = 96
BIAS_ROWS = 16
FF = 3072
MIB = 1 << 20


def nn(a, b):
    return jnp.dot(a, b, preferred_element_type=F32)


def nt(a, b):
    return lax.dot_general(a, b, (((1,), (1,)), ((), ())), preferred_element_type=F32)


def tn(a, b):
    return lax.dot_general(a, b, (((0,), (0,)), ((), ())), preferred_element_type=F32)


def lane_ids(shape):
    return lax.broadcasted_iota(jnp.int32, shape, len(shape) - 1)


def pair_lanes(p):
    return pl.ds(pl.multiple_of(p * PAIR, PAIR), PAIR)


def normalize(total):
    center = total - jnp.mean(total, axis=-1, keepdims=True)
    scale = lax.rsqrt(jnp.mean(center * center, axis=-1, keepdims=True) + EPS)
    return center * scale, scale


def norm_back(grad, hat, scale, gain):
    scaled = grad * gain
    inner = scaled - jnp.mean(scaled, axis=-1, keepdims=True)
    return scale * (inner - hat * jnp.mean(scaled * hat, axis=-1, keepdims=True))


def column(values):
    return jnp.sum(values.astype(F32), axis=0, keepdims=True)


def pick_lane(ref, rows, lane):
    block = ref[rows, :]
    return jnp.sum(jnp.where(lane_ids(block.shape) == lane, block, 0.0), axis=-1, keepdims=True)


def start(copies):
    for one in copies:
        one.start()


def finish(copies):
    for one in copies:
        one.wait()


def by_core(core, body):
    for value in (0, 1):

        @pl.when(core == value)
        def _():
            body(value)


class Row:
    def __init__(self, ref, row):
        self.ref, self.row = ref, row

    def __getitem__(self, _):
        return self.ref[self.row : self.row + 1, :]


class Late:
    def __init__(self, source, held, sem, now):
        self.copy = pltpu.make_async_copy(source, held, sem)
        self.held = held
        self.started = self.waited = False
        if now:
            self.begin()

    def begin(self):
        if not self.started:
            self.copy.start()
            self.started = True

    def get(self):
        self.begin()
        if not self.waited:
            self.copy.wait()
            self.waited = True
        return self.held


class Early:
    def __init__(self, held, target, sem):
        self.copy = pltpu.make_async_copy(held, target, sem)
        self.held = held
        self.sent = False

    def send(self):
        self.copy.start()
        self.sent = True


class Pieces:
    def __init__(self, both, rows, own, snd, sems):
        self.both, self.rows, self.targets, self.sems = both, rows, (own, snd), sems
        self.copies = []

    def send(self, at, count):
        for n in (1, 0):
            self.copies.append(
                pltpu.make_async_copy(
                    self.both.at[pl.ds(n * self.rows + at, count)],
                    self.targets[n].at[pl.ds(at, count)],
                    self.sems.at[len(self.copies)],
                )
            )
            self.copies[-1].start()

    def put(self, core, half, at, block):
        to = jnp.where(core == half, 0, self.rows) + at
        self.both[pl.ds(pl.multiple_of(to, 16), block.shape[0]), :] = block

    def put_both(self, at, block):
        put_rows(self.both, at, block)
        put_rows(self.both, self.rows + at, block)

    def put_own(self, at, block):
        put_rows(self.both, at, block)

    def put_snd(self, at, block):
        put_rows(self.both, self.rows + at, block)


def call(kernel, ins, outs, scratch, name, pins=()):
    vmem, anywhere = pl.BlockSpec(memory_space=pltpu.VMEM), pl.BlockSpec(memory_space=pl.ANY)
    smem = pl.BlockSpec(memory_space=pltpu.SMEM)
    specs = {"v": vmem, "a": anywhere, "l": anywhere, "d": anywhere, "e": anywhere, "p": anywhere}
    specs["s"] = smem
    late = [(n, x) for n, (x, kind) in enumerate(ins) if kind in "ld"]
    early = [(n, out) for n, out in enumerate(outs) if out[2] == "e"]
    pair = [n for n, out in enumerate(outs) if out[2] == "p"]
    first = len(ins)
    last = first + len(pins)
    end = last + len(outs)

    def body(*refs):
        took, gave, rest = list(refs[:first]), list(refs[last:end]), list(refs[end + 1 :])
        own, rest = rest[: len(scratch)], rest[len(scratch) :]
        for n, (at, _) in enumerate(late):
            took[at] = Late(took[at], rest[n], rest[-1].at[n], ins[at][1] == "l")
        rest = rest[len(late) :]
        for n, (at, _) in enumerate(early):
            gave[at] = Early(rest[n], gave[at], rest[-1].at[len(late) + n])
        results, pieces = list(gave), []
        if pair:
            rows = outs[pair[0]][0][0]
            pieces = [Pieces(rest[-3], rows, gave[pair[0]], gave[pair[1]], rest[-2])]
            results[pair[0] : pair[1] + 1] = pieces
        kernel(*took, *results, *own)
        refs[end][...] = jnp.zeros((8, 128), F32)
        for at, _ in late:
            took[at].get()
        for at, _ in early:
            if not gave[at].sent:
                gave[at].send()
        for at, _ in early:
            gave[at].copy.wait()
        for one in pieces:
            finish(one.copies)

    extra = [pltpu.VMEM(x.shape, x.dtype) for _, x in late]
    extra += [pltpu.VMEM(out[0], out[1]) for _, out in early]
    if pair:
        extra += [pltpu.VMEM((2 * outs[pair[0]][0][0], D), BF), pltpu.SemaphoreType.DMA((8,))]
    extra += [pltpu.SemaphoreType.DMA((max(len(late) + len(early), 1),))]
    return pl.pallas_call(
        body,
        in_specs=[specs[kind] for _, kind in ins] + [anywhere] * len(pins),
        out_specs=[specs[out[2]] for out in outs] + [vmem],
        out_shape=[jax.ShapeDtypeStruct(out[0], out[1]) for out in outs]
        + [jax.ShapeDtypeStruct((8, 128), F32)],
        scratch_shapes=list(scratch) + extra,
        compiler_params=pltpu.CompilerParams(vmem_limit_bytes=64 * MIB - 65536),
        cost_estimate=pl.CostEstimate(flops=1000, bytes_accessed=1000, transcendentals=0),
        name=name,
    )(*[x for x, _ in ins], *pins)


def after(value, zero):
    return value + zero[0, 0].astype(value.dtype)


def weight_copies(w, slot, core, own, near, far, dst, sems):
    copies = [pltpu.make_async_copy(own[w], dst.at[pl.ds(0, GROUP)], sems.at[slot, 0])]
    rows = pl.ds(w * PIECE, PIECE)
    for i in (1, 2, 3):
        for at, which, refs in ((i, core, near), (3 + i, 1 - core, far)):
            to = pl.multiple_of(GROUP * i + PIECE * which, PIECE)
            copies.append(
                pltpu.make_async_copy(
                    refs[i - 1].at[rows], dst.at[pl.ds(to, PIECE)], sems.at[slot, at]
                )
            )
    return copies


def bias_copies(near, lines, sems):
    return [
        pltpu.make_async_copy(ref.at[pl.ds(ref.shape[0] - 16, 16)], lines.at[i], sems.at[i])
        for i, ref in enumerate(near)
    ]


def gathered_bias(own_line, lines, which):
    parts = [own_line]
    for i in range(3):
        split = lines[i, 3 * which : 3 * which + 3, :GROUP].astype(F32)
        parts.append(split[0:1] + split[1:2] + split[2:3])
    return jnp.concatenate(parts, axis=1)


def put_rows(target, at, block):
    target[at : at + block.shape[0], :] = block


def store_pieces(core, block, places, pieces):
    for g, at in enumerate(places):
        for half in (0, 1):
            row = g * GROUP + half * PIECE
            pieces.put(core, half, at, block[row : row + PIECE])


def store_bias(row, places, pieces):
    for i, at in enumerate(places):
        one = jnp.concatenate(
            [row[:, i * GROUP : (i + 1) * GROUP], jnp.zeros((1, D - GROUP), F32)], axis=1
        )
        block = jnp.concatenate([one, jnp.zeros((BIAS_ROWS - 1, D), F32)], axis=0).astype(BF)
        pieces.put_both(at + PIECE, block)


def forward_heads(q2, keys, values, bias, row_stats, p):
    lane = lane_ids(q2.shape)
    outs = []
    for t in (0, 1):
        query = jnp.where((lane // HEAD) == t, q2, jnp.zeros_like(q2))
        scores = nt(query, keys)
        if bias is not None:
            scores = scores + bias
        highest = jnp.max(scores, axis=-1, keepdims=True)
        raised = jnp.exp(scores - highest)
        total = jnp.sum(raised, axis=-1, keepdims=True)
        outs.append(nn(raised.astype(BF), values) / total)
        row_stats = jnp.where(
            lane_ids(row_stats.shape) == 2 * p + t, highest + jnp.log(total), row_stats
        )
    return jnp.where((lane // HEAD) == 0, outs[0], outs[1]).astype(BF), row_stats


def backward_heads(q2, g2, o2, keys, values, bias, stats, p):
    count = q2.shape[0]
    first = (lane_ids(q2.shape) // HEAD) == 0
    zero = jnp.zeros_like(q2)

    def stacked(a):
        return jnp.concatenate([jnp.where(first, a, zero), jnp.where(first, zero, a)], axis=0)

    query, grad = stacked(q2), stacked(g2)
    product = g2.astype(F32) * o2.astype(F32)
    inner = jnp.concatenate(
        [
            jnp.sum(jnp.where(first, product, 0.0), axis=-1, keepdims=True),
            jnp.sum(jnp.where(first, 0.0, product), axis=-1, keepdims=True),
        ],
        axis=0,
    )
    lanes = lane_ids(stats.shape)
    lse = jnp.concatenate(
        [
            jnp.sum(jnp.where(lanes == 2 * p + t, stats, 0.0), axis=-1, keepdims=True)
            for t in (0, 1)
        ],
        axis=0,
    )
    scores = nt(query, keys)
    if bias is not None:
        scores = scores + jnp.concatenate([bias, bias], axis=0)
    shares = jnp.exp(scores - lse)
    grad_scores = (shares * (nt(grad, values) - inner)).astype(BF)
    grad_q = nn(grad_scores, keys)
    return (
        jnp.where(first, grad_q[:count], grad_q[count:]),
        tn(grad_scores, query),
        tn(shares.astype(BF), grad),
    )


def document_ends(xa, place):
    pair_at = place[1] // 2
    lengths = jnp.where(
        pair_at == 0,
        xa[0:1, :8] * 16.0 + xa[2:3, :8],
        xa[1:2, :8] * 16.0
        + xa[3:4, :8],
    )
    ends, total = [], 0.0
    for d in range(8):
        total = total + lengths[:, d : d + 1]
        ends.append(total)
    return ends


def mask_bias(ends, chunk, width):
    qpos = chunk * CHUNK + lax.broadcasted_iota(jnp.int32, (CHUNK, 1), 0)
    kpos = lax.broadcasted_iota(jnp.int32, (1, width), 1)
    qat, kat = qpos.astype(F32), kpos.astype(F32)
    qseg = jnp.zeros((CHUNK, 1), F32)
    kseg = jnp.zeros((1, width), F32)
    for end in ends:
        qseg = qseg + jnp.where(qat >= end, 1.0, 0.0)
        kseg = kseg + jnp.where(kat >= end, 1.0, 0.0)
    return jnp.where((qseg == kseg) & (kpos <= qpos), 0.0, -1000000000.0)


def chunk_of(core, which):
    return (2 * core, 3 - 2 * core, 2 - 2 * core, 1 + 2 * core)[which]


def chunk_rows(core, which):
    return pl.ds(pl.multiple_of(chunk_of(core, which) * CHUNK, 16), CHUNK)


def key_counts(core):
    return ((0, 1), (1, 4)) if core == 0 else ((0, 3), (1, 2))


def prepare(
    place, x, lengths, wq, wk, wv, qbias, vbias, so, cwq, cwk, cwv, cwo, cqbias, cvbias, out_grad, enc,
    xa, xb, mine, mine_cross, mine_again, ga, gb, enc_out,
):
    core = place[0]
    enc_out[...] = enc[...]
    ga[...] = out_grad[0:CHUNK, :]
    gb[...] = out_grad[CHUNK:OWN, :]
    xa[0:CHUNK, :] = x[0:CHUNK, :]
    xa[CHUNK : CHUNK + 16, :] = jnp.zeros((16, D), BF)
    xa[CHUNK : CHUNK + 16, 0:128] = lengths[...]
    xb[...] = x[CHUNK:OWN, :]
    prepare_weights(core, (wq, wk, wv), qbias, vbias, mine)
    prepare_weights(core, (cwq, cwk, cwv, cwo, so), cqbias, cvbias, mine_cross)
    mine_again[...] = mine_cross[...]


def prepare_weights(core, weights, qbias, vbias, mine):
    half = pl.ds(pl.multiple_of(core * PIECE, PIECE), PIECE)
    for w, one in enumerate(weights):
        mine[w * PIECE : (w + 1) * PIECE, :] = one[half, :]
    rows = []
    for one in (qbias[...], vbias[...]):
        for _ in range(3):
            top = one.astype(BF).astype(F32)
            rows.append(top)
            one = one - top
    rows = jnp.concatenate(rows + [jnp.zeros((10, GROUP), F32)], axis=0)
    at = len(weights) * PIECE
    mine[at : at + 16, :] = jnp.concatenate(
        [rows, jnp.zeros((16, D - GROUP), F32)], axis=1
    ).astype(BF)


def gate(*refs):
    pass


def row_copies(core, xs, full, sems):
    return [
        pltpu.make_async_copy(
            x.at[pl.ds(0, CHUNK)], full.at[chunk_rows(core, which)], sems.at[which]
        )
        for which, x in enumerate(xs)
    ]


def self_forward(
    place, xa, xb, ya, yb, w0, w1, w2, n1, n2, n3, f1, f2, f3, qbias, vbias,
    q_out, k_out, v_out, att, stats,
    wq, wk, wv, full, bias, lines, sems, line_sems, row_sems,
):
    core = place[0]
    near, far = (n1, n2, n3), (f1, f2, f3)
    sets = [
        weight_copies(w, w, core, (w0, w1, w2), near, far, dst, sems)
        for w, dst in enumerate((wq, wk, wv))
    ]
    held = bias_copies(near, lines, line_sems)
    rows = row_copies(core, (xa, xb, ya, yb), full, row_sems)
    start(rows)
    start(held)
    for one in sets:
        start(one)
    finish(rows[:1])
    tail = pltpu.make_async_copy(xa.at[pl.ds(CHUNK, 16)], lines.at[3], line_sems.at[3])
    tail.start()
    tail.wait()
    ends = document_ends(lines[3].astype(F32), place)
    for slot in (0, 1):
        bias[slot] = mask_bias(ends, chunk_of(core, slot), ROW)
    finish(rows[1:])
    finish(held)
    for one in sets:
        finish(one)
    line = gathered_bias(qbias[...], lines, 0)
    k_out.held[...] = nt(full[...], wk[...]).astype(BF)
    k_out.send()
    for which in (0, 1):
        q_out.held[which * CHUNK : (which + 1) * CHUNK, :] = (
            (nt(full[chunk_rows(core, which), :], wq[...]) + line) * 0.125
        ).astype(BF)
    q_out.send()
    line = gathered_bias(vbias[...], lines, 1)
    v_out.held[...] = (nt(full[...], wv[...]) + line).astype(BF)
    v_out.send()
    q, k, v = q_out.held, k_out.held, v_out.held
    stats[...] = jnp.zeros_like(stats)

    def attend(value):
        def pair(p, carry):
            lanes = pair_lanes(p)
            for slot, count in key_counts(value):
                rows = pl.ds(slot * CHUNK, CHUNK)
                width = count * CHUNK
                out, now = forward_heads(
                    q[rows, lanes], k[0:width, lanes], v[0:width, lanes],
                    bias[slot, :, 0:width], stats[rows, :], p,
                )
                att[rows, lanes] = out
                stats[rows, :] = now
            return carry

        lax.fori_loop(0, 6, pair, 0)

    by_core(core, attend)


def cross_forward(
    place, xa, xb, self_att, params, ea, eb, w0, w1, w2, w3, w4, n1, n2, n3,
    f1, f2, f3, qbias, vbias,
    hat1, scale1, q_out, k_out, v_out, att, stats, hat_out,
    wq, wk, wv, wo, full, lines, sems, line_sems, row_sems, self_wo, self_sems,
):
    core = place[0]
    self_bias, gain1, shift1, obias = (Row(params, n) for n in range(4))
    near, far = (n1, n2, n3), (f1, f2, f3)
    rows = [
        pltpu.make_async_copy(e, full.at[pl.ds(i * HALF_ENC, HALF_ENC)], row_sems.at[i])
        for i, e in enumerate((ea, eb))
    ]
    held = bias_copies(near, lines, line_sems)
    sets = [
        weight_copies(w, w, core, (w0, w1, w2, w3), near, far, dst, sems)
        for w, dst in enumerate((wq, wk, wv, wo))
    ]
    self_set = weight_copies(
        4, 0, core, (None, None, None, None, w4), near, far, self_wo, self_sems
    )
    start(self_set)
    start(held)
    start(sets[0])
    start(rows)
    for one in sets[1:]:
        start(one)
    finish(self_set)
    product = nn(self_att[...], self_wo[...]) + self_bias[...]
    for which, x in enumerate((xa, xb)):
        part = slice(which * CHUNK, (which + 1) * CHUNK)
        hat, scale = normalize(x[0:CHUNK, :].astype(F32) + product[part])
        hat1.held[part, :] = hat
        scale1[part, :] = jnp.broadcast_to(scale, (CHUNK, 128))
    hat1.send()
    hidden = (hat1.held[...] * gain1[...] + shift1[...]).astype(BF)
    finish(held)
    finish(sets[0])
    line = gathered_bias(qbias[...], lines, 0)
    q_out.held[...] = ((nt(hidden, wq[...]) + line) * 0.125).astype(BF)
    q_out.send()
    finish(rows)
    finish(sets[1])
    k_out.held[...] = nt(full[...], wk[...]).astype(BF)
    k_out.send()
    finish(sets[2])
    line = gathered_bias(vbias[...], lines, 1)
    v_out.held[...] = (nt(full[...], wv[...]) + line).astype(BF)
    v_out.send()
    finish(sets[3])
    q, k, v = q_out.held, k_out.held, v_out.held
    stats[...] = jnp.zeros_like(stats)

    def pair(p, carry):
        lanes = pair_lanes(p)
        for slot in (0, 1):
            rows = pl.ds(slot * CHUNK, CHUNK)
            out, now = forward_heads(
                q[rows, lanes], k[:, lanes], v[:, lanes], None, stats[rows, :], p
            )
            att[rows, lanes] = out
            stats[rows, :] = now
        return carry

    lax.fori_loop(0, 6, pair, 0, unroll=True)
    hidden = hat1.held[...] * gain1[...] + shift1[...]
    hat, scale = normalize(hidden + (nn(att[...], wo[...]) + obias[...]))
    hat_out[...] = hat
    stats[...] = jnp.where(lane_ids(stats.shape) == 12, scale, stats[...])


FF_STEP = 512
FF_BLOCK = 768


def gelu_parts(u):
    size = jnp.abs(u)
    t = 1.0 / (1.0 + (0.3275911 * 0.7071067811865476) * size)
    poly = t * (
        0.254829592
        + t * (-0.284496736 + t * (1.421413741 + t * (-1.453152027 + t * 1.061405429)))
    )
    bell = jnp.exp(-0.5 * u * u)
    tail = 0.5 * poly * bell
    phi = jnp.where(u >= 0.0, 1.0 - tail, tail)
    return u * phi, phi + u * bell * 0.3989422804014327


def feed_forward(
    place, hat2, stats, params, up_hbm, up_bias, down_hbm, ga_here, ga, gb,
    out_a, out_b, dsecond, left, right, snd, vec, upb,
    up, down, active, slope, hid, total, third, grads, held, sems, out_sems,
):
    core, group = place[0], place[1]
    gain2, shift2, down_bias, gain3, shift3 = (Row(params, 4 + n) for n in range(5))
    steps = FF // FF_STEP
    ups = [
        pltpu.make_async_copy(
            up_hbm.at[:, pl.ds(i * FF_STEP, FF_STEP)],
            up.at[:, pl.ds(i * FF_STEP, FF_STEP)],
            sems.at[0, i],
        )
        for i in range(steps)
    ]
    downs = [
        pltpu.make_async_copy(
            down_hbm.at[pl.ds(i * FF_STEP, FF_STEP)],
            down.at[pl.ds(i * FF_STEP, FF_STEP)],
            sems.at[1, i],
        )
        for i in range(steps)
    ]
    for i in range(steps):
        ups[i].start()
        downs[i].start()
    second = hat2[...] * gain2[...] + shift2[...]
    hid[...] = second.astype(BF)
    total[...] = second + down_bias[...]
    for i in range(steps):
        cols = pl.ds(i * FF_STEP, FF_STEP)
        ups[i].wait()
        u = nn(hid[...], up[:, cols]) + up_bias[:, cols]
        act, slo = gelu_parts(u)
        active[:, cols] = act.astype(BF)
        slope[:, cols] = slo
        downs[i].wait()
        total[...] += nn(active[:, cols], down[cols, :])
    hat3, scale3 = normalize(total[...])
    out = (hat3 * gain3[...] + shift3[...]).astype(BF)
    out_a[...] = out[0:CHUNK]
    out_b[...] = out[CHUNK:OWN]
    first = jnp.where(core == group % 2, ga_here.get()[...], ga.get()[...])
    grad = jnp.concatenate([first, gb.get()[...]], axis=0).astype(F32)
    vec[0:1, :] = column(grad * hat3)
    vec[1:2, :] = column(grad)
    dthird = norm_back(grad, hat3, scale3, gain3[...])
    total[...] = dthird
    third[...] = dthird.astype(BF)
    vec[2:3, :] = column(third[...])
    for i in range(FF // FF_BLOCK):
        cols = pl.ds(i * FF_BLOCK, FF_BLOCK)
        du = (nt(third[...], down[cols, :]) * slope[:, cols]).astype(BF)
        grads[:, cols] = du
        upb[:, cols] = column(du)
        total[...] += nt(du, up[:, cols])
    grad = total[...]
    hat = hat2[...]
    scale = pick_lane(stats, slice(None), 12)
    vec[3:4, :] = column(grad * hat)
    vec[4:5, :] = column(grad)
    dsec = norm_back(grad, hat, scale, gain2[...])
    dsecond.held[...] = dsec
    dsecond.send()
    vec[5:6, :] = column(dsec.astype(BF))
    vec[6:8, :] = jnp.zeros((2, D), F32)

    def hand_over(value):
        pairs = ((grads, hid), (active, third))
        mine, other = pairs[value], pairs[1 - value]
        copies = [
            pltpu.make_async_copy(mine[0], left, out_sems.at[4]),
            pltpu.make_async_copy(mine[1], right, out_sems.at[5]),
        ]
        start(copies)
        for i in range(4):
            cols = pl.ds(pl.multiple_of((group ^ i) * D, D), D)
            rows = pl.ds(i * D, D)
            held[rows, :] = tn(other[0][:, cols], other[1][...]).astype(BF)
            copies.append(pltpu.make_async_copy(held.at[rows], snd.at[rows], out_sems.at[i]))
            copies[-1].start()
        finish(copies)

    by_core(core, hand_over)


def ff_weight_grads(place, left, right, out, held, left_held, right_held, sems):
    copies = [pltpu.make_async_copy(right, right_held, sems.at[0])]
    for i in range(4):
        cols = pl.ds(pl.multiple_of((place[1] ^ i) * D, D), D)
        copies.append(pltpu.make_async_copy(left.at[:, cols], left_held.at[i], sems.at[1 + i]))
    start(copies[:2])
    finish(copies[:2])
    start(copies[2:])
    outs = []
    for i in range(4):
        if i:
            copies[1 + i].wait()
        rows = pl.ds(i * D, D)
        held[rows, :] = tn(left_held[i], right_held[...]).astype(BF)
        outs.append(pltpu.make_async_copy(held.at[rows], out.at[rows], sems.at[5 + i]))
        outs[i].start()
    finish(outs)


def out_grads(core, att, low, wo, grad, places, pieces):
    store_pieces(core, tn(att[...], low[...]).astype(BF), places, pieces)
    store_bias(jnp.zeros((1, D), F32), places, pieces)
    grad[...] = nt(low[...], wo[...]).astype(BF)


def weight_grads(core, dq, dk, dv, queries, keys, places, pieces):
    store_pieces(core, tn(dq[...], queries).astype(BF), places[0], pieces)
    store_pieces(core, tn(dk[...], keys).astype(BF), places[1], pieces)
    store_pieces(core, tn(dv[...], keys).astype(BF), places[2], pieces)
    store_bias(column(dq[...]), places[0], pieces)
    store_bias(jnp.zeros((1, dk.shape[1]), F32), places[1], pieces)
    store_bias(column(dv[...]), places[2], pieces)


def cross_part(core, first, grad, att, q, k, v, stats, queries, full, places, pieces, dq, dk, dv):

    def pair(p, carry):
        lanes = pair_lanes(first + p)
        out = pair_lanes(p)
        gq, gk, gv = backward_heads(
            q[:, lanes], grad[:, lanes], att[:, lanes], k[:, lanes], v[:, lanes],
            None, stats[...], first + p,
        )
        dq[:, out] = (gq * 0.125).astype(BF)
        dk[:, out] = gk.astype(BF)
        dv[:, out] = gv.astype(BF)
        return carry

    lax.fori_loop(0, 3, pair, 0, unroll=True)
    half = pl.ds(0, D // 2)
    weight_grads(
        core, dq.at[:, half], dk.at[:, half], dv.at[:, half], queries(), full[...], places, pieces
    )


def cross_backward_a(
    place, dsecond, att, q, k, v, stats, hat1, params, ea, eb, w3, n1, n2, n3, f1, f2, f3,
    dq, dk, dv, grad, pieces,
    wo, low, full, sems, row_sems,
):
    core = place[0]
    gain1, shift1 = Row(params, 1), Row(params, 2)
    copies = weight_copies(
        3, 0, core, (None, None, None, w3), (n1, n2, n3), (f1, f2, f3), wo, sems
    )
    rows = [
        pltpu.make_async_copy(e, full.at[pl.ds(i * HALF_ENC, HALF_ENC)], row_sems.at[i])
        for i, e in enumerate((ea, eb))
    ]
    start(copies)
    low[...] = dsecond.get()[...].astype(BF)
    size = pieces.rows // 10
    places = [[(4 * g + w) * size for g in (0, 1)] for w in range(3)]
    places_o = [8 * size, 9 * size, 3 * size, 7 * size]
    att = att.get()
    finish(copies)
    out_grads(core, att, low, wo, grad.held, places_o, pieces)
    grad.send()
    q, k, v, stats = q.get(), k.get(), v.get(), stats.get()
    start(rows)
    hat1.begin()

    def queries():
        for one in (dq, dk, dv):
            one.send()
        finish(rows)
        return (hat1.get()[...] * gain1[...] + shift1[...]).astype(BF)

    cross_part(
        core, 3, grad.held, att, q, k, v, stats, queries, full, places, pieces,
        dq.held, dk.held, dv.held,
    )
    pieces.send(0, 10 * size)


def cross_backward_b(
    place, dq_a, dk_a, dv_a, dsecond, grad, att, q, k, v, stats, hat1, scale1, params, ea, eb,
    vec_a, upb, w0, w1, w2, n1, n2, n3, f1, f2, f3,
    dfirst, pieces, vec,
    wq, wk, wv, dq, dk, dv, full, sems, row_sems,
):
    core = place[0]
    gain1, shift1 = Row(params, 1), Row(params, 2)
    near, far, ws = (n1, n2, n3), (f1, f2, f3), (w0, w1, w2)
    sets = [
        weight_copies(w, w, core, ws, near, far, dst, sems)
        for w, dst in enumerate((wq, wk, wv))
    ]
    rows = [
        pltpu.make_async_copy(e, full.at[pl.ds(i * HALF_ENC, HALF_ENC)], row_sems.at[i])
        for i, e in enumerate((ea, eb))
    ]
    second = pl.ds(D // 2, D // 2)
    parts = [
        pltpu.make_async_copy(one, dst.at[:, second], row_sems.at[2 + n])
        for n, (one, dst) in enumerate(((dq_a, dq), (dk_a, dk), (dv_a, dv)))
    ]
    grad, att, stats = grad.get(), att.get(), stats.get()
    q, k, v = q.get(), k.get(), v.get()
    start(rows)
    hat1.begin()
    for one in sets:
        start(one)
    start(parts)
    dsecond.begin()
    scale1.begin()
    size = (pieces.rows - HALF_ENC) // 6
    places = [[(3 * g + w) * size for g in (0, 1)] for w in range(3)]

    def queries():
        finish(rows)
        return (hat1.get()[...] * gain1[...] + shift1[...]).astype(BF)

    cross_part(
        core, 0, grad, att, q, k, v, stats, queries, full, places, pieces, dq, dk, dv
    )
    pieces.send(0, 6 * size)
    finish(parts)
    for one in sets:
        finish(one)
    enc = nn(dk[...], wk[...]) + nn(dv[...], wv[...])
    pieces.put_own(6 * size, enc[0:HALF_ENC].astype(BF))
    pieces.put_snd(6 * size, enc[HALF_ENC:ENC].astype(BF))
    pieces.send(6 * size, HALF_ENC)
    total = dsecond.get()[...] + nn(dq[...], wq[...])
    hat = hat1.get()[...]
    vec[0:6, :] = vec_a[0:6, :]
    vec[6:7, :] = column(total * hat)
    vec[7:8, :] = column(total)
    dfi = norm_back(total, hat, scale1.get()[:, 0:1], gain1[...])
    dfirst.held[...] = dfi
    dfirst.send()
    vec[8:9, :] = column(dfi.astype(BF))
    for n in range(4):
        vec[9 + n : 10 + n, :] = upb[:, n * D : (n + 1) * D]
    vec[13:16, :] = jnp.zeros((3, D), F32)


def self_part(
    core, first, ends, grad, att, q, k, v, stats, full, places, pieces, dq, dk, dv, bias, rows
):
    for slot in (0, 1):
        bias[slot] = mask_bias(ends, chunk_of(core, slot), ROW)

    def attend(value):
        def pair(p, carry):
            lanes = pair_lanes(first + p)
            out = pair_lanes(p)
            (low_slot, low), (high_slot, high) = sorted(key_counts(value), key=lambda x: x[1])
            parts = {}
            for slot, count in ((low_slot, low), (high_slot, high)):
                rows = pl.ds(slot * CHUNK, CHUNK)
                width = count * CHUNK
                gq, gk, gv = backward_heads(
                    q[rows, lanes], grad[rows, lanes], att[rows, lanes],
                    k[0:width, lanes], v[0:width, lanes],
                    bias[slot, :, 0:width], stats[rows, :], first + p,
                )
                dq[rows, out] = (gq * 0.125).astype(BF)
                parts[slot] = (gk, gv)
            for n, dst in ((0, dk), (1, dv)):
                wide, narrow = parts[high_slot][n], parts[low_slot][n]
                shared, reach = low * CHUNK, high * CHUNK
                dst[0:shared, out] = (wide[0:shared] + narrow).astype(BF)
                dst[shared:reach, out] = wide[shared:reach].astype(BF)
                if reach < ROW:
                    dst[reach:ROW, out] = jnp.zeros((ROW - reach, PAIR), BF)
            return carry

        lax.fori_loop(0, 3, pair, 0)

    by_core(core, attend)
    finish(rows)
    half = pl.ds(0, D // 2)
    queries = jnp.concatenate([full[chunk_rows(core, n), :] for n in (0, 1)], axis=0)
    weight_grads(
        core, dq.at[:, half], dk.at[:, half], dv.at[:, half], queries, full[...], places, pieces
    )


def self_backward_a(
    place, dfirst, att, q, k, v, stats, xa, xb, ya, yb, w3, m1, m2, m3, g1, g2, g3,
    dq, dk, dv, grad, pieces,
    wo, low, bias, full, lines, sems, row_sems,
):
    core = place[0]
    copies = weight_copies(
        4, 0, core, (None, None, None, None, w3), (m1, m2, m3), (g1, g2, g3), wo, sems
    )
    tail = pltpu.make_async_copy(xa.at[pl.ds(CHUNK, 16)], lines, row_sems.at[4])
    rows = row_copies(core, (xa, xb, ya, yb), full, row_sems)
    start(copies)
    tail.start()
    low[...] = dfirst.get()[...].astype(BF)
    size = pieces.rows // 10
    places = [[(4 * g + w) * size for g in (0, 1)] for w in range(3)]
    places_o = [8 * size, 9 * size, 3 * size, 7 * size]
    att = att.get()
    finish(copies)
    out_grads(core, att, low, wo, grad.held, places_o, pieces)
    grad.send()
    tail.wait()
    q, k, v, stats = q.get(), k.get(), v.get(), stats.get()
    start(rows)
    self_part(
        core, 3, document_ends(lines[...].astype(F32), place), grad.held, att, q, k, v, stats, full,
        places, pieces, dq.held, dk.held, dv.held, bias, rows,
    )
    pieces.send(0, 10 * size)
    for one in (dq, dk, dv):
        one.send()


def self_backward_b(
    place, dq_a, dk_a, dv_a, dfirst, grad, att, q, k, v, stats, xa, xb, ya, yb,
    w0, w1, w2, n1, n2, n3, f1, f2, f3,
    pieces,
    wq, wk, wv, dq, dk, dv, bias, full, total, lines, sems, row_sems,
):
    core = place[0]
    size = (pieces.rows - 2 * CHUNK) // 6
    places = [[(3 * g + w) * size for g in (0, 1)] for w in range(3)]
    near, far, ws = (n1, n2, n3), (f1, f2, f3), (w0, w1, w2)
    sets = [
        weight_copies(w, w, core, ws, near, far, dst, sems)
        for w, dst in enumerate((wq, wk, wv))
    ]
    tail = pltpu.make_async_copy(xa.at[pl.ds(CHUNK, 16)], lines, row_sems.at[4])
    rows = row_copies(core, (xa, xb, ya, yb), full, row_sems)
    second = pl.ds(D // 2, D // 2)
    parts = [
        pltpu.make_async_copy(one, dst.at[:, second], row_sems.at[5 + n])
        for n, (one, dst) in enumerate(((dq_a, dq), (dk_a, dk), (dv_a, dv)))
    ]
    tail.start()
    tail.wait()
    grad, att, stats = grad.get(), att.get(), stats.get()
    q, k, v = q.get(), k.get(), v.get()
    start(rows)
    for one in sets:
        start(one)
    start(parts)
    dfirst.begin()
    self_part(
        core, 0, document_ends(lines[...].astype(F32), place), grad, att, q, k, v, stats, full,
        places, pieces, dq, dk, dv, bias, rows,
    )
    pieces.send(0, 6 * size)
    finish(parts)
    for one in sets:
        finish(one)
    total[...] = nn(dk[...], wk[...]) + nn(dv[...], wv[...])
    mine = nn(dq[...], wq[...]) + dfirst.get()[...]
    for n in (0, 1):
        at = 6 * size + n * CHUNK
        pieces.put_snd(at, total[chunk_rows(core, 2 + n), :].astype(BF))
        pieces.put_own(
            at, (mine[n * CHUNK : (n + 1) * CHUNK] + total[chunk_rows(core, n), :]).astype(BF)
        )
    pieces.send(6 * size, 2 * CHUNK)


def add_jobs(jobs, ins, store, held, sems):
    copies, at, most = [], 0, job_most(jobs)
    for _, rows, sources in jobs:
        mine = []
        for operand, row in sources:
            mine.append(
                (
                    pltpu.make_async_copy(
                        ins[operand].at[pl.ds(row, rows)], held.at[pl.ds(at, rows)],
                        sems.at[len(copies) * most + len(mine)],
                    ),
                    at,
                )
            )
            at += rows
        copies.append(mine)
    for mine in copies:
        for copy, _ in mine:
            copy.start()
    for (place, rows, _), mine in zip(jobs, copies):
        total = 0.0
        for copy, row in mine:
            copy.wait()
            total = total + held[row : row + rows, :].astype(F32)
        store(place, total)


def job_most(jobs):
    return max(len(sources) for _, _, sources in jobs)


def job_rows(jobs):
    return sum(rows * len(sources) for _, rows, sources in jobs)


def add_call(name, place, arrays, outs, jobs, pins=()):
    count = len(arrays)

    def kernel(place, *refs):
        ins, targets = refs[:count], refs[count : count + len(outs)]
        held, out_held, sems, out_sems = refs[count + len(outs) :]
        copies = []

        def store(where, total):
            at = sum(outs[: where[0]]) + where[1]
            put_rows(out_held, at, total.astype(BF))
            rows = pl.ds(at, total.shape[0])
            copies.append(
                pltpu.make_async_copy(
                    out_held.at[rows],
                    targets[where[0]].at[pl.ds(where[1], total.shape[0])],
                    out_sems.at[len(copies)],
                )
            )
            copies[-1].start()

        add_jobs(jobs, ins, store, held, sems)
        finish(copies)

    dma = pltpu.SemaphoreType.DMA
    return call(
        kernel, [(place, "s")] + [(one, "a") for one in arrays],
        [((rows, D), BF, "a") for rows in outs],
        [
            pltpu.VMEM((job_rows(jobs), D), BF), pltpu.VMEM((sum(outs), D), BF),
            dma((job_most(jobs) * len(jobs),)), dma((len(jobs),)),
        ],
        name, pins=pins,
    )


def total_call(name, place, arrays, total_rows, jobs, groups, depth, pins=(), mine_type=F32):
    count = len(arrays)
    size = total_rows // groups // depth

    def kernel(place, *refs):
        mine, parts = refs[count], refs[count + 1 : count + depth]
        held, total, sems = refs[count + depth :]

        def store(row, value):
            put_rows(total, row, value)

        add_jobs(jobs, refs[:count], store, held, sems)
        for d in range(depth):
            for g in range(groups):
                at = pl.multiple_of(
                    g * (total_rows // groups) + (place[2] ^ d) * size, 8
                )
                block = total[pl.ds(at, size), :]
                if d == 0:
                    put_rows(mine, g * size, block.astype(mine_type))
                else:
                    put_rows(parts[d - 1], g * size, block.astype(BF))

    return call(
        kernel, [(place, "s")] + [(one, "a") for one in arrays],
        [((groups * size, D), mine_type, "v")] + [((groups * size, D), BF, "v")] * (depth - 1),
        [
            pltpu.VMEM((job_rows(jobs), D), BF), pltpu.VMEM((total_rows, D), F32),
            pltpu.SemaphoreType.DMA((job_most(jobs) * len(jobs),)),
        ],
        name, pins=pins,
    )


def spread(depth, count):
    def kernel(place, *refs):
        own, other, refs = refs[:count], refs[count : 2 * count], refs[2 * count :]
        outs, biases, total = refs[:4], refs[4:-1], refs[-1]
        core, k = place[0], place[2]
        size = total.shape[1] // depth
        for which, parts in enumerate((own, other)):
            for d in range(depth):
                at = pl.multiple_of((k ^ d) * size, 8)
                ref, row = (parts[d], 0) if count == depth else (parts[0], d * size)
                total[which, pl.ds(at, size), :] = ref[row : row + size, :].astype(F32)
        rows = total.shape[1] // 4
        for n, out in enumerate(outs):
            for which, half in ((0, core), (1, 1 - core)):
                to = pl.ds(pl.multiple_of(half * PIECE, PIECE), PIECE)
                out[to, :] = total[which, n * rows : n * rows + PIECE, :]
        for n, bias in zip((0, 2), biases):
            at = n * rows + PIECE
            bias[...] = total[0, at : at + 1, :GROUP]

    return kernel


def solution(mesh):
    names = tuple(mesh.axis_names)
    heads, rows = mesh.shape["heads"], mesh.shape["rows"]
    depth = rows // 2
    piece = FF // (heads * rows)
    weight_rows = PIECE + BIAS_ROWS
    while (4 * weight_rows) % (8 * depth):
        weight_rows += BIAS_ROWS
    def send(value, where, label="moved"):
        pairs = []
        for r in range(rows):
            for h in range(heads):
                to_r, to_h = where(r, h)
                if (to_r, to_h) == (r, h):
                    continue
                index = {"rows": (r, to_r), "heads": (h, to_h)}
                a = b = 0
                for name in names:
                    a = a * mesh.shape[name] + index[name][0]
                    b = b * mesh.shape[name] + index[name][1]
                pairs.append((a, b))
        with jax.named_scope(label):
            return lax.ppermute(value, names, pairs)

    def swap(r, h):
        return (r & ~1) | (h & 1), (h & ~1) | (r & 1)

    def swap_b(r, h):
        return (r & ~1) | (1 - (h & 1)), (h & ~1) | (r & 1)

    def swap_b_back(r, h):
        return (r & ~1) | (h & 1), (h & ~1) | (1 - (r & 1))

    def core_to(r, h):
        return r ^ 1, h

    def head_to(d):
        return lambda r, h: (r, h ^ d)

    def depth_to(d):
        return lambda r, h: (r ^ (2 * d), h)

    def shards(
        layer_input, encoder_out, doc_lengths,
        self_query, self_qbias, self_key_weight, self_value, self_vbias, self_out, self_obias,
        first_gain, first_shift,
        cross_query, cross_qbias, cross_key, cross_value, cross_vbias, cross_out, cross_obias,
        second_gain, second_shift, up_weight, up_bias, down_weight, down_bias,
        third_gain, third_shift, out_grad,
    ):
        h = lax.axis_index("heads")
        r = lax.axis_index("rows")
        core, k = r % 2, r // 2
        place = jnp.stack([core, h, k]).astype(jnp.int32)
        stays = core == h % 2

        def line(vector):
            return vector.reshape(1, -1)

        params = jnp.stack(
            [
                self_obias, first_gain, first_shift, cross_obias, second_gain, second_shift,
                down_bias, third_gain, third_shift,
            ]
        )

        def v(*arrays):
            return [(one, "v") for one in arrays]

        def a(*arrays):
            return [(one, "a") for one in arrays]

        def l(*arrays):
            return [(one, "l") for one in arrays]

        def d(*arrays):
            return [(one, "d") for one in arrays]

        here = [(place, "s")]

        lengths = jnp.concatenate([doc_lengths // 16, doc_lengths % 16], axis=0).astype(BF)
        lengths = jnp.pad(lengths, ((0, 12), (0, 120)))
        self_own = [self_query.T, self_key_weight.T, self_value.T]
        cross_own = [cross_query.T, cross_key.T, cross_value.T, cross_out, self_out]
        xa, xb, mine, mine_cross, mine_again, ga, gb, enc, _ = call(
            prepare,
            here + v(layer_input, lengths, *self_own, line(self_qbias), line(self_vbias), self_out)
            + v(*cross_own[:4], line(cross_qbias), line(cross_vbias), out_grad, encoder_out),
            [
                ((CHUNK + 16, D), BF, "v"), ((CHUNK, D), BF, "v"),
                ((3 * PIECE + 16, D), BF, "v"), ((5 * PIECE + 16, D), BF, "v"),
                ((5 * PIECE + 16, D), BF, "v"),
                ((CHUNK, D), BF, "v"), ((CHUNK, D), BF, "v"), ((HALF_ENC, D), BF, "v"),
            ],
            [], "prepare",
        )

        def gather_groups(mine, label):
            x, y = send(mine, head_to(1), label), send(mine, head_to(2), label)
            return [x, y, send(x, head_to(2), label + "_2")]

        self_near = gather_groups(mine, "w_self_near")
        xb = send(xb, swap_b, "x_b")
        xa = jnp.where(stays, xa, send(xa, swap, "x_a"))
        ya = send(xa, core_to, "y_a")
        yb = send(xb, core_to, "y_b")
        self_far = [send(one, core_to, "w_self_far") for one in self_near]
        self_w = self_near + self_far

        def gated(values, pins, name):
            count = len(values)
            anywhere = pl.BlockSpec(memory_space=pl.ANY)
            return pl.pallas_call(
                gate,
                in_specs=[anywhere] * (count + len(pins)),
                out_specs=[anywhere] * count,
                out_shape=[jax.ShapeDtypeStruct(one.shape, one.dtype) for one in values],
                input_output_aliases={n: n for n in range(count)},
                name=name,
            )(*values, *pins)

        mine_cross, enc = gated([mine_cross, enc], [self_near[0], xa, xb], "gate_x")
        (mine_again,) = gated([mine_again], [self_near[2]], "gate_y")
        cross_near = [send(mine_cross, head_to(1), "w_cross_near")] + [
            send(mine_again, head_to(d), "w_cross_near") for d in (2, 3)
        ]
        ea = send(enc, swap_b, "e_a")

        dma = pltpu.SemaphoreType.DMA
        weight = pltpu.VMEM((D, D), BF)
        half_weight = pltpu.VMEM((D // 2, D), BF)
        masks = pltpu.VMEM((2, CHUNK, ROW), F32)
        lines_bf = pltpu.VMEM((4, 16, D), BF)
        row_full = pltpu.VMEM((ROW, D), BF)
        enc_full = pltpu.VMEM((ENC, D), BF)
        tokens = (OWN, D)
        q, kk, vv, att, stats1, zero = call(
            self_forward,
            here + a(xa, xb, ya, yb) + a(*self_own, *self_w) + v(line(self_qbias), line(self_vbias)),
            [
                (tokens, BF, "e"), ((ROW, D), BF, "e"), ((ROW, D), BF, "e"), (tokens, BF, "v"),
                ((OWN, 128), F32, "v"),
            ],
            [weight] * 3 + [row_full, masks, lines_bf, dma((3, 7)), dma((4,)), dma((4,))],
            "self_forward", pins=[mine_cross, mine_again, enc],
        )
        *cross_near, ea, ga_here, gb = gated(cross_near + [ea, ga, gb], [zero], "gate_far")
        cross_far = [send(one, core_to, "w_cross_far") for one in cross_near]
        eb = send(ea, core_to, "e_b")
        ga = send(ga_here, swap, "g_a")
        gb = send(gb, swap_b, "g_b")
        cross_w = cross_near + cross_far
        hat1, scale1, cq, ck, cv, catt, stats2, hat2, zero = call(
            cross_forward,
            here + v(xa, xb, att, params) + a(ea, eb)
            + a(*cross_own, *cross_w) + v(line(cross_qbias), line(cross_vbias)),
            [
                (tokens, F32, "e"), ((OWN, 128), F32, "v"),
                (tokens, BF, "e"), ((ENC, D), BF, "e"), ((ENC, D), BF, "e"), (tokens, BF, "v"),
                ((OWN, 128), F32, "v"), (tokens, F32, "v"),
            ],
            [weight] * 4 + [
                enc_full, lines_bf, dma((4, 7)), dma((4,)), dma((2,)), weight, dma((1, 7)),
            ],
            "cross_forward",
        )
        chunk = ((CHUNK, D), BF, "v")
        out_a, out_b, dsecond, left, right, ff_snd, vec_a, upb, zero = call(
            feed_forward,
            here + v(hat2, stats2, params) + a(up_weight) + v(line(up_bias)) + a(down_weight)
            + l(ga_here, ga, gb),
            [
                chunk, chunk, (tokens, F32, "e"), ((OWN, FF), BF, "a"), (tokens, BF, "a"),
                ((FF, D), BF, "a"), ((8, D), F32, "v"), ((1, FF), F32, "v"),
            ],
            [
                pltpu.VMEM((D, FF), BF), pltpu.VMEM((FF, D), BF), pltpu.VMEM((OWN, FF), BF),
                pltpu.VMEM((OWN, FF), F32), pltpu.VMEM(tokens, BF), pltpu.VMEM(tokens, F32),
                pltpu.VMEM(tokens, BF), pltpu.VMEM((OWN, FF), BF), pltpu.VMEM((FF, D), BF),
                dma((2, FF // FF_STEP)), dma((6,)),
            ],
            "feed_forward",
        )
        ff_got = send(ff_snd, core_to, "ff_core")
        out_got = send(out_a, swap, "out_a")
        out_b = send(out_b, swap_b_back, "out_b")
        ff_own, _ = call(
            ff_weight_grads, here + a(left, right), [((FF, D), BF, "a")],
            [
                pltpu.VMEM((FF, D), BF), pltpu.VMEM((4, OWN, D), BF), pltpu.VMEM(tokens, BF),
                dma((9,)),
            ],
            "ff_weight_grads",
        )
        output = jnp.concatenate([jnp.where(stays, out_a, out_got), out_b], axis=0)

        half = D // 2

        def ff_row(g, which):
            return g * D + which * half

        def both(row):
            return [(0, row), (1, row)]

        ff_x, ff_y, _ = add_call(
            "ff_add_1", place, [ff_own, ff_got], [D, D],
            [
                ((0, 0), half, both(ff_row(1, 0))), ((0, half), half, both(ff_row(3, 0))),
                ((1, 0), half, both(ff_row(2, 1))), ((1, half), half, both(ff_row(3, 1))),
            ],
            pins=[out_got, out_b],
        )
        ff_gx = send(ff_x, head_to(1), "ff_heads")
        ff_gy = send(ff_y, head_to(2), "ff_heads")

        wr = weight_rows
        rows_a = [((10 * wr, D), BF, "p")] * 2
        half_e = ((OWN, D // 2), BF, "e")
        cross_w4, self_w4 = cross_own[3], self_out
        enc_half, enc_grads = ((ENC, D // 2), BF, "e"), [enc_full] * 2
        cdq, cdk, cdv, cgrad, ca_own, ca_snd, zero = call(
            cross_backward_a,
            here + l(dsecond, catt, cq, ck, cv, stats2) + d(hat1)
            + v(params) + a(ea, eb, cross_w4, *cross_w),
            [half_e, enc_half, enc_half, (tokens, BF, "e")] + rows_a,
            [weight, pltpu.VMEM(tokens, BF), enc_full, dma((1, 7)), dma((2,))],
            "cross_backward_a", pins=[ff_x, ff_y],
        )
        (ca_snd,) = gated([ca_snd], [ff_gx, ff_gy], "gate_ca")
        ca_got = send(ca_snd, core_to, "ca_core")
        ff_x2, ff_y2, _ = add_call(
            "ff_add_2", place, [ff_own, ff_got, ff_gx, ff_gy], [half, half],
            [
                ((0, 0), half, both(ff_row(2, 0)) + [(2, half)]),
                ((1, 0), half, both(ff_row(1, 1)) + [(3, half)]),
            ],
            pins=[zero],
        )
        ff_gx2 = send(ff_x2, head_to(2), "ff_heads_2")
        ff_gy2 = send(ff_y2, head_to(1), "ff_heads_2")
        c_x3, _ = add_call(
            "c_add_1", place, [ca_own, ca_got], [4 * wr], [((0, 0), 4 * wr, both(4 * wr))],
            pins=[ff_x2],
        )
        c_gx3 = send(c_x3, head_to(1), "c_heads")
        dfirst, cb_own, cb_snd, vectors, zero = call(
            cross_backward_b,
            here + a(cdq, cdk, cdv) + d(dsecond) + l(cgrad, catt, cq, ck, cv, stats2)
            + d(hat1, scale1) + v(params) + a(ea, eb) + v(vec_a, upb)
            + a(*cross_own[:3], *cross_w),
            [
                (tokens, F32, "e"), ((6 * wr + HALF_ENC, D), BF, "p"),
                ((6 * wr + HALF_ENC, D), BF, "p"), ((16, D), F32, "v"),
            ],
            [weight] * 3 + [pltpu.VMEM(tokens, BF)] + enc_grads + [enc_full, dma((3, 7)), dma((5,))],
            "cross_backward_b", pins=[ff_x2, ff_y2, c_x3],
        )
        vectors = lax.all_gather(vectors, names)
        (cb_snd,) = gated([cb_snd], [ff_gx2, ff_gy2, c_gx3], "gate_cb")
        cb_got = send(cb_snd, core_to, "cb_core")

        def depth_send(parts, label):
            return [send(one, depth_to(d + 1), label) for d, one in enumerate(parts)]

        ff_mine, *ff_parts, _ = total_call(
            "ff_add_3", place, [ff_own, ff_got, ff_gx, ff_gy, ff_gx2, ff_gy2], D,
            [
                (0, half, both(ff_row(0, 0)) + [(2, 0), (4, 0)]),
                (half, half, both(ff_row(0, 1)) + [(3, 0), (5, 0)]),
            ],
            1, depth, pins=[zero],
        )
        ff_back = depth_send(ff_parts, "ff_depth")
        c_y2, c_x1, _ = add_call(
            "c_add_2", place, [ca_own, ca_got, cb_own, cb_got, c_gx3], [4 * wr, 4 * wr],
            [
                ((0, 0), 4 * wr, both(0) + [(4, 0)]),
                ((1, 0), 3 * wr, [(2, 3 * wr), (3, 3 * wr)]), ((1, 3 * wr), wr, both(9 * wr)),
            ],
            pins=[ff_parts[0]],
        )
        c_gy2 = send(c_y2, head_to(2), "c_heads_2")
        c_gx1 = send(c_x1, head_to(1), "c_heads_2")

        row_half, row_grads = ((ROW, D // 2), BF, "e"), [row_full] * 2
        sdq, sdk, sdv, sgrad, sa_own, sa_snd, zero = call(
            self_backward_a,
            here + l(dfirst, att, q, kk, vv, stats1) + a(xa, xb, ya, yb)
            + a(self_w4, *cross_w),
            [half_e, row_half, row_half, (tokens, BF, "e")] + rows_a,
            [weight, pltpu.VMEM(tokens, BF), masks]
            + [row_full, pltpu.VMEM((16, D), BF), dma((1, 7)), dma((5,))],
            "self_backward_a", pins=[*ff_parts, c_y2, c_x1],
        )
        (sa_snd,) = gated([sa_snd], [*ff_back, c_gy2, c_gx1], "gate_sa")
        sa_got = send(sa_snd, core_to, "sa_core")
        c_mine, *c_parts, _ = total_call(
            "c_add_3", place, [ca_own, ca_got, cb_own, cb_got, c_gy2, c_gx1], 4 * wr,
            [
                (0, 3 * wr, [(2, 0), (3, 0), (4, 0), (5, 0)]),
                (3 * wr, wr, [(0, 8 * wr), (1, 8 * wr), (4, 3 * wr), (5, 3 * wr)]),
            ],
            1, depth, pins=[zero], mine_type=BF,
        )
        c_depth = depth_send(c_parts, "c_depth")
        s_y, enc_sum, _ = add_call(
            "s_add_1", place, [sa_own, sa_got, cb_own, cb_got], [8 * wr, HALF_ENC],
            [((0, 0), 8 * wr, both(0)), ((1, 0), HALF_ENC, [(2, 6 * wr), (3, 6 * wr)])],
            pins=[c_parts[0]],
        )
        encoder_g = send(enc_sum, swap_b_back, "enc_grad")
        s_gy = send(s_y, head_to(2), "s_heads")
        sb_own, sb_snd, zero = call(
            self_backward_b,
            here + a(sdq, sdk, sdv) + d(dfirst) + l(sgrad, att, q, kk, vv, stats1)
            + a(xa, xb, ya, yb) + a(*self_own, *self_w),
            [((6 * wr + 2 * CHUNK, D), BF, "p"), ((6 * wr + 2 * CHUNK, D), BF, "p")],
            [weight] * 3 + [pltpu.VMEM(tokens, BF)] + row_grads + [masks]
            + [row_full, pltpu.VMEM((ROW, D), F32), pltpu.VMEM((16, D), BF), dma((3, 7)), dma((8,))],
            "self_backward_b", pins=[*c_parts, s_y, enc_sum],
        )
        (sb_snd,) = gated([sb_snd], [*c_depth, s_gy, encoder_g], "gate_sb")
        sb_got = send(sb_snd, core_to, "sb_core")

        def depth_sum(mine, got):
            for one in got:
                mine = mine + one.astype(F32)
            return mine

        part_rows = 4 * wr // depth
        s_x, in_a, in_b, c_part, _ = add_call(
            "s_add_2", place, [sa_own, sa_got, sb_own, sb_got, s_gy, c_mine, *c_depth],
            [4 * wr, CHUNK, CHUNK, part_rows],
            [
                ((0, 0), 3 * wr, [(2, 3 * wr), (3, 3 * wr), (4, 4 * wr)]),
                ((0, 3 * wr), wr, both(9 * wr) + [(4, 7 * wr)]),
                ((1, 0), CHUNK, [(2, 6 * wr), (3, 6 * wr)]),
                ((2, 0), CHUNK, [(2, 6 * wr + CHUNK), (3, 6 * wr + CHUNK)]),
                ((3, 0), part_rows, [(5 + n, 0) for n in range(depth)]),
            ],
        )
        c_back = [send(c_part, depth_to(d), "c_back") for d in range(1, depth)]
        s_gx = send(s_x, head_to(1), "s_heads_2")
        in_got = send(in_a, swap, "in_a")
        in_b = send(in_b, swap_b_back, "in_b")
        s_mine, *s_parts, _ = total_call(
            "s_add_3", place, [sa_own, sa_got, sb_own, sb_got, s_gy, s_gx], 4 * wr,
            [
                (0, 3 * wr, [(2, 0), (3, 0), (4, 0), (5, 0)]),
                (3 * wr, wr, [(0, 8 * wr), (1, 8 * wr), (4, 3 * wr), (5, 3 * wr)]),
            ],
            1, depth, pins=c_back,
        )
        s_depth = depth_send(s_parts, "s_depth")

        def whole_grads(own, other, label):
            *grads, qbias, vbias, _ = call(
                spread(depth, len(own)), here + v(*own, *other),
                [((GROUP, D), F32, "v")] * 4 + [((1, GROUP), F32, "v")] * 2,
                [pltpu.VMEM((2, 4 * wr, D), F32)], label + "_spread",
            )
            return grads, qbias[0], vbias[0]

        input_g = jnp.concatenate([jnp.where(stays, in_a, in_got), in_b], axis=0)
        c_own = jnp.concatenate(gated([c_part, *c_back], s_parts, "gate_c_far"), axis=0)
        c_other = send(c_own, core_to, "c_far")
        (cq_g, ck_g, cv_g, co_g), cqb, cvb = whole_grads([c_own], [c_other], "c")
        s_part = depth_sum(s_mine, s_depth).astype(BF)
        s_back = [send(s_part, depth_to(d), "s_back") for d in range(1, depth)]
        s_own = gated([s_part, *s_back], [cq_g, input_g, output], "gate_s_far")
        s_other = [send(one, core_to, "s_far") for one in s_own]
        (sq_g, sk_g, sv_g, so_g), sqb, svb = whole_grads(s_own, s_other, "s")

        ff = depth_sum(ff_mine, ff_back).reshape(2, piece, D)
        ff_here = lax.dynamic_index_in_dim(ff, core, 0, keepdims=False)
        ff_there = send(lax.dynamic_index_in_dim(ff, 1 - core, 0, keepdims=False), core_to, "ff_last")
        upweight_g = jnp.where(core == 0, ff_here, ff_there).T
        downweight_g = jnp.where(core == 0, ff_there, ff_here)

        vectors = jnp.sum(vectors, axis=0)
        ff_at = (h * rows + r) * piece
        upbias_g = lax.dynamic_slice_in_dim(vectors[9:13].reshape(FF), ff_at, piece)
        return (
            output, input_g, encoder_g,
            sq_g.T, sqb, sk_g.T, sv_g.T, svb, so_g, vectors[8], vectors[6], vectors[7],
            cq_g.T, cqb, ck_g.T, cv_g.T, cvb, co_g, vectors[5],
            vectors[3], vectors[4], upweight_g, upbias_g, downweight_g, vectors[2],
            vectors[0], vectors[1],
        )

    rowed, headed = P(("rows", "heads"), None), P(None, "heads")
    by_head, by_head_rows, whole = P("heads"), P("heads", None), P()
    ffed = ("heads", "rows")
    return jax.shard_map(
        shards,
        mesh=mesh,
        in_specs=(
            rowed, rowed, P("rows", None),
            headed, by_head, headed, headed, by_head, by_head_rows, whole, whole, whole,
            headed, by_head, headed, headed, by_head, by_head_rows, whole, whole, whole,
            whole, whole, whole, whole, whole, whole, rowed,
        ),
        out_specs=(
            rowed, rowed, rowed,
            headed, by_head, headed, headed, by_head, by_head_rows, whole, whole, whole,
            headed, by_head, headed, headed, by_head, by_head_rows, whole, whole, whole,
            P(None, ffed), P(ffed), P(ffed, None), whole, whole, whole,
        ),
        check_vma=False,
    )
```

```python
import jax
import jax.numpy as jnp
from jax import lax
from jax.experimental import pallas as pl
from jax.experimental.pallas import tpu as pltpu
from jax.sharding import PartitionSpec as P

BF = jnp.bfloat16
F32 = jnp.float32
HEAD = 64
PAIR = 128
EPS = 1e-05
ROW = 1088
CHUNK = 272
OWN = 544
ENC = 1024
HALF_ENC = 512
D = 768
GROUP = 192
PIECE = 96
BIAS_ROWS = 16
FF = 3072
MIB = 1 << 20


def nn(a, b):
    return jnp.dot(a, b, preferred_element_type=F32)


def nt(a, b):
    return lax.dot_general(a, b, (((1,), (1,)), ((), ())), preferred_element_type=F32)


def tn(a, b):
    return lax.dot_general(a, b, (((0,), (0,)), ((), ())), preferred_element_type=F32)


def lane_ids(shape):
    return lax.broadcasted_iota(jnp.int32, shape, len(shape) - 1)


def pair_lanes(p):
    return pl.ds(pl.multiple_of(p * PAIR, PAIR), PAIR)


def normalize(total):
    center = total - jnp.mean(total, axis=-1, keepdims=True)
    scale = lax.rsqrt(jnp.mean(center * center, axis=-1, keepdims=True) + EPS)
    return center * scale, scale


def norm_back(grad, hat, scale, gain):
    scaled = grad * gain
    inner = scaled - jnp.mean(scaled, axis=-1, keepdims=True)
    return scale * (inner - hat * jnp.mean(scaled * hat, axis=-1, keepdims=True))


def column(values):
    return jnp.sum(values.astype(F32), axis=0, keepdims=True)


def pick_lane(ref, rows, lane):
    block = ref[rows, :]
    return jnp.sum(jnp.where(lane_ids(block.shape) == lane, block, 0.0), axis=-1, keepdims=True)


def start(copies):
    for one in copies:
        one.start()


def finish(copies):
    for one in copies:
        one.wait()


def by_core(core, body):
    for value in (0, 1):

        @pl.when(core == value)
        def _():
            body(value)


class Row:
    def __init__(self, ref, row):
        self.ref, self.row = ref, row

    def __getitem__(self, _):
        return self.ref[self.row : self.row + 1, :]


class Late:
    def __init__(self, source, held, sem, now):
        self.copy = pltpu.make_async_copy(source, held, sem)
        self.held = held
        self.started = self.waited = False
        if now:
            self.begin()

    def begin(self):
        if not self.started:
            self.copy.start()
            self.started = True

    def get(self):
        self.begin()
        if not self.waited:
            self.copy.wait()
            self.waited = True
        return self.held


class Early:
    def __init__(self, held, target, sem):
        self.copy = pltpu.make_async_copy(held, target, sem)
        self.held = held
        self.sent = False

    def send(self):
        self.copy.start()
        self.sent = True


class Pieces:
    def __init__(self, both, rows, own, snd, sems):
        self.both, self.rows, self.targets, self.sems = both, rows, (own, snd), sems
        self.copies = []

    def send(self, at, count):
        for n in (1, 0):
            self.copies.append(
                pltpu.make_async_copy(
                    self.both.at[pl.ds(n * self.rows + at, count)],
                    self.targets[n].at[pl.ds(at, count)],
                    self.sems.at[len(self.copies)],
                )
            )
            self.copies[-1].start()

    def put(self, core, half, at, block):
        to = jnp.where(core == half, 0, self.rows) + at
        self.both[pl.ds(pl.multiple_of(to, 16), block.shape[0]), :] = block

    def put_both(self, at, block):
        put_rows(self.both, at, block)
        put_rows(self.both, self.rows + at, block)

    def put_own(self, at, block):
        put_rows(self.both, at, block)

    def put_snd(self, at, block):
        put_rows(self.both, self.rows + at, block)


def call(kernel, ins, outs, scratch, name, pins=()):
    vmem, anywhere = pl.BlockSpec(memory_space=pltpu.VMEM), pl.BlockSpec(memory_space=pl.ANY)
    smem = pl.BlockSpec(memory_space=pltpu.SMEM)
    specs = {"v": vmem, "a": anywhere, "l": anywhere, "d": anywhere, "e": anywhere, "p": anywhere}
    specs["s"] = smem
    late = [(n, x) for n, (x, kind) in enumerate(ins) if kind in "ld"]
    early = [(n, out) for n, out in enumerate(outs) if out[2] == "e"]
    pair = [n for n, out in enumerate(outs) if out[2] == "p"]
    first = len(ins)
    last = first + len(pins)
    end = last + len(outs)

    def body(*refs):
        took, gave, rest = list(refs[:first]), list(refs[last:end]), list(refs[end + 1 :])
        own, rest = rest[: len(scratch)], rest[len(scratch) :]
        for n, (at, _) in enumerate(late):
            took[at] = Late(took[at], rest[n], rest[-1].at[n], ins[at][1] == "l")
        rest = rest[len(late) :]
        for n, (at, _) in enumerate(early):
            gave[at] = Early(rest[n], gave[at], rest[-1].at[len(late) + n])
        results, pieces = list(gave), []
        if pair:
            rows = outs[pair[0]][0][0]
            pieces = [Pieces(rest[-3], rows, gave[pair[0]], gave[pair[1]], rest[-2])]
            results[pair[0] : pair[1] + 1] = pieces
        kernel(*took, *results, *own)
        refs[end][...] = jnp.zeros((8, 128), F32)
        for at, _ in late:
            took[at].get()
        for at, _ in early:
            if not gave[at].sent:
                gave[at].send()
        for at, _ in early:
            gave[at].copy.wait()
        for one in pieces:
            finish(one.copies)

    extra = [pltpu.VMEM(x.shape, x.dtype) for _, x in late]
    extra += [pltpu.VMEM(out[0], out[1]) for _, out in early]
    if pair:
        extra += [pltpu.VMEM((2 * outs[pair[0]][0][0], D), BF), pltpu.SemaphoreType.DMA((8,))]
    extra += [pltpu.SemaphoreType.DMA((max(len(late) + len(early), 1),))]
    return pl.pallas_call(
        body,
        in_specs=[specs[kind] for _, kind in ins] + [anywhere] * len(pins),
        out_specs=[specs[out[2]] for out in outs] + [vmem],
        out_shape=[jax.ShapeDtypeStruct(out[0], out[1]) for out in outs]
        + [jax.ShapeDtypeStruct((8, 128), F32)],
        scratch_shapes=list(scratch) + extra,
        compiler_params=pltpu.CompilerParams(vmem_limit_bytes=64 * MIB - 65536),
        cost_estimate=pl.CostEstimate(flops=1000, bytes_accessed=1000, transcendentals=0),
        name=name,
    )(*[x for x, _ in ins], *pins)


def after(value, zero):
    return value + zero[0, 0].astype(value.dtype)


def weight_copies(w, slot, core, own, near, far, dst, sems):
    copies = [pltpu.make_async_copy(own[w], dst.at[pl.ds(0, GROUP)], sems.at[slot, 0])]
    rows = pl.ds(w * PIECE, PIECE)
    for i in (1, 2, 3):
        for at, which, refs in ((i, core, near), (3 + i, 1 - core, far)):
            to = pl.multiple_of(GROUP * i + PIECE * which, PIECE)
            copies.append(
                pltpu.make_async_copy(
                    refs[i - 1].at[rows], dst.at[pl.ds(to, PIECE)], sems.at[slot, at]
                )
            )
    return copies


def half_weight_copies(w, slot, core, own, near, far, half, dst, sems):
    copies = []
    rows = pl.ds(w * PIECE, PIECE)
    for n in (0, 1):
        i = 2 * half + n
        if i == 0:
            copies.append(
                pltpu.make_async_copy(own[w], dst.at[pl.ds(0, GROUP)], sems.at[slot, 0])
            )
            continue
        for at, which, refs in ((i, core, near), (3 + i, 1 - core, far)):
            to = pl.multiple_of(GROUP * n + PIECE * which, PIECE)
            copies.append(
                pltpu.make_async_copy(
                    refs[i - 1].at[rows], dst.at[pl.ds(to, PIECE)], sems.at[slot, at]
                )
            )
    return copies


def bias_copies(near, lines, sems):
    return [
        pltpu.make_async_copy(ref.at[pl.ds(ref.shape[0] - 16, 16)], lines.at[i], sems.at[i])
        for i, ref in enumerate(near)
    ]


def gathered_bias(parts, lines, count, which):
    for i in range(count):
        split = lines[i, 3 * which : 3 * which + 3, :GROUP].astype(F32)
        parts = parts + [split[0:1] + split[1:2] + split[2:3]]
    return jnp.concatenate(parts, axis=1)


def put_rows(target, at, block):
    target[at : at + block.shape[0], :] = block


def store_pieces(core, block, places, pieces):
    for g, at in enumerate(places):
        for half in (0, 1):
            row = g * GROUP + half * PIECE
            pieces.put(core, half, at, block[row : row + PIECE])


def store_bias(row, places, pieces):
    for i, at in enumerate(places):
        one = jnp.concatenate(
            [row[:, i * GROUP : (i + 1) * GROUP], jnp.zeros((1, D - GROUP), F32)], axis=1
        )
        block = jnp.concatenate([one, jnp.zeros((BIAS_ROWS - 1, D), F32)], axis=0).astype(BF)
        pieces.put_both(at + PIECE, block)


def forward_heads(q2, keys, values, bias, row_stats, p):
    lane = lane_ids(q2.shape)
    outs = []
    for t in (0, 1):
        query = jnp.where((lane // HEAD) == t, q2, jnp.zeros_like(q2))
        scores = nt(query, keys)
        if bias is not None:
            scores = scores + bias
        highest = jnp.max(scores, axis=-1, keepdims=True)
        raised = jnp.exp(scores - highest)
        total = jnp.sum(raised, axis=-1, keepdims=True)
        outs.append(nn(raised.astype(BF), values) / total)
        row_stats = jnp.where(
            lane_ids(row_stats.shape) == 2 * p + t, highest + jnp.log(total), row_stats
        )
    return jnp.where((lane // HEAD) == 0, outs[0], outs[1]).astype(BF), row_stats


def backward_heads(q2, g2, o2, keys, values, bias, stats, p):
    count = q2.shape[0]
    first = (lane_ids(q2.shape) // HEAD) == 0
    zero = jnp.zeros_like(q2)

    def stacked(a):
        return jnp.concatenate([jnp.where(first, a, zero), jnp.where(first, zero, a)], axis=0)

    query, grad = stacked(q2), stacked(g2)
    product = g2.astype(F32) * o2.astype(F32)
    inner = jnp.concatenate(
        [
            jnp.sum(jnp.where(first, product, 0.0), axis=-1, keepdims=True),
            jnp.sum(jnp.where(first, 0.0, product), axis=-1, keepdims=True),
        ],
        axis=0,
    )
    lanes = lane_ids(stats.shape)
    lse = jnp.concatenate(
        [
            jnp.sum(jnp.where(lanes == 2 * p + t, stats, 0.0), axis=-1, keepdims=True)
            for t in (0, 1)
        ],
        axis=0,
    )
    scores = nt(query, keys)
    if bias is not None:
        scores = scores + jnp.concatenate([bias, bias], axis=0)
    shares = jnp.exp(scores - lse)
    grad_scores = (shares * (nt(grad, values) - inner)).astype(BF)
    grad_q = nn(grad_scores, keys)
    return (
        jnp.where(first, grad_q[:count], grad_q[count:]),
        tn(grad_scores, query),
        tn(shares.astype(BF), grad),
    )


def document_ends(xa, place):
    pair_at = place[1] // 2
    lengths = jnp.where(
        pair_at == 0,
        xa[0:1, :8] * 16.0 + xa[2:3, :8],
        xa[1:2, :8] * 16.0
        + xa[3:4, :8],
    )
    ends, total = [], 0.0
    for d in range(8):
        total = total + lengths[:, d : d + 1]
        ends.append(total)
    return ends


def mask_bias(ends, chunk, width):
    qpos = chunk * CHUNK + lax.broadcasted_iota(jnp.int32, (CHUNK, 1), 0)
    kpos = lax.broadcasted_iota(jnp.int32, (1, width), 1)
    qat, kat = qpos.astype(F32), kpos.astype(F32)
    qseg = jnp.zeros((CHUNK, 1), F32)
    kseg = jnp.zeros((1, width), F32)
    for end in ends:
        qseg = qseg + jnp.where(qat >= end, 1.0, 0.0)
        kseg = kseg + jnp.where(kat >= end, 1.0, 0.0)
    return jnp.where((qseg == kseg) & (kpos <= qpos), 0.0, -1000000000.0)


def chunk_of(core, which):
    return (2 * core, 3 - 2 * core, 2 - 2 * core, 1 + 2 * core)[which]


def chunk_rows(core, which):
    return pl.ds(pl.multiple_of(chunk_of(core, which) * CHUNK, 16), CHUNK)


def key_counts(core):
    return ((0, 1), (1, 4)) if core == 0 else ((0, 3), (1, 2))


def prepare(place, x, lengths, wq, wk, wv, qbias, vbias, xa, xb, mine):
    xa[0:CHUNK, :] = x[0:CHUNK, :]
    xa[CHUNK : CHUNK + 16, :] = jnp.zeros((16, D), BF)
    counts = lengths[...].astype(F32)
    high = jnp.floor(counts * 0.0625)
    rows = jnp.concatenate([high, counts - high * 16.0, jnp.zeros((12, 8), F32)], axis=0)
    rows = jnp.concatenate([rows, jnp.zeros((16, 120), F32)], axis=1)
    xa[CHUNK : CHUNK + 16, 0:128] = rows.astype(BF)
    xb[...] = x[CHUNK:OWN, :]
    prepare_weights(place[0], (wq, wk, wv), qbias, vbias, mine)


def prepare_more(
    place, so, wq, wk, wv, wo, qbias, vbias, out_grad, enc,
    mine, ga, gb, enc_out,
):
    ga[...] = out_grad[0:CHUNK, :]
    gb[...] = out_grad[CHUNK:OWN, :]
    enc_out[...] = enc[...]
    prepare_weights(place[0], (wq, wk, wv, wo, so), qbias, vbias, mine)


def prepare_weights(core, weights, qbias, vbias, mine):
    half = pl.ds(pl.multiple_of(core * PIECE, PIECE), PIECE)
    for w, one in enumerate(weights):
        mine[w * PIECE : (w + 1) * PIECE, :] = one[half, :]
    rows = []
    for one in (qbias[...], vbias[...]):
        for _ in range(3):
            top = one.astype(BF).astype(F32)
            rows.append(top)
            one = one - top
    rows = jnp.concatenate(rows + [jnp.zeros((10, GROUP), F32)], axis=0)
    at = len(weights) * PIECE
    mine[at : at + 16, :] = jnp.concatenate(
        [rows, jnp.zeros((16, D - GROUP), F32)], axis=1
    ).astype(BF)


def move(place, source, target):
    target[...] = source[...]


def gate(*refs):
    pass


def row_copies(core, xs, full, sems):
    return [
        pltpu.make_async_copy(
            x.at[pl.ds(0, CHUNK)], full.at[chunk_rows(core, which)], sems.at[which]
        )
        for which, x in enumerate(xs)
    ]


def self_forward(half):
    def kernel(
        place, xa, xb, ya, yb, w0, w1, w2, na, fa, nb, fb, qbias, vbias,
        q_out, k_out, v_out, att, stats,
        wq, wk, wv, full, bias, lines, sems, line_sems, row_sems,
    ):
        core = place[0]
        near, far = (na, na, nb), (fa, fa, fb)
        sets = [
            half_weight_copies(w, w, core, (w0, w1, w2), near, far, half, dst, sems)
            for w, dst in enumerate((wq, wk, wv))
        ]
        groups = [na] if half == 0 else [na, nb]
        held = bias_copies(groups, lines, line_sems)
        rows = row_copies(core, (xa, xb, ya, yb), full, row_sems)
        start(rows)
        start(held)
        for one in sets:
            start(one)
        finish(rows[:1])
        tail = pltpu.make_async_copy(xa.at[pl.ds(CHUNK, 16)], lines.at[3], line_sems.at[3])
        tail.start()
        tail.wait()
        ends = document_ends(lines[3].astype(F32), place)
        for slot in (0, 1):
            bias[slot] = mask_bias(ends, chunk_of(core, slot), ROW)
        finish(rows[1:])
        finish(held)
        for one in sets:
            finish(one)

        def line(own, which):
            return gathered_bias([own[...]] if half == 0 else [], lines, len(groups), which)

        k_out.held[...] = nt(full[...], wk[...]).astype(BF)
        k_out.send()
        query_line = line(qbias, 0)
        for which in (0, 1):
            q_out.held[which * CHUNK : (which + 1) * CHUNK, :] = (
                (nt(full[chunk_rows(core, which), :], wq[...]) + query_line) * 0.125
            ).astype(BF)
        q_out.send()
        v_out.held[...] = (nt(full[...], wv[...]) + line(vbias, 1)).astype(BF)
        v_out.send()
        q, k, v = q_out.held, k_out.held, v_out.held
        stats[...] = jnp.zeros_like(stats)

        def attend(value):
            def pair(p, carry):
                lanes = pair_lanes(p)
                for slot, count in key_counts(value):
                    rows = pl.ds(slot * CHUNK, CHUNK)
                    width = count * CHUNK
                    out, now = forward_heads(
                        q[rows, lanes], k[0:width, lanes], v[0:width, lanes],
                        bias[slot, :, 0:width], stats[rows, :], p,
                    )
                    att[rows, lanes] = out
                    stats[rows, :] = now
                return carry

            lax.fori_loop(0, 3, pair, 0)

        by_core(core, attend)

    return kernel


def att_copies(att_a, att_b, full, sems):
    half = D // 2
    return [
        pltpu.make_async_copy(one, full.at[:, pl.ds(n * half, half)], sems.at[n])
        for n, one in enumerate((att_a, att_b))
    ]


def cross_forward(
    place, xa, xb, att_a, att_b, params, ea, eb, w0, w1, w2, w3, w4, n1, n2, n3,
    f1, f2, f3, qbias, vbias,
    hat1, scale1, q_out, k_out, v_out, att, stats, hat_out,
    wq, wk, wv, wo, full, lines, sems, line_sems, row_sems, self_wo, self_sems, self_att, att_sems,
):
    core = place[0]
    self_bias, gain1, shift1, obias = (Row(params, n) for n in range(4))
    near, far = (n1, n2, n3), (f1, f2, f3)
    rows = [
        pltpu.make_async_copy(e, full.at[pl.ds(i * HALF_ENC, HALF_ENC)], row_sems.at[i])
        for i, e in enumerate((ea, eb))
    ]
    held = bias_copies(near, lines, line_sems)
    sets = [
        weight_copies(w, w, core, (w0, w1, w2, w3), near, far, dst, sems)
        for w, dst in enumerate((wq, wk, wv, wo))
    ]
    self_set = weight_copies(
        4, 0, core, (None, None, None, None, w4), near, far, self_wo, self_sems
    )
    halves = att_copies(att_a, att_b, self_att, att_sems)
    start(halves)
    start(self_set)
    start(held)
    start(sets[0])
    start(rows)
    for one in sets[1:]:
        start(one)
    finish(halves)
    finish(self_set)
    product = nn(self_att[...], self_wo[...]) + self_bias[...]
    for which, x in enumerate((xa, xb)):
        part = slice(which * CHUNK, (which + 1) * CHUNK)
        hat, scale = normalize(x[0:CHUNK, :].astype(F32) + product[part])
        hat1.held[part, :] = hat
        scale1[part, :] = jnp.broadcast_to(scale, (CHUNK, 128))
    hat1.send()
    hidden = (hat1.held[...] * gain1[...] + shift1[...]).astype(BF)
    finish(held)
    finish(sets[0])
    line = gathered_bias([qbias[...]], lines, 3, 0)
    q_out.held[...] = ((nt(hidden, wq[...]) + line) * 0.125).astype(BF)
    q_out.send()
    finish(rows)
    finish(sets[1])
    k_out.held[...] = nt(full[...], wk[...]).astype(BF)
    k_out.send()
    finish(sets[2])
    line = gathered_bias([vbias[...]], lines, 3, 1)
    v_out.held[...] = (nt(full[...], wv[...]) + line).astype(BF)
    v_out.send()
    finish(sets[3])
    q, k, v = q_out.held, k_out.held, v_out.held
    stats[...] = jnp.zeros_like(stats)

    def pair(p, carry):
        lanes = pair_lanes(p)
        for slot in (0, 1):
            rows = pl.ds(slot * CHUNK, CHUNK)
            out, now = forward_heads(
                q[rows, lanes], k[:, lanes], v[:, lanes], None, stats[rows, :], p
            )
            att[rows, lanes] = out
            stats[rows, :] = now
        return carry

    lax.fori_loop(0, 6, pair, 0, unroll=True)
    hidden = hat1.held[...] * gain1[...] + shift1[...]
    hat, scale = normalize(hidden + (nn(att[...], wo[...]) + obias[...]))
    hat_out[...] = hat
    stats[...] = jnp.where(lane_ids(stats.shape) == 12, scale, stats[...])


FF_STEP = 512
FF_BLOCK = 768


def gelu_parts(u):
    size = jnp.abs(u)
    t = 1.0 / (1.0 + (0.3275911 * 0.7071067811865476) * size)
    poly = t * (
        0.254829592
        + t * (-0.284496736 + t * (1.421413741 + t * (-1.453152027 + t * 1.061405429)))
    )
    bell = jnp.exp(-0.5 * u * u)
    tail = 0.5 * poly * bell
    phi = jnp.where(u >= 0.0, 1.0 - tail, tail)
    return u * phi, phi + u * bell * 0.3989422804014327


def feed_forward(
    place, hat2, stats, params, up_hbm, up_bias, down_hbm, ga_here, ga, gb,
    out_a, out_b, dsecond, left, right, snd, vec, upb,
    up, down, active, slope, hid, total, third, grads, held, sems, out_sems,
):
    core, group = place[0], place[1]
    gain2, shift2, down_bias, gain3, shift3 = (Row(params, 4 + n) for n in range(5))
    steps = FF // FF_STEP
    ups = [
        pltpu.make_async_copy(
            up_hbm.at[:, pl.ds(i * FF_STEP, FF_STEP)],
            up.at[:, pl.ds(i * FF_STEP, FF_STEP)],
            sems.at[0, i],
        )
        for i in range(steps)
    ]
    downs = [
        pltpu.make_async_copy(
            down_hbm.at[pl.ds(i * FF_STEP, FF_STEP)],
            down.at[pl.ds(i * FF_STEP, FF_STEP)],
            sems.at[1, i],
        )
        for i in range(steps)
    ]
    for i in range(steps):
        ups[i].start()
        downs[i].start()
    second = hat2[...] * gain2[...] + shift2[...]
    hid[...] = second.astype(BF)
    total[...] = second + down_bias[...]
    for i in range(steps):
        cols = pl.ds(i * FF_STEP, FF_STEP)
        ups[i].wait()
        u = nn(hid[...], up[:, cols]) + up_bias[:, cols]
        act, slo = gelu_parts(u)
        active[:, cols] = act.astype(BF)
        slope[:, cols] = slo
        downs[i].wait()
        total[...] += nn(active[:, cols], down[cols, :])
    hat3, scale3 = normalize(total[...])
    out = (hat3 * gain3[...] + shift3[...]).astype(BF)
    out_a[...] = out[0:CHUNK]
    out_b[...] = out[CHUNK:OWN]
    first = jnp.where(core == group % 2, ga_here.get()[...], ga.get()[...])
    grad = jnp.concatenate([first, gb.get()[...]], axis=0).astype(F32)
    vec[0:1, :] = column(grad * hat3)
    vec[1:2, :] = column(grad)
    dthird = norm_back(grad, hat3, scale3, gain3[...])
    total[...] = dthird
    third[...] = dthird.astype(BF)
    vec[2:3, :] = column(third[...])
    for i in range(FF // FF_BLOCK):
        cols = pl.ds(i * FF_BLOCK, FF_BLOCK)
        du = (nt(third[...], down[cols, :]) * slope[:, cols]).astype(BF)
        grads[:, cols] = du
        upb[:, cols] = column(du)
        total[...] += nt(du, up[:, cols])
    grad = total[...]
    hat = hat2[...]
    scale = pick_lane(stats, slice(None), 12)
    vec[3:4, :] = column(grad * hat)
    vec[4:5, :] = column(grad)
    dsec = norm_back(grad, hat, scale, gain2[...])
    dsecond.held[...] = dsec
    dsecond.send()
    vec[5:6, :] = column(dsec.astype(BF))
    vec[6:8, :] = jnp.zeros((2, D), F32)

    def hand_over(value):
        pairs = ((grads, hid), (active, third))
        mine, other = pairs[value], pairs[1 - value]
        copies = [
            pltpu.make_async_copy(mine[0], left, out_sems.at[4]),
            pltpu.make_async_copy(mine[1], right, out_sems.at[5]),
        ]
        start(copies)
        for i in range(4):
            cols = pl.ds(pl.multiple_of((group ^ i) * D, D), D)
            rows = pl.ds(i * D, D)
            held[rows, :] = tn(other[0][:, cols], other[1][...]).astype(BF)
            copies.append(pltpu.make_async_copy(held.at[rows], snd.at[rows], out_sems.at[i]))
            copies[-1].start()
        finish(copies)

    by_core(core, hand_over)


def ff_weight_grads(place, left, right, out, held, left_held, right_held, sems):
    copies = [pltpu.make_async_copy(right, right_held, sems.at[0])]
    for i in range(4):
        cols = pl.ds(pl.multiple_of((place[1] ^ i) * D, D), D)
        copies.append(pltpu.make_async_copy(left.at[:, cols], left_held.at[i], sems.at[1 + i]))
    start(copies[:2])
    finish(copies[:2])
    start(copies[2:])
    outs = []
    for i in range(4):
        if i:
            copies[1 + i].wait()
        rows = pl.ds(i * D, D)
        held[rows, :] = tn(left_held[i], right_held[...]).astype(BF)
        outs.append(pltpu.make_async_copy(held.at[rows], out.at[rows], sems.at[5 + i]))
        outs[i].start()
    finish(outs)


def out_grads(core, att, low, wo, grad, places, pieces):
    store_pieces(core, tn(att[...], low[...]).astype(BF), places, pieces)
    store_bias(jnp.zeros((1, D), F32), places, pieces)
    grad[...] = nt(low[...], wo[...]).astype(BF)


def weight_grads(core, dq, dk, dv, queries, keys, places, pieces):
    store_pieces(core, tn(dq[...], queries).astype(BF), places[0], pieces)
    store_pieces(core, tn(dk[...], keys).astype(BF), places[1], pieces)
    store_pieces(core, tn(dv[...], keys).astype(BF), places[2], pieces)
    store_bias(column(dq[...]), places[0], pieces)
    store_bias(jnp.zeros((1, dk.shape[1]), F32), places[1], pieces)
    store_bias(column(dv[...]), places[2], pieces)


def cross_part(core, first, grad, att, q, k, v, stats, queries, full, places, pieces, dq, dk, dv):

    def pair(p, carry):
        lanes = pair_lanes(first + p)
        out = pair_lanes(p)
        gq, gk, gv = backward_heads(
            q[:, lanes], grad[:, lanes], att[:, lanes], k[:, lanes], v[:, lanes],
            None, stats[...], first + p,
        )
        dq[:, out] = (gq * 0.125).astype(BF)
        dk[:, out] = gk.astype(BF)
        dv[:, out] = gv.astype(BF)
        return carry

    lax.fori_loop(0, 3, pair, 0, unroll=True)
    half = pl.ds(0, D // 2)
    weight_grads(
        core, dq.at[:, half], dk.at[:, half], dv.at[:, half], queries(), full[...], places, pieces
    )


def cross_backward_a(
    place, dsecond, att, q, k, v, stats, hat1, params, ea, eb, w3, n1, n2, n3, f1, f2, f3,
    dq, dk, dv, grad, pieces,
    wo, low, full, sems, row_sems,
):
    core = place[0]
    gain1, shift1 = Row(params, 1), Row(params, 2)
    copies = weight_copies(
        3, 0, core, (None, None, None, w3), (n1, n2, n3), (f1, f2, f3), wo, sems
    )
    rows = [
        pltpu.make_async_copy(e, full.at[pl.ds(i * HALF_ENC, HALF_ENC)], row_sems.at[i])
        for i, e in enumerate((ea, eb))
    ]
    start(copies)
    low[...] = dsecond.get()[...].astype(BF)
    size = pieces.rows // 10
    places = [[(4 * g + w) * size for g in (0, 1)] for w in range(3)]
    places_o = [8 * size, 9 * size, 3 * size, 7 * size]
    att = att.get()
    finish(copies)
    out_grads(core, att, low, wo, grad.held, places_o, pieces)
    grad.send()
    q, k, v, stats = q.get(), k.get(), v.get(), stats.get()
    start(rows)
    hat1.begin()

    def queries():
        for one in (dq, dk, dv):
            one.send()
        finish(rows)
        return (hat1.get()[...] * gain1[...] + shift1[...]).astype(BF)

    cross_part(
        core, 3, grad.held, att, q, k, v, stats, queries, full, places, pieces,
        dq.held, dk.held, dv.held,
    )
    pieces.send(0, 10 * size)


def cross_backward_b(
    place, dq_a, dk_a, dv_a, dsecond, grad, att, q, k, v, stats, hat1, scale1, params, ea, eb,
    vec_a, upb, w0, w1, w2, n1, n2, n3, f1, f2, f3,
    dfirst, pieces, vec,
    wq, wk, wv, dq, dk, dv, full, sems, row_sems,
):
    core = place[0]
    gain1, shift1 = Row(params, 1), Row(params, 2)
    near, far, ws = (n1, n2, n3), (f1, f2, f3), (w0, w1, w2)
    sets = [
        weight_copies(w, w, core, ws, near, far, dst, sems)
        for w, dst in enumerate((wq, wk, wv))
    ]
    rows = [
        pltpu.make_async_copy(e, full.at[pl.ds(i * HALF_ENC, HALF_ENC)], row_sems.at[i])
        for i, e in enumerate((ea, eb))
    ]
    second = pl.ds(D // 2, D // 2)
    parts = [
        pltpu.make_async_copy(one, dst.at[:, second], row_sems.at[2 + n])
        for n, (one, dst) in enumerate(((dq_a, dq), (dk_a, dk), (dv_a, dv)))
    ]
    grad, att, stats = grad.get(), att.get(), stats.get()
    q, k, v = q.get(), k.get(), v.get()
    start(rows)
    hat1.begin()
    for one in sets:
        start(one)
    start(parts)
    dsecond.begin()
    scale1.begin()
    size = (pieces.rows - HALF_ENC) // 6
    places = [[(3 * g + w) * size for g in (0, 1)] for w in range(3)]

    def queries():
        finish(rows)
        return (hat1.get()[...] * gain1[...] + shift1[...]).astype(BF)

    cross_part(
        core, 0, grad, att, q, k, v, stats, queries, full, places, pieces, dq, dk, dv
    )
    pieces.send(0, 6 * size)
    finish(parts)
    for one in sets:
        finish(one)
    enc = nn(dk[...], wk[...]) + nn(dv[...], wv[...])
    pieces.put_own(6 * size, enc[0:HALF_ENC].astype(BF))
    pieces.put_snd(6 * size, enc[HALF_ENC:ENC].astype(BF))
    pieces.send(6 * size, HALF_ENC)
    total = dsecond.get()[...] + nn(dq[...], wq[...])
    hat = hat1.get()[...]
    vec[0:6, :] = vec_a[0:6, :]
    vec[6:7, :] = column(total * hat)
    vec[7:8, :] = column(total)
    dfi = norm_back(total, hat, scale1.get()[:, 0:1], gain1[...])
    dfirst.held[...] = dfi
    dfirst.send()
    vec[8:9, :] = column(dfi.astype(BF))
    for n in range(4):
        vec[9 + n : 10 + n, :] = upb[:, n * D : (n + 1) * D]
    vec[13:16, :] = jnp.zeros((3, D), F32)


def self_part(
    core, first, ends, grad, att, q, k, v, stats, full, places, pieces, dq, dk, dv, bias, rows
):
    for slot in (0, 1):
        bias[slot] = mask_bias(ends, chunk_of(core, slot), ROW)

    def attend(value):
        def pair(p, carry):
            lanes = pair_lanes(first + p)
            out = pair_lanes(p)
            (low_slot, low), (high_slot, high) = sorted(key_counts(value), key=lambda x: x[1])
            parts = {}
            for slot, count in ((low_slot, low), (high_slot, high)):
                rows = pl.ds(slot * CHUNK, CHUNK)
                width = count * CHUNK
                gq, gk, gv = backward_heads(
                    q[rows, out], grad[rows, lanes], att[rows, out],
                    k[0:width, out], v[0:width, out],
                    bias[slot, :, 0:width], stats[rows, :], p,
                )
                dq[rows, out] = (gq * 0.125).astype(BF)
                parts[slot] = (gk, gv)
            for n, dst in ((0, dk), (1, dv)):
                wide, narrow = parts[high_slot][n], parts[low_slot][n]
                shared, reach = low * CHUNK, high * CHUNK
                dst[0:shared, out] = (wide[0:shared] + narrow).astype(BF)
                dst[shared:reach, out] = wide[shared:reach].astype(BF)
                if reach < ROW:
                    dst[reach:ROW, out] = jnp.zeros((ROW - reach, PAIR), BF)
            return carry

        lax.fori_loop(0, 3, pair, 0)

    by_core(core, attend)
    finish(rows)
    half = pl.ds(0, D // 2)
    queries = jnp.concatenate([full[chunk_rows(core, n), :] for n in (0, 1)], axis=0)
    weight_grads(
        core, dq.at[:, half], dk.at[:, half], dv.at[:, half], queries, full[...], places, pieces
    )


def self_backward_a(
    place, dfirst, q, k, v, stats, att_a, att_b, xa, xb, ya, yb, w3, m1, m2, m3, g1, g2, g3,
    dq, dk, dv, grad, pieces,
    wo, low, bias, full, lines, sems, row_sems, att, att_sems,
):
    core = place[0]
    copies = weight_copies(
        4, 0, core, (None, None, None, None, w3), (m1, m2, m3), (g1, g2, g3), wo, sems
    )
    tail = pltpu.make_async_copy(xa.at[pl.ds(CHUNK, 16)], lines, row_sems.at[4])
    rows = row_copies(core, (xa, xb, ya, yb), full, row_sems)
    halves = att_copies(att_a, att_b, att, att_sems)
    start(copies)
    start(halves)
    tail.start()
    low[...] = dfirst.get()[...].astype(BF)
    size = pieces.rows // 10
    places = [[(4 * g + w) * size for g in (0, 1)] for w in range(3)]
    places_o = [8 * size, 9 * size, 3 * size, 7 * size]
    finish(halves)
    finish(copies)
    out_grads(core, att, low, wo, grad.held, places_o, pieces)
    grad.send()
    tail.wait()
    q, k, v, stats = q.get(), k.get(), v.get(), stats.get()
    start(rows)
    self_part(
        core, 3, document_ends(lines[...].astype(F32), place), grad.held,
        att.at[:, pl.ds(D // 2, D // 2)], q, k, v, stats, full,
        places, pieces, dq.held, dk.held, dv.held, bias, rows,
    )
    pieces.send(0, 10 * size)
    for one in (dq, dk, dv):
        one.send()


def self_backward_b(
    place, dq_a, dk_a, dv_a, dfirst, grad, att, q, k, v, stats, xa, xb, ya, yb,
    w0, w1, w2, n1, n2, n3, f1, f2, f3,
    pieces,
    wq, wk, wv, dq, dk, dv, bias, full, total, lines, sems, row_sems,
):
    core = place[0]
    size = (pieces.rows - 2 * CHUNK) // 6
    places = [[(3 * g + w) * size for g in (0, 1)] for w in range(3)]
    near, far, ws = (n1, n2, n3), (f1, f2, f3), (w0, w1, w2)
    sets = [
        weight_copies(w, w, core, ws, near, far, dst, sems)
        for w, dst in enumerate((wq, wk, wv))
    ]
    tail = pltpu.make_async_copy(xa.at[pl.ds(CHUNK, 16)], lines, row_sems.at[4])
    rows = row_copies(core, (xa, xb, ya, yb), full, row_sems)
    second = pl.ds(D // 2, D // 2)
    parts = [
        pltpu.make_async_copy(one, dst.at[:, second], row_sems.at[5 + n])
        for n, (one, dst) in enumerate(((dq_a, dq), (dk_a, dk), (dv_a, dv)))
    ]
    tail.start()
    tail.wait()
    grad, att, stats = grad.get(), att.get(), stats.get()
    q, k, v = q.get(), k.get(), v.get()
    start(rows)
    for one in sets:
        start(one)
    start(parts)
    dfirst.begin()
    self_part(
        core, 0, document_ends(lines[...].astype(F32), place), grad, att, q, k, v, stats, full,
        places, pieces, dq, dk, dv, bias, rows,
    )
    pieces.send(0, 6 * size)
    finish(parts)
    for one in sets:
        finish(one)
    total[...] = nn(dk[...], wk[...]) + nn(dv[...], wv[...])
    mine = nn(dq[...], wq[...]) + dfirst.get()[...]
    for n in (0, 1):
        at = 6 * size + n * CHUNK
        pieces.put_snd(at, total[chunk_rows(core, 2 + n), :].astype(BF))
        pieces.put_own(
            at, (mine[n * CHUNK : (n + 1) * CHUNK] + total[chunk_rows(core, n), :]).astype(BF)
        )
    pieces.send(6 * size, 2 * CHUNK)


def add_jobs(jobs, ins, store, held, sems):
    copies, at, most = [], 0, job_most(jobs)
    for _, rows, sources in jobs:
        mine = []
        for operand, row in sources:
            mine.append(
                (
                    pltpu.make_async_copy(
                        ins[operand].at[pl.ds(row, rows)], held.at[pl.ds(at, rows)],
                        sems.at[len(copies) * most + len(mine)],
                    ),
                    at,
                )
            )
            at += rows
        copies.append(mine)
    for mine in copies:
        for copy, _ in mine:
            copy.start()
    for (place, rows, _), mine in zip(jobs, copies):
        total = 0.0
        for copy, row in mine:
            copy.wait()
            total = total + held[row : row + rows, :].astype(F32)
        store(place, total)


def job_most(jobs):
    return max(len(sources) for _, _, sources in jobs)


def job_rows(jobs):
    return sum(rows * len(sources) for _, rows, sources in jobs)


def add_call(name, place, arrays, outs, jobs, pins=()):
    count = len(arrays)

    def kernel(place, *refs):
        ins, targets = refs[:count], refs[count : count + len(outs)]
        held, out_held, sems, out_sems = refs[count + len(outs) :]
        copies = []

        def store(where, total):
            at = sum(outs[: where[0]]) + where[1]
            put_rows(out_held, at, total.astype(BF))
            rows = pl.ds(at, total.shape[0])
            copies.append(
                pltpu.make_async_copy(
                    out_held.at[rows],
                    targets[where[0]].at[pl.ds(where[1], total.shape[0])],
                    out_sems.at[len(copies)],
                )
            )
            copies[-1].start()

        add_jobs(jobs, ins, store, held, sems)
        finish(copies)

    dma = pltpu.SemaphoreType.DMA
    return call(
        kernel, [(place, "s")] + [(one, "a") for one in arrays],
        [((rows, D), BF, "a") for rows in outs],
        [
            pltpu.VMEM((job_rows(jobs), D), BF), pltpu.VMEM((sum(outs), D), BF),
            dma((job_most(jobs) * len(jobs),)), dma((len(jobs),)),
        ],
        name, pins=pins,
    )


def total_call(name, place, arrays, total_rows, jobs, groups, depth, pins=(), mine_type=F32):
    count = len(arrays)
    size = total_rows // groups // depth

    def kernel(place, *refs):
        mine, parts = refs[count], refs[count + 1 : count + depth]
        held, total, sems = refs[count + depth :]

        def store(row, value):
            put_rows(total, row, value)

        add_jobs(jobs, refs[:count], store, held, sems)
        for d in range(depth):
            for g in range(groups):
                at = pl.multiple_of(
                    g * (total_rows // groups) + (place[2] ^ d) * size, 8
                )
                block = total[pl.ds(at, size), :]
                if d == 0:
                    put_rows(mine, g * size, block.astype(mine_type))
                else:
                    put_rows(parts[d - 1], g * size, block.astype(BF))

    return call(
        kernel, [(place, "s")] + [(one, "a") for one in arrays],
        [((groups * size, D), mine_type, "v")] + [((groups * size, D), BF, "v")] * (depth - 1),
        [
            pltpu.VMEM((job_rows(jobs), D), BF), pltpu.VMEM((total_rows, D), F32),
            pltpu.SemaphoreType.DMA((job_most(jobs) * len(jobs),)),
        ],
        name, pins=pins,
    )


def spread(depth, count):
    def kernel(place, *refs):
        own, other, refs = refs[:count], refs[count : 2 * count], refs[2 * count :]
        outs, biases, total = refs[:4], refs[4:-1], refs[-1]
        core, k = place[0], place[2]
        size = total.shape[1] // depth
        for which, parts in enumerate((own, other)):
            for d in range(depth):
                at = pl.multiple_of((k ^ d) * size, 8)
                ref, row = (parts[d], 0) if count == depth else (parts[0], d * size)
                total[which, pl.ds(at, size), :] = ref[row : row + size, :].astype(F32)
        rows = total.shape[1] // 4
        for n, out in enumerate(outs):
            for which, half in ((0, core), (1, 1 - core)):
                to = pl.ds(pl.multiple_of(half * PIECE, PIECE), PIECE)
                out[to, :] = total[which, n * rows : n * rows + PIECE, :]
        for n, bias in zip((0, 2), biases):
            at = n * rows + PIECE
            bias[...] = total[0, at : at + 1, :GROUP]

    return kernel


def solution(mesh):
    names = tuple(mesh.axis_names)
    heads, rows = mesh.shape["heads"], mesh.shape["rows"]
    depth = rows // 2
    piece = FF // (heads * rows)
    weight_rows = PIECE + BIAS_ROWS
    while (4 * weight_rows) % (8 * depth):
        weight_rows += BIAS_ROWS
    def send(value, where, label="moved"):
        pairs = []
        for r in range(rows):
            for h in range(heads):
                to_r, to_h = where(r, h)
                if (to_r, to_h) == (r, h):
                    continue
                index = {"rows": (r, to_r), "heads": (h, to_h)}
                a = b = 0
                for name in names:
                    a = a * mesh.shape[name] + index[name][0]
                    b = b * mesh.shape[name] + index[name][1]
                pairs.append((a, b))
        with jax.named_scope(label):
            return lax.ppermute(value, names, pairs)

    def swap(r, h):
        return (r & ~1) | (h & 1), (h & ~1) | (r & 1)

    def swap_b(r, h):
        return (r & ~1) | (1 - (h & 1)), (h & ~1) | (r & 1)

    def swap_b_back(r, h):
        return (r & ~1) | (h & 1), (h & ~1) | (1 - (r & 1))

    def core_to(r, h):
        return r ^ 1, h

    def head_to(d):
        return lambda r, h: (r, h ^ d)

    def depth_to(d):
        return lambda r, h: (r ^ (2 * d), h)

    def shards(
        layer_input, encoder_out, doc_lengths,
        self_query, self_qbias, self_key_weight, self_value, self_vbias, self_out, self_obias,
        first_gain, first_shift,
        cross_query, cross_qbias, cross_key, cross_value, cross_vbias, cross_out, cross_obias,
        second_gain, second_shift, up_weight, up_bias, down_weight, down_bias,
        third_gain, third_shift, out_grad,
    ):
        h = lax.axis_index("heads")
        r = lax.axis_index("rows")
        core, k = r % 2, r // 2
        place = jnp.stack([core, h, k]).astype(jnp.int32)
        stays = core == h % 2

        def line(vector):
            return vector.reshape(1, -1)

        params = jnp.stack(
            [
                self_obias, first_gain, first_shift, cross_obias, second_gain, second_shift,
                down_bias, third_gain, third_shift,
            ]
        )

        def v(*arrays):
            return [(one, "v") for one in arrays]

        def a(*arrays):
            return [(one, "a") for one in arrays]

        def l(*arrays):
            return [(one, "l") for one in arrays]

        def d(*arrays):
            return [(one, "d") for one in arrays]

        here = [(place, "s")]

        self_own = [self_query.T, self_key_weight.T, self_value.T]
        cross_own = [cross_query.T, cross_key.T, cross_value.T, cross_out, self_out]
        chunk = ((CHUNK, D), BF, "v")
        xa, xb, mine, zero = call(
            prepare,
            here + v(layer_input, doc_lengths, *self_own, line(self_qbias), line(self_vbias)),
            [((CHUNK + 16, D), BF, "v"), chunk, ((3 * PIECE + 16, D), BF, "v")], [], "prepare",
        )

        def gather_groups(mine, label):
            x, y = send(mine, head_to(1), label), send(mine, head_to(2), label)
            return [x, y, send(x, head_to(2), label + "_2")]

        self_near = gather_groups(mine, "w_self_near")
        xb = send(xb, swap_b, "x_b")
        xa = jnp.where(stays, xa, send(xa, swap, "x_a"))
        mine, ga, gb, enc, _ = call(
            prepare_more,
            here + v(self_out, *cross_own[:4], line(cross_qbias), line(cross_vbias))
            + v(out_grad, encoder_out),
            [((5 * PIECE + 16, D), BF, "v"), chunk, chunk, ((HALF_ENC, D), BF, "v")],
            [], "prepare_more", pins=[zero],
        )
        ya = send(xa, core_to, "y_a")
        yb = send(xb, core_to, "y_b")
        self_far = [send(one, core_to, "w_self_far") for one in self_near]
        self_w = self_near + self_far

        def gated(values, pins, name):
            count = len(values)
            anywhere = pl.BlockSpec(memory_space=pl.ANY)
            return pl.pallas_call(
                gate,
                in_specs=[anywhere] * (count + len(pins)),
                out_specs=[anywhere] * count,
                out_shape=[jax.ShapeDtypeStruct(one.shape, one.dtype) for one in values],
                input_output_aliases={n: n for n in range(count)},
                name=name,
            )(*values, *pins)

        mine, enc = gated([mine, enc], [self_near[0], self_near[1], xa, xb, params], "gate_cross")
        cross_x, cross_y = (send(mine, head_to(d), "w_cross_near") for d in (1, 2))
        ea = send(enc, swap_b, "e_a")

        dma = pltpu.SemaphoreType.DMA
        weight = pltpu.VMEM((D, D), BF)
        half_weight = pltpu.VMEM((D // 2, D), BF)
        masks = pltpu.VMEM((2, CHUNK, ROW), F32)
        lines_bf = pltpu.VMEM((4, 16, D), BF)
        row_full = pltpu.VMEM((ROW, D), BF)
        enc_full = pltpu.VMEM((ENC, D), BF)
        tokens = (OWN, D)

        def self_half(half, weights, pins):
            narrow = ((ROW, D // 2), BF, "e")
            return call(
                self_forward(half),
                here + a(xa, xb, ya, yb, *self_own, *weights)
                + v(line(self_qbias), line(self_vbias)),
                [
                    ((OWN, D // 2), BF, "e"), narrow, narrow, ((OWN, D // 2), BF, "v"),
                    ((OWN, 128), F32, "v"),
                ],
                [half_weight] * 3
                + [row_full, masks, lines_bf, dma((3, 7)), dma((4,)), dma((4,))],
                "self_forward_" + "ab"[half], pins=pins,
            )

        sq, sk, sv, att_a, stats_a, zero = self_half(
            0, [self_near[0], self_far[0]] * 2, [mine, enc]
        )
        (cross_x,) = gated([cross_x], [zero], "gate_forward")
        cross_near = [cross_x, cross_y, send(cross_x, head_to(2), "w_cross_near_2")]
        tq, tk, tv, att_b, stats_b, zero = self_half(
            1, [self_near[1], self_far[1], self_near[2], self_far[2]], [zero, cross_near[0]]
        )
        *cross_near, ea, ga_here, gb = gated(cross_near + [ea, ga, gb], [zero], "gate_far")
        cross_far = [send(one, core_to, "w_cross_far") for one in cross_near]
        eb = send(ea, core_to, "e_b")
        ga = send(ga_here, swap, "g_a")
        gb = send(gb, swap_b, "g_b")
        cross_w = cross_near + cross_far
        hat1, scale1, cq, ck, cv, catt, stats2, hat2, zero = call(
            cross_forward,
            here + v(xa, xb) + a(att_a, att_b) + v(params) + a(ea, eb)
            + a(*cross_own, *cross_w) + v(line(cross_qbias), line(cross_vbias)),
            [
                (tokens, F32, "e"), ((OWN, 128), F32, "v"),
                (tokens, BF, "e"), ((ENC, D), BF, "e"), ((ENC, D), BF, "e"), (tokens, BF, "v"),
                ((OWN, 128), F32, "v"), (tokens, F32, "v"),
            ],
            [weight] * 4 + [
                enc_full, lines_bf, dma((4, 7)), dma((4,)), dma((2,)), weight, dma((1, 7)),
                pltpu.VMEM(tokens, BF), dma((2,)),
            ],
            "cross_forward",
        )
        out_a, out_b, dsecond, left, right, ff_snd, vec_a, upb, zero = call(
            feed_forward,
            here + v(hat2, stats2, params) + a(up_weight) + v(line(up_bias)) + a(down_weight)
            + l(ga_here, ga, gb),
            [
                chunk, chunk, (tokens, F32, "e"), ((OWN, FF), BF, "a"), (tokens, BF, "a"),
                ((FF, D), BF, "a"), ((8, D), F32, "v"), ((1, FF), F32, "v"),
            ],
            [
                pltpu.VMEM((D, FF), BF), pltpu.VMEM((FF, D), BF), pltpu.VMEM((OWN, FF), BF),
                pltpu.VMEM((OWN, FF), F32), pltpu.VMEM(tokens, BF), pltpu.VMEM(tokens, F32),
                pltpu.VMEM(tokens, BF), pltpu.VMEM((OWN, FF), BF), pltpu.VMEM((FF, D), BF),
                dma((2, FF // FF_STEP)), dma((6,)),
            ],
            "feed_forward",
        )
        ff_got = send(ff_snd, core_to, "ff_core")
        out_got = send(out_a, swap, "out_a")
        out_b = send(out_b, swap_b_back, "out_b")
        ff_own, _ = call(
            ff_weight_grads, here + a(left, right), [((FF, D), BF, "a")],
            [
                pltpu.VMEM((FF, D), BF), pltpu.VMEM((4, OWN, D), BF), pltpu.VMEM(tokens, BF),
                dma((9,)),
            ],
            "ff_weight_grads",
        )
        output = jnp.concatenate([jnp.where(stays, out_a, out_got), out_b], axis=0)

        half = D // 2

        def ff_row(g, which):
            return g * D + which * half

        def both(row):
            return [(0, row), (1, row)]

        ff_x, ff_y, _ = add_call(
            "ff_add_1", place, [ff_own, ff_got], [D, D],
            [
                ((0, 0), half, both(ff_row(1, 0))), ((0, half), half, both(ff_row(3, 0))),
                ((1, 0), half, both(ff_row(2, 1))), ((1, half), half, both(ff_row(3, 1))),
            ],
            pins=[out_got, out_b],
        )
        ff_gx = send(ff_x, head_to(1), "ff_heads")
        ff_gy = send(ff_y, head_to(2), "ff_heads")

        wr = weight_rows
        rows_a = [((10 * wr, D), BF, "p")] * 2
        half_e = ((OWN, D // 2), BF, "e")
        cross_w4, self_w4 = cross_own[3], self_out
        enc_half, enc_grads = ((ENC, D // 2), BF, "e"), [enc_full] * 2
        cdq, cdk, cdv, cgrad, ca_own, ca_snd, zero = call(
            cross_backward_a,
            here + l(dsecond, catt, cq, ck, cv, stats2) + d(hat1)
            + v(params) + a(ea, eb, cross_w4, *cross_w),
            [half_e, enc_half, enc_half, (tokens, BF, "e")] + rows_a,
            [weight, pltpu.VMEM(tokens, BF), enc_full, dma((1, 7)), dma((2,))],
            "cross_backward_a", pins=[ff_x, ff_y],
        )
        (ca_snd,) = gated([ca_snd], [ff_gx, ff_gy, output], "gate_ca")
        ca_got = send(ca_snd, core_to, "ca_core")
        ff_x2, ff_y2, _ = add_call(
            "ff_add_2", place, [ff_own, ff_got, ff_gx, ff_gy], [half, half],
            [
                ((0, 0), half, both(ff_row(2, 0)) + [(2, half)]),
                ((1, 0), half, both(ff_row(1, 1)) + [(3, half)]),
            ],
            pins=[zero],
        )
        ff_gx2 = send(ff_x2, head_to(2), "ff_heads_2")
        ff_gy2 = send(ff_y2, head_to(1), "ff_heads_2")
        c_x3, _ = add_call(
            "c_add_1", place, [ca_own, ca_got], [4 * wr], [((0, 0), 4 * wr, both(4 * wr))],
            pins=[ff_x2],
        )
        c_gx3 = send(c_x3, head_to(1), "c_heads")
        dfirst, cb_own, cb_snd, vectors, zero = call(
            cross_backward_b,
            here + a(cdq, cdk, cdv) + d(dsecond) + l(cgrad, catt, cq, ck, cv, stats2)
            + d(hat1, scale1) + v(params) + a(ea, eb) + v(vec_a, upb)
            + a(*cross_own[:3], *cross_w),
            [
                (tokens, F32, "e"), ((6 * wr + HALF_ENC, D), BF, "p"),
                ((6 * wr + HALF_ENC, D), BF, "p"), ((16, D), F32, "v"),
            ],
            [weight] * 3 + [pltpu.VMEM(tokens, BF)] + enc_grads + [enc_full, dma((3, 7)), dma((5,))],
            "cross_backward_b", pins=[ff_x2, ff_y2, c_x3],
        )
        vectors = lax.all_gather(vectors, names)
        (cb_snd,) = gated([cb_snd], [ff_gx2, ff_gy2, c_gx3], "gate_cb")
        cb_got = send(cb_snd, core_to, "cb_core")

        def depth_send(parts, label):
            return [send(one, depth_to(d + 1), label) for d, one in enumerate(parts)]

        ff_mine, *ff_parts, _ = total_call(
            "ff_add_3", place, [ff_own, ff_got, ff_gx, ff_gy, ff_gx2, ff_gy2], D,
            [
                (0, half, both(ff_row(0, 0)) + [(2, 0), (4, 0)]),
                (half, half, both(ff_row(0, 1)) + [(3, 0), (5, 0)]),
            ],
            1, depth, pins=[zero],
        )
        ff_back = depth_send(ff_parts, "ff_depth")
        c_y2, c_x1, _ = add_call(
            "c_add_2", place, [ca_own, ca_got, cb_own, cb_got, c_gx3], [4 * wr, 4 * wr],
            [
                ((0, 0), 4 * wr, both(0) + [(4, 0)]),
                ((1, 0), 3 * wr, [(2, 3 * wr), (3, 3 * wr)]), ((1, 3 * wr), wr, both(9 * wr)),
            ],
            pins=[ff_parts[0]],
        )
        c_gy2 = send(c_y2, head_to(2), "c_heads_2")
        c_gx1 = send(c_x1, head_to(1), "c_heads_2")

        row_half, row_grads = ((ROW, D // 2), BF, "e"), [row_full] * 2
        sdq, sdk, sdv, sgrad, sa_own, sa_snd, zero = call(
            self_backward_a,
            here + l(dfirst, tq, tk, tv, stats_b) + a(att_a, att_b, xa, xb, ya, yb)
            + a(self_w4, *cross_w),
            [half_e, row_half, row_half, (tokens, BF, "e")] + rows_a,
            [weight, pltpu.VMEM(tokens, BF), masks]
            + [row_full, pltpu.VMEM((16, D), BF), dma((1, 7)), dma((5,))]
            + [pltpu.VMEM(tokens, BF), dma((2,))],
            "self_backward_a", pins=[*ff_parts, c_y2, c_x1],
        )
        (sa_snd,) = gated([sa_snd], [*ff_back, c_gy2, c_gx1], "gate_sa")
        sa_got = send(sa_snd, core_to, "sa_core")
        c_mine, *c_parts, _ = total_call(
            "c_add_3", place, [ca_own, ca_got, cb_own, cb_got, c_gy2, c_gx1], 4 * wr,
            [
                (0, 3 * wr, [(2, 0), (3, 0), (4, 0), (5, 0)]),
                (3 * wr, wr, [(0, 8 * wr), (1, 8 * wr), (4, 3 * wr), (5, 3 * wr)]),
            ],
            1, depth, pins=[zero], mine_type=BF,
        )
        c_depth = depth_send(c_parts, "c_depth")
        s_y, enc_sum, _ = add_call(
            "s_add_1", place, [sa_own, sa_got, cb_own, cb_got], [8 * wr, HALF_ENC],
            [((0, 0), 8 * wr, both(0)), ((1, 0), HALF_ENC, [(2, 6 * wr), (3, 6 * wr)])],
            pins=[c_parts[0]],
        )
        encoder_g = send(enc_sum, swap_b_back, "enc_grad")
        s_gy = send(s_y, head_to(2), "s_heads")
        sb_own, sb_snd, zero = call(
            self_backward_b,
            here + a(sdq, sdk, sdv) + d(dfirst) + l(sgrad, att_a, sq, sk, sv, stats_a)
            + a(xa, xb, ya, yb) + a(*self_own, *self_w),
            [((6 * wr + 2 * CHUNK, D), BF, "p"), ((6 * wr + 2 * CHUNK, D), BF, "p")],
            [weight] * 3 + [pltpu.VMEM(tokens, BF)] + row_grads + [masks]
            + [row_full, pltpu.VMEM((ROW, D), F32), pltpu.VMEM((16, D), BF), dma((3, 7)), dma((8,))],
            "self_backward_b", pins=[*c_parts, s_y, enc_sum],
        )
        (sb_snd,) = gated([sb_snd], [*c_depth, s_gy, encoder_g], "gate_sb")
        sb_got = send(sb_snd, core_to, "sb_core")

        def depth_sum(mine, got):
            for one in got:
                mine = mine + one.astype(F32)
            return mine

        part_rows = 4 * wr // depth
        s_x, in_a, in_b, c_part, _ = add_call(
            "s_add_2", place, [sa_own, sa_got, sb_own, sb_got, s_gy, c_mine, *c_depth],
            [4 * wr, CHUNK, CHUNK, part_rows],
            [
                ((0, 0), 3 * wr, [(2, 3 * wr), (3, 3 * wr), (4, 4 * wr)]),
                ((0, 3 * wr), wr, both(9 * wr) + [(4, 7 * wr)]),
                ((1, 0), CHUNK, [(2, 6 * wr), (3, 6 * wr)]),
                ((2, 0), CHUNK, [(2, 6 * wr + CHUNK), (3, 6 * wr + CHUNK)]),
                ((3, 0), part_rows, [(5 + n, 0) for n in range(depth)]),
            ],
        )
        c_back = [send(c_part, depth_to(d), "c_back") for d in range(1, depth)]
        s_gx = send(s_x, head_to(1), "s_heads_2")
        in_got = send(in_a, swap, "in_a")
        in_b = send(in_b, swap_b_back, "in_b")
        s_mine, *s_parts, _ = total_call(
            "s_add_3", place, [sa_own, sa_got, sb_own, sb_got, s_gy, s_gx], 4 * wr,
            [
                (0, 3 * wr, [(2, 0), (3, 0), (4, 0), (5, 0)]),
                (3 * wr, wr, [(0, 8 * wr), (1, 8 * wr), (4, 3 * wr), (5, 3 * wr)]),
            ],
            1, depth, pins=c_back,
        )
        s_depth = depth_send(s_parts, "s_depth")

        def whole_grads(own, other, label):
            *grads, qbias, vbias, _ = call(
                spread(depth, len(own)), here + v(*own, *other),
                [((GROUP, D), F32, "v")] * 4 + [((1, GROUP), F32, "v")] * 2,
                [pltpu.VMEM((2, 4 * wr, D), F32)], label + "_spread",
            )
            return grads, qbias[0], vbias[0]

        input_g = jnp.concatenate([jnp.where(stays, in_a, in_got), in_b], axis=0)
        c_own = jnp.concatenate(gated([c_part, *c_back], s_parts, "gate_c_far"), axis=0)
        c_other = send(c_own, core_to, "c_far")
        (cq_g, ck_g, cv_g, co_g), cqb, cvb = whole_grads([c_own], [c_other], "c")
        s_part = depth_sum(s_mine, s_depth).astype(BF)
        s_back = [send(s_part, depth_to(d), "s_back") for d in range(1, depth)]
        ff = depth_sum(ff_mine, ff_back).reshape(2, piece, D)
        ff_here = lax.dynamic_index_in_dim(ff, core, 0, keepdims=False)
        ff_there = send(lax.dynamic_index_in_dim(ff, 1 - core, 0, keepdims=False), core_to, "ff_last")
        upweight_g = jnp.where(core == 0, ff_here, ff_there).T
        downweight_g = jnp.where(core == 0, ff_there, ff_here)

        vectors = jnp.sum(vectors, axis=0)
        ff_at = (h * rows + r) * piece
        upbias_g = lax.dynamic_slice_in_dim(vectors[9:13].reshape(FF), ff_at, piece)
        (encoder_g, _) = call(
            move, here + v(encoder_g), [((HALF_ENC, D), BF, "v")], [], "encoder_grad", pins=s_parts
        )
        s_own = gated([s_part, *s_back], [cq_g, input_g, ff_here, ff_there, vectors, encoder_g], "gate_s_far")
        s_other = [send(one, core_to, "s_far") for one in s_own]
        (sq_g, sk_g, sv_g, so_g), sqb, svb = whole_grads(s_own, s_other, "s")

        return (
            output, input_g, encoder_g,
            sq_g.T, sqb, sk_g.T, sv_g.T, svb, so_g, vectors[8], vectors[6], vectors[7],
            cq_g.T, cqb, ck_g.T, cv_g.T, cvb, co_g, vectors[5],
            vectors[3], vectors[4], upweight_g, upbias_g, downweight_g, vectors[2],
            vectors[0], vectors[1],
        )

    rowed, headed = P(("rows", "heads"), None), P(None, "heads")
    by_head, by_head_rows, whole = P("heads"), P("heads", None), P()
    ffed = ("heads", "rows")
    return jax.shard_map(
        shards,
        mesh=mesh,
        in_specs=(
            rowed, rowed, P("rows", None),
            headed, by_head, headed, headed, by_head, by_head_rows, whole, whole, whole,
            headed, by_head, headed, headed, by_head, by_head_rows, whole, whole, whole,
            whole, whole, whole, whole, whole, whole, rowed,
        ),
        out_specs=(
            rowed, rowed, rowed,
            headed, by_head, headed, headed, by_head, by_head_rows, whole, whole, whole,
            headed, by_head, headed, headed, by_head, by_head_rows, whole, whole, whole,
            P(None, ffed), P(ffed), P(ffed, None), whole, whole, whole,
        ),
        check_vma=False,
    )
```

```python
import jax
import jax.numpy as jnp
from jax import lax
from jax.experimental import pallas as pl
from jax.experimental.pallas import tpu as pltpu
from jax.sharding import PartitionSpec as P

BF = jnp.bfloat16
F32 = jnp.float32
HEAD = 64
PAIR = 128
EPS = 1e-05
ROW = 1088
CHUNK = 272
OWN = 544
ENC = 1024
HALF_ENC = 512
D = 768
GROUP = 192
PIECE = 96
BIAS_ROWS = 16
FF = 3072
MIB = 1 << 20


def nn(a, b):
    return jnp.dot(a, b, preferred_element_type=F32)


def nt(a, b):
    return lax.dot_general(a, b, (((1,), (1,)), ((), ())), preferred_element_type=F32)


def tn(a, b):
    return lax.dot_general(a, b, (((0,), (0,)), ((), ())), preferred_element_type=F32)


def lane_ids(shape):
    return lax.broadcasted_iota(jnp.int32, shape, len(shape) - 1)


def pair_lanes(p):
    return pl.ds(pl.multiple_of(p * PAIR, PAIR), PAIR)


def normalize(total):
    center = total - jnp.mean(total, axis=-1, keepdims=True)
    scale = lax.rsqrt(jnp.mean(center * center, axis=-1, keepdims=True) + EPS)
    return center * scale, scale


def norm_back(grad, hat, scale, gain):
    scaled = grad * gain
    inner = scaled - jnp.mean(scaled, axis=-1, keepdims=True)
    return scale * (inner - hat * jnp.mean(scaled * hat, axis=-1, keepdims=True))


def column(values):
    return jnp.sum(values.astype(F32), axis=0, keepdims=True)


def pick_lane(ref, rows, lane):
    block = ref[rows, :]
    return jnp.sum(jnp.where(lane_ids(block.shape) == lane, block, 0.0), axis=-1, keepdims=True)


def start(copies):
    for one in copies:
        one.start()


def finish(copies):
    for one in copies:
        one.wait()


def by_core(core, body):
    for value in (0, 1):

        @pl.when(core == value)
        def _():
            body(value)


class Row:
    def __init__(self, ref, row):
        self.ref, self.row = ref, row

    def __getitem__(self, _):
        return self.ref[self.row : self.row + 1, :]


class Late:
    def __init__(self, source, held, sem, now):
        self.copy = pltpu.make_async_copy(source, held, sem)
        self.held = held
        self.started = self.waited = False
        if now:
            self.begin()

    def begin(self):
        if not self.started:
            self.copy.start()
            self.started = True

    def get(self):
        self.begin()
        if not self.waited:
            self.copy.wait()
            self.waited = True
        return self.held


class Early:
    def __init__(self, held, target, sem):
        self.copy = pltpu.make_async_copy(held, target, sem)
        self.held = held
        self.sent = False

    def send(self):
        self.copy.start()
        self.sent = True


class Pieces:
    def __init__(self, both, rows, own, snd, sems):
        self.both, self.rows, self.targets, self.sems = both, rows, (own, snd), sems
        self.copies = []

    def send(self, at, count):
        for n in (1, 0):
            self.copies.append(
                pltpu.make_async_copy(
                    self.both.at[pl.ds(n * self.rows + at, count)],
                    self.targets[n].at[pl.ds(at, count)],
                    self.sems.at[len(self.copies)],
                )
            )
            self.copies[-1].start()

    def put(self, core, half, at, block):
        to = jnp.where(core == half, 0, self.rows) + at
        self.both[pl.ds(pl.multiple_of(to, 16), block.shape[0]), :] = block

    def put_both(self, at, block):
        put_rows(self.both, at, block)
        put_rows(self.both, self.rows + at, block)

    def put_own(self, at, block):
        put_rows(self.both, at, block)

    def put_snd(self, at, block):
        put_rows(self.both, self.rows + at, block)


def call(kernel, ins, outs, scratch, name, pins=()):
    vmem, anywhere = pl.BlockSpec(memory_space=pltpu.VMEM), pl.BlockSpec(memory_space=pl.ANY)
    smem = pl.BlockSpec(memory_space=pltpu.SMEM)
    specs = {"v": vmem, "a": anywhere, "l": anywhere, "d": anywhere, "e": anywhere, "p": anywhere}
    specs["s"] = smem
    late = [(n, x) for n, (x, kind) in enumerate(ins) if kind in "ld"]
    early = [(n, out) for n, out in enumerate(outs) if out[2] == "e"]
    pair = [n for n, out in enumerate(outs) if out[2] == "p"]
    first = len(ins)
    last = first + len(pins)
    end = last + len(outs)

    def body(*refs):
        took, gave, rest = list(refs[:first]), list(refs[last:end]), list(refs[end + 1 :])
        own, rest = rest[: len(scratch)], rest[len(scratch) :]
        for n, (at, _) in enumerate(late):
            took[at] = Late(took[at], rest[n], rest[-1].at[n], ins[at][1] == "l")
        rest = rest[len(late) :]
        for n, (at, _) in enumerate(early):
            gave[at] = Early(rest[n], gave[at], rest[-1].at[len(late) + n])
        results, pieces = list(gave), []
        if pair:
            rows = outs[pair[0]][0][0]
            pieces = [Pieces(rest[-3], rows, gave[pair[0]], gave[pair[1]], rest[-2])]
            results[pair[0] : pair[1] + 1] = pieces
        kernel(*took, *results, *own)
        refs[end][...] = jnp.zeros((8, 128), F32)
        for at, _ in late:
            took[at].get()
        for at, _ in early:
            if not gave[at].sent:
                gave[at].send()
        for at, _ in early:
            gave[at].copy.wait()
        for one in pieces:
            finish(one.copies)

    extra = [pltpu.VMEM(x.shape, x.dtype) for _, x in late]
    extra += [pltpu.VMEM(out[0], out[1]) for _, out in early]
    if pair:
        extra += [pltpu.VMEM((2 * outs[pair[0]][0][0], D), BF), pltpu.SemaphoreType.DMA((8,))]
    extra += [pltpu.SemaphoreType.DMA((max(len(late) + len(early), 1),))]
    return pl.pallas_call(
        body,
        in_specs=[specs[kind] for _, kind in ins] + [anywhere] * len(pins),
        out_specs=[specs[out[2]] for out in outs] + [vmem],
        out_shape=[jax.ShapeDtypeStruct(out[0], out[1]) for out in outs]
        + [jax.ShapeDtypeStruct((8, 128), F32)],
        scratch_shapes=list(scratch) + extra,
        compiler_params=pltpu.CompilerParams(vmem_limit_bytes=64 * MIB - 65536),
        cost_estimate=pl.CostEstimate(flops=1000, bytes_accessed=1000, transcendentals=0),
        name=name,
    )(*[x for x, _ in ins], *pins)


def after(value, zero):
    return value + zero[0, 0].astype(value.dtype)


def weight_copies(w, slot, core, own, near, far, dst, sems):
    copies = [pltpu.make_async_copy(own[w], dst.at[pl.ds(0, GROUP)], sems.at[slot, 0])]
    rows = pl.ds(w * PIECE, PIECE)
    for i in (1, 2, 3):
        for at, which, refs in ((i, core, near), (3 + i, 1 - core, far)):
            to = pl.multiple_of(GROUP * i + PIECE * which, PIECE)
            copies.append(
                pltpu.make_async_copy(
                    refs[i - 1].at[rows], dst.at[pl.ds(to, PIECE)], sems.at[slot, at]
                )
            )
    return copies


def half_weight_copies(w, slot, core, own, near, far, half, dst, sems):
    copies = []
    rows = pl.ds(w * PIECE, PIECE)
    for n in (0, 1):
        i = 2 * half + n
        if i == 0:
            copies.append(
                pltpu.make_async_copy(own[w], dst.at[pl.ds(0, GROUP)], sems.at[slot, 0])
            )
            continue
        for at, which, refs in ((i, core, near), (3 + i, 1 - core, far)):
            to = pl.multiple_of(GROUP * n + PIECE * which, PIECE)
            copies.append(
                pltpu.make_async_copy(
                    refs[i - 1].at[rows], dst.at[pl.ds(to, PIECE)], sems.at[slot, at]
                )
            )
    return copies


def bias_copies(near, lines, sems):
    return [
        pltpu.make_async_copy(ref.at[pl.ds(ref.shape[0] - 16, 16)], lines.at[i], sems.at[i])
        for i, ref in enumerate(near)
    ]


def gathered_bias(parts, lines, count, which):
    for i in range(count):
        split = lines[i, 3 * which : 3 * which + 3, :GROUP].astype(F32)
        parts = parts + [split[0:1] + split[1:2] + split[2:3]]
    return jnp.concatenate(parts, axis=1)


def put_rows(target, at, block):
    target[at : at + block.shape[0], :] = block


def store_pieces(core, block, places, pieces):
    for g, at in enumerate(places):
        for half in (0, 1):
            row = g * GROUP + half * PIECE
            pieces.put(core, half, at, block[row : row + PIECE])


def store_bias(row, places, pieces):
    for i, at in enumerate(places):
        one = jnp.concatenate(
            [row[:, i * GROUP : (i + 1) * GROUP], jnp.zeros((1, D - GROUP), F32)], axis=1
        )
        block = jnp.concatenate([one, jnp.zeros((BIAS_ROWS - 1, D), F32)], axis=0).astype(BF)
        pieces.put_both(at + PIECE, block)


def forward_heads(q2, keys, values, bias, row_stats, p):
    lane = lane_ids(q2.shape)
    outs = []
    for t in (0, 1):
        query = jnp.where((lane // HEAD) == t, q2, jnp.zeros_like(q2))
        scores = nt(query, keys)
        if bias is not None:
            scores = scores + bias
        highest = jnp.max(scores, axis=-1, keepdims=True)
        raised = jnp.exp(scores - highest)
        total = jnp.sum(raised, axis=-1, keepdims=True)
        outs.append(nn(raised.astype(BF), values) / total)
        row_stats = jnp.where(
            lane_ids(row_stats.shape) == 2 * p + t, highest + jnp.log(total), row_stats
        )
    return jnp.where((lane // HEAD) == 0, outs[0], outs[1]).astype(BF), row_stats


def backward_heads(q2, g2, o2, keys, values, bias, stats, p):
    count = q2.shape[0]
    first = (lane_ids(q2.shape) // HEAD) == 0
    zero = jnp.zeros_like(q2)

    def stacked(a):
        return jnp.concatenate([jnp.where(first, a, zero), jnp.where(first, zero, a)], axis=0)

    query, grad = stacked(q2), stacked(g2)
    product = g2.astype(F32) * o2.astype(F32)
    inner = jnp.concatenate(
        [
            jnp.sum(jnp.where(first, product, 0.0), axis=-1, keepdims=True),
            jnp.sum(jnp.where(first, 0.0, product), axis=-1, keepdims=True),
        ],
        axis=0,
    )
    lanes = lane_ids(stats.shape)
    lse = jnp.concatenate(
        [
            jnp.sum(jnp.where(lanes == 2 * p + t, stats, 0.0), axis=-1, keepdims=True)
            for t in (0, 1)
        ],
        axis=0,
    )
    scores = nt(query, keys)
    if bias is not None:
        scores = scores + jnp.concatenate([bias, bias], axis=0)
    shares = jnp.exp(scores - lse)
    grad_scores = (shares * (nt(grad, values) - inner)).astype(BF)
    grad_q = nn(grad_scores, keys)
    return (
        jnp.where(first, grad_q[:count], grad_q[count:]),
        tn(grad_scores, query),
        tn(shares.astype(BF), grad),
    )


def document_ends(xa, place):
    pair_at = place[1] // 2
    lengths = jnp.where(
        pair_at == 0,
        xa[0:1, :8] * 16.0 + xa[2:3, :8],
        xa[1:2, :8] * 16.0
        + xa[3:4, :8],
    )
    ends, total = [], 0.0
    for d in range(8):
        total = total + lengths[:, d : d + 1]
        ends.append(total)
    return ends


def mask_bias(ends, chunk, width):
    qpos = chunk * CHUNK + lax.broadcasted_iota(jnp.int32, (CHUNK, 1), 0)
    kpos = lax.broadcasted_iota(jnp.int32, (1, width), 1)
    qat, kat = qpos.astype(F32), kpos.astype(F32)
    qseg = jnp.zeros((CHUNK, 1), F32)
    kseg = jnp.zeros((1, width), F32)
    for end in ends:
        qseg = qseg + jnp.where(qat >= end, 1.0, 0.0)
        kseg = kseg + jnp.where(kat >= end, 1.0, 0.0)
    return jnp.where((qseg == kseg) & (kpos <= qpos), 0.0, -1000000000.0)


def chunk_of(core, which):
    return (2 * core, 3 - 2 * core, 2 - 2 * core, 1 + 2 * core)[which]


def chunk_rows(core, which):
    return pl.ds(pl.multiple_of(chunk_of(core, which) * CHUNK, 16), CHUNK)


def key_counts(core):
    return ((0, 1), (1, 4)) if core == 0 else ((0, 3), (1, 2))


def prepare(place, x, lengths, wq, wk, wv, qbias, vbias, xa, xb, mine):
    xa[0:CHUNK, :] = x[0:CHUNK, :]
    xa[CHUNK : CHUNK + 16, :] = jnp.zeros((16, D), BF)
    counts = lengths[...].astype(F32)
    high = jnp.floor(counts * 0.0625)
    rows = jnp.concatenate([high, counts - high * 16.0, jnp.zeros((12, 8), F32)], axis=0)
    rows = jnp.concatenate([rows, jnp.zeros((16, 120), F32)], axis=1)
    xa[CHUNK : CHUNK + 16, 0:128] = rows.astype(BF)
    xb[...] = x[CHUNK:OWN, :]
    prepare_weights(place[0], (wq, wk, wv), qbias, vbias, mine)


def prepare_more(
    place, so, wq, wk, wv, wo, qbias, vbias, out_grad, enc,
    mine, ga, gb, enc_out,
):
    ga[...] = out_grad[0:CHUNK, :]
    gb[...] = out_grad[CHUNK:OWN, :]
    enc_out[...] = enc[...]
    prepare_weights(place[0], (wq, wk, wv, wo, so), qbias, vbias, mine)


def prepare_weights(core, weights, qbias, vbias, mine):
    half = pl.ds(pl.multiple_of(core * PIECE, PIECE), PIECE)
    for w, one in enumerate(weights):
        mine[w * PIECE : (w + 1) * PIECE, :] = one[half, :]
    rows = []
    for one in (qbias[...], vbias[...]):
        for _ in range(3):
            top = one.astype(BF).astype(F32)
            rows.append(top)
            one = one - top
    rows = jnp.concatenate(rows + [jnp.zeros((10, GROUP), F32)], axis=0)
    at = len(weights) * PIECE
    mine[at : at + 16, :] = jnp.concatenate(
        [rows, jnp.zeros((16, D - GROUP), F32)], axis=1
    ).astype(BF)


def join(place, *refs):
    at = 0
    for one in refs[:-1]:
        put_rows(refs[-1], at, one[...])
        at += one.shape[0]


def move(place, source, target):
    target[...] = source[...]


def gate(*refs):
    pass


def row_copies(core, xs, full, sems):
    return [
        pltpu.make_async_copy(
            x.at[pl.ds(0, CHUNK)], full.at[chunk_rows(core, which)], sems.at[which]
        )
        for which, x in enumerate(xs)
    ]


def self_forward(half):
    def kernel(
        place, xa, xb, ya, yb, w0, w1, w2, na, fa, nb, fb, qbias, vbias,
        q_out, k_out, v_out, att, stats,
        wq, wk, wv, full, bias, lines, sems, line_sems, row_sems,
    ):
        core = place[0]
        near, far = (na, na, nb), (fa, fa, fb)
        sets = [
            half_weight_copies(w, w, core, (w0, w1, w2), near, far, half, dst, sems)
            for w, dst in enumerate((wq, wk, wv))
        ]
        groups = [na] if half == 0 else [na, nb]
        held = bias_copies(groups, lines, line_sems)
        rows = row_copies(core, (xa, xb, ya, yb), full, row_sems)
        start(rows)
        start(held)
        for one in sets:
            start(one)
        finish(rows[:1])
        tail = pltpu.make_async_copy(xa.at[pl.ds(CHUNK, 16)], lines.at[3], line_sems.at[3])
        tail.start()
        tail.wait()
        ends = document_ends(lines[3].astype(F32), place)
        for slot in (0, 1):
            bias[slot] = mask_bias(ends, chunk_of(core, slot), ROW)
        finish(rows[1:])
        finish(held)
        for one in sets:
            finish(one)

        def line(own, which):
            return gathered_bias([own[...]] if half == 0 else [], lines, len(groups), which)

        k_out.held[...] = nt(full[...], wk[...]).astype(BF)
        k_out.send()
        query_line = line(qbias, 0)
        for which in (0, 1):
            q_out.held[which * CHUNK : (which + 1) * CHUNK, :] = (
                (nt(full[chunk_rows(core, which), :], wq[...]) + query_line) * 0.125
            ).astype(BF)
        q_out.send()
        v_out.held[...] = (nt(full[...], wv[...]) + line(vbias, 1)).astype(BF)
        v_out.send()
        q, k, v = q_out.held, k_out.held, v_out.held
        stats[...] = jnp.zeros_like(stats)

        def attend(value):
            def pair(p, carry):
                lanes = pair_lanes(p)
                for slot, count in key_counts(value):
                    rows = pl.ds(slot * CHUNK, CHUNK)
                    width = count * CHUNK
                    out, now = forward_heads(
                        q[rows, lanes], k[0:width, lanes], v[0:width, lanes],
                        bias[slot, :, 0:width], stats[rows, :], p,
                    )
                    att[rows, lanes] = out
                    stats[rows, :] = now
                return carry

            lax.fori_loop(0, 3, pair, 0)

        by_core(core, attend)

    return kernel


def att_copies(att_a, att_b, full, sems):
    half = D // 2
    return [
        pltpu.make_async_copy(one, full.at[:, pl.ds(n * half, half)], sems.at[n])
        for n, one in enumerate((att_a, att_b))
    ]


def cross_forward(
    place, xa, xb, att_a, att_b, params, ea, eb, w0, w1, w2, w3, w4, n1, n2, n3,
    f1, f2, f3, qbias, vbias,
    hat1, scale1, q_out, k_out, v_out, att, stats, hat_out,
    wq, wk, wv, wo, full, lines, sems, line_sems, row_sems, self_wo, self_sems, self_att, att_sems,
):
    core = place[0]
    self_bias, gain1, shift1, obias = (Row(params, n) for n in range(4))
    near, far = (n1, n2, n3), (f1, f2, f3)
    rows = [
        pltpu.make_async_copy(e, full.at[pl.ds(i * HALF_ENC, HALF_ENC)], row_sems.at[i])
        for i, e in enumerate((ea, eb))
    ]
    held = bias_copies(near, lines, line_sems)
    sets = [
        weight_copies(w, w, core, (w0, w1, w2, w3), near, far, dst, sems)
        for w, dst in enumerate((wq, wk, wv, wo))
    ]
    self_set = weight_copies(
        4, 0, core, (None, None, None, None, w4), near, far, self_wo, self_sems
    )
    halves = att_copies(att_a, att_b, self_att, att_sems)
    start(halves)
    start(self_set)
    start(held)
    start(sets[0])
    start(rows)
    for one in sets[1:]:
        start(one)
    finish(halves)
    finish(self_set)
    product = nn(self_att[...], self_wo[...]) + self_bias[...]
    for which, x in enumerate((xa, xb)):
        part = slice(which * CHUNK, (which + 1) * CHUNK)
        hat, scale = normalize(x[0:CHUNK, :].astype(F32) + product[part])
        hat1.held[part, :] = hat
        scale1[part, :] = jnp.broadcast_to(scale, (CHUNK, 128))
    hat1.send()
    hidden = (hat1.held[...] * gain1[...] + shift1[...]).astype(BF)
    finish(held)
    finish(sets[0])
    line = gathered_bias([qbias[...]], lines, 3, 0)
    q_out.held[...] = ((nt(hidden, wq[...]) + line) * 0.125).astype(BF)
    q_out.send()
    finish(rows)
    finish(sets[1])
    k_out.held[...] = nt(full[...], wk[...]).astype(BF)
    k_out.send()
    finish(sets[2])
    line = gathered_bias([vbias[...]], lines, 3, 1)
    v_out.held[...] = (nt(full[...], wv[...]) + line).astype(BF)
    v_out.send()
    finish(sets[3])
    q, k, v = q_out.held, k_out.held, v_out.held
    stats[...] = jnp.zeros_like(stats)

    def pair(p, carry):
        lanes = pair_lanes(p)
        for slot in (0, 1):
            rows = pl.ds(slot * CHUNK, CHUNK)
            out, now = forward_heads(
                q[rows, lanes], k[:, lanes], v[:, lanes], None, stats[rows, :], p
            )
            att[rows, lanes] = out
            stats[rows, :] = now
        return carry

    lax.fori_loop(0, 6, pair, 0, unroll=2)
    hidden = hat1.held[...] * gain1[...] + shift1[...]
    hat, scale = normalize(hidden + (nn(att[...], wo[...]) + obias[...]))
    hat_out[...] = hat
    stats[...] = jnp.where(lane_ids(stats.shape) == 12, scale, stats[...])


FF_STEP = 512
FF_BLOCK = 768


def gelu_parts(u):
    size = jnp.abs(u)
    t = 1.0 / (1.0 + (0.3275911 * 0.7071067811865476) * size)
    poly = t * (
        0.254829592
        + t * (-0.284496736 + t * (1.421413741 + t * (-1.453152027 + t * 1.061405429)))
    )
    bell = jnp.exp(-0.5 * u * u)
    tail = 0.5 * poly * bell
    phi = jnp.where(u >= 0.0, 1.0 - tail, tail)
    return u * phi, phi + u * bell * 0.3989422804014327


def feed_forward(
    place, hat2, stats, params, up_hbm, up_bias, down_hbm, ga_here, ga, gb,
    out_a, out_b, dsecond, left, right, snd, vec, upb,
    up, down, active, slope, hid, total, third, grads, held, sems, out_sems,
):
    core, group = place[0], place[1]
    gain2, shift2, down_bias, gain3, shift3 = (Row(params, 4 + n) for n in range(5))
    steps = FF // FF_STEP
    ups = [
        pltpu.make_async_copy(
            up_hbm.at[:, pl.ds(i * FF_STEP, FF_STEP)],
            up.at[:, pl.ds(i * FF_STEP, FF_STEP)],
            sems.at[0, i],
        )
        for i in range(steps)
    ]
    downs = [
        pltpu.make_async_copy(
            down_hbm.at[pl.ds(i * FF_STEP, FF_STEP)],
            down.at[pl.ds(i * FF_STEP, FF_STEP)],
            sems.at[1, i],
        )
        for i in range(steps)
    ]
    for i in range(steps):
        ups[i].start()
        downs[i].start()
    second = hat2[...] * gain2[...] + shift2[...]
    hid[...] = second.astype(BF)
    total[...] = second + down_bias[...]
    for i in range(steps):
        cols = pl.ds(i * FF_STEP, FF_STEP)
        ups[i].wait()
        u = nn(hid[...], up[:, cols]) + up_bias[:, cols]
        act, slo = gelu_parts(u)
        active[:, cols] = act.astype(BF)
        slope[:, cols] = slo
        downs[i].wait()
        total[...] += nn(active[:, cols], down[cols, :])
    hat3, scale3 = normalize(total[...])
    out = (hat3 * gain3[...] + shift3[...]).astype(BF)
    out_a[...] = out[0:CHUNK]
    out_b[...] = out[CHUNK:OWN]
    first = jnp.where(core == group % 2, ga_here.get()[...], ga.get()[...])
    grad = jnp.concatenate([first, gb.get()[...]], axis=0).astype(F32)
    vec[0:1, :] = column(grad * hat3)
    vec[1:2, :] = column(grad)
    dthird = norm_back(grad, hat3, scale3, gain3[...])
    total[...] = dthird
    third[...] = dthird.astype(BF)
    vec[2:3, :] = column(third[...])
    for i in range(FF // FF_BLOCK):
        cols = pl.ds(i * FF_BLOCK, FF_BLOCK)
        du = (nt(third[...], down[cols, :]) * slope[:, cols]).astype(BF)
        grads[:, cols] = du
        upb[:, cols] = column(du)
        total[...] += nt(du, up[:, cols])
    grad = total[...]
    hat = hat2[...]
    scale = pick_lane(stats, slice(None), 12)
    vec[3:4, :] = column(grad * hat)
    vec[4:5, :] = column(grad)
    dsec = norm_back(grad, hat, scale, gain2[...])
    dsecond.held[...] = dsec
    dsecond.send()
    vec[5:6, :] = column(dsec.astype(BF))
    vec[6:8, :] = jnp.zeros((2, D), F32)

    def hand_over(value):
        pairs = ((grads, hid), (active, third))
        mine, other = pairs[value], pairs[1 - value]
        copies = [
            pltpu.make_async_copy(mine[0], left, out_sems.at[4]),
            pltpu.make_async_copy(mine[1], right, out_sems.at[5]),
        ]
        start(copies)
        for i in range(4):
            cols = pl.ds(pl.multiple_of((group ^ i) * D, D), D)
            rows = pl.ds(i * D, D)
            held[rows, :] = tn(other[0][:, cols], other[1][...]).astype(BF)
            copies.append(pltpu.make_async_copy(held.at[rows], snd.at[rows], out_sems.at[i]))
            copies[-1].start()
        finish(copies)

    by_core(core, hand_over)


def ff_weight_grads(place, left, right, out, held, left_held, right_held, sems):
    copies = [pltpu.make_async_copy(right, right_held, sems.at[0])]
    for i in range(4):
        cols = pl.ds(pl.multiple_of((place[1] ^ i) * D, D), D)
        copies.append(pltpu.make_async_copy(left.at[:, cols], left_held.at[i], sems.at[1 + i]))
    start(copies[:2])
    finish(copies[:2])
    start(copies[2:])
    outs = []
    for i in range(4):
        if i:
            copies[1 + i].wait()
        rows = pl.ds(i * D, D)
        held[rows, :] = tn(left_held[i], right_held[...]).astype(BF)
        outs.append(pltpu.make_async_copy(held.at[rows], out.at[rows], sems.at[5 + i]))
        outs[i].start()
    finish(outs)


def out_grads(core, att, low, wo, grad, places, pieces):
    store_pieces(core, tn(att[...], low[...]).astype(BF), places, pieces)
    store_bias(jnp.zeros((1, D), F32), places, pieces)
    grad[...] = nt(low[...], wo[...]).astype(BF)


def weight_grads(core, dq, dk, dv, queries, keys, places, pieces):
    store_pieces(core, tn(dq[...], queries).astype(BF), places[0], pieces)
    store_pieces(core, tn(dk[...], keys).astype(BF), places[1], pieces)
    store_pieces(core, tn(dv[...], keys).astype(BF), places[2], pieces)
    store_bias(column(dq[...]), places[0], pieces)
    store_bias(jnp.zeros((1, dk.shape[1]), F32), places[1], pieces)
    store_bias(column(dv[...]), places[2], pieces)


def cross_part(core, first, grad, att, q, k, v, stats, queries, full, places, pieces, dq, dk, dv):

    def pair(p, carry):
        lanes = pair_lanes(first + p)
        out = pair_lanes(p)
        gq, gk, gv = backward_heads(
            q[:, lanes], grad[:, lanes], att[:, lanes], k[:, lanes], v[:, lanes],
            None, stats[...], first + p,
        )
        dq[:, out] = (gq * 0.125).astype(BF)
        dk[:, out] = gk.astype(BF)
        dv[:, out] = gv.astype(BF)
        return carry

    lax.fori_loop(0, 3, pair, 0)
    half = pl.ds(0, D // 2)
    weight_grads(
        core, dq.at[:, half], dk.at[:, half], dv.at[:, half], queries(), full[...], places, pieces
    )


def cross_backward_a(
    place, dsecond, att, q, k, v, stats, hat1, params, ea, eb, w3, n1, n2, n3, f1, f2, f3,
    dq, dk, dv, grad, pieces,
    wo, low, full, sems, row_sems,
):
    core = place[0]
    gain1, shift1 = Row(params, 1), Row(params, 2)
    copies = weight_copies(
        3, 0, core, (None, None, None, w3), (n1, n2, n3), (f1, f2, f3), wo, sems
    )
    rows = [
        pltpu.make_async_copy(e, full.at[pl.ds(i * HALF_ENC, HALF_ENC)], row_sems.at[i])
        for i, e in enumerate((ea, eb))
    ]
    start(copies)
    low[...] = dsecond.get()[...].astype(BF)
    size = pieces.rows // 10
    places = [[(4 * g + w) * size for g in (0, 1)] for w in range(3)]
    places_o = [8 * size, 9 * size, 3 * size, 7 * size]
    att = att.get()
    finish(copies)
    out_grads(core, att, low, wo, grad.held, places_o, pieces)
    grad.send()
    q, k, v, stats = q.get(), k.get(), v.get(), stats.get()
    start(rows)
    hat1.begin()

    def queries():
        for one in (dq, dk, dv):
            one.send()
        finish(rows)
        return (hat1.get()[...] * gain1[...] + shift1[...]).astype(BF)

    cross_part(
        core, 3, grad.held, att, q, k, v, stats, queries, full, places, pieces,
        dq.held, dk.held, dv.held,
    )
    pieces.send(0, 10 * size)


def cross_backward_b(
    place, dq_a, dk_a, dv_a, dsecond, grad, att, q, k, v, stats, hat1, scale1, params, ea, eb,
    vec_a, upb, w0, w1, w2, n1, n2, n3, f1, f2, f3,
    dfirst, pieces, vec,
    wq, wk, wv, dq, dk, dv, full, sems, row_sems,
):
    core = place[0]
    gain1, shift1 = Row(params, 1), Row(params, 2)
    near, far, ws = (n1, n2, n3), (f1, f2, f3), (w0, w1, w2)
    sets = [
        weight_copies(w, w, core, ws, near, far, dst, sems)
        for w, dst in enumerate((wq, wk, wv))
    ]
    rows = [
        pltpu.make_async_copy(e, full.at[pl.ds(i * HALF_ENC, HALF_ENC)], row_sems.at[i])
        for i, e in enumerate((ea, eb))
    ]
    second = pl.ds(D // 2, D // 2)
    parts = [
        pltpu.make_async_copy(one, dst.at[:, second], row_sems.at[2 + n])
        for n, (one, dst) in enumerate(((dq_a, dq), (dk_a, dk), (dv_a, dv)))
    ]
    grad, att, stats = grad.get(), att.get(), stats.get()
    q, k, v = q.get(), k.get(), v.get()
    start(rows)
    hat1.begin()
    for one in sets:
        start(one)
    start(parts)
    dsecond.begin()
    scale1.begin()
    size = (pieces.rows - HALF_ENC) // 6
    places = [[(3 * g + w) * size for g in (0, 1)] for w in range(3)]

    def queries():
        finish(rows)
        return (hat1.get()[...] * gain1[...] + shift1[...]).astype(BF)

    cross_part(
        core, 0, grad, att, q, k, v, stats, queries, full, places, pieces, dq, dk, dv
    )
    pieces.send(0, 6 * size)
    finish(parts)
    for one in sets:
        finish(one)
    enc = nn(dk[...], wk[...]) + nn(dv[...], wv[...])
    pieces.put_own(6 * size, enc[0:HALF_ENC].astype(BF))
    pieces.put_snd(6 * size, enc[HALF_ENC:ENC].astype(BF))
    pieces.send(6 * size, HALF_ENC)
    total = dsecond.get()[...] + nn(dq[...], wq[...])
    hat = hat1.get()[...]
    vec[0:6, :] = vec_a[0:6, :]
    vec[6:7, :] = column(total * hat)
    vec[7:8, :] = column(total)
    dfi = norm_back(total, hat, scale1.get()[:, 0:1], gain1[...])
    dfirst.held[...] = dfi
    dfirst.send()
    vec[8:9, :] = column(dfi.astype(BF))
    for n in range(4):
        vec[9 + n : 10 + n, :] = upb[:, n * D : (n + 1) * D]
    vec[13:16, :] = jnp.zeros((3, D), F32)


def self_part(
    core, first, ends, grad, att, q, k, v, stats, full, places, pieces, dq, dk, dv, bias, rows
):
    for slot in (0, 1):
        bias[slot] = mask_bias(ends, chunk_of(core, slot), ROW)

    def attend(value):
        def pair(p, carry):
            lanes = pair_lanes(first + p)
            out = pair_lanes(p)
            (low_slot, low), (high_slot, high) = sorted(key_counts(value), key=lambda x: x[1])
            parts = {}
            for slot, count in ((low_slot, low), (high_slot, high)):
                rows = pl.ds(slot * CHUNK, CHUNK)
                width = count * CHUNK
                gq, gk, gv = backward_heads(
                    q[rows, out], grad[rows, lanes], att[rows, out],
                    k[0:width, out], v[0:width, out],
                    bias[slot, :, 0:width], stats[rows, :], p,
                )
                dq[rows, out] = (gq * 0.125).astype(BF)
                parts[slot] = (gk, gv)
            for n, dst in ((0, dk), (1, dv)):
                wide, narrow = parts[high_slot][n], parts[low_slot][n]
                shared, reach = low * CHUNK, high * CHUNK
                dst[0:shared, out] = (wide[0:shared] + narrow).astype(BF)
                dst[shared:reach, out] = wide[shared:reach].astype(BF)
                if reach < ROW:
                    dst[reach:ROW, out] = jnp.zeros((ROW - reach, PAIR), BF)
            return carry

        lax.fori_loop(0, 3, pair, 0)

    by_core(core, attend)
    finish(rows)
    half = pl.ds(0, D // 2)
    queries = jnp.concatenate([full[chunk_rows(core, n), :] for n in (0, 1)], axis=0)
    weight_grads(
        core, dq.at[:, half], dk.at[:, half], dv.at[:, half], queries, full[...], places, pieces
    )


def self_backward_a(
    place, dfirst, q, k, v, stats, att_a, att_b, xa, xb, ya, yb, w3, m1, m2, m3, g1, g2, g3,
    dq, dk, dv, grad, pieces,
    wo, low, bias, full, lines, sems, row_sems, att, att_sems,
):
    core = place[0]
    copies = weight_copies(
        4, 0, core, (None, None, None, None, w3), (m1, m2, m3), (g1, g2, g3), wo, sems
    )
    tail = pltpu.make_async_copy(xa.at[pl.ds(CHUNK, 16)], lines, row_sems.at[4])
    rows = row_copies(core, (xa, xb, ya, yb), full, row_sems)
    halves = att_copies(att_a, att_b, att, att_sems)
    start(copies)
    start(halves)
    tail.start()
    low[...] = dfirst.get()[...].astype(BF)
    size = pieces.rows // 10
    places = [[(4 * g + w) * size for g in (0, 1)] for w in range(3)]
    places_o = [8 * size, 9 * size, 3 * size, 7 * size]
    finish(halves)
    finish(copies)
    out_grads(core, att, low, wo, grad.held, places_o, pieces)
    grad.send()
    tail.wait()
    q, k, v, stats = q.get(), k.get(), v.get(), stats.get()
    start(rows)
    self_part(
        core, 3, document_ends(lines[...].astype(F32), place), grad.held,
        att.at[:, pl.ds(D // 2, D // 2)], q, k, v, stats, full,
        places, pieces, dq.held, dk.held, dv.held, bias, rows,
    )
    pieces.send(0, 10 * size)
    for one in (dq, dk, dv):
        one.send()


def self_backward_b(
    place, dq_a, dk_a, dv_a, dfirst, grad, att, q, k, v, stats, xa, xb, ya, yb,
    w0, w1, w2, n1, n2, n3, f1, f2, f3,
    pieces,
    wq, wk, wv, dq, dk, dv, bias, full, total, lines, sems, row_sems,
):
    core = place[0]
    size = (pieces.rows - 2 * CHUNK) // 6
    places = [[(3 * g + w) * size for g in (0, 1)] for w in range(3)]
    near, far, ws = (n1, n2, n3), (f1, f2, f3), (w0, w1, w2)
    sets = [
        weight_copies(w, w, core, ws, near, far, dst, sems)
        for w, dst in enumerate((wq, wk, wv))
    ]
    tail = pltpu.make_async_copy(xa.at[pl.ds(CHUNK, 16)], lines, row_sems.at[4])
    rows = row_copies(core, (xa, xb, ya, yb), full, row_sems)
    second = pl.ds(D // 2, D // 2)
    parts = [
        pltpu.make_async_copy(one, dst.at[:, second], row_sems.at[5 + n])
        for n, (one, dst) in enumerate(((dq_a, dq), (dk_a, dk), (dv_a, dv)))
    ]
    tail.start()
    tail.wait()
    grad, att, stats = grad.get(), att.get(), stats.get()
    q, k, v = q.get(), k.get(), v.get()
    start(rows)
    for one in sets:
        start(one)
    start(parts)
    dfirst.begin()
    self_part(
        core, 0, document_ends(lines[...].astype(F32), place), grad, att, q, k, v, stats, full,
        places, pieces, dq, dk, dv, bias, rows,
    )
    pieces.send(0, 6 * size)
    finish(parts)
    for one in sets:
        finish(one)
    total[...] = nn(dk[...], wk[...]) + nn(dv[...], wv[...])
    mine = nn(dq[...], wq[...]) + dfirst.get()[...]
    for n in (0, 1):
        at = 6 * size + n * CHUNK
        pieces.put_snd(at, total[chunk_rows(core, 2 + n), :].astype(BF))
        pieces.put_own(
            at, (mine[n * CHUNK : (n + 1) * CHUNK] + total[chunk_rows(core, n), :]).astype(BF)
        )
    pieces.send(6 * size, 2 * CHUNK)


def add_jobs(jobs, ins, store, held, sems):
    copies, at, most = [], 0, job_most(jobs)
    for _, rows, sources in jobs:
        mine = []
        for operand, row in sources:
            mine.append(
                (
                    pltpu.make_async_copy(
                        ins[operand].at[pl.ds(row, rows)], held.at[pl.ds(at, rows)],
                        sems.at[len(copies) * most + len(mine)],
                    ),
                    at,
                )
            )
            at += rows
        copies.append(mine)
    for mine in copies:
        for copy, _ in mine:
            copy.start()
    for (place, rows, _), mine in zip(jobs, copies):
        total = 0.0
        for copy, row in mine:
            copy.wait()
            total = total + held[row : row + rows, :].astype(F32)
        store(place, total)


def job_most(jobs):
    return max(len(sources) for _, _, sources in jobs)


def job_rows(jobs):
    return sum(rows * len(sources) for _, rows, sources in jobs)


def add_call(name, place, arrays, outs, jobs, pins=()):
    count = len(arrays)

    def kernel(place, *refs):
        ins, targets = refs[:count], refs[count : count + len(outs)]
        held, out_held, sems, out_sems = refs[count + len(outs) :]
        copies = []

        def store(where, total):
            at = sum(outs[: where[0]]) + where[1]
            put_rows(out_held, at, total.astype(BF))
            rows = pl.ds(at, total.shape[0])
            copies.append(
                pltpu.make_async_copy(
                    out_held.at[rows],
                    targets[where[0]].at[pl.ds(where[1], total.shape[0])],
                    out_sems.at[len(copies)],
                )
            )
            copies[-1].start()

        add_jobs(jobs, ins, store, held, sems)
        finish(copies)

    dma = pltpu.SemaphoreType.DMA
    return call(
        kernel, [(place, "s")] + [(one, "a") for one in arrays],
        [((rows, D), BF, "a") for rows in outs],
        [
            pltpu.VMEM((job_rows(jobs), D), BF), pltpu.VMEM((sum(outs), D), BF),
            dma((job_most(jobs) * len(jobs),)), dma((len(jobs),)),
        ],
        name, pins=pins,
    )


def total_call(name, place, arrays, total_rows, jobs, groups, depth, pins=(), mine_type=F32):
    count = len(arrays)
    size = total_rows // groups // depth

    def kernel(place, *refs):
        mine, parts = refs[count], refs[count + 1 : count + depth]
        held, total, sems = refs[count + depth :]

        def store(row, value):
            put_rows(total, row, value)

        add_jobs(jobs, refs[:count], store, held, sems)
        for d in range(depth):
            for g in range(groups):
                at = pl.multiple_of(
                    g * (total_rows // groups) + (place[2] ^ d) * size, 8
                )
                block = total[pl.ds(at, size), :]
                if d == 0:
                    put_rows(mine, g * size, block.astype(mine_type))
                else:
                    put_rows(parts[d - 1], g * size, block.astype(BF))

    return call(
        kernel, [(place, "s")] + [(one, "a") for one in arrays],
        [((groups * size, D), mine_type, "v")] + [((groups * size, D), BF, "v")] * (depth - 1),
        [
            pltpu.VMEM((job_rows(jobs), D), BF), pltpu.VMEM((total_rows, D), F32),
            pltpu.SemaphoreType.DMA((job_most(jobs) * len(jobs),)),
        ],
        name, pins=pins,
    )


def spread(depth, count):
    def kernel(place, *refs):
        own, other, refs = refs[:count], refs[count : 2 * count], refs[2 * count :]
        outs, biases, total = refs[:4], refs[4:-1], refs[-1]
        core, k = place[0], place[2]
        size = total.shape[1] // depth
        for which, parts in enumerate((own, other)):
            for d in range(depth):
                at = pl.multiple_of((k ^ d) * size, 8)
                ref, row = (parts[d], 0) if count == depth else (parts[0], d * size)
                total[which, pl.ds(at, size), :] = ref[row : row + size, :].astype(F32)
        rows = total.shape[1] // 4
        for n, out in enumerate(outs):
            for which, half in ((0, core), (1, 1 - core)):
                to = pl.ds(pl.multiple_of(half * PIECE, PIECE), PIECE)
                out[to, :] = total[which, n * rows : n * rows + PIECE, :]
        for n, bias in zip((0, 2), biases):
            at = n * rows + PIECE
            bias[...] = total[0, at : at + 1, :GROUP]

    return kernel


def solution(mesh):
    names = tuple(mesh.axis_names)
    heads, rows = mesh.shape["heads"], mesh.shape["rows"]
    depth = rows // 2
    piece = FF // (heads * rows)
    weight_rows = PIECE + BIAS_ROWS
    while (4 * weight_rows) % (8 * depth):
        weight_rows += BIAS_ROWS
    def send(value, where, label="moved"):
        pairs = []
        for r in range(rows):
            for h in range(heads):
                to_r, to_h = where(r, h)
                if (to_r, to_h) == (r, h):
                    continue
                index = {"rows": (r, to_r), "heads": (h, to_h)}
                a = b = 0
                for name in names:
                    a = a * mesh.shape[name] + index[name][0]
                    b = b * mesh.shape[name] + index[name][1]
                pairs.append((a, b))
        with jax.named_scope(label):
            return lax.ppermute(value, names, pairs)

    def swap(r, h):
        return (r & ~1) | (h & 1), (h & ~1) | (r & 1)

    def swap_b(r, h):
        return (r & ~1) | (1 - (h & 1)), (h & ~1) | (r & 1)

    def swap_b_back(r, h):
        return (r & ~1) | (h & 1), (h & ~1) | (1 - (r & 1))

    def core_to(r, h):
        return r ^ 1, h

    def head_to(d):
        return lambda r, h: (r, h ^ d)

    def depth_to(d):
        return lambda r, h: (r ^ (2 * d), h)

    def shards(
        layer_input, encoder_out, doc_lengths,
        self_query, self_qbias, self_key_weight, self_value, self_vbias, self_out, self_obias,
        first_gain, first_shift,
        cross_query, cross_qbias, cross_key, cross_value, cross_vbias, cross_out, cross_obias,
        second_gain, second_shift, up_weight, up_bias, down_weight, down_bias,
        third_gain, third_shift, out_grad,
    ):
        h = lax.axis_index("heads")
        r = lax.axis_index("rows")
        core, k = r % 2, r // 2
        place = jnp.stack([core, h, k]).astype(jnp.int32)
        stays = core == h % 2

        def line(vector):
            return vector.reshape(1, -1)

        params = jnp.stack(
            [
                self_obias, first_gain, first_shift, cross_obias, second_gain, second_shift,
                down_bias, third_gain, third_shift,
            ]
        )

        def v(*arrays):
            return [(one, "v") for one in arrays]

        def a(*arrays):
            return [(one, "a") for one in arrays]

        def l(*arrays):
            return [(one, "l") for one in arrays]

        def d(*arrays):
            return [(one, "d") for one in arrays]

        here = [(place, "s")]

        self_own = [self_query.T, self_key_weight.T, self_value.T]
        cross_own = [cross_query.T, cross_key.T, cross_value.T, cross_out, self_out]
        chunk = ((CHUNK, D), BF, "v")
        xa, xb, mine, zero = call(
            prepare,
            here + v(layer_input, doc_lengths, *self_own, line(self_qbias), line(self_vbias)),
            [((CHUNK + 16, D), BF, "v"), chunk, ((3 * PIECE + 16, D), BF, "v")], [], "prepare",
        )

        def gather_groups(mine, label):
            x, y = send(mine, head_to(1), label), send(mine, head_to(2), label)
            return [x, y, send(x, head_to(2), label + "_2")]

        self_near = gather_groups(mine, "w_self_near")
        xb = send(xb, swap_b, "x_b")
        xa = jnp.where(stays, xa, send(xa, swap, "x_a"))
        mine, ga, gb, enc, _ = call(
            prepare_more,
            here + v(self_out, *cross_own[:4], line(cross_qbias), line(cross_vbias))
            + v(out_grad, encoder_out),
            [((5 * PIECE + 16, D), BF, "v"), chunk, chunk, ((HALF_ENC, D), BF, "v")],
            [], "prepare_more", pins=[zero],
        )
        ya = send(xa, core_to, "y_a")
        yb = send(xb, core_to, "y_b")
        self_far = [send(one, core_to, "w_self_far") for one in self_near]
        self_w = self_near + self_far

        def gated(values, pins, name):
            count = len(values)
            anywhere = pl.BlockSpec(memory_space=pl.ANY)
            return pl.pallas_call(
                gate,
                in_specs=[anywhere] * (count + len(pins)),
                out_specs=[anywhere] * count,
                out_shape=[jax.ShapeDtypeStruct(one.shape, one.dtype) for one in values],
                input_output_aliases={n: n for n in range(count)},
                name=name,
            )(*values, *pins)

        mine, enc = gated([mine, enc], [self_near[0], self_near[1], xa, xb, params], "gate_cross")
        cross_x, cross_y = (send(mine, head_to(d), "w_cross_near") for d in (1, 2))
        ea = send(enc, swap_b, "e_a")

        dma = pltpu.SemaphoreType.DMA
        weight = pltpu.VMEM((D, D), BF)
        half_weight = pltpu.VMEM((D // 2, D), BF)
        masks = pltpu.VMEM((2, CHUNK, ROW), F32)
        lines_bf = pltpu.VMEM((4, 16, D), BF)
        row_full = pltpu.VMEM((ROW, D), BF)
        enc_full = pltpu.VMEM((ENC, D), BF)
        tokens = (OWN, D)

        def self_half(half, weights, pins):
            narrow = ((ROW, D // 2), BF, "e")
            return call(
                self_forward(half),
                here + a(xa, xb, ya, yb, *self_own, *weights)
                + v(line(self_qbias), line(self_vbias)),
                [
                    ((OWN, D // 2), BF, "e"), narrow, narrow, ((OWN, D // 2), BF, "v"),
                    ((OWN, 128), F32, "v"),
                ],
                [half_weight] * 3
                + [row_full, masks, lines_bf, dma((3, 7)), dma((4,)), dma((4,))],
                "self_forward_" + "ab"[half], pins=pins,
            )

        sq, sk, sv, att_a, stats_a, zero = self_half(
            0, [self_near[0], self_far[0]] * 2, [mine, enc]
        )
        (cross_x,) = gated([cross_x], [zero], "gate_forward")
        cross_near = [cross_x, cross_y, send(cross_x, head_to(2), "w_cross_near_2")]
        tq, tk, tv, att_b, stats_b, zero = self_half(
            1, [self_near[1], self_far[1], self_near[2], self_far[2]], [zero, cross_near[0]]
        )
        *cross_near, ea, ga_here, gb = gated(cross_near + [ea, ga, gb], [zero], "gate_far")
        cross_far = [send(one, core_to, "w_cross_far") for one in cross_near]
        eb = send(ea, core_to, "e_b")
        ga = send(ga_here, swap, "g_a")
        gb = send(gb, swap_b, "g_b")
        cross_w = cross_near + cross_far
        hat1, scale1, cq, ck, cv, catt, stats2, hat2, zero = call(
            cross_forward,
            here + v(xa, xb) + a(att_a, att_b) + v(params) + a(ea, eb)
            + a(*cross_own, *cross_w) + v(line(cross_qbias), line(cross_vbias)),
            [
                (tokens, F32, "e"), ((OWN, 128), F32, "v"),
                (tokens, BF, "e"), ((ENC, D), BF, "e"), ((ENC, D), BF, "e"), (tokens, BF, "v"),
                ((OWN, 128), F32, "v"), (tokens, F32, "v"),
            ],
            [weight] * 4 + [
                enc_full, lines_bf, dma((4, 7)), dma((4,)), dma((2,)), weight, dma((1, 7)),
                pltpu.VMEM(tokens, BF), dma((2,)),
            ],
            "cross_forward",
        )
        out_a, out_b, dsecond, left, right, ff_snd, vec_a, upb, zero = call(
            feed_forward,
            here + v(hat2, stats2, params) + a(up_weight) + v(line(up_bias)) + a(down_weight)
            + l(ga_here, ga, gb),
            [
                chunk, chunk, (tokens, F32, "e"), ((OWN, FF), BF, "a"), (tokens, BF, "a"),
                ((FF, D), BF, "a"), ((8, D), F32, "v"), ((1, FF), F32, "v"),
            ],
            [
                pltpu.VMEM((D, FF), BF), pltpu.VMEM((FF, D), BF), pltpu.VMEM((OWN, FF), BF),
                pltpu.VMEM((OWN, FF), F32), pltpu.VMEM(tokens, BF), pltpu.VMEM(tokens, F32),
                pltpu.VMEM(tokens, BF), pltpu.VMEM((OWN, FF), BF), pltpu.VMEM((FF, D), BF),
                dma((2, FF // FF_STEP)), dma((6,)),
            ],
            "feed_forward",
        )
        ff_got = send(ff_snd, core_to, "ff_core")
        out_got = send(out_a, swap, "out_a")
        out_b = send(out_b, swap_b_back, "out_b")
        ff_own, _ = call(
            ff_weight_grads, here + a(left, right), [((FF, D), BF, "a")],
            [
                pltpu.VMEM((FF, D), BF), pltpu.VMEM((4, OWN, D), BF), pltpu.VMEM(tokens, BF),
                dma((9,)),
            ],
            "ff_weight_grads",
        )
        output = jnp.concatenate([jnp.where(stays, out_a, out_got), out_b], axis=0)

        half = D // 2

        def ff_row(g, which):
            return g * D + which * half

        def both(row):
            return [(0, row), (1, row)]

        ff_x, ff_y, _ = add_call(
            "ff_add_1", place, [ff_own, ff_got], [D, D],
            [
                ((0, 0), half, both(ff_row(1, 0))), ((0, half), half, both(ff_row(3, 0))),
                ((1, 0), half, both(ff_row(2, 1))), ((1, half), half, both(ff_row(3, 1))),
            ],
            pins=[out_got, out_b],
        )
        ff_gx = send(ff_x, head_to(1), "ff_heads")
        ff_gy = send(ff_y, head_to(2), "ff_heads")

        wr = weight_rows
        rows_a = [((10 * wr, D), BF, "p")] * 2
        half_e = ((OWN, D // 2), BF, "e")
        cross_w4, self_w4 = cross_own[3], self_out
        enc_half, enc_grads = ((ENC, D // 2), BF, "e"), [enc_full] * 2
        cdq, cdk, cdv, cgrad, ca_own, ca_snd, zero = call(
            cross_backward_a,
            here + l(dsecond, catt, cq, ck, cv, stats2) + d(hat1)
            + v(params) + a(ea, eb, cross_w4, *cross_w),
            [half_e, enc_half, enc_half, (tokens, BF, "e")] + rows_a,
            [weight, pltpu.VMEM(tokens, BF), enc_full, dma((1, 7)), dma((2,))],
            "cross_backward_a", pins=[ff_x, ff_y],
        )
        (ca_snd,) = gated([ca_snd], [ff_gx, ff_gy, output], "gate_ca")
        ca_got = send(ca_snd, core_to, "ca_core")
        ff_x2, ff_y2, _ = add_call(
            "ff_add_2", place, [ff_own, ff_got, ff_gx, ff_gy], [half, half],
            [
                ((0, 0), half, both(ff_row(2, 0)) + [(2, half)]),
                ((1, 0), half, both(ff_row(1, 1)) + [(3, half)]),
            ],
            pins=[zero],
        )
        ff_gx2 = send(ff_x2, head_to(2), "ff_heads_2")
        ff_gy2 = send(ff_y2, head_to(1), "ff_heads_2")
        c_x3, _ = add_call(
            "c_add_1", place, [ca_own, ca_got], [4 * wr], [((0, 0), 4 * wr, both(4 * wr))],
            pins=[ff_x2],
        )
        c_gx3 = send(c_x3, head_to(1), "c_heads")
        dfirst, cb_own, cb_snd, vectors, zero = call(
            cross_backward_b,
            here + a(cdq, cdk, cdv) + d(dsecond) + l(cgrad, catt, cq, ck, cv, stats2)
            + d(hat1, scale1) + v(params) + a(ea, eb) + v(vec_a, upb)
            + a(*cross_own[:3], *cross_w),
            [
                (tokens, F32, "e"), ((6 * wr + HALF_ENC, D), BF, "p"),
                ((6 * wr + HALF_ENC, D), BF, "p"), ((16, D), F32, "v"),
            ],
            [weight] * 3 + [pltpu.VMEM(tokens, BF)] + enc_grads + [enc_full, dma((3, 7)), dma((5,))],
            "cross_backward_b", pins=[ff_x2, ff_y2, c_x3],
        )
        vectors = lax.all_gather(vectors, "heads")
        (cb_snd,) = gated([cb_snd], [ff_gx2, ff_gy2, c_gx3], "gate_cb")
        cb_got = send(cb_snd, core_to, "cb_core")

        def depth_send(parts, label):
            return [send(one, depth_to(d + 1), label) for d, one in enumerate(parts)]

        ff_mine, *ff_parts, _ = total_call(
            "ff_add_3", place, [ff_own, ff_got, ff_gx, ff_gy, ff_gx2, ff_gy2], D,
            [
                (0, half, both(ff_row(0, 0)) + [(2, 0), (4, 0)]),
                (half, half, both(ff_row(0, 1)) + [(3, 0), (5, 0)]),
            ],
            1, depth, pins=[zero],
        )
        ff_back = depth_send(ff_parts, "ff_depth")
        c_y2, c_x1, _ = add_call(
            "c_add_2", place, [ca_own, ca_got, cb_own, cb_got, c_gx3], [4 * wr, 4 * wr],
            [
                ((0, 0), 4 * wr, both(0) + [(4, 0)]),
                ((1, 0), 3 * wr, [(2, 3 * wr), (3, 3 * wr)]), ((1, 3 * wr), wr, both(9 * wr)),
            ],
            pins=[ff_parts[0]],
        )
        c_gy2 = send(c_y2, head_to(2), "c_heads_2")
        c_gx1 = send(c_x1, head_to(1), "c_heads_2")

        row_half, row_grads = ((ROW, D // 2), BF, "e"), [row_full] * 2
        sdq, sdk, sdv, sgrad, sa_own, sa_snd, zero = call(
            self_backward_a,
            here + l(dfirst, tq, tk, tv, stats_b) + a(att_a, att_b, xa, xb, ya, yb)
            + a(self_w4, *cross_w),
            [half_e, row_half, row_half, (tokens, BF, "e")] + rows_a,
            [weight, pltpu.VMEM(tokens, BF), masks]
            + [row_full, pltpu.VMEM((16, D), BF), dma((1, 7)), dma((5,))]
            + [pltpu.VMEM(tokens, BF), dma((2,))],
            "self_backward_a", pins=[*ff_parts, c_y2, c_x1],
        )
        (sa_snd,) = gated([sa_snd], [*ff_back, c_gy2, c_gx1], "gate_sa")
        sa_got = send(sa_snd, core_to, "sa_core")
        c_mine, *c_parts, _ = total_call(
            "c_add_3", place, [ca_own, ca_got, cb_own, cb_got, c_gy2, c_gx1], 4 * wr,
            [
                (0, 3 * wr, [(2, 0), (3, 0), (4, 0), (5, 0)]),
                (3 * wr, wr, [(0, 8 * wr), (1, 8 * wr), (4, 3 * wr), (5, 3 * wr)]),
            ],
            1, depth, pins=[zero], mine_type=BF,
        )
        c_depth = depth_send(c_parts, "c_depth")
        s_y, enc_sum, _ = add_call(
            "s_add_1", place, [sa_own, sa_got, cb_own, cb_got], [8 * wr, HALF_ENC],
            [((0, 0), 8 * wr, both(0)), ((1, 0), HALF_ENC, [(2, 6 * wr), (3, 6 * wr)])],
            pins=[c_parts[0]],
        )
        vectors = jnp.sum(vectors, axis=0)
        encoder_g = send(enc_sum, swap_b_back, "enc_grad")
        s_gy = send(s_y, head_to(2), "s_heads")
        sb_own, sb_snd, zero = call(
            self_backward_b,
            here + a(sdq, sdk, sdv) + d(dfirst) + l(sgrad, att_a, sq, sk, sv, stats_a)
            + a(xa, xb, ya, yb) + a(*self_own, *self_w),
            [((6 * wr + 2 * CHUNK, D), BF, "p"), ((6 * wr + 2 * CHUNK, D), BF, "p")],
            [weight] * 3 + [pltpu.VMEM(tokens, BF)] + row_grads + [masks]
            + [row_full, pltpu.VMEM((ROW, D), F32), pltpu.VMEM((16, D), BF), dma((3, 7)), dma((8,))],
            "self_backward_b", pins=[*c_parts, s_y, enc_sum, vectors],
        )
        vectors = lax.all_gather(vectors, "rows")
        (sb_snd,) = gated([sb_snd], [*c_depth, s_gy, encoder_g], "gate_sb")
        sb_got = send(sb_snd, core_to, "sb_core")

        def depth_sum(mine, got):
            for one in got:
                mine = mine + one.astype(F32)
            return mine

        part_rows = 4 * wr // depth
        s_x, in_a, in_b, c_part, _ = add_call(
            "s_add_2", place, [sa_own, sa_got, sb_own, sb_got, s_gy, c_mine, *c_depth],
            [4 * wr, CHUNK, CHUNK, part_rows],
            [
                ((0, 0), 3 * wr, [(2, 3 * wr), (3, 3 * wr), (4, 4 * wr)]),
                ((0, 3 * wr), wr, both(9 * wr) + [(4, 7 * wr)]),
                ((1, 0), CHUNK, [(2, 6 * wr), (3, 6 * wr)]),
                ((2, 0), CHUNK, [(2, 6 * wr + CHUNK), (3, 6 * wr + CHUNK)]),
                ((3, 0), part_rows, [(5 + n, 0) for n in range(depth)]),
            ],
        )
        c_back = [send(c_part, depth_to(d), "c_back") for d in range(1, depth)]
        s_gx = send(s_x, head_to(1), "s_heads_2")
        in_got = send(in_a, swap, "in_a")
        in_b = send(in_b, swap_b_back, "in_b")
        s_mine, *s_parts, _ = total_call(
            "s_add_3", place, [sa_own, sa_got, sb_own, sb_got, s_gy, s_gx], 4 * wr,
            [
                (0, 3 * wr, [(2, 0), (3, 0), (4, 0), (5, 0)]),
                (3 * wr, wr, [(0, 8 * wr), (1, 8 * wr), (4, 3 * wr), (5, 3 * wr)]),
            ],
            1, depth, pins=c_back,
        )
        s_depth = depth_send(s_parts, "s_depth")

        def whole_grads(own, other, label):
            *grads, qbias, vbias, _ = call(
                spread(depth, len(own)), here + v(*own, *other),
                [((GROUP, D), F32, "v")] * 4 + [((1, GROUP), F32, "v")] * 2,
                [pltpu.VMEM((2, 4 * wr, D), F32)], label + "_spread",
            )
            return grads, qbias[0], vbias[0]

        input_g = jnp.concatenate([jnp.where(stays, in_a, in_got), in_b], axis=0)
        c_own, _ = call(
            join, here + v(c_part, *c_back), [((4 * wr, D), BF, "v")], [], "c_join", pins=s_parts
        )
        c_other = send(c_own, core_to, "c_far")
        (cq_g, ck_g, cv_g, co_g), cqb, cvb = whole_grads([c_own], [c_other], "c")
        s_part = depth_sum(s_mine, s_depth).astype(BF)
        s_back = [send(s_part, depth_to(d), "s_back") for d in range(1, depth)]
        ff = depth_sum(ff_mine, ff_back).reshape(2, piece, D)
        ff_here = lax.dynamic_index_in_dim(ff, core, 0, keepdims=False)
        ff_there = send(lax.dynamic_index_in_dim(ff, 1 - core, 0, keepdims=False), core_to, "ff_last")
        upweight_g = jnp.where(core == 0, ff_here, ff_there).T
        downweight_g = jnp.where(core == 0, ff_there, ff_here)

        vectors = jnp.sum(vectors, axis=0)
        ff_at = (h * rows + r) * piece
        upbias_g = lax.dynamic_slice_in_dim(vectors[9:13].reshape(FF), ff_at, piece)
        (encoder_g, _) = call(
            move, here + v(encoder_g), [((HALF_ENC, D), BF, "v")], [], "encoder_grad", pins=s_parts
        )
        s_own = gated([s_part, *s_back], [cq_g, input_g, ff_here, ff_there, encoder_g], "gate_s_far")
        s_other = [send(one, core_to, "s_far") for one in s_own]
        (sq_g, sk_g, sv_g, so_g), sqb, svb = whole_grads(s_own, s_other, "s")

        return (
            output, input_g, encoder_g,
            sq_g.T, sqb, sk_g.T, sv_g.T, svb, so_g, vectors[8], vectors[6], vectors[7],
            cq_g.T, cqb, ck_g.T, cv_g.T, cvb, co_g, vectors[5],
            vectors[3], vectors[4], upweight_g, upbias_g, downweight_g, vectors[2],
            vectors[0], vectors[1],
        )

    rowed, headed = P(("rows", "heads"), None), P(None, "heads")
    by_head, by_head_rows, whole = P("heads"), P("heads", None), P()
    ffed = ("heads", "rows")
    return jax.shard_map(
        shards,
        mesh=mesh,
        in_specs=(
            rowed, rowed, P("rows", None),
            headed, by_head, headed, headed, by_head, by_head_rows, whole, whole, whole,
            headed, by_head, headed, headed, by_head, by_head_rows, whole, whole, whole,
            whole, whole, whole, whole, whole, whole, rowed,
        ),
        out_specs=(
            rowed, rowed, rowed,
            headed, by_head, headed, headed, by_head, by_head_rows, whole, whole, whole,
            headed, by_head, headed, headed, by_head, by_head_rows, whole, whole, whole,
            P(None, ffed), P(ffed), P(ffed, None), whole, whole, whole,
        ),
        check_vma=False,
    )
```

```python
import jax
import jax.numpy as jnp
from jax import lax
from jax.experimental import pallas as pl
from jax.experimental.pallas import tpu as pltpu
from jax.sharding import PartitionSpec as P

BF = jnp.bfloat16
F32 = jnp.float32
HEAD = 64
PAIR = 128
EPS = 1e-05
ROW = 1088
CHUNK = 272
OWN = 544
ENC = 1024
HALF_ENC = 512
D = 768
GROUP = 192
PIECE = 96
BIAS_ROWS = 16
FF = 3072
MIB = 1 << 20


def nn(a, b):
    return jnp.dot(a, b, preferred_element_type=F32)


def nt(a, b):
    return lax.dot_general(a, b, (((1,), (1,)), ((), ())), preferred_element_type=F32)


def tn(a, b):
    return lax.dot_general(a, b, (((0,), (0,)), ((), ())), preferred_element_type=F32)


def lane_ids(shape):
    return lax.broadcasted_iota(jnp.int32, shape, len(shape) - 1)


def pair_lanes(p):
    return pl.ds(pl.multiple_of(p * PAIR, PAIR), PAIR)


def normalize(total):
    center = total - jnp.mean(total, axis=-1, keepdims=True)
    scale = lax.rsqrt(jnp.mean(center * center, axis=-1, keepdims=True) + EPS)
    return center * scale, scale


def norm_back(grad, hat, scale, gain):
    scaled = grad * gain
    inner = scaled - jnp.mean(scaled, axis=-1, keepdims=True)
    return scale * (inner - hat * jnp.mean(scaled * hat, axis=-1, keepdims=True))


def column(values):
    return jnp.sum(values.astype(F32), axis=0, keepdims=True)


def pick_lane(ref, rows, lane):
    block = ref[rows, :]
    return jnp.sum(jnp.where(lane_ids(block.shape) == lane, block, 0.0), axis=-1, keepdims=True)


def start(copies):
    for one in copies:
        one.start()


def finish(copies):
    for one in copies:
        one.wait()


def by_core(core, body):
    for value in (0, 1):

        @pl.when(core == value)
        def _():
            body(value)


class Row:
    def __init__(self, ref, row):
        self.ref, self.row = ref, row

    def __getitem__(self, _):
        return self.ref[self.row : self.row + 1, :]


class Late:
    def __init__(self, source, held, sem, now):
        self.copy = pltpu.make_async_copy(source, held, sem)
        self.held = held
        self.started = self.waited = False
        if now:
            self.begin()

    def begin(self):
        if not self.started:
            self.copy.start()
            self.started = True

    def get(self):
        self.begin()
        if not self.waited:
            self.copy.wait()
            self.waited = True
        return self.held


class Early:
    def __init__(self, held, target, sem):
        self.copy = pltpu.make_async_copy(held, target, sem)
        self.held = held
        self.sent = False

    def send(self):
        self.copy.start()
        self.sent = True


class Pieces:
    def __init__(self, both, rows, own, snd, sems):
        self.both, self.rows, self.targets, self.sems = both, rows, (own, snd), sems
        self.copies = []

    def send(self, at, count):
        for n in (1, 0):
            self.copies.append(
                pltpu.make_async_copy(
                    self.both.at[pl.ds(n * self.rows + at, count)],
                    self.targets[n].at[pl.ds(at, count)],
                    self.sems.at[len(self.copies)],
                )
            )
            self.copies[-1].start()

    def put(self, core, half, at, block):
        to = jnp.where(core == half, 0, self.rows) + at
        self.both[pl.ds(pl.multiple_of(to, 16), block.shape[0]), :] = block

    def put_both(self, at, block):
        put_rows(self.both, at, block)
        put_rows(self.both, self.rows + at, block)

    def put_own(self, at, block):
        put_rows(self.both, at, block)

    def put_snd(self, at, block):
        put_rows(self.both, self.rows + at, block)


def call(kernel, ins, outs, scratch, name, pins=()):
    vmem, anywhere = pl.BlockSpec(memory_space=pltpu.VMEM), pl.BlockSpec(memory_space=pl.ANY)
    smem = pl.BlockSpec(memory_space=pltpu.SMEM)
    specs = {"v": vmem, "a": anywhere, "l": anywhere, "d": anywhere, "e": anywhere, "p": anywhere}
    specs["s"] = smem
    late = [(n, x) for n, (x, kind) in enumerate(ins) if kind in "ld"]
    early = [(n, out) for n, out in enumerate(outs) if out[2] == "e"]
    pair = [n for n, out in enumerate(outs) if out[2] == "p"]
    first = len(ins)
    last = first + len(pins)
    end = last + len(outs)

    def body(*refs):
        took, gave, rest = list(refs[:first]), list(refs[last:end]), list(refs[end + 1 :])
        own, rest = rest[: len(scratch)], rest[len(scratch) :]
        for n, (at, _) in enumerate(late):
            took[at] = Late(took[at], rest[n], rest[-1].at[n], ins[at][1] == "l")
        rest = rest[len(late) :]
        for n, (at, _) in enumerate(early):
            gave[at] = Early(rest[n], gave[at], rest[-1].at[len(late) + n])
        results, pieces = list(gave), []
        if pair:
            rows = outs[pair[0]][0][0]
            pieces = [Pieces(rest[-3], rows, gave[pair[0]], gave[pair[1]], rest[-2])]
            results[pair[0] : pair[1] + 1] = pieces
        kernel(*took, *results, *own)
        refs[end][...] = jnp.zeros((8, 128), F32)
        for at, _ in late:
            took[at].get()
        for at, _ in early:
            if not gave[at].sent:
                gave[at].send()
        for at, _ in early:
            gave[at].copy.wait()
        for one in pieces:
            finish(one.copies)

    extra = [pltpu.VMEM(x.shape, x.dtype) for _, x in late]
    extra += [pltpu.VMEM(out[0], out[1]) for _, out in early]
    if pair:
        extra += [pltpu.VMEM((2 * outs[pair[0]][0][0], D), BF), pltpu.SemaphoreType.DMA((8,))]
    extra += [pltpu.SemaphoreType.DMA((max(len(late) + len(early), 1),))]
    return pl.pallas_call(
        body,
        in_specs=[specs[kind] for _, kind in ins] + [anywhere] * len(pins),
        out_specs=[specs[out[2]] for out in outs] + [vmem],
        out_shape=[jax.ShapeDtypeStruct(out[0], out[1]) for out in outs]
        + [jax.ShapeDtypeStruct((8, 128), F32)],
        scratch_shapes=list(scratch) + extra,
        compiler_params=pltpu.CompilerParams(vmem_limit_bytes=64 * MIB - 65536),
        cost_estimate=pl.CostEstimate(flops=1000, bytes_accessed=1000, transcendentals=0),
        name=name,
    )(*[x for x, _ in ins], *pins)


def after(value, zero):
    return value + zero[0, 0].astype(value.dtype)


def weight_copies(w, slot, core, own, near, far, dst, sems):
    copies = [pltpu.make_async_copy(own[w], dst.at[pl.ds(0, GROUP)], sems.at[slot, 0])]
    rows = pl.ds(w * PIECE, PIECE)
    for i in (1, 2, 3):
        for at, which, refs in ((i, core, near), (3 + i, 1 - core, far)):
            to = pl.multiple_of(GROUP * i + PIECE * which, PIECE)
            copies.append(
                pltpu.make_async_copy(
                    refs[i - 1].at[rows], dst.at[pl.ds(to, PIECE)], sems.at[slot, at]
                )
            )
    return copies


def half_weight_copies(w, slot, core, own, near, far, half, dst, sems):
    copies = []
    rows = pl.ds(w * PIECE, PIECE)
    for n in (0, 1):
        i = 2 * half + n
        if i == 0:
            copies.append(
                pltpu.make_async_copy(own[w], dst.at[pl.ds(0, GROUP)], sems.at[slot, 0])
            )
            continue
        for at, which, refs in ((i, core, near), (3 + i, 1 - core, far)):
            to = pl.multiple_of(GROUP * n + PIECE * which, PIECE)
            copies.append(
                pltpu.make_async_copy(
                    refs[i - 1].at[rows], dst.at[pl.ds(to, PIECE)], sems.at[slot, at]
                )
            )
    return copies


def bias_copies(near, lines, sems):
    return [
        pltpu.make_async_copy(ref.at[pl.ds(ref.shape[0] - 16, 16)], lines.at[i], sems.at[i])
        for i, ref in enumerate(near)
    ]


def gathered_bias(parts, lines, count, which):
    for i in range(count):
        split = lines[i, 3 * which : 3 * which + 3, :GROUP].astype(F32)
        parts = parts + [split[0:1] + split[1:2] + split[2:3]]
    return jnp.concatenate(parts, axis=1)


def put_rows(target, at, block):
    target[at : at + block.shape[0], :] = block


def store_pieces(core, block, places, pieces):
    for g, at in enumerate(places):
        for half in (0, 1):
            row = g * GROUP + half * PIECE
            pieces.put(core, half, at, block[row : row + PIECE])


def store_bias(row, places, pieces):
    for i, at in enumerate(places):
        one = jnp.concatenate(
            [row[:, i * GROUP : (i + 1) * GROUP], jnp.zeros((1, D - GROUP), F32)], axis=1
        )
        block = jnp.concatenate([one, jnp.zeros((BIAS_ROWS - 1, D), F32)], axis=0).astype(BF)
        pieces.put_both(at + PIECE, block)


def forward_heads(q2, keys, values, bias, row_stats, p):
    lane = lane_ids(q2.shape)
    outs = []
    for t in (0, 1):
        query = jnp.where((lane // HEAD) == t, q2, jnp.zeros_like(q2))
        scores = nt(query, keys)
        if bias is not None:
            scores = scores + bias
        highest = jnp.max(scores, axis=-1, keepdims=True)
        raised = jnp.exp(scores - highest)
        total = jnp.sum(raised, axis=-1, keepdims=True)
        outs.append(nn(raised.astype(BF), values) / total)
        row_stats = jnp.where(
            lane_ids(row_stats.shape) == 2 * p + t, highest + jnp.log(total), row_stats
        )
    return jnp.where((lane // HEAD) == 0, outs[0], outs[1]).astype(BF), row_stats


def backward_heads(q2, g2, o2, keys, values, bias, stats, p):
    count = q2.shape[0]
    first = (lane_ids(q2.shape) // HEAD) == 0
    zero = jnp.zeros_like(q2)

    def stacked(a):
        return jnp.concatenate([jnp.where(first, a, zero), jnp.where(first, zero, a)], axis=0)

    query, grad = stacked(q2), stacked(g2)
    product = g2.astype(F32) * o2.astype(F32)
    inner = jnp.concatenate(
        [
            jnp.sum(jnp.where(first, product, 0.0), axis=-1, keepdims=True),
            jnp.sum(jnp.where(first, 0.0, product), axis=-1, keepdims=True),
        ],
        axis=0,
    )
    lanes = lane_ids(stats.shape)
    lse = jnp.concatenate(
        [
            jnp.sum(jnp.where(lanes == 2 * p + t, stats, 0.0), axis=-1, keepdims=True)
            for t in (0, 1)
        ],
        axis=0,
    )
    scores = nt(query, keys)
    if bias is not None:
        scores = scores + jnp.concatenate([bias, bias], axis=0)
    shares = jnp.exp(scores - lse)
    grad_scores = (shares * (nt(grad, values) - inner)).astype(BF)
    grad_q = nn(grad_scores, keys)
    return (
        jnp.where(first, grad_q[:count], grad_q[count:]),
        tn(grad_scores, query),
        tn(shares.astype(BF), grad),
    )


def document_ends(xa, place):
    pair_at = place[1] // 2
    lengths = jnp.where(
        pair_at == 0,
        xa[0:1, :8] * 16.0 + xa[2:3, :8],
        xa[1:2, :8] * 16.0
        + xa[3:4, :8],
    )
    ends, total = [], 0.0
    for d in range(8):
        total = total + lengths[:, d : d + 1]
        ends.append(total)
    return ends


def mask_bias(ends, chunk, width):
    qpos = chunk * CHUNK + lax.broadcasted_iota(jnp.int32, (CHUNK, 1), 0)
    kpos = lax.broadcasted_iota(jnp.int32, (1, width), 1)
    qat, kat = qpos.astype(F32), kpos.astype(F32)
    qseg = jnp.zeros((CHUNK, 1), F32)
    kseg = jnp.zeros((1, width), F32)
    for end in ends:
        qseg = qseg + jnp.where(qat >= end, 1.0, 0.0)
        kseg = kseg + jnp.where(kat >= end, 1.0, 0.0)
    return jnp.where((qseg == kseg) & (kpos <= qpos), 0.0, -1000000000.0)


def chunk_of(core, which):
    return (2 * core, 3 - 2 * core, 2 - 2 * core, 1 + 2 * core)[which]


def chunk_rows(core, which):
    return pl.ds(pl.multiple_of(chunk_of(core, which) * CHUNK, 16), CHUNK)


def key_counts(core):
    return ((0, 1), (1, 4)) if core == 0 else ((0, 3), (1, 2))


def prepare(place, x, lengths, wq, wk, wv, qbias, vbias, xa, xb, mine):
    xa[0:CHUNK, :] = x[0:CHUNK, :]
    xa[CHUNK : CHUNK + 16, :] = jnp.zeros((16, D), BF)
    counts = lengths[...].astype(F32)
    high = jnp.floor(counts * 0.0625)
    rows = jnp.concatenate([high, counts - high * 16.0, jnp.zeros((12, 8), F32)], axis=0)
    rows = jnp.concatenate([rows, jnp.zeros((16, 120), F32)], axis=1)
    xa[CHUNK : CHUNK + 16, 0:128] = rows.astype(BF)
    xb[...] = x[CHUNK:OWN, :]
    prepare_weights(place[0], (wq, wk, wv), qbias, vbias, mine)


def prepare_more(
    place, so, wq, wk, wv, wo, qbias, vbias, out_grad, enc,
    mine, ga, gb, enc_out,
):
    ga[...] = out_grad[0:CHUNK, :]
    gb[...] = out_grad[CHUNK:OWN, :]
    enc_out[...] = enc[...]
    prepare_weights(place[0], (wq, wk, wv, wo, so), qbias, vbias, mine)


def prepare_weights(core, weights, qbias, vbias, mine):
    half = pl.ds(pl.multiple_of(core * PIECE, PIECE), PIECE)
    for w, one in enumerate(weights):
        mine[w * PIECE : (w + 1) * PIECE, :] = one[half, :]
    rows = []
    for one in (qbias[...], vbias[...]):
        for _ in range(3):
            top = one.astype(BF).astype(F32)
            rows.append(top)
            one = one - top
    rows = jnp.concatenate(rows + [jnp.zeros((10, GROUP), F32)], axis=0)
    at = len(weights) * PIECE
    mine[at : at + 16, :] = jnp.concatenate(
        [rows, jnp.zeros((16, D - GROUP), F32)], axis=1
    ).astype(BF)


def join(place, *refs):
    at = 0
    for one in refs[:-1]:
        put_rows(refs[-1], at, one[...])
        at += one.shape[0]


def move(place, source, target):
    target[...] = source[...]


def gate(*refs):
    pass


def row_copies(core, xs, full, sems):
    return [
        pltpu.make_async_copy(
            x.at[pl.ds(0, CHUNK)], full.at[chunk_rows(core, which)], sems.at[which]
        )
        for which, x in enumerate(xs)
    ]


def self_forward(half):
    def kernel(
        place, xa, xb, ya, yb, w0, w1, w2, na, fa, nb, fb, qbias, vbias,
        q_out, k_out, v_out, att, stats,
        wq, wk, wv, full, bias, lines, sems, line_sems, row_sems,
    ):
        core = place[0]
        near, far = (na, na, nb), (fa, fa, fb)
        sets = [
            half_weight_copies(w, w, core, (w0, w1, w2), near, far, half, dst, sems)
            for w, dst in enumerate((wq, wk, wv))
        ]
        groups = [na] if half == 0 else [na, nb]
        held = bias_copies(groups, lines, line_sems)
        rows = row_copies(core, (xa, xb, ya, yb), full, row_sems)
        start(rows)
        start(held)
        for one in sets:
            start(one)
        finish(rows[:1])
        tail = pltpu.make_async_copy(xa.at[pl.ds(CHUNK, 16)], lines.at[3], line_sems.at[3])
        tail.start()
        tail.wait()
        ends = document_ends(lines[3].astype(F32), place)
        for slot in (0, 1):
            bias[slot] = mask_bias(ends, chunk_of(core, slot), ROW)
        finish(rows[1:])
        finish(held)
        for one in sets:
            finish(one)

        def line(own, which):
            return gathered_bias([own[...]] if half == 0 else [], lines, len(groups), which)

        k_out.held[...] = nt(full[...], wk[...]).astype(BF)
        k_out.send()
        query_line = line(qbias, 0)
        for which in (0, 1):
            q_out.held[which * CHUNK : (which + 1) * CHUNK, :] = (
                (nt(full[chunk_rows(core, which), :], wq[...]) + query_line) * 0.125
            ).astype(BF)
        q_out.send()
        v_out.held[...] = (nt(full[...], wv[...]) + line(vbias, 1)).astype(BF)
        v_out.send()
        q, k, v = q_out.held, k_out.held, v_out.held
        stats[...] = jnp.zeros_like(stats)

        def attend(value):
            def pair(p, carry):
                lanes = pair_lanes(p)
                for slot, count in key_counts(value):
                    rows = pl.ds(slot * CHUNK, CHUNK)
                    width = count * CHUNK
                    out, now = forward_heads(
                        q[rows, lanes], k[0:width, lanes], v[0:width, lanes],
                        bias[slot, :, 0:width], stats[rows, :], p,
                    )
                    att[rows, lanes] = out
                    stats[rows, :] = now
                return carry

            lax.fori_loop(0, 3, pair, 0)

        by_core(core, attend)

    return kernel


def att_copies(att_a, att_b, full, sems):
    half = D // 2
    return [
        pltpu.make_async_copy(one, full.at[:, pl.ds(n * half, half)], sems.at[n])
        for n, one in enumerate((att_a, att_b))
    ]


def cross_forward(
    place, xa, xb, att_a, att_b, params, ea, eb, w0, w1, w2, w3, w4, n1, n2, n3,
    f1, f2, f3, qbias, vbias,
    hat1, scale1, q_out, k_out, v_out, att, stats, hat_out,
    wq, wk, wv, wo, full, lines, sems, line_sems, row_sems, self_wo, self_sems, self_att, att_sems,
):
    core = place[0]
    self_bias, gain1, shift1, obias = (Row(params, n) for n in range(4))
    near, far = (n1, n2, n3), (f1, f2, f3)
    rows = [
        pltpu.make_async_copy(e, full.at[pl.ds(i * HALF_ENC, HALF_ENC)], row_sems.at[i])
        for i, e in enumerate((ea, eb))
    ]
    held = bias_copies(near, lines, line_sems)
    sets = [
        weight_copies(w, w, core, (w0, w1, w2, w3), near, far, dst, sems)
        for w, dst in enumerate((wq, wk, wv, wo))
    ]
    self_set = weight_copies(
        4, 0, core, (None, None, None, None, w4), near, far, self_wo, self_sems
    )
    halves = att_copies(att_a, att_b, self_att, att_sems)
    start(halves)
    start(self_set)
    start(held)
    start(sets[0])
    start(rows)
    for one in sets[1:]:
        start(one)
    finish(halves)
    finish(self_set)
    product = nn(self_att[...], self_wo[...]) + self_bias[...]
    for which, x in enumerate((xa, xb)):
        part = slice(which * CHUNK, (which + 1) * CHUNK)
        hat, scale = normalize(x[0:CHUNK, :].astype(F32) + product[part])
        hat1.held[part, :] = hat
        scale1[part, :] = jnp.broadcast_to(scale, (CHUNK, 128))
    hat1.send()
    hidden = (hat1.held[...] * gain1[...] + shift1[...]).astype(BF)
    finish(held)
    finish(sets[0])
    line = gathered_bias([qbias[...]], lines, 3, 0)
    q_out.held[...] = ((nt(hidden, wq[...]) + line) * 0.125).astype(BF)
    q_out.send()
    finish(rows)
    finish(sets[1])
    k_out.held[...] = nt(full[...], wk[...]).astype(BF)
    k_out.send()
    finish(sets[2])
    line = gathered_bias([vbias[...]], lines, 3, 1)
    v_out.held[...] = (nt(full[...], wv[...]) + line).astype(BF)
    v_out.send()
    finish(sets[3])
    q, k, v = q_out.held, k_out.held, v_out.held
    stats[...] = jnp.zeros_like(stats)

    def pair(p, carry):
        lanes = pair_lanes(p)
        for slot in (0, 1):
            rows = pl.ds(slot * CHUNK, CHUNK)
            out, now = forward_heads(
                q[rows, lanes], k[:, lanes], v[:, lanes], None, stats[rows, :], p
            )
            att[rows, lanes] = out
            stats[rows, :] = now
        return carry

    lax.fori_loop(0, 6, pair, 0, unroll=2)
    hidden = hat1.held[...] * gain1[...] + shift1[...]
    hat, scale = normalize(hidden + (nn(att[...], wo[...]) + obias[...]))
    hat_out[...] = hat
    stats[...] = jnp.where(lane_ids(stats.shape) == 12, scale, stats[...])


FF_STEP = 512
FF_BLOCK = 768


def gelu_parts(u):
    size = jnp.abs(u)
    t = 1.0 / (1.0 + (0.3275911 * 0.7071067811865476) * size)
    poly = t * (
        0.254829592
        + t * (-0.284496736 + t * (1.421413741 + t * (-1.453152027 + t * 1.061405429)))
    )
    bell = jnp.exp(-0.5 * u * u)
    tail = 0.5 * poly * bell
    phi = jnp.where(u >= 0.0, 1.0 - tail, tail)
    return u * phi, phi + u * bell * 0.3989422804014327


def feed_forward(
    place, hat2, stats, params, up_hbm, up_bias, down_hbm, ga_here, ga, gb,
    out_a, out_b, dsecond, left, right, snd, vec, upb,
    up, down, active, slope, hid, total, third, grads, held, sems, out_sems,
):
    core, group = place[0], place[1]
    gain2, shift2, down_bias, gain3, shift3 = (Row(params, 4 + n) for n in range(5))
    steps = FF // FF_STEP
    ups = [
        pltpu.make_async_copy(
            up_hbm.at[:, pl.ds(i * FF_STEP, FF_STEP)],
            up.at[:, pl.ds(i * FF_STEP, FF_STEP)],
            sems.at[0, i],
        )
        for i in range(steps)
    ]
    downs = [
        pltpu.make_async_copy(
            down_hbm.at[pl.ds(i * FF_STEP, FF_STEP)],
            down.at[pl.ds(i * FF_STEP, FF_STEP)],
            sems.at[1, i],
        )
        for i in range(steps)
    ]
    for i in range(steps):
        ups[i].start()
        downs[i].start()
    second = hat2[...] * gain2[...] + shift2[...]
    hid[...] = second.astype(BF)
    total[...] = second + down_bias[...]
    for i in range(steps):
        cols = pl.ds(i * FF_STEP, FF_STEP)
        ups[i].wait()
        u = nn(hid[...], up[:, cols]) + up_bias[:, cols]
        act, slo = gelu_parts(u)
        active[:, cols] = act.astype(BF)
        slope[:, cols] = slo
        downs[i].wait()
        total[...] += nn(active[:, cols], down[cols, :])
    hat3, scale3 = normalize(total[...])
    out = (hat3 * gain3[...] + shift3[...]).astype(BF)
    out_a[...] = out[0:CHUNK]
    out_b[...] = out[CHUNK:OWN]
    first = jnp.where(core == group % 2, ga_here.get()[...], ga.get()[...])
    grad = jnp.concatenate([first, gb.get()[...]], axis=0).astype(F32)
    vec[0:1, :] = column(grad * hat3)
    vec[1:2, :] = column(grad)
    dthird = norm_back(grad, hat3, scale3, gain3[...])
    total[...] = dthird
    third[...] = dthird.astype(BF)
    vec[2:3, :] = column(third[...])
    for i in range(FF // FF_BLOCK):
        cols = pl.ds(i * FF_BLOCK, FF_BLOCK)
        du = (nt(third[...], down[cols, :]) * slope[:, cols]).astype(BF)
        grads[:, cols] = du
        upb[:, cols] = column(du)
        total[...] += nt(du, up[:, cols])
    grad = total[...]
    hat = hat2[...]
    scale = pick_lane(stats, slice(None), 12)
    vec[3:4, :] = column(grad * hat)
    vec[4:5, :] = column(grad)
    dsec = norm_back(grad, hat, scale, gain2[...])
    dsecond.held[...] = dsec
    dsecond.send()
    vec[5:6, :] = column(dsec.astype(BF))
    vec[6:8, :] = jnp.zeros((2, D), F32)

    def hand_over(value):
        pairs = ((grads, hid), (active, third))
        mine, other = pairs[value], pairs[1 - value]
        copies = [
            pltpu.make_async_copy(mine[0], left, out_sems.at[4]),
            pltpu.make_async_copy(mine[1], right, out_sems.at[5]),
        ]
        start(copies)
        for i in range(4):
            cols = pl.ds(pl.multiple_of((group ^ i) * D, D), D)
            rows = pl.ds(i * D, D)
            held[rows, :] = tn(other[0][:, cols], other[1][...]).astype(BF)
            copies.append(pltpu.make_async_copy(held.at[rows], snd.at[rows], out_sems.at[i]))
            copies[-1].start()
        finish(copies)

    by_core(core, hand_over)


def ff_weight_grads(place, left, right, out, held, left_held, right_held, sems):
    copies = [pltpu.make_async_copy(right, right_held, sems.at[0])]
    for i in range(4):
        cols = pl.ds(pl.multiple_of((place[1] ^ i) * D, D), D)
        copies.append(pltpu.make_async_copy(left.at[:, cols], left_held.at[i], sems.at[1 + i]))
    start(copies[:2])
    finish(copies[:2])
    start(copies[2:])
    outs = []
    for i in range(4):
        if i:
            copies[1 + i].wait()
        rows = pl.ds(i * D, D)
        held[rows, :] = tn(left_held[i], right_held[...]).astype(BF)
        outs.append(pltpu.make_async_copy(held.at[rows], out.at[rows], sems.at[5 + i]))
        outs[i].start()
    finish(outs)


def out_grads(core, att, low, wo, grad, places, pieces):
    store_pieces(core, tn(att[...], low[...]).astype(BF), places, pieces)
    store_bias(jnp.zeros((1, D), F32), places, pieces)
    grad[...] = nt(low[...], wo[...]).astype(BF)


def weight_grads(core, dq, dk, dv, queries, keys, places, pieces):
    store_pieces(core, tn(dq[...], queries).astype(BF), places[0], pieces)
    store_pieces(core, tn(dk[...], keys).astype(BF), places[1], pieces)
    store_pieces(core, tn(dv[...], keys).astype(BF), places[2], pieces)
    store_bias(column(dq[...]), places[0], pieces)
    store_bias(jnp.zeros((1, dk.shape[1]), F32), places[1], pieces)
    store_bias(column(dv[...]), places[2], pieces)


def cross_part(core, first, grad, att, q, k, v, stats, queries, full, places, pieces, dq, dk, dv):

    def pair(p, carry):
        lanes = pair_lanes(first + p)
        out = pair_lanes(p)
        gq, gk, gv = backward_heads(
            q[:, lanes], grad[:, lanes], att[:, lanes], k[:, lanes], v[:, lanes],
            None, stats[...], first + p,
        )
        dq[:, out] = (gq * 0.125).astype(BF)
        dk[:, out] = gk.astype(BF)
        dv[:, out] = gv.astype(BF)
        return carry

    lax.fori_loop(0, 3, pair, 0)
    half = pl.ds(0, D // 2)
    weight_grads(
        core, dq.at[:, half], dk.at[:, half], dv.at[:, half], queries(), full[...], places, pieces
    )


def cross_backward_a(
    place, dsecond, att, q, k, v, stats, hat1, params, ea, eb, w3, n1, n2, n3, f1, f2, f3,
    dq, dk, dv, grad, pieces,
    wo, low, full, sems, row_sems,
):
    core = place[0]
    gain1, shift1 = Row(params, 1), Row(params, 2)
    copies = weight_copies(
        3, 0, core, (None, None, None, w3), (n1, n2, n3), (f1, f2, f3), wo, sems
    )
    rows = [
        pltpu.make_async_copy(e, full.at[pl.ds(i * HALF_ENC, HALF_ENC)], row_sems.at[i])
        for i, e in enumerate((ea, eb))
    ]
    start(copies)
    low[...] = dsecond.get()[...].astype(BF)
    size = pieces.rows // 10
    places = [[(4 * g + w) * size for g in (0, 1)] for w in range(3)]
    places_o = [8 * size, 9 * size, 3 * size, 7 * size]
    att = att.get()
    finish(copies)
    out_grads(core, att, low, wo, grad.held, places_o, pieces)
    grad.send()
    q, k, v, stats = q.get(), k.get(), v.get(), stats.get()
    start(rows)
    hat1.begin()

    def queries():
        for one in (dq, dk, dv):
            one.send()
        finish(rows)
        return (hat1.get()[...] * gain1[...] + shift1[...]).astype(BF)

    cross_part(
        core, 3, grad.held, att, q, k, v, stats, queries, full, places, pieces,
        dq.held, dk.held, dv.held,
    )
    pieces.send(0, 10 * size)


def cross_backward_b(
    place, dq_a, dk_a, dv_a, dsecond, grad, att, q, k, v, stats, hat1, scale1, params, ea, eb,
    vec_a, upb, w0, w1, w2, n1, n2, n3, f1, f2, f3,
    dfirst, pieces, vec,
    wq, wk, wv, dq, dk, dv, full, sems, row_sems,
):
    core = place[0]
    gain1, shift1 = Row(params, 1), Row(params, 2)
    near, far, ws = (n1, n2, n3), (f1, f2, f3), (w0, w1, w2)
    sets = [
        weight_copies(w, w, core, ws, near, far, dst, sems)
        for w, dst in enumerate((wq, wk, wv))
    ]
    rows = [
        pltpu.make_async_copy(e, full.at[pl.ds(i * HALF_ENC, HALF_ENC)], row_sems.at[i])
        for i, e in enumerate((ea, eb))
    ]
    second = pl.ds(D // 2, D // 2)
    parts = [
        pltpu.make_async_copy(one, dst.at[:, second], row_sems.at[2 + n])
        for n, (one, dst) in enumerate(((dq_a, dq), (dk_a, dk), (dv_a, dv)))
    ]
    grad, att, stats = grad.get(), att.get(), stats.get()
    q, k, v = q.get(), k.get(), v.get()
    start(rows)
    hat1.begin()
    for one in sets:
        start(one)
    start(parts)
    dsecond.begin()
    scale1.begin()
    size = (pieces.rows - HALF_ENC) // 6
    places = [[(3 * g + w) * size for g in (0, 1)] for w in range(3)]

    def queries():
        finish(rows)
        return (hat1.get()[...] * gain1[...] + shift1[...]).astype(BF)

    cross_part(
        core, 0, grad, att, q, k, v, stats, queries, full, places, pieces, dq, dk, dv
    )
    pieces.send(0, 6 * size)
    finish(parts)
    for one in sets:
        finish(one)
    enc = nn(dk[...], wk[...]) + nn(dv[...], wv[...])
    pieces.put_own(6 * size, enc[0:HALF_ENC].astype(BF))
    pieces.put_snd(6 * size, enc[HALF_ENC:ENC].astype(BF))
    pieces.send(6 * size, HALF_ENC)
    total = dsecond.get()[...] + nn(dq[...], wq[...])
    hat = hat1.get()[...]
    vec[0:6, :] = vec_a[0:6, :]
    vec[6:7, :] = column(total * hat)
    vec[7:8, :] = column(total)
    dfi = norm_back(total, hat, scale1.get()[:, 0:1], gain1[...])
    dfirst.held[...] = dfi
    dfirst.send()
    vec[8:9, :] = column(dfi.astype(BF))
    for n in range(4):
        vec[9 + n : 10 + n, :] = upb[:, n * D : (n + 1) * D]
    vec[13:16, :] = jnp.zeros((3, D), F32)


def self_part(
    core, first, ends, grad, att, q, k, v, stats, full, places, pieces, dq, dk, dv, bias, rows
):
    for slot in (0, 1):
        bias[slot] = mask_bias(ends, chunk_of(core, slot), ROW)

    def attend(value):
        def pair(p, carry):
            lanes = pair_lanes(first + p)
            out = pair_lanes(p)
            (low_slot, low), (high_slot, high) = sorted(key_counts(value), key=lambda x: x[1])
            parts = {}
            for slot, count in ((low_slot, low), (high_slot, high)):
                rows = pl.ds(slot * CHUNK, CHUNK)
                width = count * CHUNK
                gq, gk, gv = backward_heads(
                    q[rows, out], grad[rows, lanes], att[rows, out],
                    k[0:width, out], v[0:width, out],
                    bias[slot, :, 0:width], stats[rows, :], p,
                )
                dq[rows, out] = (gq * 0.125).astype(BF)
                parts[slot] = (gk, gv)
            for n, dst in ((0, dk), (1, dv)):
                wide, narrow = parts[high_slot][n], parts[low_slot][n]
                shared, reach = low * CHUNK, high * CHUNK
                dst[0:shared, out] = (wide[0:shared] + narrow).astype(BF)
                dst[shared:reach, out] = wide[shared:reach].astype(BF)
                if reach < ROW:
                    dst[reach:ROW, out] = jnp.zeros((ROW - reach, PAIR), BF)
            return carry

        lax.fori_loop(0, 3, pair, 0)

    by_core(core, attend)
    finish(rows)
    half = pl.ds(0, D // 2)
    queries = jnp.concatenate([full[chunk_rows(core, n), :] for n in (0, 1)], axis=0)
    weight_grads(
        core, dq.at[:, half], dk.at[:, half], dv.at[:, half], queries, full[...], places, pieces
    )


def self_backward_a(
    place, dfirst, q, k, v, stats, att_a, att_b, xa, xb, ya, yb, w3, m1, m2, m3, g1, g2, g3,
    dq, dk, dv, grad, pieces,
    wo, low, bias, full, lines, sems, row_sems, att, att_sems,
):
    core = place[0]
    copies = weight_copies(
        4, 0, core, (None, None, None, None, w3), (m1, m2, m3), (g1, g2, g3), wo, sems
    )
    tail = pltpu.make_async_copy(xa.at[pl.ds(CHUNK, 16)], lines, row_sems.at[4])
    rows = row_copies(core, (xa, xb, ya, yb), full, row_sems)
    halves = att_copies(att_a, att_b, att, att_sems)
    start(copies)
    start(halves)
    tail.start()
    low[...] = dfirst.get()[...].astype(BF)
    size = pieces.rows // 10
    places = [[(4 * g + w) * size for g in (0, 1)] for w in range(3)]
    places_o = [8 * size, 9 * size, 3 * size, 7 * size]
    finish(halves)
    finish(copies)
    out_grads(core, att, low, wo, grad.held, places_o, pieces)
    grad.send()
    tail.wait()
    q, k, v, stats = q.get(), k.get(), v.get(), stats.get()
    start(rows)
    self_part(
        core, 3, document_ends(lines[...].astype(F32), place), grad.held,
        att.at[:, pl.ds(D // 2, D // 2)], q, k, v, stats, full,
        places, pieces, dq.held, dk.held, dv.held, bias, rows,
    )
    pieces.send(0, 10 * size)
    for one in (dq, dk, dv):
        one.send()


def self_backward_b(
    place, dq_a, dk_a, dv_a, dfirst, grad, att, q, k, v, stats, xa, xb, ya, yb,
    w0, w1, w2, n1, n2, n3, f1, f2, f3,
    pieces,
    wq, wk, wv, dq, dk, dv, bias, full, total, lines, sems, row_sems,
):
    core = place[0]
    size = (pieces.rows - 2 * CHUNK) // 6
    places = [[(3 * g + w) * size for g in (0, 1)] for w in range(3)]
    near, far, ws = (n1, n2, n3), (f1, f2, f3), (w0, w1, w2)
    sets = [
        weight_copies(w, w, core, ws, near, far, dst, sems)
        for w, dst in enumerate((wq, wk, wv))
    ]
    tail = pltpu.make_async_copy(xa.at[pl.ds(CHUNK, 16)], lines, row_sems.at[4])
    rows = row_copies(core, (xa, xb, ya, yb), full, row_sems)
    second = pl.ds(D // 2, D // 2)
    parts = [
        pltpu.make_async_copy(one, dst.at[:, second], row_sems.at[5 + n])
        for n, (one, dst) in enumerate(((dq_a, dq), (dk_a, dk), (dv_a, dv)))
    ]
    tail.start()
    tail.wait()
    grad, att, stats = grad.get(), att.get(), stats.get()
    q, k, v = q.get(), k.get(), v.get()
    start(rows)
    for one in sets:
        start(one)
    start(parts)
    dfirst.begin()
    self_part(
        core, 0, document_ends(lines[...].astype(F32), place), grad, att, q, k, v, stats, full,
        places, pieces, dq, dk, dv, bias, rows,
    )
    pieces.send(0, 6 * size)
    finish(parts)
    for one in sets:
        finish(one)
    total[...] = nn(dk[...], wk[...]) + nn(dv[...], wv[...])
    mine = nn(dq[...], wq[...]) + dfirst.get()[...]
    for n in (0, 1):
        at = 6 * size + n * CHUNK
        pieces.put_snd(at, total[chunk_rows(core, 2 + n), :].astype(BF))
        pieces.put_own(
            at, (mine[n * CHUNK : (n + 1) * CHUNK] + total[chunk_rows(core, n), :]).astype(BF)
        )
    pieces.send(6 * size, 2 * CHUNK)


def add_jobs(jobs, ins, store, held, sems):
    copies, at, most = [], 0, job_most(jobs)
    for _, rows, sources in jobs:
        mine = []
        for operand, row in sources:
            mine.append(
                (
                    pltpu.make_async_copy(
                        ins[operand].at[pl.ds(row, rows)], held.at[pl.ds(at, rows)],
                        sems.at[len(copies) * most + len(mine)],
                    ),
                    at,
                )
            )
            at += rows
        copies.append(mine)
    for mine in copies:
        for copy, _ in mine:
            copy.start()
    for (place, rows, _), mine in zip(jobs, copies):
        total = 0.0
        for copy, row in mine:
            copy.wait()
            total = total + held[row : row + rows, :].astype(F32)
        store(place, total)


def job_most(jobs):
    return max(len(sources) for _, _, sources in jobs)


def job_rows(jobs):
    return sum(rows * len(sources) for _, rows, sources in jobs)


def add_call(name, place, arrays, outs, jobs, pins=()):
    count = len(arrays)

    def kernel(place, *refs):
        ins, targets = refs[:count], refs[count : count + len(outs)]
        held, out_held, sems, out_sems = refs[count + len(outs) :]
        copies = []

        def store(where, total):
            at = sum(outs[: where[0]]) + where[1]
            put_rows(out_held, at, total.astype(BF))
            rows = pl.ds(at, total.shape[0])
            copies.append(
                pltpu.make_async_copy(
                    out_held.at[rows],
                    targets[where[0]].at[pl.ds(where[1], total.shape[0])],
                    out_sems.at[len(copies)],
                )
            )
            copies[-1].start()

        add_jobs(jobs, ins, store, held, sems)
        finish(copies)

    dma = pltpu.SemaphoreType.DMA
    return call(
        kernel, [(place, "s")] + [(one, "a") for one in arrays],
        [((rows, D), BF, "a") for rows in outs],
        [
            pltpu.VMEM((job_rows(jobs), D), BF), pltpu.VMEM((sum(outs), D), BF),
            dma((job_most(jobs) * len(jobs),)), dma((len(jobs),)),
        ],
        name, pins=pins,
    )


def total_call(name, place, arrays, total_rows, jobs, groups, depth, pins=(), mine_type=F32):
    count = len(arrays)
    size = total_rows // groups // depth

    def kernel(place, *refs):
        mine, parts = refs[count], refs[count + 1 : count + depth]
        held, total, sems = refs[count + depth :]

        def store(row, value):
            put_rows(total, row, value)

        add_jobs(jobs, refs[:count], store, held, sems)
        for d in range(depth):
            for g in range(groups):
                at = pl.multiple_of(
                    g * (total_rows // groups) + (place[2] ^ d) * size, 8
                )
                block = total[pl.ds(at, size), :]
                if d == 0:
                    put_rows(mine, g * size, block.astype(mine_type))
                else:
                    put_rows(parts[d - 1], g * size, block.astype(BF))

    return call(
        kernel, [(place, "s")] + [(one, "a") for one in arrays],
        [((groups * size, D), mine_type, "v")] + [((groups * size, D), BF, "v")] * (depth - 1),
        [
            pltpu.VMEM((job_rows(jobs), D), BF), pltpu.VMEM((total_rows, D), F32),
            pltpu.SemaphoreType.DMA((job_most(jobs) * len(jobs),)),
        ],
        name, pins=pins,
    )


def spread(depth, count):
    def kernel(place, *refs):
        own, other, refs = refs[:count], refs[count : 2 * count], refs[2 * count :]
        outs, biases, total = refs[:4], refs[4:-1], refs[-1]
        core, k = place[0], place[2]
        size = total.shape[1] // depth
        for which, parts in enumerate((own, other)):
            for d in range(depth):
                at = pl.multiple_of((k ^ d) * size, 8)
                ref, row = (parts[d], 0) if count == depth else (parts[0], d * size)
                total[which, pl.ds(at, size), :] = ref[row : row + size, :].astype(F32)
        rows = total.shape[1] // 4
        for n, out in enumerate(outs):
            for which, half in ((0, core), (1, 1 - core)):
                to = pl.ds(pl.multiple_of(half * PIECE, PIECE), PIECE)
                out[to, :] = total[which, n * rows : n * rows + PIECE, :]
        for n, bias in zip((0, 2), biases):
            at = n * rows + PIECE
            bias[...] = total[0, at : at + 1, :GROUP]

    return kernel


def solution(mesh):
    names = tuple(mesh.axis_names)
    heads, rows = mesh.shape["heads"], mesh.shape["rows"]
    depth = rows // 2
    piece = FF // (heads * rows)
    weight_rows = PIECE + BIAS_ROWS
    while (4 * weight_rows) % (8 * depth):
        weight_rows += BIAS_ROWS
    def send(value, where, label="moved"):
        pairs = []
        for r in range(rows):
            for h in range(heads):
                to_r, to_h = where(r, h)
                if (to_r, to_h) == (r, h):
                    continue
                index = {"rows": (r, to_r), "heads": (h, to_h)}
                a = b = 0
                for name in names:
                    a = a * mesh.shape[name] + index[name][0]
                    b = b * mesh.shape[name] + index[name][1]
                pairs.append((a, b))
        with jax.named_scope(label):
            return lax.ppermute(value, names, pairs)

    def swap(r, h):
        return (r & ~1) | (h & 1), (h & ~1) | (r & 1)

    def swap_b(r, h):
        return (r & ~1) | (1 - (h & 1)), (h & ~1) | (r & 1)

    def swap_b_back(r, h):
        return (r & ~1) | (h & 1), (h & ~1) | (1 - (r & 1))

    def core_to(r, h):
        return r ^ 1, h

    def head_to(d):
        return lambda r, h: (r, h ^ d)

    def depth_to(d):
        return lambda r, h: (r ^ (2 * d), h)

    def shards(
        layer_input, encoder_out, doc_lengths,
        self_query, self_qbias, self_key_weight, self_value, self_vbias, self_out, self_obias,
        first_gain, first_shift,
        cross_query, cross_qbias, cross_key, cross_value, cross_vbias, cross_out, cross_obias,
        second_gain, second_shift, up_weight, up_bias, down_weight, down_bias,
        third_gain, third_shift, out_grad,
    ):
        h = lax.axis_index("heads")
        r = lax.axis_index("rows")
        core, k = r % 2, r // 2
        place = jnp.stack([core, h, k]).astype(jnp.int32)
        stays = core == h % 2

        def line(vector):
            return vector.reshape(1, -1)

        params = jnp.stack(
            [
                self_obias, first_gain, first_shift, cross_obias, second_gain, second_shift,
                down_bias, third_gain, third_shift,
            ]
        )

        def v(*arrays):
            return [(one, "v") for one in arrays]

        def a(*arrays):
            return [(one, "a") for one in arrays]

        def l(*arrays):
            return [(one, "l") for one in arrays]

        def d(*arrays):
            return [(one, "d") for one in arrays]

        here = [(place, "s")]

        self_own = [self_query.T, self_key_weight.T, self_value.T]
        cross_own = [cross_query.T, cross_key.T, cross_value.T, cross_out, self_out]
        chunk = ((CHUNK, D), BF, "v")
        xa, xb, mine, zero = call(
            prepare,
            here + v(layer_input, doc_lengths, *self_own, line(self_qbias), line(self_vbias)),
            [((CHUNK + 16, D), BF, "v"), chunk, ((3 * PIECE + 16, D), BF, "v")], [], "prepare",
        )

        def gather_groups(mine, label):
            x, y = send(mine, head_to(1), label), send(mine, head_to(2), label)
            return [x, y, send(x, head_to(2), label + "_2")]

        self_near = gather_groups(mine, "w_self_near")
        xb = send(xb, swap_b, "x_b")
        xa = jnp.where(stays, xa, send(xa, swap, "x_a"))
        mine, ga, gb, enc, _ = call(
            prepare_more,
            here + v(self_out, *cross_own[:4], line(cross_qbias), line(cross_vbias))
            + v(out_grad, encoder_out),
            [((5 * PIECE + 16, D), BF, "v"), chunk, chunk, ((HALF_ENC, D), BF, "v")],
            [], "prepare_more", pins=[zero],
        )
        ya = send(xa, core_to, "y_a")
        yb = send(xb, core_to, "y_b")
        self_far = [send(one, core_to, "w_self_far") for one in self_near]
        self_w = self_near + self_far

        def gated(values, pins, name):
            count = len(values)
            anywhere = pl.BlockSpec(memory_space=pl.ANY)
            return pl.pallas_call(
                gate,
                in_specs=[anywhere] * (count + len(pins)),
                out_specs=[anywhere] * count,
                out_shape=[jax.ShapeDtypeStruct(one.shape, one.dtype) for one in values],
                input_output_aliases={n: n for n in range(count)},
                name=name,
            )(*values, *pins)

        mine, enc = gated([mine, enc], [self_near[0], self_near[1], xa, xb, params], "gate_cross")
        cross_x, cross_y = (send(mine, head_to(d), "w_cross_near") for d in (1, 2))
        ea = send(enc, swap_b, "e_a")

        dma = pltpu.SemaphoreType.DMA
        weight = pltpu.VMEM((D, D), BF)
        half_weight = pltpu.VMEM((D // 2, D), BF)
        masks = pltpu.VMEM((2, CHUNK, ROW), F32)
        lines_bf = pltpu.VMEM((4, 16, D), BF)
        row_full = pltpu.VMEM((ROW, D), BF)
        enc_full = pltpu.VMEM((ENC, D), BF)
        tokens = (OWN, D)

        def self_half(half, weights, pins):
            narrow = ((ROW, D // 2), BF, "e")
            return call(
                self_forward(half),
                here + a(xa, xb, ya, yb, *self_own, *weights)
                + v(line(self_qbias), line(self_vbias)),
                [
                    ((OWN, D // 2), BF, "e"), narrow, narrow, ((OWN, D // 2), BF, "v"),
                    ((OWN, 128), F32, "v"),
                ],
                [half_weight] * 3
                + [row_full, masks, lines_bf, dma((3, 7)), dma((4,)), dma((4,))],
                "self_forward_" + "ab"[half], pins=pins,
            )

        sq, sk, sv, att_a, stats_a, zero = self_half(
            0, [self_near[0], self_far[0]] * 2, [mine, enc]
        )
        (cross_x,) = gated([cross_x], [zero], "gate_forward")
        cross_near = [cross_x, cross_y, send(cross_x, head_to(2), "w_cross_near_2")]
        tq, tk, tv, att_b, stats_b, zero = self_half(
            1, [self_near[1], self_far[1], self_near[2], self_far[2]], [zero, cross_near[0]]
        )
        *cross_near, ea, ga_here, gb = gated(cross_near + [ea, ga, gb], [zero], "gate_far")
        cross_far = [send(one, core_to, "w_cross_far") for one in cross_near]
        eb = send(ea, core_to, "e_b")
        ga = send(ga_here, swap, "g_a")
        gb = send(gb, swap_b, "g_b")
        cross_w = cross_near + cross_far
        hat1, scale1, cq, ck, cv, catt, stats2, hat2, zero = call(
            cross_forward,
            here + v(xa, xb) + a(att_a, att_b) + v(params) + a(ea, eb)
            + a(*cross_own, *cross_w) + v(line(cross_qbias), line(cross_vbias)),
            [
                (tokens, F32, "e"), ((OWN, 128), F32, "v"),
                (tokens, BF, "e"), ((ENC, D), BF, "e"), ((ENC, D), BF, "e"), (tokens, BF, "v"),
                ((OWN, 128), F32, "v"), (tokens, F32, "v"),
            ],
            [weight] * 4 + [
                enc_full, lines_bf, dma((4, 7)), dma((4,)), dma((2,)), weight, dma((1, 7)),
                pltpu.VMEM(tokens, BF), dma((2,)),
            ],
            "cross_forward",
        )
        out_a, out_b, dsecond, left, right, ff_snd, vec_a, upb, zero = call(
            feed_forward,
            here + v(hat2, stats2, params) + a(up_weight) + v(line(up_bias)) + a(down_weight)
            + l(ga_here, ga, gb),
            [
                chunk, chunk, (tokens, F32, "e"), ((OWN, FF), BF, "a"), (tokens, BF, "a"),
                ((FF, D), BF, "a"), ((8, D), F32, "v"), ((1, FF), F32, "v"),
            ],
            [
                pltpu.VMEM((D, FF), BF), pltpu.VMEM((FF, D), BF), pltpu.VMEM((OWN, FF), BF),
                pltpu.VMEM((OWN, FF), F32), pltpu.VMEM(tokens, BF), pltpu.VMEM(tokens, F32),
                pltpu.VMEM(tokens, BF), pltpu.VMEM((OWN, FF), BF), pltpu.VMEM((FF, D), BF),
                dma((2, FF // FF_STEP)), dma((6,)),
            ],
            "feed_forward",
        )
        ff_got = send(ff_snd, core_to, "ff_core")
        out_got = send(out_a, swap, "out_a")
        out_b = send(out_b, swap_b_back, "out_b")
        ff_own, _ = call(
            ff_weight_grads, here + a(left, right), [((FF, D), BF, "a")],
            [
                pltpu.VMEM((FF, D), BF), pltpu.VMEM((4, OWN, D), BF), pltpu.VMEM(tokens, BF),
                dma((9,)),
            ],
            "ff_weight_grads",
        )
        output = jnp.concatenate([jnp.where(stays, out_a, out_got), out_b], axis=0)

        half = D // 2

        def ff_row(g, which):
            return g * D + which * half

        def both(row):
            return [(0, row), (1, row)]

        ff_x, ff_y, _ = add_call(
            "ff_add_1", place, [ff_own, ff_got], [D, D],
            [
                ((0, 0), half, both(ff_row(1, 0))), ((0, half), half, both(ff_row(3, 0))),
                ((1, 0), half, both(ff_row(2, 1))), ((1, half), half, both(ff_row(3, 1))),
            ],
            pins=[out_got, out_b],
        )
        ff_gx = send(ff_x, head_to(1), "ff_heads")
        ff_gy = send(ff_y, head_to(2), "ff_heads")

        wr = weight_rows
        rows_a = [((10 * wr, D), BF, "p")] * 2
        half_e = ((OWN, D // 2), BF, "e")
        cross_w4, self_w4 = cross_own[3], self_out
        enc_half, enc_grads = ((ENC, D // 2), BF, "e"), [enc_full] * 2
        cdq, cdk, cdv, cgrad, ca_own, ca_snd, zero = call(
            cross_backward_a,
            here + l(dsecond, catt, cq, ck, cv, stats2) + d(hat1)
            + v(params) + a(ea, eb, cross_w4, *cross_w),
            [half_e, enc_half, enc_half, (tokens, BF, "e")] + rows_a,
            [weight, pltpu.VMEM(tokens, BF), enc_full, dma((1, 7)), dma((2,))],
            "cross_backward_a", pins=[ff_x, ff_y],
        )
        (ca_snd,) = gated([ca_snd], [ff_gx, ff_gy, output], "gate_ca")
        ca_got = send(ca_snd, core_to, "ca_core")
        ff_x2, ff_y2, _ = add_call(
            "ff_add_2", place, [ff_own, ff_got, ff_gx, ff_gy], [half, half],
            [
                ((0, 0), half, both(ff_row(2, 0)) + [(2, half)]),
                ((1, 0), half, both(ff_row(1, 1)) + [(3, half)]),
            ],
            pins=[zero],
        )
        ff_gx2 = send(ff_x2, head_to(2), "ff_heads_2")
        ff_gy2 = send(ff_y2, head_to(1), "ff_heads_2")
        c_x3, _ = add_call(
            "c_add_1", place, [ca_own, ca_got], [4 * wr], [((0, 0), 4 * wr, both(4 * wr))],
            pins=[ff_x2],
        )
        c_gx3 = send(c_x3, head_to(1), "c_heads")
        dfirst, cb_own, cb_snd, vectors, zero = call(
            cross_backward_b,
            here + a(cdq, cdk, cdv) + d(dsecond) + l(cgrad, catt, cq, ck, cv, stats2)
            + d(hat1, scale1) + v(params) + a(ea, eb) + v(vec_a, upb)
            + a(*cross_own[:3], *cross_w),
            [
                (tokens, F32, "e"), ((6 * wr + HALF_ENC, D), BF, "p"),
                ((6 * wr + HALF_ENC, D), BF, "p"), ((16, D), F32, "v"),
            ],
            [weight] * 3 + [pltpu.VMEM(tokens, BF)] + enc_grads + [enc_full, dma((3, 7)), dma((5,))],
            "cross_backward_b", pins=[ff_x2, ff_y2, c_x3],
        )
        vectors = lax.all_gather(vectors, names)
        (cb_snd,) = gated([cb_snd], [ff_gx2, ff_gy2, c_gx3], "gate_cb")
        cb_got = send(cb_snd, core_to, "cb_core")

        def depth_send(parts, label):
            return [send(one, depth_to(d + 1), label) for d, one in enumerate(parts)]

        ff_mine, *ff_parts, _ = total_call(
            "ff_add_3", place, [ff_own, ff_got, ff_gx, ff_gy, ff_gx2, ff_gy2], D,
            [
                (0, half, both(ff_row(0, 0)) + [(2, 0), (4, 0)]),
                (half, half, both(ff_row(0, 1)) + [(3, 0), (5, 0)]),
            ],
            1, depth, pins=[zero],
        )
        ff_back = depth_send(ff_parts, "ff_depth")
        c_y2, c_x1, _ = add_call(
            "c_add_2", place, [ca_own, ca_got, cb_own, cb_got, c_gx3], [4 * wr, 4 * wr],
            [
                ((0, 0), 4 * wr, both(0) + [(4, 0)]),
                ((1, 0), 3 * wr, [(2, 3 * wr), (3, 3 * wr)]), ((1, 3 * wr), wr, both(9 * wr)),
            ],
            pins=[ff_parts[0]],
        )
        c_gy2 = send(c_y2, head_to(2), "c_heads_2")
        c_gx1 = send(c_x1, head_to(1), "c_heads_2")

        row_half, row_grads = ((ROW, D // 2), BF, "e"), [row_full] * 2
        sdq, sdk, sdv, sgrad, sa_own, sa_snd, zero = call(
            self_backward_a,
            here + l(dfirst, tq, tk, tv, stats_b) + a(att_a, att_b, xa, xb, ya, yb)
            + a(self_w4, *cross_w),
            [half_e, row_half, row_half, (tokens, BF, "e")] + rows_a,
            [weight, pltpu.VMEM(tokens, BF), masks]
            + [row_full, pltpu.VMEM((16, D), BF), dma((1, 7)), dma((5,))]
            + [pltpu.VMEM(tokens, BF), dma((2,))],
            "self_backward_a", pins=[*ff_parts, c_y2, c_x1],
        )
        (sa_snd,) = gated([sa_snd], [*ff_back, c_gy2, c_gx1], "gate_sa")
        sa_got = send(sa_snd, core_to, "sa_core")
        c_mine, *c_parts, _ = total_call(
            "c_add_3", place, [ca_own, ca_got, cb_own, cb_got, c_gy2, c_gx1], 4 * wr,
            [
                (0, 3 * wr, [(2, 0), (3, 0), (4, 0), (5, 0)]),
                (3 * wr, wr, [(0, 8 * wr), (1, 8 * wr), (4, 3 * wr), (5, 3 * wr)]),
            ],
            1, depth, pins=[zero], mine_type=BF,
        )
        c_depth = depth_send(c_parts, "c_depth")
        s_y, enc_sum, _ = add_call(
            "s_add_1", place, [sa_own, sa_got, cb_own, cb_got], [8 * wr, HALF_ENC],
            [((0, 0), 8 * wr, both(0)), ((1, 0), HALF_ENC, [(2, 6 * wr), (3, 6 * wr)])],
            pins=[c_parts[0]],
        )
        encoder_g = send(enc_sum, swap_b_back, "enc_grad")
        s_gy = send(s_y, head_to(2), "s_heads")
        sb_own, sb_snd, zero = call(
            self_backward_b,
            here + a(sdq, sdk, sdv) + d(dfirst) + l(sgrad, att_a, sq, sk, sv, stats_a)
            + a(xa, xb, ya, yb) + a(*self_own, *self_w),
            [((6 * wr + 2 * CHUNK, D), BF, "p"), ((6 * wr + 2 * CHUNK, D), BF, "p")],
            [weight] * 3 + [pltpu.VMEM(tokens, BF)] + row_grads + [masks]
            + [row_full, pltpu.VMEM((ROW, D), F32), pltpu.VMEM((16, D), BF), dma((3, 7)), dma((8,))],
            "self_backward_b", pins=[*c_parts, s_y, enc_sum],
        )
        (sb_snd,) = gated([sb_snd], [*c_depth, s_gy, encoder_g], "gate_sb")
        sb_got = send(sb_snd, core_to, "sb_core")

        def depth_sum(mine, got):
            for one in got:
                mine = mine + one.astype(F32)
            return mine

        part_rows = 4 * wr // depth
        s_x, in_a, in_b, c_part, _ = add_call(
            "s_add_2", place, [sa_own, sa_got, sb_own, sb_got, s_gy, c_mine, *c_depth],
            [4 * wr, CHUNK, CHUNK, part_rows],
            [
                ((0, 0), 3 * wr, [(2, 3 * wr), (3, 3 * wr), (4, 4 * wr)]),
                ((0, 3 * wr), wr, both(9 * wr) + [(4, 7 * wr)]),
                ((1, 0), CHUNK, [(2, 6 * wr), (3, 6 * wr)]),
                ((2, 0), CHUNK, [(2, 6 * wr + CHUNK), (3, 6 * wr + CHUNK)]),
                ((3, 0), part_rows, [(5 + n, 0) for n in range(depth)]),
            ],
        )
        c_back = [send(c_part, depth_to(d), "c_back") for d in range(1, depth)]
        s_gx = send(s_x, head_to(1), "s_heads_2")
        in_got = send(in_a, swap, "in_a")
        in_b = send(in_b, swap_b_back, "in_b")
        s_mine, *s_parts, _ = total_call(
            "s_add_3", place, [sa_own, sa_got, sb_own, sb_got, s_gy, s_gx], 4 * wr,
            [
                (0, 3 * wr, [(2, 0), (3, 0), (4, 0), (5, 0)]),
                (3 * wr, wr, [(0, 8 * wr), (1, 8 * wr), (4, 3 * wr), (5, 3 * wr)]),
            ],
            1, depth, pins=c_back,
        )
        s_depth = depth_send(s_parts, "s_depth")

        def whole_grads(own, other, label):
            *grads, qbias, vbias, _ = call(
                spread(depth, len(own)), here + v(*own, *other),
                [((GROUP, D), F32, "v")] * 4 + [((1, GROUP), F32, "v")] * 2,
                [pltpu.VMEM((2, 4 * wr, D), F32)], label + "_spread",
            )
            return grads, qbias[0], vbias[0]

        input_g = jnp.concatenate([jnp.where(stays, in_a, in_got), in_b], axis=0)
        c_own, _ = call(
            join, here + v(c_part, *c_back), [((4 * wr, D), BF, "v")], [], "c_join", pins=s_parts
        )
        c_other = send(c_own, core_to, "c_far")
        (cq_g, ck_g, cv_g, co_g), cqb, cvb = whole_grads([c_own], [c_other], "c")
        s_part = depth_sum(s_mine, s_depth).astype(BF)
        s_back = [send(s_part, depth_to(d), "s_back") for d in range(1, depth)]
        ff = depth_sum(ff_mine, ff_back).reshape(2, piece, D)
        ff_here = lax.dynamic_index_in_dim(ff, core, 0, keepdims=False)
        ff_there = send(lax.dynamic_index_in_dim(ff, 1 - core, 0, keepdims=False), core_to, "ff_last")
        upweight_g = jnp.where(core == 0, ff_here, ff_there).T
        downweight_g = jnp.where(core == 0, ff_there, ff_here)

        vectors = jnp.sum(vectors, axis=0)
        ff_at = (h * rows + r) * piece
        upbias_g = lax.dynamic_slice_in_dim(vectors[9:13].reshape(FF), ff_at, piece)
        (encoder_g, _) = call(
            move, here + v(encoder_g), [((HALF_ENC, D), BF, "v")], [], "encoder_grad", pins=s_parts
        )
        s_own = gated([s_part, *s_back], [cq_g, input_g, ff_here, ff_there, encoder_g], "gate_s_far")
        s_other = [send(one, core_to, "s_far") for one in s_own]
        (sq_g, sk_g, sv_g, so_g), sqb, svb = whole_grads(s_own, s_other, "s")

        return (
            output, input_g, encoder_g,
            sq_g.T, sqb, sk_g.T, sv_g.T, svb, so_g, vectors[8], vectors[6], vectors[7],
            cq_g.T, cqb, ck_g.T, cv_g.T, cvb, co_g, vectors[5],
            vectors[3], vectors[4], upweight_g, upbias_g, downweight_g, vectors[2],
            vectors[0], vectors[1],
        )

    rowed, headed = P(("rows", "heads"), None), P(None, "heads")
    by_head, by_head_rows, whole = P("heads"), P("heads", None), P()
    ffed = ("heads", "rows")
    return jax.shard_map(
        shards,
        mesh=mesh,
        in_specs=(
            rowed, rowed, P("rows", None),
            headed, by_head, headed, headed, by_head, by_head_rows, whole, whole, whole,
            headed, by_head, headed, headed, by_head, by_head_rows, whole, whole, whole,
            whole, whole, whole, whole, whole, whole, rowed,
        ),
        out_specs=(
            rowed, rowed, rowed,
            headed, by_head, headed, headed, by_head, by_head_rows, whole, whole, whole,
            headed, by_head, headed, headed, by_head, by_head_rows, whole, whole, whole,
            P(None, ffed), P(ffed), P(ffed, None), whole, whole, whole,
        ),
        check_vma=False,
    )
```

```python
import jax
import jax.numpy as jnp
from jax import lax
from jax.experimental import pallas as pl
from jax.experimental.pallas import tpu as pltpu
from jax.sharding import PartitionSpec as P

BF = jnp.bfloat16
F32 = jnp.float32
HEAD = 64
PAIR = 128
EPS = 1e-05
ROW = 1088
CHUNK = 272
OWN = 544
ENC = 1024
HALF_ENC = 512
D = 768
GROUP = 192
PIECE = 96
BIAS_ROWS = 16
FF = 3072
MIB = 1 << 20


def nn(a, b):
    return jnp.dot(a, b, preferred_element_type=F32)


def nt(a, b):
    return lax.dot_general(a, b, (((1,), (1,)), ((), ())), preferred_element_type=F32)


def tn(a, b):
    return lax.dot_general(a, b, (((0,), (0,)), ((), ())), preferred_element_type=F32)


def lane_ids(shape):
    return lax.broadcasted_iota(jnp.int32, shape, len(shape) - 1)


def pair_lanes(p):
    return pl.ds(pl.multiple_of(p * PAIR, PAIR), PAIR)


def normalize(total):
    center = total - jnp.mean(total, axis=-1, keepdims=True)
    scale = lax.rsqrt(jnp.mean(center * center, axis=-1, keepdims=True) + EPS)
    return center * scale, scale


def norm_back(grad, hat, scale, gain):
    scaled = grad * gain
    inner = scaled - jnp.mean(scaled, axis=-1, keepdims=True)
    return scale * (inner - hat * jnp.mean(scaled * hat, axis=-1, keepdims=True))


def column(values):
    return jnp.sum(values.astype(F32), axis=0, keepdims=True)


def pick_lane(ref, rows, lane):
    block = ref[rows, :]
    return jnp.sum(jnp.where(lane_ids(block.shape) == lane, block, 0.0), axis=-1, keepdims=True)


def start(copies):
    for one in copies:
        one.start()


def finish(copies):
    for one in copies:
        one.wait()


def by_core(core, body):
    for value in (0, 1):

        @pl.when(core == value)
        def _():
            body(value)


class Row:
    def __init__(self, ref, row):
        self.ref, self.row = ref, row

    def __getitem__(self, _):
        return self.ref[self.row : self.row + 1, :]


class Late:
    def __init__(self, source, held, sem, now):
        self.copy = pltpu.make_async_copy(source, held, sem)
        self.held = held
        self.started = self.waited = False
        if now:
            self.begin()

    def begin(self):
        if not self.started:
            self.copy.start()
            self.started = True

    def get(self):
        self.begin()
        if not self.waited:
            self.copy.wait()
            self.waited = True
        return self.held


class Early:
    def __init__(self, held, target, sem):
        self.copy = pltpu.make_async_copy(held, target, sem)
        self.held = held
        self.sent = False

    def send(self):
        self.copy.start()
        self.sent = True


class Pieces:
    def __init__(self, both, rows, own, snd, sems):
        self.both, self.rows, self.targets, self.sems = both, rows, (own, snd), sems
        self.copies = []

    def send(self, at, count):
        for n in (1, 0):
            self.copies.append(
                pltpu.make_async_copy(
                    self.both.at[pl.ds(n * self.rows + at, count)],
                    self.targets[n].at[pl.ds(at, count)],
                    self.sems.at[len(self.copies)],
                )
            )
            self.copies[-1].start()

    def put(self, core, half, at, block):
        to = jnp.where(core == half, 0, self.rows) + at
        self.both[pl.ds(pl.multiple_of(to, 16), block.shape[0]), :] = block

    def put_both(self, at, block):
        put_rows(self.both, at, block)
        put_rows(self.both, self.rows + at, block)

    def put_own(self, at, block):
        put_rows(self.both, at, block)

    def put_snd(self, at, block):
        put_rows(self.both, self.rows + at, block)


def call(kernel, ins, outs, scratch, name, pins=()):
    vmem, anywhere = pl.BlockSpec(memory_space=pltpu.VMEM), pl.BlockSpec(memory_space=pl.ANY)
    smem = pl.BlockSpec(memory_space=pltpu.SMEM)
    specs = {"v": vmem, "a": anywhere, "l": anywhere, "d": anywhere, "e": anywhere, "p": anywhere}
    specs["s"] = smem
    late = [(n, x) for n, (x, kind) in enumerate(ins) if kind in "ld"]
    early = [(n, out) for n, out in enumerate(outs) if out[2] == "e"]
    pair = [n for n, out in enumerate(outs) if out[2] == "p"]
    first = len(ins)
    last = first + len(pins)
    end = last + len(outs)

    def body(*refs):
        took, gave, rest = list(refs[:first]), list(refs[last:end]), list(refs[end + 1 :])
        own, rest = rest[: len(scratch)], rest[len(scratch) :]
        for n, (at, _) in enumerate(late):
            took[at] = Late(took[at], rest[n], rest[-1].at[n], ins[at][1] == "l")
        rest = rest[len(late) :]
        for n, (at, _) in enumerate(early):
            gave[at] = Early(rest[n], gave[at], rest[-1].at[len(late) + n])
        results, pieces = list(gave), []
        if pair:
            rows = outs[pair[0]][0][0]
            pieces = [Pieces(rest[-3], rows, gave[pair[0]], gave[pair[1]], rest[-2])]
            results[pair[0] : pair[1] + 1] = pieces
        kernel(*took, *results, *own)
        refs[end][...] = jnp.zeros((8, 128), F32)
        for at, _ in late:
            took[at].get()
        for at, _ in early:
            if not gave[at].sent:
                gave[at].send()
        for at, _ in early:
            gave[at].copy.wait()
        for one in pieces:
            finish(one.copies)

    extra = [pltpu.VMEM(x.shape, x.dtype) for _, x in late]
    extra += [pltpu.VMEM(out[0], out[1]) for _, out in early]
    if pair:
        extra += [pltpu.VMEM((2 * outs[pair[0]][0][0], D), BF), pltpu.SemaphoreType.DMA((8,))]
    extra += [pltpu.SemaphoreType.DMA((max(len(late) + len(early), 1),))]
    return pl.pallas_call(
        body,
        in_specs=[specs[kind] for _, kind in ins] + [anywhere] * len(pins),
        out_specs=[specs[out[2]] for out in outs] + [vmem],
        out_shape=[jax.ShapeDtypeStruct(out[0], out[1]) for out in outs]
        + [jax.ShapeDtypeStruct((8, 128), F32)],
        scratch_shapes=list(scratch) + extra,
        compiler_params=pltpu.CompilerParams(vmem_limit_bytes=64 * MIB - 65536),
        cost_estimate=pl.CostEstimate(flops=1000, bytes_accessed=1000, transcendentals=0),
        name=name,
    )(*[x for x, _ in ins], *pins)


def after(value, zero):
    return value + zero[0, 0].astype(value.dtype)


def weight_copies(w, slot, core, own, near, far, dst, sems):
    copies = [pltpu.make_async_copy(own[w], dst.at[pl.ds(0, GROUP)], sems.at[slot, 0])]
    rows = pl.ds(w * PIECE, PIECE)
    for i in (1, 2, 3):
        for at, which, refs in ((i, core, near), (3 + i, 1 - core, far)):
            to = pl.multiple_of(GROUP * i + PIECE * which, PIECE)
            copies.append(
                pltpu.make_async_copy(
                    refs[i - 1].at[rows], dst.at[pl.ds(to, PIECE)], sems.at[slot, at]
                )
            )
    return copies


def half_weight_copies(w, slot, core, own, near, far, half, dst, sems):
    copies = []
    rows = pl.ds(w * PIECE, PIECE)
    for n in (0, 1):
        i = 2 * half + n
        if i == 0:
            copies.append(
                pltpu.make_async_copy(own[w], dst.at[pl.ds(0, GROUP)], sems.at[slot, 0])
            )
            continue
        for at, which, refs in ((i, core, near), (3 + i, 1 - core, far)):
            to = pl.multiple_of(GROUP * n + PIECE * which, PIECE)
            copies.append(
                pltpu.make_async_copy(
                    refs[i - 1].at[rows], dst.at[pl.ds(to, PIECE)], sems.at[slot, at]
                )
            )
    return copies


def bias_copies(near, lines, sems):
    return [
        pltpu.make_async_copy(ref.at[pl.ds(ref.shape[0] - 16, 16)], lines.at[i], sems.at[i])
        for i, ref in enumerate(near)
    ]


def gathered_bias(parts, lines, count, which):
    for i in range(count):
        split = lines[i, 3 * which : 3 * which + 3, :GROUP].astype(F32)
        parts = parts + [split[0:1] + split[1:2] + split[2:3]]
    return jnp.concatenate(parts, axis=1)


def put_rows(target, at, block):
    target[at : at + block.shape[0], :] = block


def store_pieces(core, block, places, pieces):
    for g, at in enumerate(places):
        for half in (0, 1):
            row = g * GROUP + half * PIECE
            pieces.put(core, half, at, block[row : row + PIECE])


def store_bias(row, places, pieces):
    for i, at in enumerate(places):
        one = jnp.concatenate(
            [row[:, i * GROUP : (i + 1) * GROUP], jnp.zeros((1, D - GROUP), F32)], axis=1
        )
        block = jnp.concatenate([one, jnp.zeros((BIAS_ROWS - 1, D), F32)], axis=0).astype(BF)
        pieces.put_both(at + PIECE, block)


def forward_heads(q2, keys, values, bias, row_stats, p):
    lane = lane_ids(q2.shape)
    outs = []
    for t in (0, 1):
        query = jnp.where((lane // HEAD) == t, q2, jnp.zeros_like(q2))
        scores = nt(query, keys)
        if bias is not None:
            scores = scores + bias
        highest = jnp.max(scores, axis=-1, keepdims=True)
        raised = jnp.exp(scores - highest)
        total = jnp.sum(raised, axis=-1, keepdims=True)
        outs.append(nn(raised.astype(BF), values) / total)
        row_stats = jnp.where(
            lane_ids(row_stats.shape) == 2 * p + t, highest + jnp.log(total), row_stats
        )
    return jnp.where((lane // HEAD) == 0, outs[0], outs[1]).astype(BF), row_stats


def backward_heads(q2, g2, o2, keys, values, bias, stats, p):
    count = q2.shape[0]
    first = (lane_ids(q2.shape) // HEAD) == 0
    zero = jnp.zeros_like(q2)

    def stacked(a):
        return jnp.concatenate([jnp.where(first, a, zero), jnp.where(first, zero, a)], axis=0)

    query, grad = stacked(q2), stacked(g2)
    product = g2.astype(F32) * o2.astype(F32)
    inner = jnp.concatenate(
        [
            jnp.sum(jnp.where(first, product, 0.0), axis=-1, keepdims=True),
            jnp.sum(jnp.where(first, 0.0, product), axis=-1, keepdims=True),
        ],
        axis=0,
    )
    lanes = lane_ids(stats.shape)
    lse = jnp.concatenate(
        [
            jnp.sum(jnp.where(lanes == 2 * p + t, stats, 0.0), axis=-1, keepdims=True)
            for t in (0, 1)
        ],
        axis=0,
    )
    scores = nt(query, keys)
    if bias is not None:
        scores = scores + jnp.concatenate([bias, bias], axis=0)
    shares = jnp.exp(scores - lse)
    grad_scores = (shares * (nt(grad, values) - inner)).astype(BF)
    grad_q = nn(grad_scores, keys)
    return (
        jnp.where(first, grad_q[:count], grad_q[count:]),
        tn(grad_scores, query),
        tn(shares.astype(BF), grad),
    )


def document_ends(xa, place):
    pair_at = place[1] // 2
    lengths = jnp.where(
        pair_at == 0,
        xa[0:1, :8] * 16.0 + xa[2:3, :8],
        xa[1:2, :8] * 16.0
        + xa[3:4, :8],
    )
    ends, total = [], 0.0
    for d in range(8):
        total = total + lengths[:, d : d + 1]
        ends.append(total)
    return ends


def mask_bias(ends, chunk, width):
    qpos = chunk * CHUNK + lax.broadcasted_iota(jnp.int32, (CHUNK, 1), 0)
    kpos = lax.broadcasted_iota(jnp.int32, (1, width), 1)
    qat, kat = qpos.astype(F32), kpos.astype(F32)
    qseg = jnp.zeros((CHUNK, 1), F32)
    kseg = jnp.zeros((1, width), F32)
    for end in ends:
        qseg = qseg + jnp.where(qat >= end, 1.0, 0.0)
        kseg = kseg + jnp.where(kat >= end, 1.0, 0.0)
    return jnp.where((qseg == kseg) & (kpos <= qpos), 0.0, -1000000000.0)


def chunk_of(core, which):
    return (2 * core, 3 - 2 * core, 2 - 2 * core, 1 + 2 * core)[which]


def chunk_rows(core, which):
    return pl.ds(pl.multiple_of(chunk_of(core, which) * CHUNK, 16), CHUNK)


def key_counts(core):
    return ((0, 1), (1, 4)) if core == 0 else ((0, 3), (1, 2))


def prepare(place, x, lengths, wq, wk, wv, qbias, vbias, xa, xb, mine):
    xa[0:CHUNK, :] = x[0:CHUNK, :]
    xa[CHUNK : CHUNK + 16, :] = jnp.zeros((16, D), BF)
    counts = lengths[...].astype(F32)
    high = jnp.floor(counts * 0.0625)
    rows = jnp.concatenate([high, counts - high * 16.0, jnp.zeros((12, 8), F32)], axis=0)
    rows = jnp.concatenate([rows, jnp.zeros((16, 120), F32)], axis=1)
    xa[CHUNK : CHUNK + 16, 0:128] = rows.astype(BF)
    xb[...] = x[CHUNK:OWN, :]
    prepare_weights(place[0], (wq, wk, wv), qbias, vbias, mine)


def prepare_more(
    place, so, wq, wk, wv, wo, qbias, vbias, out_grad, enc,
    mine, ga, gb, enc_out,
):
    ga[...] = out_grad[0:CHUNK, :]
    gb[...] = out_grad[CHUNK:OWN, :]
    enc_out[...] = enc[...]
    prepare_weights(place[0], (wq, wk, wv, wo, so), qbias, vbias, mine)


def prepare_weights(core, weights, qbias, vbias, mine):
    half = pl.ds(pl.multiple_of(core * PIECE, PIECE), PIECE)
    for w, one in enumerate(weights):
        mine[w * PIECE : (w + 1) * PIECE, :] = one[half, :]
    rows = []
    for one in (qbias[...], vbias[...]):
        for _ in range(3):
            top = one.astype(BF).astype(F32)
            rows.append(top)
            one = one - top
    rows = jnp.concatenate(rows + [jnp.zeros((10, GROUP), F32)], axis=0)
    at = len(weights) * PIECE
    mine[at : at + 16, :] = jnp.concatenate(
        [rows, jnp.zeros((16, D - GROUP), F32)], axis=1
    ).astype(BF)


def join(place, *refs):
    at = 0
    for one in refs[:-1]:
        put_rows(refs[-1], at, one[...])
        at += one.shape[0]


def move(place, source, target):
    target[...] = source[...]


def gate(*refs):
    pass


def row_copies(core, xs, full, sems):
    return [
        pltpu.make_async_copy(
            x.at[pl.ds(0, CHUNK)], full.at[chunk_rows(core, which)], sems.at[which]
        )
        for which, x in enumerate(xs)
    ]


def self_forward(half):
    def kernel(
        place, xa, xb, ya, yb, w0, w1, w2, na, fa, nb, fb, qbias, vbias,
        q_out, k_out, v_out, att, stats,
        wq, wk, wv, full, bias, lines, sems, line_sems, row_sems,
    ):
        core = place[0]
        near, far = (na, na, nb), (fa, fa, fb)
        sets = [
            half_weight_copies(w, w, core, (w0, w1, w2), near, far, half, dst, sems)
            for w, dst in enumerate((wq, wk, wv))
        ]
        groups = [na] if half == 0 else [na, nb]
        held = bias_copies(groups, lines, line_sems)
        rows = row_copies(core, (xa, xb, ya, yb), full, row_sems)
        tail = pltpu.make_async_copy(xa.at[pl.ds(CHUNK, 16)], lines.at[3], line_sems.at[3])
        tail.start()
        start(rows)
        start(held)
        for one in sets:
            start(one)
        tail.wait()
        ends = document_ends(lines[3].astype(F32), place)
        for slot in (0, 1):
            bias[slot] = mask_bias(ends, chunk_of(core, slot), ROW)
        finish(rows)
        finish(held)
        for one in sets:
            finish(one)

        def line(own, which):
            return gathered_bias([own[...]] if half == 0 else [], lines, len(groups), which)

        k_out.held[...] = nt(full[...], wk[...]).astype(BF)
        k_out.send()
        query_line = line(qbias, 0)
        for which in (0, 1):
            q_out.held[which * CHUNK : (which + 1) * CHUNK, :] = (
                (nt(full[chunk_rows(core, which), :], wq[...]) + query_line) * 0.125
            ).astype(BF)
        q_out.send()
        v_out.held[...] = (nt(full[...], wv[...]) + line(vbias, 1)).astype(BF)
        v_out.send()
        q, k, v = q_out.held, k_out.held, v_out.held
        stats[...] = jnp.zeros_like(stats)

        def attend(value):
            def pair(p, carry):
                lanes = pair_lanes(p)
                for slot, count in key_counts(value):
                    rows = pl.ds(slot * CHUNK, CHUNK)
                    width = count * CHUNK
                    out, now = forward_heads(
                        q[rows, lanes], k[0:width, lanes], v[0:width, lanes],
                        bias[slot, :, 0:width], stats[rows, :], p,
                    )
                    att[rows, lanes] = out
                    stats[rows, :] = now
                return carry

            lax.fori_loop(0, 3, pair, 0)

        by_core(core, attend)

    return kernel


def att_copies(att_a, att_b, full, sems):
    half = D // 2
    return [
        pltpu.make_async_copy(one, full.at[:, pl.ds(n * half, half)], sems.at[n])
        for n, one in enumerate((att_a, att_b))
    ]


def cross_forward(
    place, xa, xb, att_a, att_b, params, ea, eb, w0, w1, w2, w3, w4, n1, n2, n3,
    f1, f2, f3, qbias, vbias,
    hat1, scale1, q_out, k_out, v_out, att, stats, hat_out,
    wq, wk, wv, wo, full, lines, sems, line_sems, row_sems, self_wo, self_sems, self_att, att_sems,
):
    core = place[0]
    self_bias, gain1, shift1, obias = (Row(params, n) for n in range(4))
    near, far = (n1, n2, n3), (f1, f2, f3)
    rows = [
        pltpu.make_async_copy(e, full.at[pl.ds(i * HALF_ENC, HALF_ENC)], row_sems.at[i])
        for i, e in enumerate((ea, eb))
    ]
    held = bias_copies(near, lines, line_sems)
    sets = [
        weight_copies(w, w, core, (w0, w1, w2, w3), near, far, dst, sems)
        for w, dst in enumerate((wq, wk, wv, wo))
    ]
    self_set = weight_copies(
        4, 0, core, (None, None, None, None, w4), near, far, self_wo, self_sems
    )
    halves = att_copies(att_a, att_b, self_att, att_sems)
    start(halves)
    start(self_set)
    start(held)
    start(sets[0])
    start(rows)
    for one in sets[1:]:
        start(one)
    finish(halves)
    finish(self_set)
    product = nn(self_att[...], self_wo[...]) + self_bias[...]
    for which, x in enumerate((xa, xb)):
        part = slice(which * CHUNK, (which + 1) * CHUNK)
        hat, scale = normalize(x[0:CHUNK, :].astype(F32) + product[part])
        hat1.held[part, :] = hat
        scale1[part, :] = jnp.broadcast_to(scale, (CHUNK, 128))
    hat1.send()
    hidden = (hat1.held[...] * gain1[...] + shift1[...]).astype(BF)
    finish(held)
    finish(sets[0])
    line = gathered_bias([qbias[...]], lines, 3, 0)
    q_out.held[...] = ((nt(hidden, wq[...]) + line) * 0.125).astype(BF)
    q_out.send()
    finish(rows)
    finish(sets[1])
    k_out.held[...] = nt(full[...], wk[...]).astype(BF)
    k_out.send()
    finish(sets[2])
    line = gathered_bias([vbias[...]], lines, 3, 1)
    v_out.held[...] = (nt(full[...], wv[...]) + line).astype(BF)
    v_out.send()
    finish(sets[3])
    q, k, v = q_out.held, k_out.held, v_out.held
    stats[...] = jnp.zeros_like(stats)

    def pair(p, carry):
        lanes = pair_lanes(p)
        for slot in (0, 1):
            rows = pl.ds(slot * CHUNK, CHUNK)
            out, now = forward_heads(
                q[rows, lanes], k[:, lanes], v[:, lanes], None, stats[rows, :], p
            )
            att[rows, lanes] = out
            stats[rows, :] = now
        return carry

    lax.fori_loop(0, 6, pair, 0, unroll=2)
    hidden = hat1.held[...] * gain1[...] + shift1[...]
    hat, scale = normalize(hidden + (nn(att[...], wo[...]) + obias[...]))
    hat_out[...] = hat
    stats[...] = jnp.where(lane_ids(stats.shape) == 12, scale, stats[...])


FF_STEP = 512
FF_BLOCK = 768


def gelu_parts(u):
    size = jnp.abs(u)
    t = 1.0 / (1.0 + (0.3275911 * 0.7071067811865476) * size)
    poly = t * (
        0.254829592
        + t * (-0.284496736 + t * (1.421413741 + t * (-1.453152027 + t * 1.061405429)))
    )
    bell = jnp.exp(-0.5 * u * u)
    tail = 0.5 * poly * bell
    phi = jnp.where(u >= 0.0, 1.0 - tail, tail)
    return u * phi, phi + u * bell * 0.3989422804014327


def feed_forward(
    place, hat2, stats, params, up_hbm, up_bias, down_hbm, ga_here, ga, gb,
    out_a, out_b, dsecond, left, right, snd, vec, upb,
    up, down, active, slope, hid, total, third, grads, held, sems, out_sems,
):
    core, group = place[0], place[1]
    gain2, shift2, down_bias, gain3, shift3 = (Row(params, 4 + n) for n in range(5))
    steps = FF // FF_STEP
    ups = [
        pltpu.make_async_copy(
            up_hbm.at[:, pl.ds(i * FF_STEP, FF_STEP)],
            up.at[:, pl.ds(i * FF_STEP, FF_STEP)],
            sems.at[0, i],
        )
        for i in range(steps)
    ]
    downs = [
        pltpu.make_async_copy(
            down_hbm.at[pl.ds(i * FF_STEP, FF_STEP)],
            down.at[pl.ds(i * FF_STEP, FF_STEP)],
            sems.at[1, i],
        )
        for i in range(steps)
    ]
    for i in range(steps):
        ups[i].start()
        downs[i].start()
    second = hat2[...] * gain2[...] + shift2[...]
    hid[...] = second.astype(BF)
    total[...] = second + down_bias[...]
    for i in range(steps):
        cols = pl.ds(i * FF_STEP, FF_STEP)
        ups[i].wait()
        u = nn(hid[...], up[:, cols]) + up_bias[:, cols]
        act, slo = gelu_parts(u)
        active[:, cols] = act.astype(BF)
        slope[:, cols] = slo
        downs[i].wait()
        total[...] += nn(active[:, cols], down[cols, :])
    hat3, scale3 = normalize(total[...])
    out = (hat3 * gain3[...] + shift3[...]).astype(BF)
    out_a[...] = out[0:CHUNK]
    out_b[...] = out[CHUNK:OWN]
    first = jnp.where(core == group % 2, ga_here.get()[...], ga.get()[...])
    grad = jnp.concatenate([first, gb.get()[...]], axis=0).astype(F32)
    vec[0:1, :] = column(grad * hat3)
    vec[1:2, :] = column(grad)
    dthird = norm_back(grad, hat3, scale3, gain3[...])
    total[...] = dthird
    third[...] = dthird.astype(BF)
    vec[2:3, :] = column(third[...])
    for i in range(FF // FF_BLOCK):
        cols = pl.ds(i * FF_BLOCK, FF_BLOCK)
        du = (nt(third[...], down[cols, :]) * slope[:, cols]).astype(BF)
        grads[:, cols] = du
        upb[:, cols] = column(du)
        total[...] += nt(du, up[:, cols])
    grad = total[...]
    hat = hat2[...]
    scale = pick_lane(stats, slice(None), 12)
    vec[3:4, :] = column(grad * hat)
    vec[4:5, :] = column(grad)
    dsec = norm_back(grad, hat, scale, gain2[...])
    dsecond.held[...] = dsec
    dsecond.send()
    vec[5:6, :] = column(dsec.astype(BF))
    vec[6:8, :] = jnp.zeros((2, D), F32)

    def hand_over(value):
        pairs = ((grads, hid), (active, third))
        mine, other = pairs[value], pairs[1 - value]
        copies = [
            pltpu.make_async_copy(mine[0], left, out_sems.at[4]),
            pltpu.make_async_copy(mine[1], right, out_sems.at[5]),
        ]
        start(copies)
        for i in range(4):
            cols = pl.ds(pl.multiple_of((group ^ i) * D, D), D)
            rows = pl.ds(i * D, D)
            held[rows, :] = tn(other[0][:, cols], other[1][...]).astype(BF)
            copies.append(pltpu.make_async_copy(held.at[rows], snd.at[rows], out_sems.at[i]))
            copies[-1].start()
        finish(copies)

    by_core(core, hand_over)


def ff_weight_grads(place, left, right, out, held, left_held, right_held, sems):
    copies = [pltpu.make_async_copy(right, right_held, sems.at[0])]
    for i in range(4):
        cols = pl.ds(pl.multiple_of((place[1] ^ i) * D, D), D)
        copies.append(pltpu.make_async_copy(left.at[:, cols], left_held.at[i], sems.at[1 + i]))
    start(copies[:2])
    finish(copies[:2])
    start(copies[2:])
    outs = []
    for i in range(4):
        if i:
            copies[1 + i].wait()
        rows = pl.ds(i * D, D)
        held[rows, :] = tn(left_held[i], right_held[...]).astype(BF)
        outs.append(pltpu.make_async_copy(held.at[rows], out.at[rows], sems.at[5 + i]))
        outs[i].start()
    finish(outs)


def out_grads(core, att, low, wo, grad, places, pieces):
    store_pieces(core, tn(att[...], low[...]).astype(BF), places, pieces)
    store_bias(jnp.zeros((1, D), F32), places, pieces)
    grad[...] = nt(low[...], wo[...]).astype(BF)


def weight_grads(core, dq, dk, dv, queries, keys, places, pieces):
    store_pieces(core, tn(dq[...], queries).astype(BF), places[0], pieces)
    store_pieces(core, tn(dk[...], keys).astype(BF), places[1], pieces)
    store_pieces(core, tn(dv[...], keys).astype(BF), places[2], pieces)
    store_bias(column(dq[...]), places[0], pieces)
    store_bias(jnp.zeros((1, dk.shape[1]), F32), places[1], pieces)
    store_bias(column(dv[...]), places[2], pieces)


def cross_part(core, first, grad, att, q, k, v, stats, queries, full, places, pieces, dq, dk, dv):

    def pair(p, carry):
        lanes = pair_lanes(first + p)
        out = pair_lanes(p)
        gq, gk, gv = backward_heads(
            q[:, lanes], grad[:, lanes], att[:, lanes], k[:, lanes], v[:, lanes],
            None, stats[...], first + p,
        )
        dq[:, out] = (gq * 0.125).astype(BF)
        dk[:, out] = gk.astype(BF)
        dv[:, out] = gv.astype(BF)
        return carry

    lax.fori_loop(0, 3, pair, 0)
    half = pl.ds(0, D // 2)
    weight_grads(
        core, dq.at[:, half], dk.at[:, half], dv.at[:, half], queries(), full[...], places, pieces
    )


def cross_backward_a(
    place, dsecond, att, q, k, v, stats, hat1, params, ea, eb, w3, n1, n2, n3, f1, f2, f3,
    dq, dk, dv, grad, pieces,
    wo, low, full, sems, row_sems,
):
    core = place[0]
    gain1, shift1 = Row(params, 1), Row(params, 2)
    copies = weight_copies(
        3, 0, core, (None, None, None, w3), (n1, n2, n3), (f1, f2, f3), wo, sems
    )
    rows = [
        pltpu.make_async_copy(e, full.at[pl.ds(i * HALF_ENC, HALF_ENC)], row_sems.at[i])
        for i, e in enumerate((ea, eb))
    ]
    start(copies)
    low[...] = dsecond.get()[...].astype(BF)
    size = pieces.rows // 10
    places = [[(4 * g + w) * size for g in (0, 1)] for w in range(3)]
    places_o = [8 * size, 9 * size, 3 * size, 7 * size]
    att = att.get()
    finish(copies)
    out_grads(core, att, low, wo, grad.held, places_o, pieces)
    grad.send()
    q, k, v, stats = q.get(), k.get(), v.get(), stats.get()
    start(rows)
    hat1.begin()

    def queries():
        for one in (dq, dk, dv):
            one.send()
        finish(rows)
        return (hat1.get()[...] * gain1[...] + shift1[...]).astype(BF)

    cross_part(
        core, 3, grad.held, att, q, k, v, stats, queries, full, places, pieces,
        dq.held, dk.held, dv.held,
    )
    pieces.send(0, 10 * size)


def cross_backward_b(
    place, dq_a, dsecond, grad, att, q, k, v, stats, hat1, scale1, params, ea, eb,
    vec_a, upb, w0, n1, n2, n3, f1, f2, f3,
    dk, dv, dfirst, pieces, vec,
    wq, dq, full, sems, row_sems,
):
    core = place[0]
    gain1, shift1 = Row(params, 1), Row(params, 2)
    copies = weight_copies(0, 0, core, (w0,), (n1, n2, n3), (f1, f2, f3), wq, sems)
    rows = [
        pltpu.make_async_copy(e, full.at[pl.ds(i * HALF_ENC, HALF_ENC)], row_sems.at[i])
        for i, e in enumerate((ea, eb))
    ]
    part = pltpu.make_async_copy(dq_a, dq.at[:, pl.ds(D // 2, D // 2)], row_sems.at[2])
    grad, att, stats = grad.get(), att.get(), stats.get()
    q, k, v = q.get(), k.get(), v.get()
    start(rows)
    hat1.begin()
    start(copies)
    part.start()
    dsecond.begin()
    scale1.begin()
    size = pieces.rows // 6
    places = [[(3 * g + w) * size for g in (0, 1)] for w in range(3)]

    def queries():
        dk.send()
        dv.send()
        finish(rows)
        return (hat1.get()[...] * gain1[...] + shift1[...]).astype(BF)

    cross_part(
        core, 0, grad, att, q, k, v, stats, queries, full, places, pieces, dq, dk.held, dv.held
    )
    pieces.send(0, 6 * size)
    part.wait()
    finish(copies)
    total = dsecond.get()[...] + nn(dq[...], wq[...])
    hat = hat1.get()[...]
    vec[0:6, :] = vec_a[0:6, :]
    vec[6:7, :] = column(total * hat)
    vec[7:8, :] = column(total)
    dfi = norm_back(total, hat, scale1.get()[:, 0:1], gain1[...])
    dfirst.held[...] = dfi
    dfirst.send()
    vec[8:9, :] = column(dfi.astype(BF))
    for n in range(4):
        vec[9 + n : 10 + n, :] = upb[:, n * D : (n + 1) * D]
    vec[13:16, :] = jnp.zeros((3, D), F32)


def self_part(
    core, first, ends, grad, att, q, k, v, stats, full, places, pieces, dq, dk, dv, bias, rows
):
    for slot in (0, 1):
        bias[slot] = mask_bias(ends, chunk_of(core, slot), ROW)

    def attend(value):
        def pair(p, carry):
            lanes = pair_lanes(first + p)
            out = pair_lanes(p)
            (low_slot, low), (high_slot, high) = sorted(key_counts(value), key=lambda x: x[1])
            parts = {}
            for slot, count in ((low_slot, low), (high_slot, high)):
                rows = pl.ds(slot * CHUNK, CHUNK)
                width = count * CHUNK
                gq, gk, gv = backward_heads(
                    q[rows, out], grad[rows, lanes], att[rows, out],
                    k[0:width, out], v[0:width, out],
                    bias[slot, :, 0:width], stats[rows, :], p,
                )
                dq[rows, out] = (gq * 0.125).astype(BF)
                parts[slot] = (gk, gv)
            for n, dst in ((0, dk), (1, dv)):
                wide, narrow = parts[high_slot][n], parts[low_slot][n]
                shared, reach = low * CHUNK, high * CHUNK
                dst[0:shared, out] = (wide[0:shared] + narrow).astype(BF)
                dst[shared:reach, out] = wide[shared:reach].astype(BF)
                if reach < ROW:
                    dst[reach:ROW, out] = jnp.zeros((ROW - reach, PAIR), BF)
            return carry

        lax.fori_loop(0, 3, pair, 0)

    by_core(core, attend)
    finish(rows)
    half = pl.ds(0, D // 2)
    queries = jnp.concatenate([full[chunk_rows(core, n), :] for n in (0, 1)], axis=0)
    weight_grads(
        core, dq.at[:, half], dk.at[:, half], dv.at[:, half], queries, full[...], places, pieces
    )


def self_backward_a(
    place, dfirst, q, k, v, stats, att_a, att_b, xa, xb, ya, yb, w3, m1, m2, m3, g1, g2, g3,
    dq, dk, dv, grad, pieces,
    wo, low, bias, full, lines, sems, row_sems, att, att_sems,
):
    core = place[0]
    copies = weight_copies(
        4, 0, core, (None, None, None, None, w3), (m1, m2, m3), (g1, g2, g3), wo, sems
    )
    tail = pltpu.make_async_copy(xa.at[pl.ds(CHUNK, 16)], lines, row_sems.at[4])
    rows = row_copies(core, (xa, xb, ya, yb), full, row_sems)
    halves = att_copies(att_a, att_b, att, att_sems)
    start(copies)
    start(halves)
    tail.start()
    low[...] = dfirst.get()[...].astype(BF)
    size = pieces.rows // 10
    places = [[(4 * g + w) * size for g in (0, 1)] for w in range(3)]
    places_o = [8 * size, 9 * size, 3 * size, 7 * size]
    finish(halves)
    finish(copies)
    out_grads(core, att, low, wo, grad.held, places_o, pieces)
    grad.send()
    tail.wait()
    q, k, v, stats = q.get(), k.get(), v.get(), stats.get()
    start(rows)
    self_part(
        core, 3, document_ends(lines[...].astype(F32), place), grad.held,
        att.at[:, pl.ds(D // 2, D // 2)], q, k, v, stats, full,
        places, pieces, dq.held, dk.held, dv.held, bias, rows,
    )
    pieces.send(0, 10 * size)
    for one in (dq, dk, dv):
        one.send()


def self_backward_b(
    place, grad, att, q, k, v, stats, xa, xb, ya, yb,
    dq, dk, dv, pieces,
    bias, full, lines, row_sems,
):
    core = place[0]
    size = pieces.rows // 6
    places = [[(3 * g + w) * size for g in (0, 1)] for w in range(3)]
    tail = pltpu.make_async_copy(xa.at[pl.ds(CHUNK, 16)], lines, row_sems.at[4])
    rows = row_copies(core, (xa, xb, ya, yb), full, row_sems)
    tail.start()
    tail.wait()
    grad, att, stats = grad.get(), att.get(), stats.get()
    q, k, v = q.get(), k.get(), v.get()
    start(rows)
    self_part(
        core, 0, document_ends(lines[...].astype(F32), place), grad, att, q, k, v, stats, full,
        places, pieces, dq.held, dk.held, dv.held, bias, rows,
    )
    pieces.send(0, 6 * size)
    for one in (dq, dk, dv):
        one.send()


def late_grads(
    place, dq_a, dq_b, dk_a, dk_b, dv_a, dv_b, ck_a, ck_b, cv_a, cv_b, dfirst,
    w0, w1, w2, n1, n2, n3, f1, f2, f3, v1, v2, m1, m2, m3, g1, g2, g3,
    pieces,
    wq, wk, wv, xk, xv, dq, dk, dv, ck, cv, total, sems, part_sems,
):
    core = place[0]
    near, far = (n1, n2, n3), (f1, f2, f3)
    cross = (None, v1, v2)
    half = D // 2
    parts = [
        pltpu.make_async_copy(one, dst.at[:, pl.ds(at, half)], part_sems.at[n])
        for n, (one, dst, at) in enumerate(
            (
                (ck_b, ck, 0), (ck_a, ck, half), (cv_b, cv, 0), (cv_a, cv, half),
                (dk_b, dk, 0), (dk_a, dk, half), (dv_b, dv, 0), (dv_a, dv, half),
                (dq_b, dq, 0), (dq_a, dq, half),
            )
        )
    ]
    sets = [
        weight_copies(1, 0, core, cross, (m1, m2, m3), (g1, g2, g3), xk, sems),
        weight_copies(2, 1, core, cross, (m1, m2, m3), (g1, g2, g3), xv, sems),
    ] + [
        weight_copies(w, 2 + w, core, (w0, w1, w2), near, far, dst, sems)
        for w, dst in enumerate((wq, wk, wv))
    ]
    for one in sets[:2]:
        start(one)
    start(parts)
    for one in sets[2:]:
        start(one)
    finish(parts)
    for one in sets[:2]:
        finish(one)
    enc = nn(ck[...], xk[...]) + nn(cv[...], xv[...])
    pieces.put_own(0, enc[0:HALF_ENC].astype(BF))
    pieces.put_snd(0, enc[HALF_ENC:ENC].astype(BF))
    pieces.send(0, HALF_ENC)
    for one in sets[2:]:
        finish(one)
    total[...] = nn(dk[...], wk[...]) + nn(dv[...], wv[...])
    mine = nn(dq[...], wq[...]) + dfirst.get()[...]
    for n in (0, 1):
        at = HALF_ENC + n * CHUNK
        pieces.put_snd(at, total[chunk_rows(core, 2 + n), :].astype(BF))
        pieces.put_own(
            at, (mine[n * CHUNK : (n + 1) * CHUNK] + total[chunk_rows(core, n), :]).astype(BF)
        )
    pieces.send(HALF_ENC, 2 * CHUNK)


def add_jobs(jobs, ins, store, held, sems):
    copies, at, most = [], 0, job_most(jobs)
    for _, rows, sources in jobs:
        mine = []
        for operand, row in sources:
            mine.append(
                (
                    pltpu.make_async_copy(
                        ins[operand].at[pl.ds(row, rows)], held.at[pl.ds(at, rows)],
                        sems.at[len(copies) * most + len(mine)],
                    ),
                    at,
                )
            )
            at += rows
        copies.append(mine)
    for mine in copies:
        for copy, _ in mine:
            copy.start()
    for (place, rows, _), mine in zip(jobs, copies):
        total = 0.0
        for copy, row in mine:
            copy.wait()
            total = total + held[row : row + rows, :].astype(F32)
        store(place, total)


def job_most(jobs):
    return max(len(sources) for _, _, sources in jobs)


def job_rows(jobs):
    return sum(rows * len(sources) for _, rows, sources in jobs)


def add_call(name, place, arrays, outs, jobs, pins=()):
    count = len(arrays)

    def kernel(place, *refs):
        ins, targets = refs[:count], refs[count : count + len(outs)]
        held, out_held, sems, out_sems = refs[count + len(outs) :]
        copies = []

        def store(where, total):
            at = sum(outs[: where[0]]) + where[1]
            put_rows(out_held, at, total.astype(BF))
            rows = pl.ds(at, total.shape[0])
            copies.append(
                pltpu.make_async_copy(
                    out_held.at[rows],
                    targets[where[0]].at[pl.ds(where[1], total.shape[0])],
                    out_sems.at[len(copies)],
                )
            )
            copies[-1].start()

        add_jobs(jobs, ins, store, held, sems)
        finish(copies)

    dma = pltpu.SemaphoreType.DMA
    return call(
        kernel, [(place, "s")] + [(one, "a") for one in arrays],
        [((rows, D), BF, "a") for rows in outs],
        [
            pltpu.VMEM((job_rows(jobs), D), BF), pltpu.VMEM((sum(outs), D), BF),
            dma((job_most(jobs) * len(jobs),)), dma((len(jobs),)),
        ],
        name, pins=pins,
    )


def total_call(name, place, arrays, total_rows, jobs, groups, depth, pins=(), mine_type=F32):
    count = len(arrays)
    size = total_rows // groups // depth

    def kernel(place, *refs):
        mine, parts = refs[count], refs[count + 1 : count + depth]
        held, total, sems = refs[count + depth :]

        def store(row, value):
            put_rows(total, row, value)

        add_jobs(jobs, refs[:count], store, held, sems)
        for d in range(depth):
            for g in range(groups):
                at = pl.multiple_of(
                    g * (total_rows // groups) + (place[2] ^ d) * size, 8
                )
                block = total[pl.ds(at, size), :]
                if d == 0:
                    put_rows(mine, g * size, block.astype(mine_type))
                else:
                    put_rows(parts[d - 1], g * size, block.astype(BF))

    return call(
        kernel, [(place, "s")] + [(one, "a") for one in arrays],
        [((groups * size, D), mine_type, "v")] + [((groups * size, D), BF, "v")] * (depth - 1),
        [
            pltpu.VMEM((job_rows(jobs), D), BF), pltpu.VMEM((total_rows, D), F32),
            pltpu.SemaphoreType.DMA((job_most(jobs) * len(jobs),)),
        ],
        name, pins=pins,
    )


def spread(depth, count):
    def kernel(place, *refs):
        own, other, refs = refs[:count], refs[count : 2 * count], refs[2 * count :]
        outs, biases, total = refs[:4], refs[4:-1], refs[-1]
        core, k = place[0], place[2]
        size = total.shape[1] // depth
        for which, parts in enumerate((own, other)):
            for d in range(depth):
                at = pl.multiple_of((k ^ d) * size, 8)
                ref, row = (parts[d], 0) if count == depth else (parts[0], d * size)
                total[which, pl.ds(at, size), :] = ref[row : row + size, :].astype(F32)
        rows = total.shape[1] // 4
        for n, out in enumerate(outs):
            for which, half in ((0, core), (1, 1 - core)):
                to = pl.ds(pl.multiple_of(half * PIECE, PIECE), PIECE)
                out[to, :] = total[which, n * rows : n * rows + PIECE, :]
        for n, bias in zip((0, 2), biases):
            at = n * rows + PIECE
            bias[...] = total[0, at : at + 1, :GROUP]

    return kernel


def solution(mesh):
    names = tuple(mesh.axis_names)
    heads, rows = mesh.shape["heads"], mesh.shape["rows"]
    depth = rows // 2
    piece = FF // (heads * rows)
    weight_rows = PIECE + BIAS_ROWS
    while (4 * weight_rows) % (8 * depth):
        weight_rows += BIAS_ROWS
    def send(value, where, label="moved"):
        pairs = []
        for r in range(rows):
            for h in range(heads):
                to_r, to_h = where(r, h)
                if (to_r, to_h) == (r, h):
                    continue
                index = {"rows": (r, to_r), "heads": (h, to_h)}
                a = b = 0
                for name in names:
                    a = a * mesh.shape[name] + index[name][0]
                    b = b * mesh.shape[name] + index[name][1]
                pairs.append((a, b))
        with jax.named_scope(label):
            return lax.ppermute(value, names, pairs)

    def swap(r, h):
        return (r & ~1) | (h & 1), (h & ~1) | (r & 1)

    def swap_b(r, h):
        return (r & ~1) | (1 - (h & 1)), (h & ~1) | (r & 1)

    def swap_b_back(r, h):
        return (r & ~1) | (h & 1), (h & ~1) | (1 - (r & 1))

    def core_to(r, h):
        return r ^ 1, h

    def head_to(d):
        return lambda r, h: (r, h ^ d)

    def depth_to(d):
        return lambda r, h: (r ^ (2 * d), h)

    def shards(
        layer_input, encoder_out, doc_lengths,
        self_query, self_qbias, self_key_weight, self_value, self_vbias, self_out, self_obias,
        first_gain, first_shift,
        cross_query, cross_qbias, cross_key, cross_value, cross_vbias, cross_out, cross_obias,
        second_gain, second_shift, up_weight, up_bias, down_weight, down_bias,
        third_gain, third_shift, out_grad,
    ):
        h = lax.axis_index("heads")
        r = lax.axis_index("rows")
        core, k = r % 2, r // 2
        place = jnp.stack([core, h, k]).astype(jnp.int32)
        stays = core == h % 2

        def line(vector):
            return vector.reshape(1, -1)

        params = jnp.stack(
            [
                self_obias, first_gain, first_shift, cross_obias, second_gain, second_shift,
                down_bias, third_gain, third_shift,
            ]
        )

        def v(*arrays):
            return [(one, "v") for one in arrays]

        def a(*arrays):
            return [(one, "a") for one in arrays]

        def l(*arrays):
            return [(one, "l") for one in arrays]

        def d(*arrays):
            return [(one, "d") for one in arrays]

        here = [(place, "s")]

        self_own = [self_query.T, self_key_weight.T, self_value.T]
        cross_own = [cross_query.T, cross_key.T, cross_value.T, cross_out, self_out]
        chunk = ((CHUNK, D), BF, "v")
        xa, xb, mine, zero = call(
            prepare,
            here + v(layer_input, doc_lengths, *self_own, line(self_qbias), line(self_vbias)),
            [((CHUNK + 16, D), BF, "v"), chunk, ((3 * PIECE + 16, D), BF, "v")], [], "prepare",
        )

        def gather_groups(mine, label):
            x, y = send(mine, head_to(1), label), send(mine, head_to(2), label)
            return [x, y, send(x, head_to(2), label + "_2")]

        self_near = gather_groups(mine, "w_self_near")
        xb = send(xb, swap_b, "x_b")
        xa = jnp.where(stays, xa, send(xa, swap, "x_a"))
        mine, ga, gb, enc, _ = call(
            prepare_more,
            here + v(self_out, *cross_own[:4], line(cross_qbias), line(cross_vbias))
            + v(out_grad, encoder_out),
            [((5 * PIECE + 16, D), BF, "v"), chunk, chunk, ((HALF_ENC, D), BF, "v")],
            [], "prepare_more", pins=[zero],
        )
        ya = send(xa, core_to, "y_a")
        yb = send(xb, core_to, "y_b")
        self_far = [send(one, core_to, "w_self_far") for one in self_near]
        self_w = self_near + self_far

        def gated(values, pins, name):
            count = len(values)
            anywhere = pl.BlockSpec(memory_space=pl.ANY)
            return pl.pallas_call(
                gate,
                in_specs=[anywhere] * (count + len(pins)),
                out_specs=[anywhere] * count,
                out_shape=[jax.ShapeDtypeStruct(one.shape, one.dtype) for one in values],
                input_output_aliases={n: n for n in range(count)},
                name=name,
            )(*values, *pins)

        mine, enc = gated([mine, enc], [self_near[0], self_near[1], xa, xb, params], "gate_cross")
        cross_x, cross_y = (send(mine, head_to(d), "w_cross_near") for d in (1, 2))
        ea = send(enc, swap_b, "e_a")

        dma = pltpu.SemaphoreType.DMA
        weight = pltpu.VMEM((D, D), BF)
        half_weight = pltpu.VMEM((D // 2, D), BF)
        masks = pltpu.VMEM((2, CHUNK, ROW), F32)
        lines_bf = pltpu.VMEM((4, 16, D), BF)
        row_full = pltpu.VMEM((ROW, D), BF)
        enc_full = pltpu.VMEM((ENC, D), BF)
        tokens = (OWN, D)

        def self_half(half, weights, pins):
            narrow = ((ROW, D // 2), BF, "e")
            return call(
                self_forward(half),
                here + a(xa, xb, ya, yb, *self_own, *weights)
                + v(line(self_qbias), line(self_vbias)),
                [
                    ((OWN, D // 2), BF, "e"), narrow, narrow, ((OWN, D // 2), BF, "v"),
                    ((OWN, 128), F32, "v"),
                ],
                [half_weight] * 3
                + [row_full, masks, lines_bf, dma((3, 7)), dma((4,)), dma((4,))],
                "self_forward_" + "ab"[half], pins=pins,
            )

        sq, sk, sv, att_a, stats_a, zero = self_half(
            0, [self_near[0], self_far[0]] * 2, [mine, enc]
        )
        (cross_x,) = gated([cross_x], [zero], "gate_forward")
        cross_near = [cross_x, cross_y, send(cross_x, head_to(2), "w_cross_near_2")]
        tq, tk, tv, att_b, stats_b, zero = self_half(
            1, [self_near[1], self_far[1], self_near[2], self_far[2]], [zero, cross_near[0]]
        )
        *cross_near, ea, ga_here, gb = gated(cross_near + [ea, ga, gb], [zero], "gate_far")
        cross_far = [send(one, core_to, "w_cross_far") for one in cross_near]
        eb = send(ea, core_to, "e_b")
        ga = send(ga_here, swap, "g_a")
        gb = send(gb, swap_b, "g_b")
        cross_w = cross_near + cross_far
        hat1, scale1, cq, ck, cv, catt, stats2, hat2, zero = call(
            cross_forward,
            here + v(xa, xb) + a(att_a, att_b) + v(params) + a(ea, eb)
            + a(*cross_own, *cross_w) + v(line(cross_qbias), line(cross_vbias)),
            [
                (tokens, F32, "e"), ((OWN, 128), F32, "v"),
                (tokens, BF, "e"), ((ENC, D), BF, "e"), ((ENC, D), BF, "e"), (tokens, BF, "v"),
                ((OWN, 128), F32, "v"), (tokens, F32, "v"),
            ],
            [weight] * 4 + [
                enc_full, lines_bf, dma((4, 7)), dma((4,)), dma((2,)), weight, dma((1, 7)),
                pltpu.VMEM(tokens, BF), dma((2,)),
            ],
            "cross_forward",
        )
        out_a, out_b, dsecond, left, right, ff_snd, vec_a, upb, zero = call(
            feed_forward,
            here + v(hat2, stats2, params) + a(up_weight) + v(line(up_bias)) + a(down_weight)
            + l(ga_here, ga, gb),
            [
                chunk, chunk, (tokens, F32, "e"), ((OWN, FF), BF, "a"), (tokens, BF, "a"),
                ((FF, D), BF, "a"), ((8, D), F32, "v"), ((1, FF), F32, "v"),
            ],
            [
                pltpu.VMEM((D, FF), BF), pltpu.VMEM((FF, D), BF), pltpu.VMEM((OWN, FF), BF),
                pltpu.VMEM((OWN, FF), F32), pltpu.VMEM(tokens, BF), pltpu.VMEM(tokens, F32),
                pltpu.VMEM(tokens, BF), pltpu.VMEM((OWN, FF), BF), pltpu.VMEM((FF, D), BF),
                dma((2, FF // FF_STEP)), dma((6,)),
            ],
            "feed_forward",
        )
        ff_got = send(ff_snd, core_to, "ff_core")
        out_got = send(out_a, swap, "out_a")
        out_b = send(out_b, swap_b_back, "out_b")
        ff_own, _ = call(
            ff_weight_grads, here + a(left, right), [((FF, D), BF, "a")],
            [
                pltpu.VMEM((FF, D), BF), pltpu.VMEM((4, OWN, D), BF), pltpu.VMEM(tokens, BF),
                dma((9,)),
            ],
            "ff_weight_grads",
        )
        output = jnp.concatenate([jnp.where(stays, out_a, out_got), out_b], axis=0)

        half = D // 2

        def ff_row(g, which):
            return g * D + which * half

        def both(row):
            return [(0, row), (1, row)]

        ff_x, ff_y, _ = add_call(
            "ff_add_1", place, [ff_own, ff_got], [D, D],
            [
                ((0, 0), half, both(ff_row(1, 0))), ((0, half), half, both(ff_row(3, 0))),
                ((1, 0), half, both(ff_row(2, 1))), ((1, half), half, both(ff_row(3, 1))),
            ],
            pins=[out_got, out_b],
        )
        ff_gx = send(ff_x, head_to(1), "ff_heads")
        ff_gy = send(ff_y, head_to(2), "ff_heads")

        wr = weight_rows
        rows_a = [((10 * wr, D), BF, "p")] * 2
        half_e = ((OWN, D // 2), BF, "e")
        cross_w4, self_w4 = cross_own[3], self_out
        enc_half = ((ENC, D // 2), BF, "e")
        cdq, cdk, cdv, cgrad, ca_own, ca_snd, zero = call(
            cross_backward_a,
            here + l(dsecond, catt, cq, ck, cv, stats2) + d(hat1)
            + v(params) + a(ea, eb, cross_w4, *cross_w),
            [half_e, enc_half, enc_half, (tokens, BF, "e")] + rows_a,
            [weight, pltpu.VMEM(tokens, BF), enc_full, dma((1, 7)), dma((2,))],
            "cross_backward_a", pins=[ff_x, ff_y],
        )
        (ca_snd,) = gated([ca_snd], [ff_gx, ff_gy, output], "gate_ca")
        ca_got = send(ca_snd, core_to, "ca_core")
        ff_x2, ff_y2, _ = add_call(
            "ff_add_2", place, [ff_own, ff_got, ff_gx, ff_gy], [half, half],
            [
                ((0, 0), half, both(ff_row(2, 0)) + [(2, half)]),
                ((1, 0), half, both(ff_row(1, 1)) + [(3, half)]),
            ],
            pins=[zero],
        )
        ff_gx2 = send(ff_x2, head_to(2), "ff_heads_2")
        ff_gy2 = send(ff_y2, head_to(1), "ff_heads_2")
        c_x3, _ = add_call(
            "c_add_1", place, [ca_own, ca_got], [4 * wr], [((0, 0), 4 * wr, both(4 * wr))],
            pins=[ff_x2],
        )
        c_gx3 = send(c_x3, head_to(1), "c_heads")
        cdk_b, cdv_b, dfirst, cb_own, cb_snd, vectors, zero = call(
            cross_backward_b,
            here + a(cdq) + d(dsecond) + l(cgrad, catt, cq, ck, cv, stats2)
            + d(hat1, scale1) + v(params) + a(ea, eb) + v(vec_a, upb)
            + a(cross_own[0], *cross_w),
            [
                enc_half, enc_half, (tokens, F32, "e"), ((6 * wr, D), BF, "p"),
                ((6 * wr, D), BF, "p"), ((16, D), F32, "v"),
            ],
            [weight, pltpu.VMEM(tokens, BF), enc_full, dma((1, 7)), dma((3,))],
            "cross_backward_b", pins=[ff_x2, ff_y2, c_x3],
        )
        vectors = lax.all_gather(vectors, names)
        (cb_snd,) = gated([cb_snd], [ff_gx2, ff_gy2, c_gx3], "gate_cb")
        cb_got = send(cb_snd, core_to, "cb_core")

        def depth_send(parts, label):
            return [send(one, depth_to(d + 1), label) for d, one in enumerate(parts)]

        ff_mine, *ff_parts, _ = total_call(
            "ff_add_3", place, [ff_own, ff_got, ff_gx, ff_gy, ff_gx2, ff_gy2], D,
            [
                (0, half, both(ff_row(0, 0)) + [(2, 0), (4, 0)]),
                (half, half, both(ff_row(0, 1)) + [(3, 0), (5, 0)]),
            ],
            1, depth, pins=[zero],
        )
        ff_back = depth_send(ff_parts, "ff_depth")
        c_y2, c_x1, _ = add_call(
            "c_add_2", place, [ca_own, ca_got, cb_own, cb_got, c_gx3], [4 * wr, 4 * wr],
            [
                ((0, 0), 4 * wr, both(0) + [(4, 0)]),
                ((1, 0), 3 * wr, [(2, 3 * wr), (3, 3 * wr)]), ((1, 3 * wr), wr, both(9 * wr)),
            ],
            pins=[ff_parts[0]],
        )
        c_gy2 = send(c_y2, head_to(2), "c_heads_2")
        c_gx1 = send(c_x1, head_to(1), "c_heads_2")

        row_half = ((ROW, D // 2), BF, "e")
        sdq, sdk, sdv, sgrad, sa_own, sa_snd, zero = call(
            self_backward_a,
            here + l(dfirst, tq, tk, tv, stats_b) + a(att_a, att_b, xa, xb, ya, yb)
            + a(self_w4, *cross_w),
            [half_e, row_half, row_half, (tokens, BF, "e")] + rows_a,
            [weight, pltpu.VMEM(tokens, BF), masks]
            + [row_full, pltpu.VMEM((16, D), BF), dma((1, 7)), dma((5,))]
            + [pltpu.VMEM(tokens, BF), dma((2,))],
            "self_backward_a", pins=[*ff_parts, c_y2, c_x1],
        )
        (sa_snd,) = gated([sa_snd], [*ff_back, c_gy2, c_gx1], "gate_sa")
        sa_got = send(sa_snd, core_to, "sa_core")
        c_mine, *c_parts, _ = total_call(
            "c_add_3", place, [ca_own, ca_got, cb_own, cb_got, c_gy2, c_gx1], 4 * wr,
            [
                (0, 3 * wr, [(2, 0), (3, 0), (4, 0), (5, 0)]),
                (3 * wr, wr, [(0, 8 * wr), (1, 8 * wr), (4, 3 * wr), (5, 3 * wr)]),
            ],
            1, depth, pins=[zero], mine_type=BF,
        )
        c_depth = depth_send(c_parts, "c_depth")
        s_y, _ = add_call(
            "s_add_1", place, [sa_own, sa_got], [8 * wr], [((0, 0), 8 * wr, both(0))],
            pins=[c_parts[0]],
        )
        s_gy = send(s_y, head_to(2), "s_heads")
        sdq_b, sdk_b, sdv_b, sb_own, sb_snd, zero = call(
            self_backward_b,
            here + l(sgrad, att_a, sq, sk, sv, stats_a) + a(xa, xb, ya, yb),
            [half_e, row_half, row_half, ((6 * wr, D), BF, "p"), ((6 * wr, D), BF, "p")],
            [masks, row_full, pltpu.VMEM((16, D), BF), dma((5,))],
            "self_backward_b", pins=[*c_parts, s_y],
        )
        (sb_snd,) = gated([sb_snd], [*c_depth, s_gy], "gate_sb")
        sb_got = send(sb_snd, core_to, "sb_core")

        def depth_sum(mine, got):
            for one in got:
                mine = mine + one.astype(F32)
            return mine

        part_rows = 4 * wr // depth
        s_x, c_part, _ = add_call(
            "s_add_2", place, [sa_own, sa_got, sb_own, sb_got, s_gy, c_mine, *c_depth],
            [4 * wr, part_rows],
            [
                ((0, 0), 3 * wr, [(2, 3 * wr), (3, 3 * wr), (4, 4 * wr)]),
                ((0, 3 * wr), wr, both(9 * wr) + [(4, 7 * wr)]),
                ((1, 0), part_rows, [(5 + n, 0) for n in range(depth)]),
            ],
        )
        c_back = [send(c_part, depth_to(d), "c_back") for d in range(1, depth)]
        s_gx = send(s_x, head_to(1), "s_heads_2")
        late_own, late_snd, _ = call(
            late_grads,
            here + a(sdq, sdq_b, sdk, sdk_b, sdv, sdv_b, cdk, cdk_b, cdv, cdv_b) + l(dfirst)
            + a(*self_own, *self_w, *cross_own[1:3], *cross_w),
            [((HALF_ENC + OWN, D), BF, "p")] * 2,
            [weight] * 5 + [pltpu.VMEM(tokens, BF)] + [row_full] * 2 + [enc_full] * 2
            + [pltpu.VMEM((ROW, D), F32), dma((5, 7)), dma((10,))],
            "late_grads", pins=[s_x],
        )
        s_mine, *s_parts, _ = total_call(
            "s_add_3", place, [sa_own, sa_got, sb_own, sb_got, s_gy, s_gx], 4 * wr,
            [
                (0, 3 * wr, [(2, 0), (3, 0), (4, 0), (5, 0)]),
                (3 * wr, wr, [(0, 8 * wr), (1, 8 * wr), (4, 3 * wr), (5, 3 * wr)]),
            ],
            1, depth, pins=[*c_back, late_own],
        )
        s_depth = depth_send(s_parts, "s_depth")
        (late_snd,) = gated([late_snd], s_parts, "gate_late")
        late_got = send(late_snd, core_to, "late_core")
        enc_sum, in_a, in_b, _ = add_call(
            "late_add", place, [late_own, late_got], [HALF_ENC, CHUNK, CHUNK],
            [
                ((0, 0), HALF_ENC, both(0)), ((1, 0), CHUNK, both(HALF_ENC)),
                ((2, 0), CHUNK, both(HALF_ENC + CHUNK)),
            ],
        )
        encoder_g = send(enc_sum, swap_b_back, "enc_grad")
        in_got = send(in_a, swap, "in_a")
        in_b = send(in_b, swap_b_back, "in_b")

        def whole_grads(own, other, label):
            *grads, qbias, vbias, _ = call(
                spread(depth, len(own)), here + v(*own, *other),
                [((GROUP, D), F32, "v")] * 4 + [((1, GROUP), F32, "v")] * 2,
                [pltpu.VMEM((2, 4 * wr, D), F32)], label + "_spread",
            )
            return grads, qbias[0], vbias[0]

        input_g = jnp.concatenate([jnp.where(stays, in_a, in_got), in_b], axis=0)
        c_own, _ = call(
            join, here + v(c_part, *c_back), [((4 * wr, D), BF, "v")], [], "c_join", pins=s_parts
        )
        c_other = send(c_own, core_to, "c_far")
        (cq_g, ck_g, cv_g, co_g), cqb, cvb = whole_grads([c_own], [c_other], "c")
        s_part = depth_sum(s_mine, s_depth).astype(BF)
        s_back = [send(s_part, depth_to(d), "s_back") for d in range(1, depth)]
        ff = depth_sum(ff_mine, ff_back).reshape(2, piece, D)
        ff_here = lax.dynamic_index_in_dim(ff, core, 0, keepdims=False)
        ff_there = send(lax.dynamic_index_in_dim(ff, 1 - core, 0, keepdims=False), core_to, "ff_last")
        upweight_g = jnp.where(core == 0, ff_here, ff_there).T
        downweight_g = jnp.where(core == 0, ff_there, ff_here)

        vectors = jnp.sum(vectors, axis=0)
        ff_at = (h * rows + r) * piece
        upbias_g = lax.dynamic_slice_in_dim(vectors[9:13].reshape(FF), ff_at, piece)
        (encoder_g, _) = call(
            move, here + v(encoder_g), [((HALF_ENC, D), BF, "v")], [], "encoder_grad"
        )
        s_own = gated([s_part, *s_back], [cq_g, input_g, ff_here, ff_there, encoder_g], "gate_s_far")
        s_other = [send(one, core_to, "s_far") for one in s_own]
        (sq_g, sk_g, sv_g, so_g), sqb, svb = whole_grads(s_own, s_other, "s")

        return (
            output, input_g, encoder_g,
            sq_g.T, sqb, sk_g.T, sv_g.T, svb, so_g, vectors[8], vectors[6], vectors[7],
            cq_g.T, cqb, ck_g.T, cv_g.T, cvb, co_g, vectors[5],
            vectors[3], vectors[4], upweight_g, upbias_g, downweight_g, vectors[2],
            vectors[0], vectors[1],
        )

    rowed, headed = P(("rows", "heads"), None), P(None, "heads")
    by_head, by_head_rows, whole = P("heads"), P("heads", None), P()
    ffed = ("heads", "rows")
    return jax.shard_map(
        shards,
        mesh=mesh,
        in_specs=(
            rowed, rowed, P("rows", None),
            headed, by_head, headed, headed, by_head, by_head_rows, whole, whole, whole,
            headed, by_head, headed, headed, by_head, by_head_rows, whole, whole, whole,
            whole, whole, whole, whole, whole, whole, rowed,
        ),
        out_specs=(
            rowed, rowed, rowed,
            headed, by_head, headed, headed, by_head, by_head_rows, whole, whole, whole,
            headed, by_head, headed, headed, by_head, by_head_rows, whole, whole, whole,
            P(None, ffed), P(ffed), P(ffed, None), whole, whole, whole,
        ),
        check_vma=False,
    )
```

```python
import jax
import jax.numpy as jnp
from jax import lax
from jax.experimental import pallas as pl
from jax.experimental.pallas import tpu as pltpu
from jax.sharding import PartitionSpec as P

BF = jnp.bfloat16
F32 = jnp.float32
HEAD = 64
PAIR = 128
EPS = 1e-05
ROW = 1088
CHUNK = 272
OWN = 544
ENC = 1024
HALF_ENC = 512
D = 768
GROUP = 192
PIECE = 96
BIAS_ROWS = 16
FF = 3072
MIB = 1 << 20


def nn(a, b):
    return jnp.dot(a, b, preferred_element_type=F32)


def nt(a, b):
    return lax.dot_general(a, b, (((1,), (1,)), ((), ())), preferred_element_type=F32)


def tn(a, b):
    return lax.dot_general(a, b, (((0,), (0,)), ((), ())), preferred_element_type=F32)


def lane_ids(shape):
    return lax.broadcasted_iota(jnp.int32, shape, len(shape) - 1)


def pair_lanes(p):
    return pl.ds(pl.multiple_of(p * PAIR, PAIR), PAIR)


def normalize(total):
    center = total - jnp.mean(total, axis=-1, keepdims=True)
    scale = lax.rsqrt(jnp.mean(center * center, axis=-1, keepdims=True) + EPS)
    return center * scale, scale


def norm_back(grad, hat, scale, gain):
    scaled = grad * gain
    inner = scaled - jnp.mean(scaled, axis=-1, keepdims=True)
    return scale * (inner - hat * jnp.mean(scaled * hat, axis=-1, keepdims=True))


def column(values):
    return jnp.sum(values.astype(F32), axis=0, keepdims=True)


def pick_lane(ref, rows, lane):
    block = ref[rows, :]
    return jnp.sum(jnp.where(lane_ids(block.shape) == lane, block, 0.0), axis=-1, keepdims=True)


def start(copies):
    for one in copies:
        one.start()


def finish(copies):
    for one in copies:
        one.wait()


def by_core(core, body):
    for value in (0, 1):

        @pl.when(core == value)
        def _():
            body(value)


class Row:
    def __init__(self, ref, row):
        self.ref, self.row = ref, row

    def __getitem__(self, _):
        return self.ref[self.row : self.row + 1, :]


class Late:
    def __init__(self, source, held, sem, now):
        self.copy = pltpu.make_async_copy(source, held, sem)
        self.held = held
        self.started = self.waited = False
        if now:
            self.begin()

    def begin(self):
        if not self.started:
            self.copy.start()
            self.started = True

    def get(self):
        self.begin()
        if not self.waited:
            self.copy.wait()
            self.waited = True
        return self.held


class Early:
    def __init__(self, held, target, sem):
        self.copy = pltpu.make_async_copy(held, target, sem)
        self.held = held
        self.sent = False

    def send(self):
        self.copy.start()
        self.sent = True


class Pieces:
    def __init__(self, both, rows, own, snd, sems):
        self.both, self.rows, self.targets, self.sems = both, rows, (own, snd), sems
        self.copies = []

    def send(self, at, count):
        for n in (1, 0):
            self.copies.append(
                pltpu.make_async_copy(
                    self.both.at[pl.ds(n * self.rows + at, count)],
                    self.targets[n].at[pl.ds(at, count)],
                    self.sems.at[len(self.copies)],
                )
            )
            self.copies[-1].start()

    def put(self, core, half, at, block):
        to = jnp.where(core == half, 0, self.rows) + at
        self.both[pl.ds(pl.multiple_of(to, 16), block.shape[0]), :] = block

    def put_both(self, at, block):
        put_rows(self.both, at, block)
        put_rows(self.both, self.rows + at, block)

    def put_own(self, at, block):
        put_rows(self.both, at, block)

    def put_snd(self, at, block):
        put_rows(self.both, self.rows + at, block)


def call(kernel, ins, outs, scratch, name, pins=()):
    vmem, anywhere = pl.BlockSpec(memory_space=pltpu.VMEM), pl.BlockSpec(memory_space=pl.ANY)
    smem = pl.BlockSpec(memory_space=pltpu.SMEM)
    specs = {"v": vmem, "a": anywhere, "l": anywhere, "d": anywhere, "e": anywhere, "p": anywhere}
    specs["s"] = smem
    late = [(n, x) for n, (x, kind) in enumerate(ins) if kind in "ld"]
    early = [(n, out) for n, out in enumerate(outs) if out[2] == "e"]
    pair = [n for n, out in enumerate(outs) if out[2] == "p"]
    first = len(ins)
    last = first + len(pins)
    end = last + len(outs)

    def body(*refs):
        took, gave, rest = list(refs[:first]), list(refs[last:end]), list(refs[end + 1 :])
        own, rest = rest[: len(scratch)], rest[len(scratch) :]
        for n, (at, _) in enumerate(late):
            took[at] = Late(took[at], rest[n], rest[-1].at[n], ins[at][1] == "l")
        rest = rest[len(late) :]
        for n, (at, _) in enumerate(early):
            gave[at] = Early(rest[n], gave[at], rest[-1].at[len(late) + n])
        results, pieces = list(gave), []
        if pair:
            rows = outs[pair[0]][0][0]
            pieces = [Pieces(rest[-3], rows, gave[pair[0]], gave[pair[1]], rest[-2])]
            results[pair[0] : pair[1] + 1] = pieces
        kernel(*took, *results, *own)
        refs[end][...] = jnp.zeros((8, 128), F32)
        for at, _ in late:
            took[at].get()
        for at, _ in early:
            if not gave[at].sent:
                gave[at].send()
        for at, _ in early:
            gave[at].copy.wait()
        for one in pieces:
            finish(one.copies)

    extra = [pltpu.VMEM(x.shape, x.dtype) for _, x in late]
    extra += [pltpu.VMEM(out[0], out[1]) for _, out in early]
    if pair:
        extra += [pltpu.VMEM((2 * outs[pair[0]][0][0], D), BF), pltpu.SemaphoreType.DMA((8,))]
    extra += [pltpu.SemaphoreType.DMA((max(len(late) + len(early), 1),))]
    return pl.pallas_call(
        body,
        in_specs=[specs[kind] for _, kind in ins] + [anywhere] * len(pins),
        out_specs=[specs[out[2]] for out in outs] + [vmem],
        out_shape=[jax.ShapeDtypeStruct(out[0], out[1]) for out in outs]
        + [jax.ShapeDtypeStruct((8, 128), F32)],
        scratch_shapes=list(scratch) + extra,
        compiler_params=pltpu.CompilerParams(vmem_limit_bytes=64 * MIB - 65536),
        cost_estimate=pl.CostEstimate(flops=1000, bytes_accessed=1000, transcendentals=0),
        name=name,
    )(*[x for x, _ in ins], *pins)


def after(value, zero):
    return value + zero[0, 0].astype(value.dtype)


def weight_copies(w, slot, core, own, near, far, dst, sems):
    copies = [pltpu.make_async_copy(own[w], dst.at[pl.ds(0, GROUP)], sems.at[slot, 0])]
    rows = pl.ds(w * PIECE, PIECE)
    for i in (1, 2, 3):
        for at, which, refs in ((i, core, near), (3 + i, 1 - core, far)):
            to = pl.multiple_of(GROUP * i + PIECE * which, PIECE)
            copies.append(
                pltpu.make_async_copy(
                    refs[i - 1].at[rows], dst.at[pl.ds(to, PIECE)], sems.at[slot, at]
                )
            )
    return copies


def half_weight_copies(w, slot, core, own, near, far, half, dst, sems):
    copies = []
    rows = pl.ds(w * PIECE, PIECE)
    for n in (0, 1):
        i = 2 * half + n
        if i == 0:
            copies.append(
                pltpu.make_async_copy(own[w], dst.at[pl.ds(0, GROUP)], sems.at[slot, 0])
            )
            continue
        for at, which, refs in ((i, core, near), (3 + i, 1 - core, far)):
            to = pl.multiple_of(GROUP * n + PIECE * which, PIECE)
            copies.append(
                pltpu.make_async_copy(
                    refs[i - 1].at[rows], dst.at[pl.ds(to, PIECE)], sems.at[slot, at]
                )
            )
    return copies


def bias_copies(near, lines, sems):
    return [
        pltpu.make_async_copy(ref.at[pl.ds(ref.shape[0] - 16, 16)], lines.at[i], sems.at[i])
        for i, ref in enumerate(near)
    ]


def gathered_bias(parts, lines, count, which):
    for i in range(count):
        split = lines[i, 3 * which : 3 * which + 3, :GROUP].astype(F32)
        parts = parts + [split[0:1] + split[1:2] + split[2:3]]
    return jnp.concatenate(parts, axis=1)


def put_rows(target, at, block):
    target[at : at + block.shape[0], :] = block


def store_pieces(core, block, places, pieces):
    for g, at in enumerate(places):
        for half in (0, 1):
            row = g * GROUP + half * PIECE
            pieces.put(core, half, at, block[row : row + PIECE])


def store_bias(row, places, pieces):
    for i, at in enumerate(places):
        one = jnp.concatenate(
            [row[:, i * GROUP : (i + 1) * GROUP], jnp.zeros((1, D - GROUP), F32)], axis=1
        )
        block = jnp.concatenate([one, jnp.zeros((BIAS_ROWS - 1, D), F32)], axis=0).astype(BF)
        pieces.put_both(at + PIECE, block)


def forward_heads(q2, keys, values, bias, row_stats, p):
    lane = lane_ids(q2.shape)
    outs = []
    for t in (0, 1):
        query = jnp.where((lane // HEAD) == t, q2, jnp.zeros_like(q2))
        scores = nt(query, keys)
        if bias is not None:
            scores = scores + bias
        highest = jnp.max(scores, axis=-1, keepdims=True)
        raised = jnp.exp(scores - highest)
        total = jnp.sum(raised, axis=-1, keepdims=True)
        outs.append(nn(raised.astype(BF), values) / total)
        row_stats = jnp.where(
            lane_ids(row_stats.shape) == 2 * p + t, highest + jnp.log(total), row_stats
        )
    return jnp.where((lane // HEAD) == 0, outs[0], outs[1]).astype(BF), row_stats


def backward_heads(q2, g2, o2, keys, values, bias, stats, p):
    count = q2.shape[0]
    first = (lane_ids(q2.shape) // HEAD) == 0
    zero = jnp.zeros_like(q2)

    def stacked(a):
        return jnp.concatenate([jnp.where(first, a, zero), jnp.where(first, zero, a)], axis=0)

    query, grad = stacked(q2), stacked(g2)
    product = g2.astype(F32) * o2.astype(F32)
    inner = jnp.concatenate(
        [
            jnp.sum(jnp.where(first, product, 0.0), axis=-1, keepdims=True),
            jnp.sum(jnp.where(first, 0.0, product), axis=-1, keepdims=True),
        ],
        axis=0,
    )
    lanes = lane_ids(stats.shape)
    lse = jnp.concatenate(
        [
            jnp.sum(jnp.where(lanes == 2 * p + t, stats, 0.0), axis=-1, keepdims=True)
            for t in (0, 1)
        ],
        axis=0,
    )
    scores = nt(query, keys)
    if bias is not None:
        scores = scores + jnp.concatenate([bias, bias], axis=0)
    shares = jnp.exp(scores - lse)
    grad_scores = (shares * (nt(grad, values) - inner)).astype(BF)
    grad_q = nn(grad_scores, keys)
    return (
        jnp.where(first, grad_q[:count], grad_q[count:]),
        tn(grad_scores, query),
        tn(shares.astype(BF), grad),
    )


def document_ends(xa, place):
    pair_at = place[1] // 2
    lengths = jnp.where(
        pair_at == 0,
        xa[0:1, :8] * 16.0 + xa[2:3, :8],
        xa[1:2, :8] * 16.0
        + xa[3:4, :8],
    )
    ends, total = [], 0.0
    for d in range(8):
        total = total + lengths[:, d : d + 1]
        ends.append(total)
    return ends


def mask_bias(ends, chunk, width):
    qpos = chunk * CHUNK + lax.broadcasted_iota(jnp.int32, (CHUNK, 1), 0)
    kpos = lax.broadcasted_iota(jnp.int32, (1, width), 1)
    qat, kat = qpos.astype(F32), kpos.astype(F32)
    qseg = jnp.zeros((CHUNK, 1), F32)
    kseg = jnp.zeros((1, width), F32)
    for end in ends:
        qseg = qseg + jnp.where(qat >= end, 1.0, 0.0)
        kseg = kseg + jnp.where(kat >= end, 1.0, 0.0)
    return jnp.where((qseg == kseg) & (kpos <= qpos), 0.0, -1000000000.0)


def chunk_of(core, which):
    return (2 * core, 3 - 2 * core, 2 - 2 * core, 1 + 2 * core)[which]


def chunk_rows(core, which):
    return pl.ds(pl.multiple_of(chunk_of(core, which) * CHUNK, 16), CHUNK)


def key_counts(core):
    return ((0, 1), (1, 4)) if core == 0 else ((0, 3), (1, 2))


def prepare(place, x, lengths, wq, wk, wv, qbias, vbias, xa, xb, mine):
    xa[0:CHUNK, :] = x[0:CHUNK, :]
    xa[CHUNK : CHUNK + 16, :] = jnp.zeros((16, D), BF)
    counts = lengths[...].astype(F32)
    high = jnp.floor(counts * 0.0625)
    rows = jnp.concatenate([high, counts - high * 16.0, jnp.zeros((12, 8), F32)], axis=0)
    rows = jnp.concatenate([rows, jnp.zeros((16, 120), F32)], axis=1)
    xa[CHUNK : CHUNK + 16, 0:128] = rows.astype(BF)
    xb[...] = x[CHUNK:OWN, :]
    prepare_weights(place[0], (wq, wk, wv), qbias, vbias, mine)


def prepare_more(
    place, so, wq, wk, wv, wo, qbias, vbias, out_grad, enc,
    mine, ga, gb, enc_out,
):
    ga[...] = out_grad[0:CHUNK, :]
    gb[...] = out_grad[CHUNK:OWN, :]
    enc_out[...] = enc[...]
    prepare_weights(place[0], (wq, wk, wv, wo, so), qbias, vbias, mine)


def prepare_weights(core, weights, qbias, vbias, mine):
    half = pl.ds(pl.multiple_of(core * PIECE, PIECE), PIECE)
    for w, one in enumerate(weights):
        mine[w * PIECE : (w + 1) * PIECE, :] = one[half, :]
    rows = []
    for one in (qbias[...], vbias[...]):
        for _ in range(3):
            top = one.astype(BF).astype(F32)
            rows.append(top)
            one = one - top
    rows = jnp.concatenate(rows + [jnp.zeros((10, GROUP), F32)], axis=0)
    at = len(weights) * PIECE
    mine[at : at + 16, :] = jnp.concatenate(
        [rows, jnp.zeros((16, D - GROUP), F32)], axis=1
    ).astype(BF)


def join(place, *refs):
    at = 0
    for one in refs[:-1]:
        put_rows(refs[-1], at, one[...])
        at += one.shape[0]


def move(place, source, target):
    target[...] = source[...]


def gate(*refs):
    pass


def row_copies(core, xs, full, sems):
    return [
        pltpu.make_async_copy(
            x.at[pl.ds(0, CHUNK)], full.at[chunk_rows(core, which)], sems.at[which]
        )
        for which, x in enumerate(xs)
    ]


def self_forward(half):
    def kernel(
        place, xa, xb, ya, yb, w0, w1, w2, na, fa, nb, fb, qbias, vbias,
        q_out, k_out, v_out, att, stats,
        wq, wk, wv, full, bias, lines, sems, line_sems, row_sems,
    ):
        core = place[0]
        near, far = (na, na, nb), (fa, fa, fb)
        sets = [
            half_weight_copies(w, w, core, (w0, w1, w2), near, far, half, dst, sems)
            for w, dst in enumerate((wq, wk, wv))
        ]
        groups = [na] if half == 0 else [na, nb]
        held = bias_copies(groups, lines, line_sems)
        rows = row_copies(core, (xa, xb, ya, yb), full, row_sems)
        tail = pltpu.make_async_copy(xa.at[pl.ds(CHUNK, 16)], lines.at[3], line_sems.at[3])
        tail.start()
        start(rows)
        start(held)
        for one in sets:
            start(one)
        tail.wait()
        ends = document_ends(lines[3].astype(F32), place)
        for slot in (0, 1):
            bias[slot] = mask_bias(ends, chunk_of(core, slot), ROW)
        finish(rows)
        finish(held)
        for one in sets:
            finish(one)

        def line(own, which):
            return gathered_bias([own[...]] if half == 0 else [], lines, len(groups), which)

        k_out.held[...] = nt(full[...], wk[...]).astype(BF)
        k_out.send()
        query_line = line(qbias, 0)
        for which in (0, 1):
            q_out.held[which * CHUNK : (which + 1) * CHUNK, :] = (
                (nt(full[chunk_rows(core, which), :], wq[...]) + query_line) * 0.125
            ).astype(BF)
        q_out.send()
        v_out.held[...] = (nt(full[...], wv[...]) + line(vbias, 1)).astype(BF)
        v_out.send()
        q, k, v = q_out.held, k_out.held, v_out.held
        stats[...] = jnp.zeros_like(stats)

        def attend(value):
            def pair(p, carry):
                lanes = pair_lanes(p)
                for slot, count in key_counts(value):
                    rows = pl.ds(slot * CHUNK, CHUNK)
                    width = count * CHUNK
                    out, now = forward_heads(
                        q[rows, lanes], k[0:width, lanes], v[0:width, lanes],
                        bias[slot, :, 0:width], stats[rows, :], p,
                    )
                    att[rows, lanes] = out
                    stats[rows, :] = now
                return carry

            lax.fori_loop(0, 3, pair, 0)

        by_core(core, attend)

    return kernel


def att_copies(att_a, att_b, full, sems):
    half = D // 2
    return [
        pltpu.make_async_copy(one, full.at[:, pl.ds(n * half, half)], sems.at[n])
        for n, one in enumerate((att_a, att_b))
    ]


def cross_forward(
    place, xa, xb, att_a, att_b, params, ea, eb, w0, w1, w2, w3, w4, n1, n2, n3,
    f1, f2, f3, qbias, vbias,
    hat1, scale1, q_out, k_out, v_out, att, stats, hat_out,
    wq, wk, wv, wo, full, lines, sems, line_sems, row_sems, self_wo, self_sems, self_att, att_sems,
):
    core = place[0]
    self_bias, gain1, shift1, obias = (Row(params, n) for n in range(4))
    near, far = (n1, n2, n3), (f1, f2, f3)
    rows = [
        pltpu.make_async_copy(e, full.at[pl.ds(i * HALF_ENC, HALF_ENC)], row_sems.at[i])
        for i, e in enumerate((ea, eb))
    ]
    held = bias_copies(near, lines, line_sems)
    sets = [
        weight_copies(w, w, core, (w0, w1, w2, w3), near, far, dst, sems)
        for w, dst in enumerate((wq, wk, wv, wo))
    ]
    self_set = weight_copies(
        4, 0, core, (None, None, None, None, w4), near, far, self_wo, self_sems
    )
    halves = att_copies(att_a, att_b, self_att, att_sems)
    start(halves)
    start(self_set)
    start(held)
    start(sets[0])
    start(rows)
    for one in sets[1:]:
        start(one)
    finish(halves)
    finish(self_set)
    product = nn(self_att[...], self_wo[...]) + self_bias[...]
    for which, x in enumerate((xa, xb)):
        part = slice(which * CHUNK, (which + 1) * CHUNK)
        hat, scale = normalize(x[0:CHUNK, :].astype(F32) + product[part])
        hat1.held[part, :] = hat
        scale1[part, :] = jnp.broadcast_to(scale, (CHUNK, 128))
    hat1.send()
    hidden = (hat1.held[...] * gain1[...] + shift1[...]).astype(BF)
    finish(held)
    finish(sets[0])
    line = gathered_bias([qbias[...]], lines, 3, 0)
    q_out.held[...] = ((nt(hidden, wq[...]) + line) * 0.125).astype(BF)
    q_out.send()
    finish(rows)
    finish(sets[1])
    k_out.held[...] = nt(full[...], wk[...]).astype(BF)
    k_out.send()
    finish(sets[2])
    line = gathered_bias([vbias[...]], lines, 3, 1)
    v_out.held[...] = (nt(full[...], wv[...]) + line).astype(BF)
    v_out.send()
    finish(sets[3])
    q, k, v = q_out.held, k_out.held, v_out.held
    stats[...] = jnp.zeros_like(stats)

    def pair(p, carry):
        lanes = pair_lanes(p)
        for slot in (0, 1):
            rows = pl.ds(slot * CHUNK, CHUNK)
            out, now = forward_heads(
                q[rows, lanes], k[:, lanes], v[:, lanes], None, stats[rows, :], p
            )
            att[rows, lanes] = out
            stats[rows, :] = now
        return carry

    lax.fori_loop(0, 6, pair, 0, unroll=2)
    hidden = hat1.held[...] * gain1[...] + shift1[...]
    hat, scale = normalize(hidden + (nn(att[...], wo[...]) + obias[...]))
    hat_out[...] = hat
    stats[...] = jnp.where(lane_ids(stats.shape) == 12, scale, stats[...])


FF_STEP = 512
FF_BLOCK = 768


def gelu_parts(u):
    size = jnp.abs(u)
    t = 1.0 / (1.0 + (0.3275911 * 0.7071067811865476) * size)
    poly = t * (
        0.254829592
        + t * (-0.284496736 + t * (1.421413741 + t * (-1.453152027 + t * 1.061405429)))
    )
    bell = jnp.exp(-0.5 * u * u)
    tail = 0.5 * poly * bell
    phi = jnp.where(u >= 0.0, 1.0 - tail, tail)
    return u * phi, phi + u * bell * 0.3989422804014327


def feed_forward(
    place, hat2, stats, params, up_hbm, up_bias, down_hbm, ga_here, ga, gb,
    out_a, out_b, dsecond, left, right, snd, vec, upb,
    up, down, active, slope, hid, total, third, grads, held, sems, out_sems,
):
    core, group = place[0], place[1]
    gain2, shift2, down_bias, gain3, shift3 = (Row(params, 4 + n) for n in range(5))
    steps = FF // FF_STEP
    ups = [
        pltpu.make_async_copy(
            up_hbm.at[:, pl.ds(i * FF_STEP, FF_STEP)],
            up.at[:, pl.ds(i * FF_STEP, FF_STEP)],
            sems.at[0, i],
        )
        for i in range(steps)
    ]
    downs = [
        pltpu.make_async_copy(
            down_hbm.at[pl.ds(i * FF_STEP, FF_STEP)],
            down.at[pl.ds(i * FF_STEP, FF_STEP)],
            sems.at[1, i],
        )
        for i in range(steps)
    ]
    for i in range(steps):
        ups[i].start()
        downs[i].start()
    second = hat2[...] * gain2[...] + shift2[...]
    hid[...] = second.astype(BF)
    total[...] = second + down_bias[...]
    for i in range(steps):
        cols = pl.ds(i * FF_STEP, FF_STEP)
        ups[i].wait()
        u = nn(hid[...], up[:, cols]) + up_bias[:, cols]
        act, slo = gelu_parts(u)
        active[:, cols] = act.astype(BF)
        slope[:, cols] = slo
        downs[i].wait()
        total[...] += nn(active[:, cols], down[cols, :])
    hat3, scale3 = normalize(total[...])
    out = (hat3 * gain3[...] + shift3[...]).astype(BF)
    out_a[...] = out[0:CHUNK]
    out_b[...] = out[CHUNK:OWN]
    first = jnp.where(core == group % 2, ga_here.get()[...], ga.get()[...])
    grad = jnp.concatenate([first, gb.get()[...]], axis=0).astype(F32)
    vec[0:1, :] = column(grad * hat3)
    vec[1:2, :] = column(grad)
    dthird = norm_back(grad, hat3, scale3, gain3[...])
    total[...] = dthird
    third[...] = dthird.astype(BF)
    vec[2:3, :] = column(third[...])
    for i in range(FF // FF_BLOCK):
        cols = pl.ds(i * FF_BLOCK, FF_BLOCK)
        du = (nt(third[...], down[cols, :]) * slope[:, cols]).astype(BF)
        grads[:, cols] = du
        upb[:, cols] = column(du)
        total[...] += nt(du, up[:, cols])
    grad = total[...]
    hat = hat2[...]
    scale = pick_lane(stats, slice(None), 12)
    vec[3:4, :] = column(grad * hat)
    vec[4:5, :] = column(grad)
    dsec = norm_back(grad, hat, scale, gain2[...])
    dsecond.held[...] = dsec
    dsecond.send()
    vec[5:6, :] = column(dsec.astype(BF))
    vec[6:8, :] = jnp.zeros((2, D), F32)

    def hand_over(value):
        pairs = ((grads, hid), (active, third))
        mine, other = pairs[value], pairs[1 - value]
        copies = [
            pltpu.make_async_copy(mine[0], left, out_sems.at[4]),
            pltpu.make_async_copy(mine[1], right, out_sems.at[5]),
        ]
        start(copies)
        for i in range(4):
            cols = pl.ds(pl.multiple_of((group ^ i) * D, D), D)
            rows = pl.ds(i * D, D)
            held[rows, :] = tn(other[0][:, cols], other[1][...]).astype(BF)
            copies.append(pltpu.make_async_copy(held.at[rows], snd.at[rows], out_sems.at[i]))
            copies[-1].start()
        finish(copies)

    by_core(core, hand_over)


def ff_weight_grads(place, left, right, out, held, left_held, right_held, sems):
    copies = [pltpu.make_async_copy(right, right_held, sems.at[0])]
    for i in range(4):
        cols = pl.ds(pl.multiple_of((place[1] ^ i) * D, D), D)
        copies.append(pltpu.make_async_copy(left.at[:, cols], left_held.at[i], sems.at[1 + i]))
    start(copies[:2])
    finish(copies[:2])
    start(copies[2:])
    outs = []
    for i in range(4):
        if i:
            copies[1 + i].wait()
        rows = pl.ds(i * D, D)
        held[rows, :] = tn(left_held[i], right_held[...]).astype(BF)
        outs.append(pltpu.make_async_copy(held.at[rows], out.at[rows], sems.at[5 + i]))
        outs[i].start()
    finish(outs)


def out_grads(core, att, low, wo, grad, places, pieces):
    store_pieces(core, tn(att[...], low[...]).astype(BF), places, pieces)
    store_bias(jnp.zeros((1, D), F32), places, pieces)
    grad[...] = nt(low[...], wo[...]).astype(BF)


def weight_grads(core, dq, dk, dv, queries, keys, places, pieces):
    store_pieces(core, tn(dq[...], queries).astype(BF), places[0], pieces)
    store_pieces(core, tn(dk[...], keys).astype(BF), places[1], pieces)
    store_pieces(core, tn(dv[...], keys).astype(BF), places[2], pieces)
    store_bias(column(dq[...]), places[0], pieces)
    store_bias(jnp.zeros((1, dk.shape[1]), F32), places[1], pieces)
    store_bias(column(dv[...]), places[2], pieces)


def cross_part(core, first, grad, att, q, k, v, stats, queries, full, places, pieces, dq, dk, dv):

    def pair(p, carry):
        lanes = pair_lanes(first + p)
        out = pair_lanes(p)
        gq, gk, gv = backward_heads(
            q[:, lanes], grad[:, lanes], att[:, lanes], k[:, lanes], v[:, lanes],
            None, stats[...], first + p,
        )
        dq[:, out] = (gq * 0.125).astype(BF)
        dk[:, out] = gk.astype(BF)
        dv[:, out] = gv.astype(BF)
        return carry

    lax.fori_loop(0, 3, pair, 0)
    half = pl.ds(0, D // 2)
    weight_grads(
        core, dq.at[:, half], dk.at[:, half], dv.at[:, half], queries(), full[...], places, pieces
    )


def cross_backward_a(
    place, dsecond, att, q, k, v, stats, hat1, params, ea, eb, w3, n1, n2, n3, f1, f2, f3,
    dq, dk, dv, grad, pieces,
    wo, low, full, sems, row_sems,
):
    core = place[0]
    gain1, shift1 = Row(params, 1), Row(params, 2)
    copies = weight_copies(
        3, 0, core, (None, None, None, w3), (n1, n2, n3), (f1, f2, f3), wo, sems
    )
    rows = [
        pltpu.make_async_copy(e, full.at[pl.ds(i * HALF_ENC, HALF_ENC)], row_sems.at[i])
        for i, e in enumerate((ea, eb))
    ]
    start(copies)
    low[...] = dsecond.get()[...].astype(BF)
    size = pieces.rows // 10
    places = [[(4 * g + w) * size for g in (0, 1)] for w in range(3)]
    places_o = [8 * size, 9 * size, 3 * size, 7 * size]
    att = att.get()
    finish(copies)
    out_grads(core, att, low, wo, grad.held, places_o, pieces)
    grad.send()
    q, k, v, stats = q.get(), k.get(), v.get(), stats.get()
    start(rows)
    hat1.begin()

    def queries():
        for one in (dq, dk, dv):
            one.send()
        finish(rows)
        return (hat1.get()[...] * gain1[...] + shift1[...]).astype(BF)

    cross_part(
        core, 3, grad.held, att, q, k, v, stats, queries, full, places, pieces,
        dq.held, dk.held, dv.held,
    )
    pieces.send(0, 10 * size)


def cross_backward_b(
    place, dq_a, dsecond, grad, att, q, k, v, stats, hat1, scale1, params, ea, eb,
    vec_a, upb, w0, n1, n2, n3, f1, f2, f3,
    dk, dv, dfirst, pieces, vec,
    wq, dq, full, sems, row_sems,
):
    core = place[0]
    gain1, shift1 = Row(params, 1), Row(params, 2)
    copies = weight_copies(0, 0, core, (w0,), (n1, n2, n3), (f1, f2, f3), wq, sems)
    rows = [
        pltpu.make_async_copy(e, full.at[pl.ds(i * HALF_ENC, HALF_ENC)], row_sems.at[i])
        for i, e in enumerate((ea, eb))
    ]
    part = pltpu.make_async_copy(dq_a, dq.at[:, pl.ds(D // 2, D // 2)], row_sems.at[2])
    grad, att, stats = grad.get(), att.get(), stats.get()
    q, k, v = q.get(), k.get(), v.get()
    start(rows)
    hat1.begin()
    start(copies)
    part.start()
    dsecond.begin()
    scale1.begin()
    size = pieces.rows // 6
    places = [[(3 * g + w) * size for g in (0, 1)] for w in range(3)]

    def queries():
        dk.send()
        dv.send()
        finish(rows)
        return (hat1.get()[...] * gain1[...] + shift1[...]).astype(BF)

    cross_part(
        core, 0, grad, att, q, k, v, stats, queries, full, places, pieces, dq, dk.held, dv.held
    )
    pieces.send(0, 6 * size)
    part.wait()
    finish(copies)
    total = dsecond.get()[...] + nn(dq[...], wq[...])
    hat = hat1.get()[...]
    vec[0:6, :] = vec_a[0:6, :]
    vec[6:7, :] = column(total * hat)
    vec[7:8, :] = column(total)
    dfi = norm_back(total, hat, scale1.get()[:, 0:1], gain1[...])
    dfirst.held[...] = dfi
    dfirst.send()
    vec[8:9, :] = column(dfi.astype(BF))
    for n in range(4):
        vec[9 + n : 10 + n, :] = upb[:, n * D : (n + 1) * D]
    vec[13:16, :] = jnp.zeros((3, D), F32)


def self_part(
    core, first, ends, grad, att, q, k, v, stats, full, places, pieces, dq, dk, dv, bias, rows
):
    for slot in (0, 1):
        bias[slot] = mask_bias(ends, chunk_of(core, slot), ROW)

    def attend(value):
        def pair(p, carry):
            lanes = pair_lanes(first + p)
            out = pair_lanes(p)
            (low_slot, low), (high_slot, high) = sorted(key_counts(value), key=lambda x: x[1])
            parts = {}
            for slot, count in ((low_slot, low), (high_slot, high)):
                rows = pl.ds(slot * CHUNK, CHUNK)
                width = count * CHUNK
                gq, gk, gv = backward_heads(
                    q[rows, out], grad[rows, lanes], att[rows, out],
                    k[0:width, out], v[0:width, out],
                    bias[slot, :, 0:width], stats[rows, :], p,
                )
                dq[rows, out] = (gq * 0.125).astype(BF)
                parts[slot] = (gk, gv)
            for n, dst in ((0, dk), (1, dv)):
                wide, narrow = parts[high_slot][n], parts[low_slot][n]
                shared, reach = low * CHUNK, high * CHUNK
                dst[0:shared, out] = (wide[0:shared] + narrow).astype(BF)
                dst[shared:reach, out] = wide[shared:reach].astype(BF)
                if reach < ROW:
                    dst[reach:ROW, out] = jnp.zeros((ROW - reach, PAIR), BF)
            return carry

        lax.fori_loop(0, 3, pair, 0)

    by_core(core, attend)
    finish(rows)
    half = pl.ds(0, D // 2)
    queries = jnp.concatenate([full[chunk_rows(core, n), :] for n in (0, 1)], axis=0)
    weight_grads(
        core, dq.at[:, half], dk.at[:, half], dv.at[:, half], queries, full[...], places, pieces
    )


def self_backward_a(
    place, dfirst, q, k, v, stats, att_a, att_b, xa, xb, ya, yb, w3, m1, m2, m3, g1, g2, g3,
    dq, dk, dv, grad, pieces,
    wo, low, bias, full, lines, sems, row_sems, att, att_sems,
):
    core = place[0]
    copies = weight_copies(
        4, 0, core, (None, None, None, None, w3), (m1, m2, m3), (g1, g2, g3), wo, sems
    )
    tail = pltpu.make_async_copy(xa.at[pl.ds(CHUNK, 16)], lines, row_sems.at[4])
    rows = row_copies(core, (xa, xb, ya, yb), full, row_sems)
    halves = att_copies(att_a, att_b, att, att_sems)
    start(copies)
    start(halves)
    tail.start()
    low[...] = dfirst.get()[...].astype(BF)
    size = pieces.rows // 10
    places = [[(4 * g + w) * size for g in (0, 1)] for w in range(3)]
    places_o = [8 * size, 9 * size, 3 * size, 7 * size]
    finish(halves)
    finish(copies)
    out_grads(core, att, low, wo, grad.held, places_o, pieces)
    grad.send()
    tail.wait()
    q, k, v, stats = q.get(), k.get(), v.get(), stats.get()
    start(rows)
    self_part(
        core, 3, document_ends(lines[...].astype(F32), place), grad.held,
        att.at[:, pl.ds(D // 2, D // 2)], q, k, v, stats, full,
        places, pieces, dq.held, dk.held, dv.held, bias, rows,
    )
    pieces.send(0, 10 * size)
    for one in (dq, dk, dv):
        one.send()


def self_backward_b(
    place, grad, att, q, k, v, stats, xa, xb, ya, yb,
    dq, dk, dv, pieces,
    bias, full, lines, row_sems,
):
    core = place[0]
    size = pieces.rows // 6
    places = [[(3 * g + w) * size for g in (0, 1)] for w in range(3)]
    tail = pltpu.make_async_copy(xa.at[pl.ds(CHUNK, 16)], lines, row_sems.at[4])
    rows = row_copies(core, (xa, xb, ya, yb), full, row_sems)
    tail.start()
    tail.wait()
    grad, att, stats = grad.get(), att.get(), stats.get()
    q, k, v = q.get(), k.get(), v.get()
    start(rows)
    self_part(
        core, 0, document_ends(lines[...].astype(F32), place), grad, att, q, k, v, stats, full,
        places, pieces, dq.held, dk.held, dv.held, bias, rows,
    )
    pieces.send(0, 6 * size)
    for one in (dq, dk, dv):
        one.send()


def late_grads(
    place, dq_a, dq_b, dk_a, dk_b, dv_a, dv_b, ck_a, ck_b, cv_a, cv_b, dfirst,
    w0, w1, w2, n1, n2, n3, f1, f2, f3, v1, v2, m1, m2, m3, g1, g2, g3,
    pieces,
    wq, wk, wv, xk, xv, dq, dk, dv, ck, cv, total, sems, part_sems,
):
    core = place[0]
    near, far = (n1, n2, n3), (f1, f2, f3)
    cross = (None, v1, v2)
    half = D // 2
    parts = [
        pltpu.make_async_copy(one, dst.at[:, pl.ds(at, half)], part_sems.at[n])
        for n, (one, dst, at) in enumerate(
            (
                (ck_b, ck, 0), (ck_a, ck, half), (cv_b, cv, 0), (cv_a, cv, half),
                (dk_b, dk, 0), (dk_a, dk, half), (dv_b, dv, 0), (dv_a, dv, half),
                (dq_b, dq, 0), (dq_a, dq, half),
            )
        )
    ]
    sets = [
        weight_copies(1, 0, core, cross, (m1, m2, m3), (g1, g2, g3), xk, sems),
        weight_copies(2, 1, core, cross, (m1, m2, m3), (g1, g2, g3), xv, sems),
    ] + [
        weight_copies(w, 2 + w, core, (w0, w1, w2), near, far, dst, sems)
        for w, dst in enumerate((wq, wk, wv))
    ]
    for one in sets[:2]:
        start(one)
    start(parts)
    for one in sets[2:]:
        start(one)
    finish(parts)
    for one in sets[:2]:
        finish(one)
    enc = nn(ck[...], xk[...]) + nn(cv[...], xv[...])
    pieces.put_own(0, enc[0:HALF_ENC].astype(BF))
    pieces.put_snd(0, enc[HALF_ENC:ENC].astype(BF))
    pieces.send(0, HALF_ENC)
    for one in sets[2:]:
        finish(one)
    total[...] = nn(dk[...], wk[...]) + nn(dv[...], wv[...])
    mine = nn(dq[...], wq[...]) + dfirst.get()[...]
    for n in (0, 1):
        at = HALF_ENC + n * CHUNK
        pieces.put_snd(at, total[chunk_rows(core, 2 + n), :].astype(BF))
        pieces.put_own(
            at, (mine[n * CHUNK : (n + 1) * CHUNK] + total[chunk_rows(core, n), :]).astype(BF)
        )
    pieces.send(HALF_ENC, 2 * CHUNK)


def add_jobs(jobs, ins, store, held, sems):
    copies, at, most = [], 0, job_most(jobs)
    for _, rows, sources in jobs:
        mine = []
        for operand, row in sources:
            mine.append(
                (
                    pltpu.make_async_copy(
                        ins[operand].at[pl.ds(row, rows)], held.at[pl.ds(at, rows)],
                        sems.at[len(copies) * most + len(mine)],
                    ),
                    at,
                )
            )
            at += rows
        copies.append(mine)
    for mine in copies:
        for copy, _ in mine:
            copy.start()
    for (place, rows, _), mine in zip(jobs, copies):
        total = 0.0
        for copy, row in mine:
            copy.wait()
            total = total + held[row : row + rows, :].astype(F32)
        store(place, total)


def job_most(jobs):
    return max(len(sources) for _, _, sources in jobs)


def job_rows(jobs):
    return sum(rows * len(sources) for _, rows, sources in jobs)


def add_call(name, place, arrays, outs, jobs, pins=()):
    count = len(arrays)

    def kernel(place, *refs):
        ins, targets = refs[:count], refs[count : count + len(outs)]
        held, out_held, sems, out_sems = refs[count + len(outs) :]
        copies = []

        def store(where, total):
            at = sum(outs[: where[0]]) + where[1]
            put_rows(out_held, at, total.astype(BF))
            rows = pl.ds(at, total.shape[0])
            copies.append(
                pltpu.make_async_copy(
                    out_held.at[rows],
                    targets[where[0]].at[pl.ds(where[1], total.shape[0])],
                    out_sems.at[len(copies)],
                )
            )
            copies[-1].start()

        add_jobs(jobs, ins, store, held, sems)
        finish(copies)

    dma = pltpu.SemaphoreType.DMA
    return call(
        kernel, [(place, "s")] + [(one, "a") for one in arrays],
        [((rows, D), BF, "a") for rows in outs],
        [
            pltpu.VMEM((job_rows(jobs), D), BF), pltpu.VMEM((sum(outs), D), BF),
            dma((job_most(jobs) * len(jobs),)), dma((len(jobs),)),
        ],
        name, pins=pins,
    )


def total_call(name, place, arrays, total_rows, jobs, groups, depth, pins=(), mine_type=F32):
    count = len(arrays)
    size = total_rows // groups // depth

    def kernel(place, *refs):
        mine, parts = refs[count], refs[count + 1 : count + depth]
        held, total, sems = refs[count + depth :]

        def store(row, value):
            put_rows(total, row, value)

        add_jobs(jobs, refs[:count], store, held, sems)
        for d in range(depth):
            for g in range(groups):
                at = pl.multiple_of(
                    g * (total_rows // groups) + (place[2] ^ d) * size, 8
                )
                block = total[pl.ds(at, size), :]
                if d == 0:
                    put_rows(mine, g * size, block.astype(mine_type))
                else:
                    put_rows(parts[d - 1], g * size, block.astype(BF))

    return call(
        kernel, [(place, "s")] + [(one, "a") for one in arrays],
        [((groups * size, D), mine_type, "v")] + [((groups * size, D), BF, "v")] * (depth - 1),
        [
            pltpu.VMEM((job_rows(jobs), D), BF), pltpu.VMEM((total_rows, D), F32),
            pltpu.SemaphoreType.DMA((job_most(jobs) * len(jobs),)),
        ],
        name, pins=pins,
    )


def spread(depth, count):
    def kernel(place, *refs):
        own, other, refs = refs[:count], refs[count : 2 * count], refs[2 * count :]
        outs, biases, total = refs[:4], refs[4:-1], refs[-1]
        core, k = place[0], place[2]
        size = total.shape[1] // depth
        for which, parts in enumerate((own, other)):
            for d in range(depth):
                at = pl.multiple_of((k ^ d) * size, 8)
                ref, row = (parts[d], 0) if count == depth else (parts[0], d * size)
                total[which, pl.ds(at, size), :] = ref[row : row + size, :].astype(F32)
        rows = total.shape[1] // 4
        for n, out in enumerate(outs):
            for which, half in ((0, core), (1, 1 - core)):
                to = pl.ds(pl.multiple_of(half * PIECE, PIECE), PIECE)
                out[to, :] = total[which, n * rows : n * rows + PIECE, :]
        for n, bias in zip((0, 2), biases):
            at = n * rows + PIECE
            bias[...] = total[0, at : at + 1, :GROUP]

    return kernel


def solution(mesh):
    names = tuple(mesh.axis_names)
    heads, rows = mesh.shape["heads"], mesh.shape["rows"]
    depth = rows // 2
    piece = FF // (heads * rows)
    weight_rows = PIECE + BIAS_ROWS
    while (4 * weight_rows) % (8 * depth):
        weight_rows += BIAS_ROWS
    def send(value, where, label="moved"):
        pairs = []
        for r in range(rows):
            for h in range(heads):
                to_r, to_h = where(r, h)
                if (to_r, to_h) == (r, h):
                    continue
                index = {"rows": (r, to_r), "heads": (h, to_h)}
                a = b = 0
                for name in names:
                    a = a * mesh.shape[name] + index[name][0]
                    b = b * mesh.shape[name] + index[name][1]
                pairs.append((a, b))
        with jax.named_scope(label):
            return lax.ppermute(value, names, pairs)

    def swap(r, h):
        return (r & ~1) | (h & 1), (h & ~1) | (r & 1)

    def swap_b(r, h):
        return (r & ~1) | (1 - (h & 1)), (h & ~1) | (r & 1)

    def swap_b_back(r, h):
        return (r & ~1) | (h & 1), (h & ~1) | (1 - (r & 1))

    def core_to(r, h):
        return r ^ 1, h

    def head_to(d):
        return lambda r, h: (r, h ^ d)

    def depth_to(d):
        return lambda r, h: (r ^ (2 * d), h)

    def shards(
        layer_input, encoder_out, doc_lengths,
        self_query, self_qbias, self_key_weight, self_value, self_vbias, self_out, self_obias,
        first_gain, first_shift,
        cross_query, cross_qbias, cross_key, cross_value, cross_vbias, cross_out, cross_obias,
        second_gain, second_shift, up_weight, up_bias, down_weight, down_bias,
        third_gain, third_shift, out_grad,
    ):
        h = lax.axis_index("heads")
        r = lax.axis_index("rows")
        core, k = r % 2, r // 2
        place = jnp.stack([core, h, k]).astype(jnp.int32)
        stays = core == h % 2

        def line(vector):
            return vector.reshape(1, -1)

        params = jnp.stack(
            [
                self_obias, first_gain, first_shift, cross_obias, second_gain, second_shift,
                down_bias, third_gain, third_shift,
            ]
        )

        def v(*arrays):
            return [(one, "v") for one in arrays]

        def a(*arrays):
            return [(one, "a") for one in arrays]

        def l(*arrays):
            return [(one, "l") for one in arrays]

        def d(*arrays):
            return [(one, "d") for one in arrays]

        here = [(place, "s")]

        self_own = [self_query.T, self_key_weight.T, self_value.T]
        cross_own = [cross_query.T, cross_key.T, cross_value.T, cross_out, self_out]
        chunk = ((CHUNK, D), BF, "v")
        xa, xb, mine, zero = call(
            prepare,
            here + v(layer_input, doc_lengths, *self_own, line(self_qbias), line(self_vbias)),
            [((CHUNK + 16, D), BF, "v"), chunk, ((3 * PIECE + 16, D), BF, "v")], [], "prepare",
        )

        def gather_groups(mine, label):
            x, y = send(mine, head_to(1), label), send(mine, head_to(2), label)
            return [x, y, send(x, head_to(2), label + "_2")]

        self_near = gather_groups(mine, "w_self_near")
        xb = send(xb, swap_b, "x_b")
        xa = jnp.where(stays, xa, send(xa, swap, "x_a"))
        mine, ga, gb, enc, _ = call(
            prepare_more,
            here + v(self_out, *cross_own[:4], line(cross_qbias), line(cross_vbias))
            + v(out_grad, encoder_out),
            [((5 * PIECE + 16, D), BF, "v"), chunk, chunk, ((HALF_ENC, D), BF, "v")],
            [], "prepare_more", pins=[zero],
        )
        ya = send(xa, core_to, "y_a")
        yb = send(xb, core_to, "y_b")
        self_far = [send(one, core_to, "w_self_far") for one in self_near]
        self_w = self_near + self_far

        def gated(values, pins, name):
            count = len(values)
            anywhere = pl.BlockSpec(memory_space=pl.ANY)
            return pl.pallas_call(
                gate,
                in_specs=[anywhere] * (count + len(pins)),
                out_specs=[anywhere] * count,
                out_shape=[jax.ShapeDtypeStruct(one.shape, one.dtype) for one in values],
                input_output_aliases={n: n for n in range(count)},
                name=name,
            )(*values, *pins)

        mine, enc = gated([mine, enc], [self_near[0], self_near[1], xa, xb, params], "gate_cross")
        cross_x, cross_y = (send(mine, head_to(d), "w_cross_near") for d in (1, 2))
        ea = send(enc, swap_b, "e_a")

        dma = pltpu.SemaphoreType.DMA
        weight = pltpu.VMEM((D, D), BF)
        half_weight = pltpu.VMEM((D // 2, D), BF)
        masks = pltpu.VMEM((2, CHUNK, ROW), F32)
        lines_bf = pltpu.VMEM((4, 16, D), BF)
        row_full = pltpu.VMEM((ROW, D), BF)
        enc_full = pltpu.VMEM((ENC, D), BF)
        tokens = (OWN, D)

        def self_half(half, weights, pins):
            narrow = ((ROW, D // 2), BF, "e")
            return call(
                self_forward(half),
                here + a(xa, xb, ya, yb, *self_own, *weights)
                + v(line(self_qbias), line(self_vbias)),
                [
                    ((OWN, D // 2), BF, "e"), narrow, narrow, ((OWN, D // 2), BF, "v"),
                    ((OWN, 128), F32, "v"),
                ],
                [half_weight] * 3
                + [row_full, masks, lines_bf, dma((3, 7)), dma((4,)), dma((4,))],
                "self_forward_" + "ab"[half], pins=pins,
            )

        sq, sk, sv, att_a, stats_a, zero = self_half(
            0, [self_near[0], self_far[0]] * 2, [mine, enc]
        )
        (cross_x,) = gated([cross_x], [zero], "gate_forward")
        cross_near = [cross_x, cross_y, send(cross_x, head_to(2), "w_cross_near_2")]
        tq, tk, tv, att_b, stats_b, zero = self_half(
            1, [self_near[1], self_far[1], self_near[2], self_far[2]], [zero, cross_near[0]]
        )
        *cross_near, ea, ga_here, gb = gated(cross_near + [ea, ga, gb], [zero], "gate_far")
        cross_far = [send(one, core_to, "w_cross_far") for one in cross_near]
        eb = send(ea, core_to, "e_b")
        ga = send(ga_here, swap, "g_a")
        gb = send(gb, swap_b, "g_b")
        cross_w = cross_near + cross_far
        hat1, scale1, cq, ck, cv, catt, stats2, hat2, zero = call(
            cross_forward,
            here + v(xa, xb) + a(att_a, att_b) + v(params) + a(ea, eb)
            + a(*cross_own, *cross_w) + v(line(cross_qbias), line(cross_vbias)),
            [
                (tokens, F32, "e"), ((OWN, 128), F32, "v"),
                (tokens, BF, "e"), ((ENC, D), BF, "e"), ((ENC, D), BF, "e"), (tokens, BF, "v"),
                ((OWN, 128), F32, "v"), (tokens, F32, "v"),
            ],
            [weight] * 4 + [
                enc_full, lines_bf, dma((4, 7)), dma((4,)), dma((2,)), weight, dma((1, 7)),
                pltpu.VMEM(tokens, BF), dma((2,)),
            ],
            "cross_forward",
        )
        out_a, out_b, dsecond, left, right, ff_snd, vec_a, upb, zero = call(
            feed_forward,
            here + v(hat2, stats2, params) + a(up_weight) + v(line(up_bias)) + a(down_weight)
            + l(ga_here, ga, gb),
            [
                chunk, chunk, (tokens, F32, "e"), ((OWN, FF), BF, "a"), (tokens, BF, "a"),
                ((FF, D), BF, "a"), ((8, D), F32, "v"), ((1, FF), F32, "v"),
            ],
            [
                pltpu.VMEM((D, FF), BF), pltpu.VMEM((FF, D), BF), pltpu.VMEM((OWN, FF), BF),
                pltpu.VMEM((OWN, FF), F32), pltpu.VMEM(tokens, BF), pltpu.VMEM(tokens, F32),
                pltpu.VMEM(tokens, BF), pltpu.VMEM((OWN, FF), BF), pltpu.VMEM((FF, D), BF),
                dma((2, FF // FF_STEP)), dma((6,)),
            ],
            "feed_forward",
        )
        ff_got = send(ff_snd, core_to, "ff_core")
        out_got = send(out_a, swap, "out_a")
        out_b = send(out_b, swap_b_back, "out_b")
        ff_own, _ = call(
            ff_weight_grads, here + a(left, right), [((FF, D), BF, "a")],
            [
                pltpu.VMEM((FF, D), BF), pltpu.VMEM((4, OWN, D), BF), pltpu.VMEM(tokens, BF),
                dma((9,)),
            ],
            "ff_weight_grads",
        )
        output = jnp.concatenate([jnp.where(stays, out_a, out_got), out_b], axis=0)

        half = D // 2

        def ff_row(g, which):
            return g * D + which * half

        def both(row):
            return [(0, row), (1, row)]

        ff_x, ff_y, _ = add_call(
            "ff_add_1", place, [ff_own, ff_got], [D, D],
            [
                ((0, 0), half, both(ff_row(1, 0))), ((0, half), half, both(ff_row(3, 0))),
                ((1, 0), half, both(ff_row(2, 1))), ((1, half), half, both(ff_row(3, 1))),
            ],
            pins=[out_got, out_b],
        )
        ff_gx = send(ff_x, head_to(1), "ff_heads")
        ff_gy = send(ff_y, head_to(2), "ff_heads")

        wr = weight_rows
        rows_a = [((10 * wr, D), BF, "p")] * 2
        half_e = ((OWN, D // 2), BF, "e")
        cross_w4, self_w4 = cross_own[3], self_out
        enc_half = ((ENC, D // 2), BF, "e")
        cdq, cdk, cdv, cgrad, ca_own, ca_snd, zero = call(
            cross_backward_a,
            here + l(dsecond, catt, cq, ck, cv, stats2) + d(hat1)
            + v(params) + a(ea, eb, cross_w4, *cross_w),
            [half_e, enc_half, enc_half, (tokens, BF, "e")] + rows_a,
            [weight, pltpu.VMEM(tokens, BF), enc_full, dma((1, 7)), dma((2,))],
            "cross_backward_a", pins=[ff_x, ff_y],
        )
        (ca_snd,) = gated([ca_snd], [ff_gx, ff_gy, output], "gate_ca")
        ca_got = send(ca_snd, core_to, "ca_core")
        ff_x2, ff_y2, _ = add_call(
            "ff_add_2", place, [ff_own, ff_got, ff_gx, ff_gy], [half, half],
            [
                ((0, 0), half, both(ff_row(2, 0)) + [(2, half)]),
                ((1, 0), half, both(ff_row(1, 1)) + [(3, half)]),
            ],
            pins=[zero],
        )
        ff_gx2 = send(ff_x2, head_to(2), "ff_heads_2")
        ff_gy2 = send(ff_y2, head_to(1), "ff_heads_2")
        c_x3, _ = add_call(
            "c_add_1", place, [ca_own, ca_got], [4 * wr], [((0, 0), 4 * wr, both(4 * wr))],
            pins=[ff_x2],
        )
        c_gx3 = send(c_x3, head_to(1), "c_heads")
        cdk_b, cdv_b, dfirst, cb_own, cb_snd, vectors, zero = call(
            cross_backward_b,
            here + a(cdq) + d(dsecond) + l(cgrad, catt, cq, ck, cv, stats2)
            + d(hat1, scale1) + v(params) + a(ea, eb) + v(vec_a, upb)
            + a(cross_own[0], *cross_w),
            [
                enc_half, enc_half, (tokens, F32, "e"), ((6 * wr, D), BF, "p"),
                ((6 * wr, D), BF, "p"), ((16, D), F32, "v"),
            ],
            [weight, pltpu.VMEM(tokens, BF), enc_full, dma((1, 7)), dma((3,))],
            "cross_backward_b", pins=[ff_x2, ff_y2, c_x3],
        )
        vectors = lax.all_gather(vectors, names)
        (cb_snd,) = gated([cb_snd], [ff_gx2, ff_gy2, c_gx3], "gate_cb")
        cb_got = send(cb_snd, core_to, "cb_core")

        def depth_send(parts, label):
            return [send(one, depth_to(d + 1), label) for d, one in enumerate(parts)]

        ff_mine, *ff_parts, _ = total_call(
            "ff_add_3", place, [ff_own, ff_got, ff_gx, ff_gy, ff_gx2, ff_gy2], D,
            [
                (0, half, both(ff_row(0, 0)) + [(2, 0), (4, 0)]),
                (half, half, both(ff_row(0, 1)) + [(3, 0), (5, 0)]),
            ],
            1, depth, pins=[zero],
        )
        ff_back = depth_send(ff_parts, "ff_depth")
        c_y2, c_x1, _ = add_call(
            "c_add_2", place, [ca_own, ca_got, cb_own, cb_got, c_gx3], [4 * wr, 4 * wr],
            [
                ((0, 0), 4 * wr, both(0) + [(4, 0)]),
                ((1, 0), 3 * wr, [(2, 3 * wr), (3, 3 * wr)]), ((1, 3 * wr), wr, both(9 * wr)),
            ],
            pins=[ff_parts[0]],
        )
        c_gy2 = send(c_y2, head_to(2), "c_heads_2")
        c_gx1 = send(c_x1, head_to(1), "c_heads_2")

        row_half = ((ROW, D // 2), BF, "e")
        sdq, sdk, sdv, sgrad, sa_own, sa_snd, zero = call(
            self_backward_a,
            here + l(dfirst, tq, tk, tv, stats_b) + a(att_a, att_b, xa, xb, ya, yb)
            + a(self_w4, *cross_w),
            [half_e, row_half, row_half, (tokens, BF, "e")] + rows_a,
            [weight, pltpu.VMEM(tokens, BF), masks]
            + [row_full, pltpu.VMEM((16, D), BF), dma((1, 7)), dma((5,))]
            + [pltpu.VMEM(tokens, BF), dma((2,))],
            "self_backward_a", pins=[*ff_parts, c_y2, c_x1],
        )
        (sa_snd,) = gated([sa_snd], [*ff_back, c_gy2, c_gx1], "gate_sa")
        sa_got = send(sa_snd, core_to, "sa_core")
        c_mine, *c_parts, _ = total_call(
            "c_add_3", place, [ca_own, ca_got, cb_own, cb_got, c_gy2, c_gx1], 4 * wr,
            [
                (0, 3 * wr, [(2, 0), (3, 0), (4, 0), (5, 0)]),
                (3 * wr, wr, [(0, 8 * wr), (1, 8 * wr), (4, 3 * wr), (5, 3 * wr)]),
            ],
            1, depth, pins=[zero], mine_type=BF,
        )
        c_depth = depth_send(c_parts, "c_depth")
        s_y, _ = add_call(
            "s_add_1", place, [sa_own, sa_got], [8 * wr], [((0, 0), 8 * wr, both(0))],
            pins=[c_parts[0]],
        )
        s_gy = send(s_y, head_to(2), "s_heads")
        sdq_b, sdk_b, sdv_b, sb_own, sb_snd, zero = call(
            self_backward_b,
            here + l(sgrad, att_a, sq, sk, sv, stats_a) + a(xa, xb, ya, yb),
            [half_e, row_half, row_half, ((6 * wr, D), BF, "p"), ((6 * wr, D), BF, "p")],
            [masks, row_full, pltpu.VMEM((16, D), BF), dma((5,))],
            "self_backward_b", pins=[*c_parts, s_y],
        )
        (sb_snd,) = gated([sb_snd], [*c_depth, s_gy], "gate_sb")
        sb_got = send(sb_snd, core_to, "sb_core")

        def depth_sum(mine, got):
            for one in got:
                mine = mine + one.astype(F32)
            return mine

        part_rows = 4 * wr // depth
        s_x, c_part, _ = add_call(
            "s_add_2", place, [sa_own, sa_got, sb_own, sb_got, s_gy, c_mine, *c_depth],
            [4 * wr, part_rows],
            [
                ((0, 0), 3 * wr, [(2, 3 * wr), (3, 3 * wr), (4, 4 * wr)]),
                ((0, 3 * wr), wr, both(9 * wr) + [(4, 7 * wr)]),
                ((1, 0), part_rows, [(5 + n, 0) for n in range(depth)]),
            ],
        )
        c_back = [send(c_part, depth_to(d), "c_back") for d in range(1, depth)]
        s_gx = send(s_x, head_to(1), "s_heads_2")
        late_own, late_snd, _ = call(
            late_grads,
            here + a(sdq, sdq_b, sdk, sdk_b, sdv, sdv_b, cdk, cdk_b, cdv, cdv_b) + l(dfirst)
            + a(*self_own, *self_w, *cross_own[1:3], *cross_w),
            [((HALF_ENC + OWN, D), BF, "p")] * 2,
            [weight] * 5 + [pltpu.VMEM(tokens, BF)] + [row_full] * 2 + [enc_full] * 2
            + [pltpu.VMEM((ROW, D), F32), dma((5, 7)), dma((10,))],
            "late_grads", pins=[s_x],
        )
        s_mine, *s_parts, _ = total_call(
            "s_add_3", place, [sa_own, sa_got, sb_own, sb_got, s_gy, s_gx], 4 * wr,
            [
                (0, 3 * wr, [(2, 0), (3, 0), (4, 0), (5, 0)]),
                (3 * wr, wr, [(0, 8 * wr), (1, 8 * wr), (4, 3 * wr), (5, 3 * wr)]),
            ],
            1, depth, pins=[*c_back, late_own],
        )
        s_depth = depth_send(s_parts, "s_depth")
        (late_snd,) = gated([late_snd], s_parts, "gate_late")
        late_got = send(late_snd, core_to, "late_core")
        enc_sum, in_a, in_b, _ = add_call(
            "late_add", place, [late_own, late_got], [HALF_ENC, CHUNK, CHUNK],
            [
                ((0, 0), HALF_ENC, both(0)), ((1, 0), CHUNK, both(HALF_ENC)),
                ((2, 0), CHUNK, both(HALF_ENC + CHUNK)),
            ],
        )
        encoder_g = send(enc_sum, swap_b_back, "enc_grad")
        in_got = send(in_a, swap, "in_a")
        in_b = send(in_b, swap_b_back, "in_b")

        def whole_grads(own, other, label):
            *grads, qbias, vbias, _ = call(
                spread(depth, len(own)), here + v(*own, *other),
                [((GROUP, D), F32, "v")] * 4 + [((1, GROUP), F32, "v")] * 2,
                [pltpu.VMEM((2, 4 * wr, D), F32)], label + "_spread",
            )
            return grads, qbias[0], vbias[0]

        input_g = jnp.concatenate([jnp.where(stays, in_a, in_got), in_b], axis=0)
        c_own, _ = call(
            join, here + v(c_part, *c_back), [((4 * wr, D), BF, "v")], [], "c_join", pins=[late_got]
        )
        c_other = send(c_own, core_to, "c_far")
        (cq_g, ck_g, cv_g, co_g), cqb, cvb = whole_grads([c_own], [c_other], "c")
        s_part = depth_sum(s_mine, s_depth).astype(BF)
        s_back = [send(s_part, depth_to(d), "s_back") for d in range(1, depth)]
        (ff_mine,) = gated([ff_mine], [late_got], "gate_ff")
        ff = depth_sum(ff_mine, ff_back).reshape(2, piece, D)
        ff_here = lax.dynamic_index_in_dim(ff, core, 0, keepdims=False)
        ff_there = send(lax.dynamic_index_in_dim(ff, 1 - core, 0, keepdims=False), core_to, "ff_last")
        upweight_g = jnp.where(core == 0, ff_here, ff_there).T
        downweight_g = jnp.where(core == 0, ff_there, ff_here)

        (encoder_g, _) = call(
            move, here + v(encoder_g), [((HALF_ENC, D), BF, "v")], [], "encoder_grad"
        )
        s_own = gated([s_part, *s_back], [cq_g, input_g, ff_here, ff_there, encoder_g], "gate_s_far")
        s_other = [send(one, core_to, "s_far") for one in s_own]
        (vectors,) = gated([vectors], s_own[:1], "gate_vectors")
        vectors = jnp.sum(vectors, axis=0)
        ff_at = (h * rows + r) * piece
        upbias_g = lax.dynamic_slice_in_dim(vectors[9:13].reshape(FF), ff_at, piece)
        (sq_g, sk_g, sv_g, so_g), sqb, svb = whole_grads(s_own, s_other, "s")

        return (
            output, input_g, encoder_g,
            sq_g.T, sqb, sk_g.T, sv_g.T, svb, so_g, vectors[8], vectors[6], vectors[7],
            cq_g.T, cqb, ck_g.T, cv_g.T, cvb, co_g, vectors[5],
            vectors[3], vectors[4], upweight_g, upbias_g, downweight_g, vectors[2],
            vectors[0], vectors[1],
        )

    rowed, headed = P(("rows", "heads"), None), P(None, "heads")
    by_head, by_head_rows, whole = P("heads"), P("heads", None), P()
    ffed = ("heads", "rows")
    return jax.shard_map(
        shards,
        mesh=mesh,
        in_specs=(
            rowed, rowed, P("rows", None),
            headed, by_head, headed, headed, by_head, by_head_rows, whole, whole, whole,
            headed, by_head, headed, headed, by_head, by_head_rows, whole, whole, whole,
            whole, whole, whole, whole, whole, whole, rowed,
        ),
        out_specs=(
            rowed, rowed, rowed,
            headed, by_head, headed, headed, by_head, by_head_rows, whole, whole, whole,
            headed, by_head, headed, headed, by_head, by_head_rows, whole, whole, whole,
            P(None, ffed), P(ffed), P(ffed, None), whole, whole, whole,
        ),
        check_vma=False,
    )
```
